32 devices in a mesh: dp: 4 (over y, x), expert: 8 (over z, core).
Axes of the slice: x: 2, y: 2, z: 4, core: 2. Of those that a mesh axis runs over, the one named last changes fastest.
Arguments:
- activations: bfloat16 [4, 1024, 1024], P('dp', 'expert'), may hold values from -6 to 6
- doc_ids: int32 [4, 1024], P('dp', 'expert'), may hold values from 0 to 3, never falling along the last dimension, each value on 1 to 512 neighbouring positions
- routes: int32 [4, 1024, 8], P('dp', 'expert'), may hold values from 0 to 15, all different within a row; in each aligned block of 128 rows (0 to 127, 128 to 255, ..., all dimensions but the last counted through in order) at most 72 rows name the same one
- gate_weights: float32 [4, 1024, 8], P('dp', 'expert'), may hold values from 0.07 to 0.2
- cotangent: bfloat16 [4, 1024, 1024], P('dp', 'expert'), may hold values from -6 to 6
- step_count: int32 [], replicated, may hold values from 1 to 20
- w_attn: float32 [1024, 3072], P(('dp', 'expert'))
- norm_gains: float32 [1024, 2], P(('dp', 'expert'))
- w_expert: float32 [16, 1024, 1536], P('expert', 'dp')
- first_attn: float32 [1024, 3072], P(('dp', 'expert')), may hold values from -0.00030517578 to 0.00030517578
- second_attn: float32 [1024, 3072], P(('dp', 'expert')), may hold values from 1.7659358e-09 to 7.0637434e-09
- first_gains: float32 [1024, 2], P(('dp', 'expert')), may hold values from -0.0012207031 to 0.0012207031
- second_gains: float32 [1024, 2], P(('dp', 'expert')), may hold values from 2.8254973e-08 to 1.13019894e-07
- first_expert: float32 [16, 1024, 1536], P('expert', 'dp'), may hold values from -0.00030517578 to 0.00030517578
- second_expert: float32 [16, 1024, 1536], P('expert', 'dp'), may hold values from 1.7659358e-09 to 7.0637434e-09
Outputs:
- block_out: bfloat16 [4, 1024, 1024], P('dp', 'expert')
- input_grad: float32 [4, 1024, 1024], P('dp', 'expert')
- grad_norm: float32 [], replicated
- new_attn: float32 [1024, 3072], P(('dp', 'expert'))
- new_first_attn: float32 [1024, 3072], P(('dp', 'expert'))
- new_second_attn: float32 [1024, 3072], P(('dp', 'expert'))
- new_gains: float32 [1024, 2], P(('dp', 'expert'))
- new_first_gains: float32 [1024, 2], P(('dp', 'expert'))
- new_second_gains: float32 [1024, 2], P(('dp', 'expert'))
- new_expert: float32 [16, 1024, 1536], P('expert', 'dp')
- new_first_expert: float32 [16, 1024, 1536], P('expert', 'dp')
- new_second_expert: float32 [16, 1024, 1536], P('expert', 'dp')
The draws below stay inside these ranges and needn't reach their ends.
Inputs may be any that keep to these rules, and one draw needn't show every extreme that they name: `routes`: each row names 8 different experts. In each aligned block of 128 rows (the rows of one device) no expert is named by more than 72 rows, a bound that some block reaches. `doc_ids`: document numbers never fall along a sequence; a document has 1 to 512 positions, and one has exactly 512.
All inputs are finite; a program needn't handle non-finite values.
Results may differ from the reference program's by a relative error of at most 0.015.
The reference program's roundings to bfloat16 on the way count: a program that leaves them out, or rounds other values in their place, can miss the bound.
Values may be sent and summed in bfloat16 or wider, within the bound.
A program may use at most 192 MiB of HBM per device.

```python
import math
import jax
import jax.numpy as jnp
import numpy as np
from jax import lax

D = 1024
H = 16
KVH = 8
HD = 64
FF = 512
TOP = 8
TOK_DEV = 128
DOCS = 4
QD = 1024
KVD = 512
QKV = 2048
COLS = 3072
EXPERTS = 16
CAP = 72
LEN = 1024
SEQS = 4
PARAMS = 28313600


def draw_w_attn(key, part):
    key = jax.random.fold_in(key, 11)
    raw_draw = jnp.clip(jax.random.normal(key, (D, COLS), jnp.float32), -5.0, 5.0)
    column = jnp.arange(COLS)
    column_scale = jnp.where(column < QKV, 1.0 / math.sqrt(D), 8.0 / math.sqrt(QD))
    return raw_draw * column_scale[None, :]


def draw_norm_gains(key, part):
    key = jax.random.fold_in(key, 23)
    fraction = jnp.arange(D, dtype=jnp.float32) / (D - 1)
    factor = jax.random.uniform(key, (D, 2), jnp.float32, 0.9, 1.1)
    row_scale = 0.5 * jnp.exp(fraction * math.log(4.0))
    return factor * row_scale[:, None]


def draw_w_expert(key, part):
    key = jax.random.fold_in(key, 37)
    raw_draw = jnp.clip(jax.random.normal(key, (EXPERTS, D, 3 * FF), jnp.float32), -5.0, 5.0)
    column = jnp.arange(3 * FF)
    column_scale = jnp.where(column < 2 * FF, 1.0 / math.sqrt(D), 4.0 / math.sqrt(FF))
    return raw_draw * column_scale[None, None, :]


def block_levels(own_key, dims, pieces, least, high):
    factor_of, own = 1.0, jax.random.fold_in(own_key, 6)
    for position, parts in pieces:
        steps = jnp.exp(jax.random.uniform(jax.random.fold_in(own, position), (parts,), jnp.float32, least / len(pieces), high / len(pieces)))
        factor_of = factor_of * jnp.repeat(steps, dims[position] // parts).reshape([-1 if axis == position else 1 for axis in range(len(dims))])
    return factor_of


def split_up(number_of, total, bound, slope):
    loads = [(1 << 20) // math.isqrt(grade ** slope) + 1 for grade in range(2, number_of + 1)]
    surplus, holding = total - bound - (number_of - 1), [1] * (number_of - 1)
    while surplus > 0:
        candidates = [i for i in range(number_of - 1) if holding[i] < bound]
        pool, left = sum([loads[i] for i in candidates]), surplus
        for i in candidates:
            addition = min(bound - holding[i], max(1, left * loads[i] // pool), surplus)
            holding[i] = holding[i] + addition
            surplus = surplus - addition
    return np.array([bound] + holding)


def uneven_parts(key, count, total, bound, skew):
    if count == 2:
        one = jax.random.randint(key, (), max(1, total - bound), min(bound, total - 1) + 1)
        return jnp.stack([one, total - one])
    tallies = jnp.asarray(split_up(count, total, bound, skew), jnp.int32)
    couples = (count - 1) // 2
    giver, taker = tallies[1:1 + 2 * couples:2], tallies[2:2 + 2 * couples:2]
    margin = jnp.minimum(giver - 1, bound - taker)
    shifted = jax.random.randint(jax.random.fold_in(key, 1), (couples,), 0, 1 << 20) % (margin + 1)
    tallies = tallies.at[1:1 + 2 * couples:2].set(giver - shifted).at[2:2 + 2 * couples:2].set(taker + shifted)
    return tallies[jax.random.permutation(jax.random.fold_in(key, 2), count)]


def deal_out(own_key, own, number, rows, count, top, limit, lean):
    sequence = jax.random.permutation(own_key, count)
    heavy_load, common = portions_of(count, rows * top, limit, lean, True), portions_of(count, rows * top, limit, lean, False)
    places = jnp.arange(count)

    def named(sizes, rotation):
        used = int((sizes > 0).sum())
        fixed = max(1, used // 4)
        moved = fixed + (places - fixed + rotation * (used - fixed)) % max(1, count - fixed)
        return jnp.zeros((count,), jnp.int32).at[sequence[jnp.where(places < fixed, places, moved)]].set(jnp.asarray(sizes, jnp.int32))

    sizes = jnp.where(number % 4 == 0, named(heavy_load, number // 4), named(common, number - number // 4 - 1))
    mixed = jax.random.permutation(jax.random.fold_in(own, 3), count)
    donor, receiver = mixed[0:count // 2 * 2:2], mixed[1:count // 2 * 2:2]
    slack = jnp.minimum(sizes[donor] - 1, limit - sizes[receiver]) // 2
    slack = jnp.where((donor == sequence[0]) | (receiver == sequence[0]) | (sizes[receiver] == 0), 0, jnp.maximum(slack, 0))
    moved = jax.random.randint(jax.random.fold_in(own, 4), (count // 2,), 0, 1 << 20) % (slack + 1)
    sizes = sizes.at[donor].add(-moved).at[receiver].add(moved)
    items = jnp.searchsorted(jnp.cumsum(sizes), jnp.arange(rows * top), side="right").astype(jnp.int32)
    table = items.reshape(top, rows).T
    table = table[jax.random.permutation(jax.random.fold_in(own, 1), rows)]
    rotation = jax.random.randint(jax.random.fold_in(own, 2), (rows, 1), 0, top)
    return jnp.take_along_axis(table, (jnp.arange(top)[None, :] + rotation) % top, axis=1)


def portions_of(amount, total, bound, slope, full):
    loads = [(1 << 20) // math.isqrt(rank ** slope) + 1 for rank in range(1, amount + 1)]
    largest = bound if full else min(bound, max(-(-total // amount), total * loads[0] // sum(loads)))
    least = 1 if total - largest >= amount - 1 else 0
    given, surplus = [largest] + [least] * (amount - 1), total - largest - least * (amount - 1)
    while surplus > 0:
        candidates = [i for i in range(1, amount) if given[i] < largest] or [i for i in range(1, amount) if given[i] < bound]
        mass, left = sum([loads[i] for i in candidates]), surplus
        for i in candidates:
            more = min(bound - given[i], max(1, left * loads[i] // mass), surplus)
            given[i] = given[i] + more
            surplus = surplus - more
    return np.array(given)


def scatter_about(own_key, extent, deviation, reach, split=(), kind=jnp.bfloat16):
    array = jax.random.normal(own_key, extent, jnp.float32) * deviation
    if len(split) > 0:
        array = block_levels(own_key, extent, split, -0.22, 0.18) * array
    return jnp.clip(array, min=-reach, max=reach).astype(kind)


def setup_inputs(seed: int = 0) -> dict:
    arg_keys = jax.random.split(jax.random.key(seed), 16)
    activations = scatter_about(arg_keys[0], (SEQS, LEN, D), 1.0, 6.0, ((0, 4), (1, 8)))
    doc_ids = jax.vmap(lambda own: jnp.searchsorted(jnp.cumsum(uneven_parts(own, DOCS, LEN, LEN // 2, 1)), jnp.arange(LEN), side="right"))(jax.random.split(arg_keys[1], SEQS)).reshape((SEQS, LEN)).astype(jnp.int32)
    routes_keys = jax.random.split(jax.random.fold_in(arg_keys[2], 1), SEQS * LEN // TOK_DEV)
    routes_turns = jax.random.permutation(jax.random.fold_in(arg_keys[2], 3), SEQS * LEN // TOK_DEV)
    routes = jax.vmap(lambda own, number: deal_out(jax.random.fold_in(arg_keys[2], 2), own, number, TOK_DEV, EXPERTS, TOP, CAP, 1))(routes_keys, routes_turns).reshape((SEQS, LEN, TOP))
    gate_weights = jnp.clip(jnp.exp(math.log(0.2) - 1.0498221 * jax.random.uniform(arg_keys[3], (SEQS, LEN, TOP), jnp.float32) ** block_levels(arg_keys[3], (SEQS, LEN, TOP), ((0, 4), (1, 8)), -0.2, 0.2)), 0.07, 0.2)
    cotangent = scatter_about(arg_keys[4], (SEQS, LEN, D), 1.0, 6.0, ((0, 4), (1, 8)))
    step_count = jax.random.randint(arg_keys[5], (), 1, 21).astype(jnp.int32)
    w_attn = draw_w_attn(jax.random.fold_in(arg_keys[15], 71), 0)
    norm_gains = draw_norm_gains(jax.random.fold_in(arg_keys[15], 71), 0)
    w_expert = draw_w_expert(jax.random.fold_in(arg_keys[15], 71), 0)
    first_attn = scatter_about(arg_keys[9], (D, COLS), (0.11 / PARAMS ** 0.5), 0.00030517578, ((0, 32),), jnp.float32)
    second_attn = jnp.clip(jnp.exp(math.log(7.0637433680076356e-09) - 1.3862944 * jax.random.uniform(arg_keys[10], (D, COLS), jnp.float32) ** block_levels(arg_keys[10], (D, COLS), ((0, 32),), -0.2, 0.2)), 1.7659358420019089e-09, 7.0637433680076356e-09)
    first_gains = scatter_about(arg_keys[11], (D, 2), (0.44 / PARAMS ** 0.5), 0.0012207031, ((0, 32),), jnp.float32)
    second_gains = jnp.clip(jnp.exp(math.log(1.1301989388812217e-07) - 1.3862944 * jax.random.uniform(arg_keys[12], (D, 2), jnp.float32) ** block_levels(arg_keys[12], (D, 2), ((0, 32),), -0.2, 0.2)), 2.8254973472030542e-08, 1.1301989388812217e-07)
    first_expert = scatter_about(arg_keys[13], (EXPERTS, D, 3 * FF), (0.11 / PARAMS ** 0.5), 0.00030517578, ((0, 8), (1, 4)), jnp.float32)
    second_expert = jnp.clip(jnp.exp(math.log(7.0637433680076356e-09) - 1.3862944 * jax.random.uniform(arg_keys[14], (EXPERTS, D, 3 * FF), jnp.float32) ** block_levels(arg_keys[14], (EXPERTS, D, 3 * FF), ((0, 8), (1, 4)), -0.2, 0.2)), 1.7659358420019089e-09, 7.0637433680076356e-09)
    return {"activations": activations, "doc_ids": doc_ids, "routes": routes, "gate_weights": gate_weights, "cotangent": cotangent, "step_count": step_count, "w_attn": w_attn, "norm_gains": norm_gains, "w_expert": w_expert, "first_attn": first_attn, "second_attn": second_attn, "first_gains": first_gains, "second_gains": second_gains, "first_expert": first_expert, "second_expert": second_expert}


EPSILON = 1e-05
ROPE_BASE = 10000.0
CLIP_NORM = 1.0
BETA_ONE = 0.9
BETA_TWO = 0.95
ADAM_EPSILON = 1e-08
LEARN_RATE = 0.03
GAIN_RATE = 0.4
WEIGHT_DECAY = 0.1
HIGHEST = lax.Precision.HIGHEST

@jax.custom_vjp
def low(v):
    return lax.optimization_barrier(v.astype(jnp.bfloat16)).astype(jnp.float32)

@jax.custom_vjp
def low_back(v):
    return v

def low_keep(v):
    return (low(v), None)

def low_pass(kept, grad):
    return (grad,)

def back_keep(v):
    return (v, None)

def back_low(kept, grad):
    return (low(grad),)
low.defvjp(low_keep, low_pass)
low_back.defvjp(back_keep, back_low)

def rms_scale(values, gain):
    return values * lax.rsqrt(lax.optimization_barrier(jnp.mean(values * values, axis=-1, keepdims=True)) + EPSILON) * gain

def rope_tables(positions, head_width):
    halves = jnp.arange(head_width // 2, dtype=jnp.float32)
    inverse = ROPE_BASE ** (-2.0 * halves / head_width)
    angles = positions.astype(jnp.float32)[:, None] * inverse[None, :]
    angles = jnp.concatenate([angles, angles], axis=-1)
    return (jnp.cos(angles)[:, None, :], jnp.sin(angles)[:, None, :])

def rotate(values, cosine, sine_table):
    middle = values.shape[-1] // 2
    turned = jnp.concatenate([-values[..., middle:], values[..., :middle]], axis=-1)
    return values * cosine + turned * sine_table

def expert_tables(route_rows, gate_rows):
    block_count = LEN // TOK_DEV
    flat_routes = route_rows.reshape(block_count, TOK_DEV * TOP)
    one_hot = (flat_routes[:, :, None] == jnp.arange(EXPERTS, dtype=jnp.int32)[None, None, :]).astype(jnp.int32)
    ranking = lax.optimization_barrier(jnp.sum((jnp.cumsum(one_hot, axis=1) - 1) * one_hot, axis=2))
    places = jnp.arange(block_count, dtype=jnp.int32)[:, None] * CAP + ranking
    owners = jnp.arange(LEN * TOP, dtype=jnp.int32) // TOP
    row_index = jnp.zeros((EXPERTS, block_count * CAP), jnp.int32).at[flat_routes.reshape(-1), places.reshape(-1)].set(owners)
    slot_gate = jnp.zeros((EXPERTS, block_count * CAP), gate_rows.dtype).at[flat_routes.reshape(-1), places.reshape(-1)].set(gate_rows.reshape(-1))
    return (row_index, slot_gate)

def attention(queries, key_heads, value_heads, documents):
    group_size = H // KVH
    keys_wide = jnp.repeat(key_heads, group_size, axis=1)
    values_wide = jnp.repeat(value_heads, group_size, axis=1)
    query_block = min(512, LEN)
    positions = jnp.arange(LEN, dtype=jnp.int32)

    def one_block(block_id):
        first_row = block_id * query_block
        query_rows = lax.dynamic_slice_in_dim(queries, first_row, query_block, 0)
        raw_scores = low_back(jnp.einsum('qhd,khd->hqk', query_rows, keys_wide, precision=HIGHEST) * HD ** (-0.5))
        query_pos = lax.dynamic_slice_in_dim(positions, first_row, query_block, 0)
        query_doc = lax.dynamic_slice_in_dim(documents, first_row, query_block, 0)
        visible = (positions[None, :] <= query_pos[:, None]) & (documents[None, :] == query_doc[:, None])
        masked = jnp.where(visible[None], raw_scores, -1e+30)
        log_total = jax.nn.logsumexp(masked, axis=-1, keepdims=True)
        weights_low = low(jnp.exp(masked - log_total))
        return jnp.einsum('hqk,khd->qhd', weights_low, values_wide, precision=HIGHEST)
    result = lax.map(jax.checkpoint(one_block), jnp.arange(LEN // query_block, dtype=jnp.int32))
    return result.reshape(LEN, H * HD)

def sequence_layer(weights, tables, inputs):
    attn_cols, gain_pair, expert_cols = weights
    cosine, sine_table = tables
    hidden_in, documents, row_index, slot_gate = inputs
    normed = low(rms_scale(hidden_in, gain_pair[:, 0]))
    projected = low_back(jnp.dot(normed, attn_cols[:, :QKV], precision=HIGHEST))
    queries = low(rotate(projected[:, :QD].reshape(LEN, H, HD), cosine, sine_table))
    key_heads = low(rotate(projected[:, QD:QD + KVD].reshape(LEN, KVH, HD), cosine, sine_table))
    value_heads = low(projected[:, QD + KVD:].reshape(LEN, KVH, HD))
    attended = low_back(low(attention(queries, key_heads, value_heads, documents)))
    branch = low_back(jnp.dot(attended, attn_cols[:, QKV:].T, precision=HIGHEST))
    residual = hidden_in + branch
    normed_two = low(rms_scale(residual, gain_pair[:, 1]))
    expert_rows = low_back(normed_two[row_index])
    gate_up = low_back(jnp.einsum('esd,edf->esf', expert_rows, expert_cols[:, :, :2 * FF], precision=HIGHEST))
    activated = low(jax.nn.silu(gate_up[..., :FF]) * gate_up[..., FF:])
    expert_out = low_back(low(jnp.einsum('esf,edf->esd', activated, expert_cols[:, :, 2 * FF:], precision=HIGHEST)))
    weighted = (expert_out * slot_gate[..., None]).reshape(-1, D)
    combined = jnp.zeros_like(residual).at[row_index.reshape(-1)].add(weighted)
    return residual + combined

def adam_update(weight, moment_one, second, gradient, steps_done, decay_rate, step_rate):
    first_new = BETA_ONE * moment_one + (1.0 - BETA_ONE) * gradient
    second_new = BETA_TWO * second + (1.0 - BETA_TWO) * gradient * gradient
    first_hat = first_new / (1.0 - BETA_ONE ** steps_done)
    second_hat = second_new / (1.0 - BETA_TWO ** steps_done)
    weight_new = weight - step_rate * (first_hat / (jnp.sqrt(second_hat) + ADAM_EPSILON) + decay_rate * weight)
    return (weight_new, first_new, second_new)

def reference(activations, doc_ids, routes, gate_weights, cotangent, step_count, w_attn, norm_gains, w_expert, first_attn, second_attn, first_gains, second_gains, first_expert, second_expert):
    cosine, sine_table = rope_tables(jnp.arange(LEN, dtype=jnp.int32), HD)
    row_index, slot_gate = jax.vmap(expert_tables)(routes, gate_weights)

    def forward(inputs_all, attn_cols, gain_pair, expert_cols):
        weights = (low(attn_cols), low(gain_pair), low(expert_cols))

        def visit(unused, inputs):
            return (unused, jax.checkpoint(sequence_layer)(weights, (cosine, sine_table), inputs))
        _, outputs = lax.scan(visit, jnp.zeros((), jnp.int32), (inputs_all, doc_ids, row_index, slot_gate))
        return outputs
    outputs, pull_back = jax.vjp(forward, activations.astype(jnp.float32), w_attn, norm_gains, w_expert)
    grad_in, grad_attn, grad_gains, grad_expert = pull_back(cotangent.astype(jnp.float32))
    squares = jnp.sum(grad_attn * grad_attn) + jnp.sum(grad_gains * grad_gains) + jnp.sum(grad_expert * grad_expert)
    grad_norm = jnp.sqrt(squares)
    clip_factor = jnp.minimum(1.0, CLIP_NORM / (grad_norm + 1e-06))
    steps_done = step_count.astype(jnp.float32)
    attn_new = adam_update(w_attn, first_attn, second_attn, grad_attn * clip_factor, steps_done, WEIGHT_DECAY, LEARN_RATE)
    gains_new = adam_update(norm_gains, first_gains, second_gains, grad_gains * clip_factor, steps_done, 0.0, GAIN_RATE)
    expert_new = adam_update(w_expert, first_expert, second_expert, grad_expert * clip_factor, steps_done, WEIGHT_DECAY, LEARN_RATE)
    return (outputs.astype(jnp.bfloat16), grad_in, grad_norm, attn_new[0], attn_new[1], attn_new[2], gains_new[0], gains_new[1], gains_new[2], expert_new[0], expert_new[1], expert_new[2])
```

```python
import jax
import jax.numpy as jnp
from jax import lax
from jax.sharding import PartitionSpec as P
import numpy as np
from jax.experimental import pallas as pl
from jax.experimental.pallas import tpu as pltpu

D = 1024
H = 16
KVH = 8
HD = 64
FF = 512
TOP = 8
QD = 1024
KVD = 512
QKV = 2048


EPSILON = 1e-05
ROPE_BASE = 10000.0
CLIP_NORM = 1.0
BETA_ONE = 0.9
BETA_TWO = 0.95
ADAM_EPSILON = 1e-08
LEARN_RATE = 0.03
GAIN_RATE = 0.4
WEIGHT_DECAY = 0.1


def rms_scale(values, gain):
    return values * lax.rsqrt(jnp.mean(values * values, axis=-1, keepdims=True) + EPSILON) * gain


def rope_tables(positions, head_width):
    halves = jnp.arange(head_width // 2, dtype=jnp.float32)
    inverse = ROPE_BASE ** (-2.0 * halves / head_width)
    angles = positions.astype(jnp.float32)[:, None] * inverse[None, :]
    angles = jnp.concatenate([angles, angles], axis=-1)
    return (jnp.cos(angles)[:, None, :], jnp.sin(angles)[:, None, :])


def rotate(values, cosine, sine_table):
    middle = values.shape[-1] // 2
    turned = jnp.concatenate([-values[..., middle:], values[..., :middle]], axis=-1)
    return values * cosine + turned * sine_table


def unrotate(gradient, cosine, sine_table):
    middle = gradient.shape[-1] // 2
    product = gradient * sine_table
    turned = jnp.concatenate([product[..., middle:], -product[..., :middle]], axis=-1)
    return gradient * cosine + turned


def adam_update(weight, moment_one, second, gradient, steps_done, decay_rate, step_rate):
    first_new = BETA_ONE * moment_one + (1.0 - BETA_ONE) * gradient
    second_new = BETA_TWO * second + (1.0 - BETA_TWO) * gradient * gradient
    first_hat = first_new / (1.0 - BETA_ONE**steps_done)
    second_hat = second_new / (1.0 - BETA_TWO**steps_done)
    weight_new = weight - step_rate * (
        first_hat / (jnp.sqrt(second_hat) + ADAM_EPSILON) + decay_rate * weight
    )
    return (weight_new, first_new, second_new)


def attn_fetch(w_attn, norm_gains):
    return (
        lax.all_gather(w_attn.astype(jnp.bfloat16), ("dp", "expert"), axis=0, tiled=True),
        lax.all_gather(norm_gains.astype(jnp.bfloat16), ("dp", "expert"), axis=0, tiled=True),
    )


def expert_fetch(w_expert):
    return lax.all_gather(w_expert.astype(jnp.bfloat16), "dp", axis=1, tiled=True)


def to_owner(buffer):
    return lax.all_to_all(buffer, "expert", split_axis=0, concat_axis=1, tiled=True)


def to_sender(buffer):
    return lax.all_to_all(buffer, "expert", split_axis=1, concat_axis=0, tiled=True)


def expert_forward(received, expert_cols):
    gate_up = jnp.einsum(
        "esd,edf->esf", received, expert_cols[:, :, : 2 * FF], preferred_element_type=jnp.float32
    )
    activated = (jax.nn.silu(gate_up[..., :FF]) * gate_up[..., FF:]).astype(jnp.bfloat16)
    return (gate_up, activated)


def general_body(
    activations,
    doc_ids,
    routes,
    gate_weights,
    cotangent,
    step_count,
    w_attn,
    norm_gains,
    w_expert,
    first_attn,
    second_attn,
    first_gains,
    second_gains,
    first_expert,
    second_expert,
):
    row_count = activations.shape[1]
    span_size = lax.axis_size("expert")
    shard_pos = lax.axis_index("expert")
    seq_length = row_count * span_size
    expert_total = w_expert.shape[0] * span_size
    capacity = (row_count * TOP * 9 + expert_total * 8 - 1) // (expert_total * 8)
    group_size = H // KVH
    score_scale = HD ** (-0.5)
    hidden_in = activations[0].astype(jnp.float32)
    upstream = cotangent[0].astype(jnp.float32)
    attn_cols, gain_pair = attn_fetch(w_attn, norm_gains)
    expert_cols = expert_fetch(w_expert)
    gain_one = gain_pair[:, 0].astype(jnp.float32)
    gain_two = gain_pair[:, 1].astype(jnp.float32)
    w_project = attn_cols[:, :QKV]
    w_output = attn_cols[:, QKV:]
    normed = rms_scale(hidden_in, gain_one).astype(jnp.bfloat16)
    projected = jnp.dot(normed, w_project, preferred_element_type=jnp.float32)
    positions = shard_pos * row_count + jnp.arange(row_count, dtype=jnp.int32)
    cosine, sine_table = rope_tables(positions, HD)
    queries = rotate(projected[:, :QD].reshape(row_count, H, HD), cosine, sine_table).astype(
        jnp.bfloat16
    )
    key_heads = rotate(
        projected[:, QD : QD + KVD].reshape(row_count, KVH, HD), cosine, sine_table
    ).astype(jnp.bfloat16)
    value_heads = projected[:, QD + KVD :].astype(jnp.bfloat16)
    key_all, value_all, doc_all = (
        lax.all_gather(key_heads.reshape(row_count, KVD), "expert", axis=0, tiled=True),
        lax.all_gather(value_heads, "expert", axis=0, tiled=True),
        lax.all_gather(doc_ids[0].astype(jnp.bfloat16), "expert", axis=0, tiled=True),
    )
    key_docs = doc_all.astype(jnp.int32)
    query_docs = doc_ids[0]
    query_groups = queries.reshape(row_count, KVH, group_size, HD)
    key_block = min(512, seq_length)
    needed = (shard_pos * row_count + row_count + key_block - 1) // key_block

    def block_scores(block_id):
        first_key = block_id * key_block
        key_part = lax.dynamic_slice_in_dim(key_all, first_key, key_block, 0).reshape(
            key_block, KVH, HD
        )
        raw_scores = (
            jnp.einsum("tgrd,kgd->grtk", query_groups, key_part, preferred_element_type=jnp.float32)
            * score_scale
        )
        key_pos = first_key + jnp.arange(key_block, dtype=jnp.int32)
        key_doc = lax.dynamic_slice_in_dim(key_docs, first_key, key_block, 0)
        visible = (key_pos[None, :] <= positions[:, None]) & (
            key_doc[None, :] == query_docs[:, None]
        )
        return (raw_scores, visible, key_part)

    def value_part(block_id):
        return lax.dynamic_slice_in_dim(value_all, block_id * key_block, key_block, 0).reshape(
            key_block, KVH, HD
        )

    def total_step(block_id, running):
        row_peak, row_total = running
        raw_scores, visible, _ = block_scores(block_id)
        masked = jnp.where(visible, raw_scores, -1e30)
        new_peak = jnp.maximum(row_peak, jnp.max(masked, axis=-1))
        scaled = jnp.where(visible, jnp.exp(masked - new_peak[..., None]), 0.0)
        return (new_peak, row_total * jnp.exp(row_peak - new_peak) + jnp.sum(scaled, axis=-1))

    start_peak = jnp.full((KVH, group_size, row_count), -1e30, jnp.float32)
    start_total = jnp.zeros((KVH, group_size, row_count), jnp.float32)
    row_peak, row_total = lax.fori_loop(0, needed, total_step, (start_peak, start_total))
    log_total = row_peak + jnp.log(row_total)

    def exact_probs(raw_scores, visible):
        return jnp.exp(jnp.where(visible, raw_scores - log_total[..., None], -1e30))

    def output_step(block_id, summed):
        raw_scores, visible, _ = block_scores(block_id)
        weights_low = exact_probs(raw_scores, visible).astype(jnp.bfloat16)
        return summed + jnp.einsum(
            "grtk,kgd->tgrd", weights_low, value_part(block_id), preferred_element_type=jnp.float32
        )

    attended = lax.fori_loop(
        0, needed, output_step, jnp.zeros((row_count, KVH, group_size, HD), jnp.float32)
    )
    attended = attended.reshape(row_count, QD).astype(jnp.bfloat16)
    branch = jnp.einsum("tc,dc->td", attended, w_output, preferred_element_type=jnp.float32)
    residual = hidden_in + branch
    normed_two = rms_scale(residual, gain_two).astype(jnp.bfloat16)
    flat_routes = routes[0].reshape(-1)
    one_hot = (flat_routes[:, None] == jnp.arange(expert_total, dtype=jnp.int32)[None, :]).astype(
        jnp.int32
    )
    ranking = jnp.sum((jnp.cumsum(one_hot, axis=0) - 1) * one_hot, axis=1)
    places = flat_routes * capacity + ranking
    owners = jnp.arange(row_count * TOP, dtype=jnp.int32) // TOP
    source = jnp.zeros((expert_total * capacity,), jnp.int32).at[places].set(owners)
    filled = jnp.zeros((expert_total * capacity,), jnp.int32).at[places].set(1) > 0
    slot_gate = (
        jnp.zeros((expert_total * capacity,), jnp.float32)
        .at[places]
        .set(gate_weights[0].reshape(-1))
    )
    outgoing = jnp.where(filled[:, None], normed_two[source], jnp.zeros((), jnp.bfloat16)).reshape(
        expert_total, capacity, D
    )
    received = to_owner(outgoing)
    gate_up, activated = expert_forward(received, expert_cols)
    expert_out = jnp.einsum(
        "esf,edf->esd", activated, expert_cols[:, :, 2 * FF :], preferred_element_type=jnp.float32
    ).astype(jnp.bfloat16)
    returned = to_sender(expert_out).reshape(expert_total * capacity, D)
    picked = returned[places].reshape(row_count, TOP, D).astype(jnp.float32)
    combined = jnp.sum(gate_weights[0][..., None] * picked, axis=1)
    block_result = (residual + combined).astype(jnp.bfloat16)
    slot_grad = jnp.where(filled[:, None], slot_gate[:, None] * upstream[source], 0.0)
    slot_grad = slot_grad.astype(jnp.bfloat16).reshape(expert_total, capacity, D)
    owner_grad = to_owner(slot_grad)
    attn_cols, gain_pair = attn_fetch(w_attn, norm_gains)
    w_project = attn_cols[:, :QKV]
    w_output = attn_cols[:, QKV:]
    expert_cols = expert_fetch(w_expert)
    gate_up, activated = expert_forward(received, expert_cols)
    gate_part = gate_up[..., :FF]
    up_part = gate_up[..., FF:]
    sigmoid_gate = jax.nn.sigmoid(gate_part)
    act_grad = jnp.einsum(
        "esd,edf->esf", owner_grad, expert_cols[:, :, 2 * FF :], preferred_element_type=jnp.float32
    )
    gate_grad = act_grad * up_part * sigmoid_gate * (1.0 + gate_part * (1.0 - sigmoid_gate))
    lift_grad = act_grad * gate_part * sigmoid_gate
    mixed_grad = jnp.concatenate([gate_grad, lift_grad], axis=-1).astype(jnp.bfloat16)
    down_grad = jnp.einsum(
        "esf,esd->edf", activated, owner_grad, preferred_element_type=jnp.float32
    )
    inward_grad = jnp.einsum(
        "esd,esf->edf", received, mixed_grad, preferred_element_type=jnp.float32
    )
    row_grads = jnp.einsum(
        "esf,edf->esd", mixed_grad, expert_cols[:, :, : 2 * FF], preferred_element_type=jnp.float32
    ).astype(jnp.bfloat16)
    back_rows = to_sender(row_grads).reshape(expert_total * capacity, D)
    normed_two_grad = jnp.sum(
        back_rows[places].reshape(row_count, TOP, D).astype(jnp.float32), axis=1
    )
    _, second_pull = jax.vjp(rms_scale, residual, gain_two)
    resid_grad, gain_two_grad = second_pull(normed_two_grad)
    resid_grad = upstream + resid_grad
    branch_grad = resid_grad.astype(jnp.bfloat16)
    output_grad = jnp.einsum("td,tc->dc", branch_grad, attended, preferred_element_type=jnp.float32)
    attended_grad = jnp.dot(branch_grad, w_output, preferred_element_type=jnp.float32).astype(
        jnp.bfloat16
    )
    grad_groups = attended_grad.reshape(row_count, KVH, group_size, HD)

    def delta_step(block_id, summed):
        raw_scores, visible, _ = block_scores(block_id)
        probs_full = exact_probs(raw_scores, visible)
        prob_grad = jnp.einsum(
            "tgrd,kgd->grtk", grad_groups, value_part(block_id), preferred_element_type=jnp.float32
        )
        return summed + jnp.sum(probs_full * prob_grad, axis=-1)

    delta_rows = lax.fori_loop(
        0, needed, delta_step, jnp.zeros((KVH, group_size, row_count), jnp.float32)
    )

    def grad_step(block_id, running):
        query_grad, key_grad, value_grad = running
        raw_scores, visible, key_part = block_scores(block_id)
        probs_full = exact_probs(raw_scores, visible)
        prob_grad = jnp.einsum(
            "tgrd,kgd->grtk", grad_groups, value_part(block_id), preferred_element_type=jnp.float32
        )
        score_grad = (probs_full * (prob_grad - delta_rows[..., None])).astype(jnp.bfloat16)
        query_grad = (
            query_grad
            + jnp.einsum("grtk,kgd->tgrd", score_grad, key_part, preferred_element_type=jnp.float32)
            * score_scale
        )
        key_piece = (
            jnp.einsum(
                "grtk,tgrd->kgd", score_grad, query_groups, preferred_element_type=jnp.float32
            )
            * score_scale
        )
        value_piece = jnp.einsum(
            "grtk,tgrd->kgd",
            probs_full.astype(jnp.bfloat16),
            grad_groups,
            preferred_element_type=jnp.float32,
        )
        first_key = block_id * key_block
        key_grad = lax.dynamic_update_slice_in_dim(
            key_grad, key_piece.reshape(key_block, KVD), first_key, 0
        )
        value_grad = lax.dynamic_update_slice_in_dim(
            value_grad, value_piece.reshape(key_block, KVD), first_key, 0
        )
        return (query_grad, key_grad, value_grad)

    start_grads = (
        jnp.zeros((row_count, KVH, group_size, HD), jnp.float32),
        jnp.zeros((seq_length, KVD), jnp.float32),
        jnp.zeros((seq_length, KVD), jnp.float32),
    )
    query_grad, key_grad, value_grad = lax.fori_loop(0, needed, grad_step, start_grads)
    key_sum, value_sum = (
        lax.psum_scatter(key_grad, "expert", scatter_dimension=0, tiled=True),
        lax.psum_scatter(value_grad, "expert", scatter_dimension=0, tiled=True),
    )
    query_back = unrotate(query_grad.reshape(row_count, H, HD), cosine, sine_table).reshape(
        row_count, QD
    )
    key_back = unrotate(key_sum.reshape(row_count, KVH, HD), cosine, sine_table).reshape(
        row_count, KVD
    )
    project_grad = jnp.concatenate([query_back, key_back, value_sum], axis=1).astype(jnp.bfloat16)
    weight_grad_qkv = jnp.einsum(
        "td,tc->dc", normed, project_grad, preferred_element_type=jnp.float32
    )
    normed_grad = jnp.einsum(
        "tc,dc->td", project_grad, w_project, preferred_element_type=jnp.float32
    )
    _, first_pull = jax.vjp(rms_scale, hidden_in, gain_one)
    input_part, gain_one_grad = first_pull(normed_grad)
    input_total = resid_grad + input_part
    attn_partial = jnp.concatenate([weight_grad_qkv, output_grad], axis=1)
    gain_partial = jnp.stack([gain_one_grad, gain_two_grad], axis=1)
    grad_attn, grad_gains = (
        lax.psum_scatter(attn_partial, ("dp", "expert"), scatter_dimension=0, tiled=True),
        lax.psum_scatter(gain_partial, ("dp", "expert"), scatter_dimension=0, tiled=True),
    )
    grad_expert = lax.psum_scatter(
        jnp.concatenate([inward_grad, down_grad], axis=2).astype(jnp.bfloat16),
        "dp",
        scatter_dimension=1,
        tiled=True,
    ).astype(jnp.float32)
    local_squares = (
        jnp.sum(grad_attn * grad_attn)
        + jnp.sum(grad_gains * grad_gains)
        + jnp.sum(grad_expert * grad_expert)
    )
    grad_norm = jnp.sqrt(lax.psum(local_squares, ("dp", "expert")))
    clip_factor = jnp.minimum(1.0, CLIP_NORM / (grad_norm + 1e-06))
    steps_done = step_count.astype(jnp.float32)
    attn_new = adam_update(
        w_attn,
        first_attn,
        second_attn,
        grad_attn * clip_factor,
        steps_done,
        WEIGHT_DECAY,
        LEARN_RATE,
    )
    gains_new = adam_update(
        norm_gains, first_gains, second_gains, grad_gains * clip_factor, steps_done, 0.0, GAIN_RATE
    )
    expert_new = adam_update(
        w_expert,
        first_expert,
        second_expert,
        grad_expert * clip_factor,
        steps_done,
        WEIGHT_DECAY,
        LEARN_RATE,
    )
    return (
        block_result[None],
        input_total[None],
        grad_norm,
        attn_new[0],
        attn_new[1],
        attn_new[2],
        gains_new[0],
        gains_new[1],
        gains_new[2],
        expert_new[0],
        expert_new[1],
        expert_new[2],
    )


def fits(mesh):
    return dict(mesh.shape) == {"dp": 4, "expert": KVH}


def half_turn(tile):
    lane = lax.broadcasted_iota(jnp.int32, tile.shape, tile.ndim - 1)
    ahead = jnp.roll(tile, -(HD // 2), axis=-1)
    behind = jnp.roll(tile, HD // 2, axis=-1)
    return jnp.where(lane % HD < HD // 2, ahead, behind)


def head_tables(length):
    cosine, sine = rope_tables(jnp.arange(length, dtype=jnp.int32), HD)
    cosine, sine = cosine[:, 0], sine[:, 0]
    lane = jnp.arange(HD)
    signed = jnp.where(lane < HD // 2, -sine, sine)
    ones, zeros = jnp.ones_like(cosine), jnp.zeros_like(sine)
    return (
        jnp.concatenate([cosine, cosine, cosine, ones], axis=1),
        jnp.concatenate([signed, signed, signed, zeros], axis=1),
    )


def group_columns(weights, groups):
    rows = weights.shape[0]
    parts = [
        weights[:, :QD].reshape(rows, groups, -1),
        weights[:, QD : QD + KVD].reshape(rows, groups, -1),
        weights[:, QD + KVD : QKV].reshape(rows, groups, -1),
        weights[:, QKV:].reshape(rows, groups, -1),
    ]
    return jnp.concatenate(parts, axis=2).transpose(1, 0, 2)


def ungroup_columns(grouped):
    rows = grouped.shape[1]
    g = grouped.transpose(1, 0, 2)
    parts = [g[:, :, :128], g[:, :, 128:192], g[:, :, 192:256], g[:, :, 256:]]
    return jnp.concatenate([p.reshape(rows, -1) for p in parts], axis=1)


def remote(source, target, sent, landed, device):
    return pltpu.make_async_remote_copy(
        src_ref=source,
        dst_ref=target,
        send_sem=sent,
        recv_sem=landed,
        device_id=device,
        device_id_type=pl.DeviceIdType.MESH,
    )


def whereabouts():
    i, e = lax.axis_index("dp"), lax.axis_index("expert")
    return i, e, e // 2, lax.rem(e, 2)


def greet(i, e):
    barrier = pltpu.get_barrier_semaphore()
    others = [(i, lax.rem(e + k, SPAN)) for k in range(1, SPAN)]
    others += [(lax.rem(i + k, PLANE), e) for k in range(1, PLANE)]
    for device in others:
        pl.semaphore_signal(barrier, inc=1, device_id=device, device_id_type=pl.DeviceIdType.MESH)
    pl.semaphore_wait(barrier, len(others))


class LineGather:
    def __init__(self, slot, where, sent, passed, landed):
        self.slot, self.where = slot, where
        self.sent, self.passed, self.landed = sent, passed, landed
        self.live = []

    def _copy(self, source, index, sem, device):
        place = self.slot(index)
        return remote(place if source is None else source, place, sem, self.landed.at[index], device)

    def start(self, source=None):
        i, e, z, c = self.where
        for k in range(1, LINE):
            there = lax.rem(z + k, LINE) * 2 + c
            copy = self._copy(source, e, self.sent.at[k], (i, there))
            copy.start()
            self.live.append(copy)
        copy = self._copy(source, e, self.sent.at[0], (i, z * 2 + 1 - c))
        copy.start()
        self.live.append(copy)

    def wait(self, index):
        i, e, z, c = self.where
        self._copy(None, index, self.sent.at[0], (i, z * 2 + 1 - c)).wait_recv()

    def sibling(self):
        _, e, z, c = self.where
        return z * 2 + 1 - c

    def near(self, k):
        _, e, z, c = self.where
        return lax.rem(z + k, LINE) * 2 + c

    def far(self, k):
        _, e, z, c = self.where
        return lax.rem(z + k, LINE) * 2 + 1 - c

    def forward(self, k):
        i, e, z, c = self.where
        index = self.near(k)
        self.wait(index)
        copy = self._copy(None, index, self.passed.at[k - 1], (i, z * 2 + 1 - c))
        copy.start()
        self.live.append(copy)

    def rest(self):
        self.wait(self.sibling())
        for k in range(1, LINE):
            self.wait(self.far(k))

    def drain(self):
        for copy in self.live:
            copy.wait_send()


def half_turn_tile(tile):
    pieces = []
    for first in range(0, tile.shape[1], 128):
        part = tile[:, first : first + 128]
        lane = lax.broadcasted_iota(jnp.int32, part.shape, 1)
        ahead = pltpu.roll(part, 128 - HD // 2, 1)
        behind = pltpu.roll(part, HD // 2, 1)
        pieces.append(jnp.where(lax.rem(lane, HD) < HD // 2, ahead, behind))
    return jnp.concatenate(pieces, axis=1)


def rms_rows(values):
    return lax.rsqrt(jnp.mean(values * values, axis=-1, keepdims=True) + EPSILON)


def dot(a, b, contract):
    return lax.dot_general(a, b, (contract, ((), ())), preferred_element_type=jnp.float32)


NN, NT, TN = ((1,), (0,)), ((1,), (1,)), ((0,), (0,))
LINE, SPAN, PLANE = 4, 8, 4
QUERY_BLOCK = 256


def block_view(first, reach):
    return max(0, first - reach), first + QUERY_BLOCK


def visible_keys(first, low, high, docs_row, docs_col):
    shape = (QUERY_BLOCK, high - low)
    key = lax.broadcasted_iota(jnp.int32, shape, 1) + low
    query = lax.broadcasted_iota(jnp.int32, shape, 0) + first
    same = docs_row[:, low:high] == docs_col[first : first + QUERY_BLOCK]
    return (key <= query) & same


def start_kernel(
    x_ref, up_ref, wq_ref, wo_ref, we_ref, pack_ref, cos_ref, sin_ref,
    x_all, up_all, h1_all, qkv_ref, w_mine, wo_all, we_all, o_own, h2_ref, r_own, cols_ref, docs_ref, gains_ref,
    o_all, r_all, pack_all, gain_sum,
    x_sent, x_passed, x_landed, up_sent, up_passed, up_landed, o_sent, o_passed, o_landed,
    wo_sent, wo_passed, wo_landed, wq_sent, wq_landed, pack_sent, pack_landed,
    wqd_sent, wqd_landed, gd_sent, gd_landed, wod_sent, wod_landed, wod_passed, wod_far, we_sent, we_landed,
):
    f32, bf16 = jnp.float32, jnp.bfloat16
    where = i, e, z, c = whereabouts()
    sibling = (i, z * 2 + 1 - c)
    rows = x_ref.shape[0]
    length = rows * SPAN
    local = we_ref.shape[0]
    live = []

    def go(*spec):
        copy = remote(*spec)
        copy.start()
        live.append(copy)

    greet(i, e)
    for k in range(1, SPAN):
        there = lax.rem(e + k, SPAN)
        go(pack_ref.at[there], pack_all.at[e], pack_sent.at[k], pack_landed.at[e], (i, there))
    for k in range(1, SPAN):
        there = lax.rem(e + k, SPAN)
        go(wq_ref.at[there], w_mine.at[i, e], wq_sent.at[k], wq_landed.at[e], (i, there))
    x_gather = LineGather(lambda s: x_all.at[s], where, x_sent, x_passed, x_landed)
    x_gather.start(x_ref)
    for l in range(local):
        for k in (1, 2, 3):
            there = lax.rem(i + k, PLANE)
            go(we_ref.at[l], we_all.at[l, i], we_sent.at[l, k], we_landed.at[l, i], (there, e))
    pack_all[e] = pack_ref[e]
    w_mine[i, e] = wq_ref[e]
    x_all[e] = x_ref[...]
    up_all[e] = up_ref[...]
    wo_all[i, z, c] = wo_ref[...]
    for l in range(local):
        we_all[l, i] = we_ref[l]

    for k in range(1, SPAN):
        there = lax.rem(e + k, SPAN)
        remote(pack_ref.at[there], pack_all.at[there], pack_sent.at[k], pack_landed.at[there], sibling).wait_recv()
    for half in range(2):
        summed = pack_all[4 * half]
        for s in range(1, 4):
            summed = summed + pack_all[4 * half + s]
        gain_sum[i, half] = summed
    for k in range(1, PLANE):
        there = lax.rem(i + k, PLANE)
        go(gain_sum.at[i], gain_sum.at[i], gd_sent.at[k], gd_landed.at[i], (there, e))
    for k in range(1, SPAN):
        there = lax.rem(e + k, SPAN)
        remote(wq_ref.at[there], w_mine.at[i, there], wq_sent.at[k], wq_landed.at[there], sibling).wait_recv()
    for k in range(1, PLANE):
        there = lax.rem(i + k, PLANE)
        go(w_mine.at[i], w_mine.at[i], wqd_sent.at[k], wqd_landed.at[i], (there, e))
    for s in range(SPAN):
        block = pack_all[s]
        tall = jnp.concatenate([block, jnp.zeros((rows - block.shape[0], rows), f32)], axis=0)
        cols_ref[s * rows : (s + 1) * rows] = tall.T
        docs_ref[:, s * rows : (s + 1) * rows] = block
    for k in range(1, PLANE):
        there = lax.rem(i + k, PLANE)
        remote(gain_sum.at[i], gain_sum.at[there], gd_sent.at[k], gd_landed.at[there], sibling).wait_recv()
    for tile in range(2 * PLANE):
        gains_ref[:, tile * 128 : (tile + 1) * 128] = gain_sum[tile // 2, tile % 2].astype(bf16).astype(f32)
    gain_one = gains_ref[3:4]
    gain_two = gains_ref[4:5]

    def first_norm(s):
        values = x_all[s].astype(f32)
        h1_all[s] = (values * rms_rows(values) * gain_one).astype(bf16)

    first_norm(e)
    for k in range(1, LINE):
        x_gather.forward(k)
        first_norm(x_gather.near(k))
    up_gather = LineGather(lambda s: up_all.at[s], where, up_sent, up_passed, up_landed)
    wo_gather = LineGather(
        lambda s: wo_all.at[i, s // 2, lax.rem(s, 2)], where, wo_sent, wo_passed, wo_landed
    )
    wo_gather.start(wo_ref)
    up_gather.start(up_ref)
    x_gather.wait(x_gather.sibling())
    first_norm(x_gather.sibling())
    for k in range(1, LINE):
        x_gather.wait(x_gather.far(k))
        first_norm(x_gather.far(k))
    for k in range(1, PLANE):
        there = lax.rem(i + k, PLANE)
        remote(w_mine.at[i], w_mine.at[there], wqd_sent.at[k], wqd_landed.at[there], sibling).wait_recv()
    weights = w_mine[...].reshape(PLANE * SPAN * w_mine.shape[2], 256)
    for first in range(0, length, QUERY_BLOCK):
        span = slice(first, first + QUERY_BLOCK)
        slots = slice(first // rows, (first + QUERY_BLOCK) // rows)
        raw = dot(h1_all[slots].reshape(QUERY_BLOCK, D), weights, NN)
        qkv_ref[span] = (raw * cos_ref[span] + half_turn_tile(raw) * sin_ref[span]).astype(bf16)

    own_cols = pl.ds(pl.multiple_of(e * 128, 128), 128)
    docs_row = docs_ref[2:3]
    docs_col = cols_ref[:, 2:3]
    for first in range(0, length, QUERY_BLOCK):
        low, high = block_view(first, length // 2)
        visible = visible_keys(first, low, high, docs_row, docs_col)
        span = slice(first, first + QUERY_BLOCK)
        outs = []
        for head in range(2):
            q = qkv_ref[span, head * HD : (head + 1) * HD]
            scores = dot(q, qkv_ref[low:high, 128:192], NT) * HD**-0.5
            scores = jnp.where(visible, scores, -1e30)
            raw = jnp.exp(scores - jnp.max(scores, axis=-1, keepdims=True))
            probs = raw * (1.0 / jnp.sum(raw, axis=-1, keepdims=True))
            outs.append(dot(probs.astype(bf16), qkv_ref[low:high, 192:256], NN))
        both = jnp.concatenate(outs, axis=1).astype(bf16)
        o_own[span] = both
        o_all[span, own_cols] = both
    o_gather = LineGather(
        lambda s: o_all.at[:, pl.ds(pl.multiple_of(s * 128, 128), 128)], where, o_sent, o_passed, o_landed
    )
    o_gather.start(o_own)

    for k in range(1, LINE):
        wo_gather.forward(k)
    for k in range(1, PLANE):
        there = lax.rem(i + k, PLANE)
        go(wo_all.at[i, :, c], wo_all.at[i, :, c], wod_sent.at[k], wod_landed.at[i], (there, e))
    for k in range(1, LINE):
        up_gather.forward(k)
    wo_gather.rest()
    for k in range(1, PLANE):
        there = lax.rem(i + k, PLANE)
        here = wo_all.at[there, :, c]
        remote(here, here, wod_sent.at[k], wod_landed.at[there], sibling).wait_recv()
        go(here, here, wod_passed.at[k], wod_far.at[there], sibling)
    for k in range(1, LINE):
        o_gather.forward(k)
    for k in range(1, PLANE):
        there = lax.rem(i + k, PLANE)
        far = wo_all.at[there, :, 1 - c]
        remote(far, far, wod_sent.at[k], wod_far.at[there], sibling).wait_recv()
    o_gather.rest()
    w_out = wo_all[...].reshape(D, D)
    for first in range(0, length, QUERY_BLOCK):
        span = slice(first, first + QUERY_BLOCK)
        slots = slice(first // rows, (first + QUERY_BLOCK) // rows)
        values = x_all[slots].reshape(QUERY_BLOCK, D).astype(f32) + dot(o_all[span], w_out, NT)
        r_all[slots] = values.reshape(-1, rows, D)
        h2_ref[span] = (values * rms_rows(values) * gain_two).astype(bf16)
    r_own[...] = r_all[e]
    up_gather.rest()
    for l in range(local):
        for k in (1, 2, 3):
            there = lax.rem(i + k, PLANE)
            remote(we_ref.at[l], we_all.at[l, there], we_sent.at[l, k], we_landed.at[l, there], sibling).wait_recv()
    for copy in live:
        copy.wait_send()
    for gather in (x_gather, up_gather, wo_gather, o_gather):
        gather.drain()


def call_start(x, up, wq, wo, we, pack, cosine, sine):
    f32, bf16 = jnp.float32, jnp.bfloat16
    rows, local = x.shape[0], we.shape[0]
    length = rows * SPAN
    part = wo.shape[0]
    shaped = jax.ShapeDtypeStruct
    vmem = pl.BlockSpec(memory_space=pltpu.VMEM)
    outs = [
        shaped((SPAN, rows, D), bf16),
        shaped((SPAN, rows, D), bf16),
        shaped((SPAN, rows, D), bf16),
        shaped((length, 256), bf16),
        shaped((PLANE, SPAN, part, 256), bf16),
        shaped((PLANE, LINE, 2, part, D), bf16),
        shaped((local, PLANE, we.shape[1], 3 * FF), bf16),
        shaped((length, 128), bf16),
        shaped((length, D), bf16),
        shaped((rows, D), f32),
        shaped((length, 128), f32),
        shaped((8, length), f32),
        shaped((8, D), f32),
    ]
    dma = pltpu.SemaphoreType.DMA
    line = [dma((LINE,)), dma((LINE - 1,)), dma((SPAN,))]
    scratch = [
        pltpu.VMEM((length, D), bf16),
        pltpu.VMEM((SPAN, rows, D), f32),
        pltpu.VMEM((SPAN, 8, rows), f32),
        pltpu.VMEM((PLANE, 2, 8, 128), f32),
        *line, *line, *line, *line,
        dma((SPAN,)), dma((SPAN,)), dma((SPAN,)), dma((SPAN,)),
        dma((PLANE,)), dma((PLANE,)), dma((PLANE,)), dma((PLANE,)),
        dma((PLANE,)), dma((PLANE,)), dma((PLANE,)), dma((PLANE,)),
        dma((local, PLANE)), dma((local, PLANE)),
    ]
    return pl.pallas_call(
        start_kernel,
        out_shape=outs,
        in_specs=[vmem] * 8,
        out_specs=[vmem] * len(outs),
        scratch_shapes=scratch,
        compiler_params=pltpu.CompilerParams(
            collective_id=0, has_side_effects=True, vmem_limit_bytes=60 * 2**20
        ),
        name="start",
    )(x, up, wq, wo, we, pack, cosine, sine)


def expert_kernel(h2_ref, up_ref, we_ref, cols_ref, y_ref, d_ref, act_ref, dgu_ref, y_sum, d_sum):
    f32, bf16 = jnp.float32, jnp.bfloat16
    local = we_ref.shape[0]
    size = 256
    for l in range(local):
        weights = we_ref[l].reshape(D, 3 * FF)

        def step(b, _, l=l, weights=weights):
            span = pl.ds(pl.multiple_of(b * size, size), size)
            gate = cols_ref[span, l : l + 1]
            routed = gate > 0
            gu = dot(h2_ref[span], weights[:, : 2 * FF], NN)
            g, u = gu[:, :FF], gu[:, FF:]
            sig = 1.0 / (1.0 + jnp.exp(-g))
            act = jnp.where(routed, g * sig * u, 0.0).astype(bf16)
            act_ref[l, span] = act
            y = gate * dot(act, weights[:, 2 * FF :], NT).astype(bf16).astype(f32)
            dy = (gate * up_ref[span].astype(f32)).astype(bf16)
            dact = dot(dy, weights[:, 2 * FF :], NN)
            dg = dact * u * sig * (1.0 + g * (1.0 - sig))
            du = dact * g * sig
            dgu = jnp.where(routed, jnp.concatenate([dg, du], axis=1), 0.0).astype(bf16)
            dgu_ref[l, span] = dgu
            d = dot(dgu, weights[:, : 2 * FF], NT).astype(bf16).astype(f32)
            if l == 0:
                y_sum[span] = y
                d_sum[span] = d
            elif l < local - 1:
                y_sum[span] += y
                d_sum[span] += d
            else:
                y_ref[span] = (y_sum[span] + y).astype(bf16)
                d_ref[span] = (d_sum[span] + d).astype(bf16)
            return 0

        lax.fori_loop(0, h2_ref.shape[0] // size, step, 0)


def call_experts(h2, up, we, cols):
    f32, bf16 = jnp.float32, jnp.bfloat16
    length, local = h2.shape[0], we.shape[0]
    shaped = jax.ShapeDtypeStruct
    vmem = pl.BlockSpec(memory_space=pltpu.VMEM)
    outs = [
        shaped((length, D), bf16),
        shaped((length, D), bf16),
        shaped((local, length, FF), bf16),
        shaped((local, length, 2 * FF), bf16),
    ]
    return pl.pallas_call(
        expert_kernel,
        out_shape=outs,
        in_specs=[vmem] * 4,
        out_specs=[vmem] * 4,
        scratch_shapes=[pltpu.VMEM((length, D), f32)] * 2,
        compiler_params=pltpu.CompilerParams(vmem_limit_bytes=60 * 2**20),
        name="experts",
    )(h2, up, we, cols)


def fast_body(
    activations,
    doc_ids,
    routes,
    gate_weights,
    cotangent,
    step_count,
    w_attn,
    norm_gains,
    w_expert,
    first_attn,
    second_attn,
    first_gains,
    second_gains,
    first_expert,
    second_expert,
):
    f32, bf16 = jnp.float32, jnp.bfloat16
    rows = activations.shape[1]
    span = lax.axis_size("expert")
    place = lax.axis_index("expert")
    length = rows * span
    local = w_expert.shape[0]
    total = local * span
    own = lambda v, size: lax.dynamic_slice_in_dim(v, place * size, size, 0)
    wa = w_attn.astype(bf16)
    grouped = group_columns(wa, span)[:, :, :256]
    hits = routes[0][:, :, None] == jnp.arange(total, dtype=jnp.int32)
    dense = jnp.sum(jnp.where(hits, gate_weights[0][:, :, None], 0.0), axis=1).T
    low = norm_gains.T
    lane = jnp.arange(rows)
    index = lax.axis_index("dp") * span + place
    spread = jnp.where(lane // low.shape[1] == index % (rows // low.shape[1]), jnp.tile(low, (1, rows // low.shape[1])), 0.0)
    shared = jnp.concatenate([doc_ids.astype(f32), spread], axis=0)
    pack = jnp.concatenate(
        [
            dense.reshape(span, local, rows),
            jnp.broadcast_to(shared[None], (span, 3, rows)),
            jnp.zeros((span, 8 - local - 3, rows), f32),
        ],
        axis=1,
    )
    cosine, sine = head_tables(length)
    x_all, up_all, h1, qkv, w_mine, w_out, w_exp, o, h2, r_own, cols, docs, gains = call_start(
        activations[0], cotangent[0], grouped, wa[:, QKV:], w_expert.astype(bf16), pack, cosine, sine
    )
    x_all, up_all, h1 = (v.reshape(length, D) for v in (x_all, up_all, h1))
    w_mine, w_out = w_mine.reshape(D, 256), w_out.reshape(D, D)
    gain_one, gain_two = gains[3], gains[4]
    y_part, d_part, act, dgu = call_experts(h2, up_all, w_exp, cols)
    grads = []
    for e in range(local):
        dy = (cols[:, e : e + 1] * up_all.astype(f32)).astype(bf16)
        inward = jnp.einsum("td,tf->df", h2, dgu[e], preferred_element_type=f32)
        down = jnp.einsum("td,tf->df", dy, act[e], preferred_element_type=f32)
        grads.append(jnp.concatenate([inward, down], axis=1))
    ge = jnp.stack(grads).astype(bf16)
    q = qkv[:, :128].reshape(length, 2, HD)
    k, v = qkv[:, 128:192], qkv[:, 192:]
    pos = jnp.arange(length)
    visible = (pos[None, :] <= pos[:, None]) & (docs[2][None, :] == cols[:, 2:3])
    s = jnp.einsum("thd,ud->htu", q, k, preferred_element_type=f32) * HD**-0.5
    s = jnp.where(visible, s, -1e30)
    peak = jnp.max(s, axis=-1, keepdims=True)
    raw = jnp.exp(s - peak)
    probs = raw / jnp.sum(raw, axis=-1, keepdims=True)
    p16 = probs.astype(bf16)
    combined = lax.psum_scatter(y_part.astype(bf16), "expert", scatter_dimension=0, tiled=True)
    dh2 = lax.psum_scatter(d_part.astype(bf16), "expert", scatter_dimension=0, tiled=True).astype(f32)
    x_own = activations[0].astype(f32)
    block = (r_own + combined.astype(f32)).astype(bf16)
    _, pull = jax.vjp(rms_scale, r_own, gain_two)
    dr, gn2 = pull(dh2)
    dr = cotangent[0].astype(f32) + dr
    da = lax.all_gather(dr.astype(bf16), "expert", axis=0, tiled=True)
    wo_mine = lax.dynamic_slice_in_dim(w_out, place * 128, 128, 1)
    do = jnp.dot(da, wo_mine, preferred_element_type=f32).astype(bf16)
    gwo = jnp.einsum("td,tc->dc", da, o, preferred_element_type=f32)
    do2 = do.reshape(length, 2, HD)
    dp = jnp.einsum("thd,ud->htu", do2, v, preferred_element_type=f32)
    delta = jnp.sum(probs * dp, axis=-1, keepdims=True)
    ds = (probs * (dp - delta)).astype(bf16)
    dq = jnp.einsum("htu,ud->thd", ds, k, preferred_element_type=f32) * HD**-0.5
    dk = jnp.einsum("htu,thd->ud", ds, q, preferred_element_type=f32) * HD**-0.5
    dv = jnp.einsum("htu,thd->ud", p16, do2, preferred_element_type=f32)
    dqkv = jnp.concatenate([dq.reshape(length, 128), dk, dv], axis=1)
    dqkv = (dqkv * cosine - half_turn(dqkv) * sine).astype(bf16)
    gqkv = jnp.einsum("td,tc->dc", h1, dqkv, preferred_element_type=f32)
    dh1_part = jnp.einsum("tc,dc->td", dqkv, w_mine, preferred_element_type=f32)
    dh1 = lax.psum_scatter(dh1_part.astype(bf16), "expert", scatter_dimension=0, tiled=True).astype(f32)
    _, pull = jax.vjp(rms_scale, x_own, gain_one)
    dx, gn1 = pull(dh1)
    input_total = dr + dx
    ga = jnp.concatenate([gqkv, gwo], axis=1).astype(bf16)
    ga = lax.psum_scatter(ga, "dp", scatter_dimension=0, tiled=True)
    squares = jnp.sum(ga.astype(f32) ** 2)
    ga = lax.all_to_all(ga.reshape(span, -1, 384), "expert", 0, 0, tiled=True)
    grad_attn = ungroup_columns(ga).astype(f32)
    grad_expert = lax.psum_scatter(ge, "dp", scatter_dimension=1, tiled=True).astype(f32)
    grad_gains = lax.psum_scatter(
        jnp.stack([gn1, gn2], axis=1), ("dp", "expert"), scatter_dimension=0, tiled=True
    )
    squares = squares + jnp.sum(grad_gains**2) + jnp.sum(grad_expert**2)
    grad_norm = jnp.sqrt(lax.psum(squares, ("dp", "expert")))
    clip = jnp.minimum(1.0, CLIP_NORM / (grad_norm + 1e-06))
    steps = step_count.astype(f32)
    attn = adam_update(
        w_attn, first_attn, second_attn, grad_attn * clip, steps, WEIGHT_DECAY, LEARN_RATE
    )
    gain = adam_update(
        norm_gains, first_gains, second_gains, grad_gains * clip, steps, 0.0, GAIN_RATE
    )
    expert = adam_update(
        w_expert, first_expert, second_expert, grad_expert * clip, steps, WEIGHT_DECAY, LEARN_RATE
    )
    return (block[None], input_total[None], grad_norm, *attn, *gain, *expert)


def solution(mesh):
    in_specs = (
        P("dp", "expert", None),
        P("dp", "expert"),
        P("dp", "expert", None),
        P("dp", "expert", None),
        P("dp", "expert", None),
        P(),
        P(("dp", "expert"), None),
        P(("dp", "expert"), None),
        P("expert", "dp", None),
        P(("dp", "expert"), None),
        P(("dp", "expert"), None),
        P(("dp", "expert"), None),
        P(("dp", "expert"), None),
        P("expert", "dp", None),
        P("expert", "dp", None),
    )
    out_specs = (
        P("dp", "expert", None),
        P("dp", "expert", None),
        P(),
        P(("dp", "expert"), None),
        P(("dp", "expert"), None),
        P(("dp", "expert"), None),
        P(("dp", "expert"), None),
        P(("dp", "expert"), None),
        P(("dp", "expert"), None),
        P("expert", "dp", None),
        P("expert", "dp", None),
        P("expert", "dp", None),
    )
    body = fast_body if fits(mesh) else general_body
    return jax.shard_map(body, mesh=mesh, in_specs=in_specs, out_specs=out_specs, check_vma=False)
```

```python
import jax
import jax.numpy as jnp
from jax import lax
from jax.sharding import PartitionSpec as P
import numpy as np
from jax.experimental import pallas as pl
from jax.experimental.pallas import tpu as pltpu

D = 1024
H = 16
KVH = 8
HD = 64
FF = 512
TOP = 8
QD = 1024
KVD = 512
QKV = 2048


EPSILON = 1e-05
ROPE_BASE = 10000.0
CLIP_NORM = 1.0
BETA_ONE = 0.9
BETA_TWO = 0.95
ADAM_EPSILON = 1e-08
LEARN_RATE = 0.03
GAIN_RATE = 0.4
WEIGHT_DECAY = 0.1


def rms_scale(values, gain):
    return values * lax.rsqrt(jnp.mean(values * values, axis=-1, keepdims=True) + EPSILON) * gain


def rope_tables(positions, head_width):
    halves = jnp.arange(head_width // 2, dtype=jnp.float32)
    inverse = ROPE_BASE ** (-2.0 * halves / head_width)
    angles = positions.astype(jnp.float32)[:, None] * inverse[None, :]
    angles = jnp.concatenate([angles, angles], axis=-1)
    return (jnp.cos(angles)[:, None, :], jnp.sin(angles)[:, None, :])


def rotate(values, cosine, sine_table):
    middle = values.shape[-1] // 2
    turned = jnp.concatenate([-values[..., middle:], values[..., :middle]], axis=-1)
    return values * cosine + turned * sine_table


def unrotate(gradient, cosine, sine_table):
    middle = gradient.shape[-1] // 2
    product = gradient * sine_table
    turned = jnp.concatenate([product[..., middle:], -product[..., :middle]], axis=-1)
    return gradient * cosine + turned


def adam_update(weight, moment_one, second, gradient, steps_done, decay_rate, step_rate):
    first_new = BETA_ONE * moment_one + (1.0 - BETA_ONE) * gradient
    second_new = BETA_TWO * second + (1.0 - BETA_TWO) * gradient * gradient
    first_hat = first_new / (1.0 - BETA_ONE**steps_done)
    second_hat = second_new / (1.0 - BETA_TWO**steps_done)
    weight_new = weight - step_rate * (
        first_hat / (jnp.sqrt(second_hat) + ADAM_EPSILON) + decay_rate * weight
    )
    return (weight_new, first_new, second_new)


def attn_fetch(w_attn, norm_gains):
    return (
        lax.all_gather(w_attn.astype(jnp.bfloat16), ("dp", "expert"), axis=0, tiled=True),
        lax.all_gather(norm_gains.astype(jnp.bfloat16), ("dp", "expert"), axis=0, tiled=True),
    )


def expert_fetch(w_expert):
    return lax.all_gather(w_expert.astype(jnp.bfloat16), "dp", axis=1, tiled=True)


def to_owner(buffer):
    return lax.all_to_all(buffer, "expert", split_axis=0, concat_axis=1, tiled=True)


def to_sender(buffer):
    return lax.all_to_all(buffer, "expert", split_axis=1, concat_axis=0, tiled=True)


def expert_forward(received, expert_cols):
    gate_up = jnp.einsum(
        "esd,edf->esf", received, expert_cols[:, :, : 2 * FF], preferred_element_type=jnp.float32
    )
    activated = (jax.nn.silu(gate_up[..., :FF]) * gate_up[..., FF:]).astype(jnp.bfloat16)
    return (gate_up, activated)


def general_body(
    activations,
    doc_ids,
    routes,
    gate_weights,
    cotangent,
    step_count,
    w_attn,
    norm_gains,
    w_expert,
    first_attn,
    second_attn,
    first_gains,
    second_gains,
    first_expert,
    second_expert,
):
    row_count = activations.shape[1]
    span_size = lax.axis_size("expert")
    shard_pos = lax.axis_index("expert")
    seq_length = row_count * span_size
    expert_total = w_expert.shape[0] * span_size
    capacity = (row_count * TOP * 9 + expert_total * 8 - 1) // (expert_total * 8)
    group_size = H // KVH
    score_scale = HD ** (-0.5)
    hidden_in = activations[0].astype(jnp.float32)
    upstream = cotangent[0].astype(jnp.float32)
    attn_cols, gain_pair = attn_fetch(w_attn, norm_gains)
    expert_cols = expert_fetch(w_expert)
    gain_one = gain_pair[:, 0].astype(jnp.float32)
    gain_two = gain_pair[:, 1].astype(jnp.float32)
    w_project = attn_cols[:, :QKV]
    w_output = attn_cols[:, QKV:]
    normed = rms_scale(hidden_in, gain_one).astype(jnp.bfloat16)
    projected = jnp.dot(normed, w_project, preferred_element_type=jnp.float32)
    positions = shard_pos * row_count + jnp.arange(row_count, dtype=jnp.int32)
    cosine, sine_table = rope_tables(positions, HD)
    queries = rotate(projected[:, :QD].reshape(row_count, H, HD), cosine, sine_table).astype(
        jnp.bfloat16
    )
    key_heads = rotate(
        projected[:, QD : QD + KVD].reshape(row_count, KVH, HD), cosine, sine_table
    ).astype(jnp.bfloat16)
    value_heads = projected[:, QD + KVD :].astype(jnp.bfloat16)
    key_all, value_all, doc_all = (
        lax.all_gather(key_heads.reshape(row_count, KVD), "expert", axis=0, tiled=True),
        lax.all_gather(value_heads, "expert", axis=0, tiled=True),
        lax.all_gather(doc_ids[0].astype(jnp.bfloat16), "expert", axis=0, tiled=True),
    )
    key_docs = doc_all.astype(jnp.int32)
    query_docs = doc_ids[0]
    query_groups = queries.reshape(row_count, KVH, group_size, HD)
    key_block = min(512, seq_length)
    needed = (shard_pos * row_count + row_count + key_block - 1) // key_block

    def block_scores(block_id):
        first_key = block_id * key_block
        key_part = lax.dynamic_slice_in_dim(key_all, first_key, key_block, 0).reshape(
            key_block, KVH, HD
        )
        raw_scores = (
            jnp.einsum("tgrd,kgd->grtk", query_groups, key_part, preferred_element_type=jnp.float32)
            * score_scale
        )
        key_pos = first_key + jnp.arange(key_block, dtype=jnp.int32)
        key_doc = lax.dynamic_slice_in_dim(key_docs, first_key, key_block, 0)
        visible = (key_pos[None, :] <= positions[:, None]) & (
            key_doc[None, :] == query_docs[:, None]
        )
        return (raw_scores, visible, key_part)

    def value_part(block_id):
        return lax.dynamic_slice_in_dim(value_all, block_id * key_block, key_block, 0).reshape(
            key_block, KVH, HD
        )

    def total_step(block_id, running):
        row_peak, row_total = running
        raw_scores, visible, _ = block_scores(block_id)
        masked = jnp.where(visible, raw_scores, -1e30)
        new_peak = jnp.maximum(row_peak, jnp.max(masked, axis=-1))
        scaled = jnp.where(visible, jnp.exp(masked - new_peak[..., None]), 0.0)
        return (new_peak, row_total * jnp.exp(row_peak - new_peak) + jnp.sum(scaled, axis=-1))

    start_peak = jnp.full((KVH, group_size, row_count), -1e30, jnp.float32)
    start_total = jnp.zeros((KVH, group_size, row_count), jnp.float32)
    row_peak, row_total = lax.fori_loop(0, needed, total_step, (start_peak, start_total))
    log_total = row_peak + jnp.log(row_total)

    def exact_probs(raw_scores, visible):
        return jnp.exp(jnp.where(visible, raw_scores - log_total[..., None], -1e30))

    def output_step(block_id, summed):
        raw_scores, visible, _ = block_scores(block_id)
        weights_low = exact_probs(raw_scores, visible).astype(jnp.bfloat16)
        return summed + jnp.einsum(
            "grtk,kgd->tgrd", weights_low, value_part(block_id), preferred_element_type=jnp.float32
        )

    attended = lax.fori_loop(
        0, needed, output_step, jnp.zeros((row_count, KVH, group_size, HD), jnp.float32)
    )
    attended = attended.reshape(row_count, QD).astype(jnp.bfloat16)
    branch = jnp.einsum("tc,dc->td", attended, w_output, preferred_element_type=jnp.float32)
    residual = hidden_in + branch
    normed_two = rms_scale(residual, gain_two).astype(jnp.bfloat16)
    flat_routes = routes[0].reshape(-1)
    one_hot = (flat_routes[:, None] == jnp.arange(expert_total, dtype=jnp.int32)[None, :]).astype(
        jnp.int32
    )
    ranking = jnp.sum((jnp.cumsum(one_hot, axis=0) - 1) * one_hot, axis=1)
    places = flat_routes * capacity + ranking
    owners = jnp.arange(row_count * TOP, dtype=jnp.int32) // TOP
    source = jnp.zeros((expert_total * capacity,), jnp.int32).at[places].set(owners)
    filled = jnp.zeros((expert_total * capacity,), jnp.int32).at[places].set(1) > 0
    slot_gate = (
        jnp.zeros((expert_total * capacity,), jnp.float32)
        .at[places]
        .set(gate_weights[0].reshape(-1))
    )
    outgoing = jnp.where(filled[:, None], normed_two[source], jnp.zeros((), jnp.bfloat16)).reshape(
        expert_total, capacity, D
    )
    received = to_owner(outgoing)
    gate_up, activated = expert_forward(received, expert_cols)
    expert_out = jnp.einsum(
        "esf,edf->esd", activated, expert_cols[:, :, 2 * FF :], preferred_element_type=jnp.float32
    ).astype(jnp.bfloat16)
    returned = to_sender(expert_out).reshape(expert_total * capacity, D)
    picked = returned[places].reshape(row_count, TOP, D).astype(jnp.float32)
    combined = jnp.sum(gate_weights[0][..., None] * picked, axis=1)
    block_result = (residual + combined).astype(jnp.bfloat16)
    slot_grad = jnp.where(filled[:, None], slot_gate[:, None] * upstream[source], 0.0)
    slot_grad = slot_grad.astype(jnp.bfloat16).reshape(expert_total, capacity, D)
    owner_grad = to_owner(slot_grad)
    attn_cols, gain_pair = attn_fetch(w_attn, norm_gains)
    w_project = attn_cols[:, :QKV]
    w_output = attn_cols[:, QKV:]
    expert_cols = expert_fetch(w_expert)
    gate_up, activated = expert_forward(received, expert_cols)
    gate_part = gate_up[..., :FF]
    up_part = gate_up[..., FF:]
    sigmoid_gate = jax.nn.sigmoid(gate_part)
    act_grad = jnp.einsum(
        "esd,edf->esf", owner_grad, expert_cols[:, :, 2 * FF :], preferred_element_type=jnp.float32
    )
    gate_grad = act_grad * up_part * sigmoid_gate * (1.0 + gate_part * (1.0 - sigmoid_gate))
    lift_grad = act_grad * gate_part * sigmoid_gate
    mixed_grad = jnp.concatenate([gate_grad, lift_grad], axis=-1).astype(jnp.bfloat16)
    down_grad = jnp.einsum(
        "esf,esd->edf", activated, owner_grad, preferred_element_type=jnp.float32
    )
    inward_grad = jnp.einsum(
        "esd,esf->edf", received, mixed_grad, preferred_element_type=jnp.float32
    )
    row_grads = jnp.einsum(
        "esf,edf->esd", mixed_grad, expert_cols[:, :, : 2 * FF], preferred_element_type=jnp.float32
    ).astype(jnp.bfloat16)
    back_rows = to_sender(row_grads).reshape(expert_total * capacity, D)
    normed_two_grad = jnp.sum(
        back_rows[places].reshape(row_count, TOP, D).astype(jnp.float32), axis=1
    )
    _, second_pull = jax.vjp(rms_scale, residual, gain_two)
    resid_grad, gain_two_grad = second_pull(normed_two_grad)
    resid_grad = upstream + resid_grad
    branch_grad = resid_grad.astype(jnp.bfloat16)
    output_grad = jnp.einsum("td,tc->dc", branch_grad, attended, preferred_element_type=jnp.float32)
    attended_grad = jnp.dot(branch_grad, w_output, preferred_element_type=jnp.float32).astype(
        jnp.bfloat16
    )
    grad_groups = attended_grad.reshape(row_count, KVH, group_size, HD)

    def delta_step(block_id, summed):
        raw_scores, visible, _ = block_scores(block_id)
        probs_full = exact_probs(raw_scores, visible)
        prob_grad = jnp.einsum(
            "tgrd,kgd->grtk", grad_groups, value_part(block_id), preferred_element_type=jnp.float32
        )
        return summed + jnp.sum(probs_full * prob_grad, axis=-1)

    delta_rows = lax.fori_loop(
        0, needed, delta_step, jnp.zeros((KVH, group_size, row_count), jnp.float32)
    )

    def grad_step(block_id, running):
        query_grad, key_grad, value_grad = running
        raw_scores, visible, key_part = block_scores(block_id)
        probs_full = exact_probs(raw_scores, visible)
        prob_grad = jnp.einsum(
            "tgrd,kgd->grtk", grad_groups, value_part(block_id), preferred_element_type=jnp.float32
        )
        score_grad = (probs_full * (prob_grad - delta_rows[..., None])).astype(jnp.bfloat16)
        query_grad = (
            query_grad
            + jnp.einsum("grtk,kgd->tgrd", score_grad, key_part, preferred_element_type=jnp.float32)
            * score_scale
        )
        key_piece = (
            jnp.einsum(
                "grtk,tgrd->kgd", score_grad, query_groups, preferred_element_type=jnp.float32
            )
            * score_scale
        )
        value_piece = jnp.einsum(
            "grtk,tgrd->kgd",
            probs_full.astype(jnp.bfloat16),
            grad_groups,
            preferred_element_type=jnp.float32,
        )
        first_key = block_id * key_block
        key_grad = lax.dynamic_update_slice_in_dim(
            key_grad, key_piece.reshape(key_block, KVD), first_key, 0
        )
        value_grad = lax.dynamic_update_slice_in_dim(
            value_grad, value_piece.reshape(key_block, KVD), first_key, 0
        )
        return (query_grad, key_grad, value_grad)

    start_grads = (
        jnp.zeros((row_count, KVH, group_size, HD), jnp.float32),
        jnp.zeros((seq_length, KVD), jnp.float32),
        jnp.zeros((seq_length, KVD), jnp.float32),
    )
    query_grad, key_grad, value_grad = lax.fori_loop(0, needed, grad_step, start_grads)
    key_sum, value_sum = (
        lax.psum_scatter(key_grad, "expert", scatter_dimension=0, tiled=True),
        lax.psum_scatter(value_grad, "expert", scatter_dimension=0, tiled=True),
    )
    query_back = unrotate(query_grad.reshape(row_count, H, HD), cosine, sine_table).reshape(
        row_count, QD
    )
    key_back = unrotate(key_sum.reshape(row_count, KVH, HD), cosine, sine_table).reshape(
        row_count, KVD
    )
    project_grad = jnp.concatenate([query_back, key_back, value_sum], axis=1).astype(jnp.bfloat16)
    weight_grad_qkv = jnp.einsum(
        "td,tc->dc", normed, project_grad, preferred_element_type=jnp.float32
    )
    normed_grad = jnp.einsum(
        "tc,dc->td", project_grad, w_project, preferred_element_type=jnp.float32
    )
    _, first_pull = jax.vjp(rms_scale, hidden_in, gain_one)
    input_part, gain_one_grad = first_pull(normed_grad)
    input_total = resid_grad + input_part
    attn_partial = jnp.concatenate([weight_grad_qkv, output_grad], axis=1)
    gain_partial = jnp.stack([gain_one_grad, gain_two_grad], axis=1)
    grad_attn, grad_gains = (
        lax.psum_scatter(attn_partial, ("dp", "expert"), scatter_dimension=0, tiled=True),
        lax.psum_scatter(gain_partial, ("dp", "expert"), scatter_dimension=0, tiled=True),
    )
    grad_expert = lax.psum_scatter(
        jnp.concatenate([inward_grad, down_grad], axis=2).astype(jnp.bfloat16),
        "dp",
        scatter_dimension=1,
        tiled=True,
    ).astype(jnp.float32)
    local_squares = (
        jnp.sum(grad_attn * grad_attn)
        + jnp.sum(grad_gains * grad_gains)
        + jnp.sum(grad_expert * grad_expert)
    )
    grad_norm = jnp.sqrt(lax.psum(local_squares, ("dp", "expert")))
    clip_factor = jnp.minimum(1.0, CLIP_NORM / (grad_norm + 1e-06))
    steps_done = step_count.astype(jnp.float32)
    attn_new = adam_update(
        w_attn,
        first_attn,
        second_attn,
        grad_attn * clip_factor,
        steps_done,
        WEIGHT_DECAY,
        LEARN_RATE,
    )
    gains_new = adam_update(
        norm_gains, first_gains, second_gains, grad_gains * clip_factor, steps_done, 0.0, GAIN_RATE
    )
    expert_new = adam_update(
        w_expert,
        first_expert,
        second_expert,
        grad_expert * clip_factor,
        steps_done,
        WEIGHT_DECAY,
        LEARN_RATE,
    )
    return (
        block_result[None],
        input_total[None],
        grad_norm,
        attn_new[0],
        attn_new[1],
        attn_new[2],
        gains_new[0],
        gains_new[1],
        gains_new[2],
        expert_new[0],
        expert_new[1],
        expert_new[2],
    )


def fits(mesh):
    return dict(mesh.shape) == {"dp": 4, "expert": KVH}


def head_tables(length):
    cosine, sine = rope_tables(jnp.arange(length, dtype=jnp.int32), HD)
    cosine, sine = cosine[:, 0], sine[:, 0]
    lane = jnp.arange(HD)
    signed = jnp.where(lane < HD // 2, -sine, sine)
    ones, zeros = jnp.ones_like(cosine), jnp.zeros_like(sine)
    return (
        jnp.concatenate([cosine, cosine, cosine, ones], axis=1),
        jnp.concatenate([signed, signed, signed, zeros], axis=1),
    )


def group_columns(weights, groups):
    rows = weights.shape[0]
    parts = [
        weights[:, :QD].reshape(rows, groups, -1),
        weights[:, QD : QD + KVD].reshape(rows, groups, -1),
        weights[:, QD + KVD : QKV].reshape(rows, groups, -1),
        weights[:, QKV:].reshape(rows, groups, -1),
    ]
    return jnp.concatenate(parts, axis=2).transpose(1, 0, 2)


def ungroup_columns(grouped):
    rows = grouped.shape[1]
    g = grouped.transpose(1, 0, 2)
    parts = [g[:, :, :128], g[:, :, 128:192], g[:, :, 192:256], g[:, :, 256:]]
    return jnp.concatenate([p.reshape(rows, -1) for p in parts], axis=1)


def remote(source, target, sent, landed, device):
    return pltpu.make_async_remote_copy(
        src_ref=source,
        dst_ref=target,
        send_sem=sent,
        recv_sem=landed,
        device_id=device,
        device_id_type=pl.DeviceIdType.MESH,
    )


def whereabouts():
    i, e = lax.axis_index("dp"), lax.axis_index("expert")
    return i, e, e // 2, lax.rem(e, 2)


def greet(i, e):
    barrier = pltpu.get_barrier_semaphore()
    others = [(i, lax.rem(e + k, SPAN)) for k in range(1, SPAN)]
    others += [(lax.rem(i + k, PLANE), e) for k in range(1, PLANE)]
    for device in others:
        pl.semaphore_signal(barrier, inc=1, device_id=device, device_id_type=pl.DeviceIdType.MESH)
    pl.semaphore_wait(barrier, len(others))


class LineGather:
    def __init__(self, slot, where, sent, passed, landed):
        self.slot, self.where = slot, where
        self.sent, self.passed, self.landed = sent, passed, landed
        self.live = []

    def _copy(self, source, index, sem, device):
        place = self.slot(index)
        return remote(place if source is None else source, place, sem, self.landed.at[index], device)

    def start(self, source=None):
        i, e, z, c = self.where
        for k in range(1, LINE):
            there = lax.rem(z + k, LINE) * 2 + c
            copy = self._copy(source, e, self.sent.at[k], (i, there))
            copy.start()
            self.live.append(copy)
        copy = self._copy(source, e, self.sent.at[0], (i, z * 2 + 1 - c))
        copy.start()
        self.live.append(copy)

    def wait(self, index):
        i, e, z, c = self.where
        self._copy(None, index, self.sent.at[0], (i, z * 2 + 1 - c)).wait_recv()

    def sibling(self):
        _, e, z, c = self.where
        return z * 2 + 1 - c

    def near(self, k):
        _, e, z, c = self.where
        return lax.rem(z + k, LINE) * 2 + c

    def far(self, k):
        _, e, z, c = self.where
        return lax.rem(z + k, LINE) * 2 + 1 - c

    def forward(self, k):
        i, e, z, c = self.where
        index = self.near(k)
        self.wait(index)
        copy = self._copy(None, index, self.passed.at[k - 1], (i, z * 2 + 1 - c))
        copy.start()
        self.live.append(copy)

    def rest(self):
        self.wait(self.sibling())
        for k in range(1, LINE):
            self.wait(self.far(k))

    def drain(self):
        for copy in self.live:
            copy.wait_send()


def half_turn_tile(tile):
    pieces = []
    for first in range(0, tile.shape[1], 128):
        part = tile[:, first : first + 128]
        lane = lax.broadcasted_iota(jnp.int32, part.shape, 1)
        ahead = pltpu.roll(part, 128 - HD // 2, 1)
        behind = pltpu.roll(part, HD // 2, 1)
        pieces.append(jnp.where(lax.rem(lane, HD) < HD // 2, ahead, behind))
    return jnp.concatenate(pieces, axis=1)


def rms_rows(values):
    return lax.rsqrt(jnp.mean(values * values, axis=-1, keepdims=True) + EPSILON)


def dot(a, b, contract):
    return lax.dot_general(a, b, (contract, ((), ())), preferred_element_type=jnp.float32)


NN, NT, TN = ((1,), (0,)), ((1,), (1,)), ((0,), (0,))
LINE, SPAN, PLANE = 4, 8, 4
QUERY_BLOCK = 256


def block_view(first, reach):
    return max(0, first - reach), first + QUERY_BLOCK


def visible_keys(first, low, high, docs_row, docs_col):
    shape = (QUERY_BLOCK, high - low)
    key = lax.broadcasted_iota(jnp.int32, shape, 1) + low
    query = lax.broadcasted_iota(jnp.int32, shape, 0) + first
    same = docs_row[:, low:high] == docs_col[first : first + QUERY_BLOCK]
    return (key <= query) & same


def start_kernel(
    x_ref, up_ref, wq_ref, wo_ref, we_ref, pack_ref, cos_ref, sin_ref,
    x_all, up_all, h1_all, qkv_ref, lse_ref, w_mine, wo_all, we_all, o_own, h2_ref, r_own, cols_ref, docs_ref, gains_ref,
    o_all, r_all, pack_all, gain_sum,
    x_sent, x_passed, x_landed, up_sent, up_passed, up_landed, o_sent, o_passed, o_landed,
    wo_sent, wo_passed, wo_landed, wq_sent, wq_landed, pack_sent, pack_landed,
    wqd_sent, wqd_landed, gd_sent, gd_landed, wod_sent, wod_landed, wod_passed, wod_far, we_sent, we_landed,
):
    f32, bf16 = jnp.float32, jnp.bfloat16
    where = i, e, z, c = whereabouts()
    sibling = (i, z * 2 + 1 - c)
    rows = x_ref.shape[0]
    length = rows * SPAN
    local = we_ref.shape[0]
    live = []

    def go(*spec):
        copy = remote(*spec)
        copy.start()
        live.append(copy)

    greet(i, e)
    for k in range(1, SPAN):
        there = lax.rem(e + k, SPAN)
        go(pack_ref.at[there], pack_all.at[e], pack_sent.at[k], pack_landed.at[e], (i, there))
    for k in range(1, SPAN):
        there = lax.rem(e + k, SPAN)
        go(wq_ref.at[there], w_mine.at[i, e], wq_sent.at[k], wq_landed.at[e], (i, there))
    x_gather = LineGather(lambda s: x_all.at[s], where, x_sent, x_passed, x_landed)
    x_gather.start(x_ref)
    for l in range(local):
        for k in (1, 2, 3):
            there = lax.rem(i + k, PLANE)
            go(we_ref.at[l], we_all.at[l, i], we_sent.at[l, k], we_landed.at[l, i], (there, e))
    pack_all[e] = pack_ref[e]
    w_mine[i, e] = wq_ref[e]
    x_all[e] = x_ref[...]
    up_all[e] = up_ref[...]
    wo_all[i, z, c] = wo_ref[...]
    for l in range(local):
        we_all[l, i] = we_ref[l]

    for k in range(1, SPAN):
        there = lax.rem(e + k, SPAN)
        remote(pack_ref.at[there], pack_all.at[there], pack_sent.at[k], pack_landed.at[there], sibling).wait_recv()
    for half in range(2):
        summed = pack_all[4 * half]
        for s in range(1, 4):
            summed = summed + pack_all[4 * half + s]
        gain_sum[i, half] = summed
    for k in range(1, PLANE):
        there = lax.rem(i + k, PLANE)
        go(gain_sum.at[i], gain_sum.at[i], gd_sent.at[k], gd_landed.at[i], (there, e))
    for k in range(1, SPAN):
        there = lax.rem(e + k, SPAN)
        remote(wq_ref.at[there], w_mine.at[i, there], wq_sent.at[k], wq_landed.at[there], sibling).wait_recv()
    for k in range(1, PLANE):
        there = lax.rem(i + k, PLANE)
        go(w_mine.at[i], w_mine.at[i], wqd_sent.at[k], wqd_landed.at[i], (there, e))
    for s in range(SPAN):
        block = pack_all[s]
        tall = jnp.concatenate([block, jnp.zeros((rows - block.shape[0], rows), f32)], axis=0)
        cols_ref[s * rows : (s + 1) * rows] = tall.T
        docs_ref[:, s * rows : (s + 1) * rows] = block
    for k in range(1, PLANE):
        there = lax.rem(i + k, PLANE)
        remote(gain_sum.at[i], gain_sum.at[there], gd_sent.at[k], gd_landed.at[there], sibling).wait_recv()
    for tile in range(2 * PLANE):
        gains_ref[:, tile * 128 : (tile + 1) * 128] = gain_sum[tile // 2, tile % 2].astype(bf16).astype(f32)
    gain_one = gains_ref[3:4]
    gain_two = gains_ref[4:5]

    def first_norm(s):
        values = x_all[s].astype(f32)
        h1_all[s] = (values * rms_rows(values) * gain_one).astype(bf16)

    first_norm(e)
    for k in range(1, LINE):
        x_gather.forward(k)
        first_norm(x_gather.near(k))
    up_gather = LineGather(lambda s: up_all.at[s], where, up_sent, up_passed, up_landed)
    wo_gather = LineGather(
        lambda s: wo_all.at[i, s // 2, lax.rem(s, 2)], where, wo_sent, wo_passed, wo_landed
    )
    wo_gather.start(wo_ref)
    up_gather.start(up_ref)
    x_gather.wait(x_gather.sibling())
    first_norm(x_gather.sibling())
    for k in range(1, LINE):
        x_gather.wait(x_gather.far(k))
        first_norm(x_gather.far(k))
    for k in range(1, PLANE):
        there = lax.rem(i + k, PLANE)
        remote(w_mine.at[i], w_mine.at[there], wqd_sent.at[k], wqd_landed.at[there], sibling).wait_recv()
    weights = w_mine[...].reshape(PLANE * SPAN * w_mine.shape[2], 256)
    for first in range(0, length, QUERY_BLOCK):
        span = slice(first, first + QUERY_BLOCK)
        slots = slice(first // rows, (first + QUERY_BLOCK) // rows)
        raw = dot(h1_all[slots].reshape(QUERY_BLOCK, D), weights, NN)
        qkv_ref[span] = (raw * cos_ref[span] + half_turn_tile(raw) * sin_ref[span]).astype(bf16)

    own_cols = pl.ds(pl.multiple_of(e * 128, 128), 128)
    docs_row = docs_ref[2:3]
    docs_col = cols_ref[:, 2:3]
    for first in range(0, length, QUERY_BLOCK):
        low, high = block_view(first, length // 2)
        visible = visible_keys(first, low, high, docs_row, docs_col)
        span = slice(first, first + QUERY_BLOCK)
        outs, logs = [], []
        for head in range(2):
            q = qkv_ref[span, head * HD : (head + 1) * HD]
            scores = dot(q, qkv_ref[low:high, 128:192], NT) * HD**-0.5
            scores = jnp.where(visible, scores, -1e30)
            peak = jnp.max(scores, axis=-1, keepdims=True)
            raw = jnp.exp(scores - peak)
            total = jnp.sum(raw, axis=-1, keepdims=True)
            probs = raw * (1.0 / total)
            logs.append(peak + jnp.log(total))
            outs.append(dot(probs.astype(bf16), qkv_ref[low:high, 192:256], NN))
        both = jnp.concatenate(outs, axis=1).astype(bf16)
        o_own[span] = both
        lane = lax.broadcasted_iota(jnp.int32, (QUERY_BLOCK, 128), 1)
        lse_ref[span] = jnp.where(lane == 0, logs[0], logs[1])
        o_all[span, own_cols] = both
    o_gather = LineGather(
        lambda s: o_all.at[:, pl.ds(pl.multiple_of(s * 128, 128), 128)], where, o_sent, o_passed, o_landed
    )
    o_gather.start(o_own)

    for k in range(1, LINE):
        wo_gather.forward(k)
    for k in range(1, PLANE):
        there = lax.rem(i + k, PLANE)
        go(wo_all.at[i, :, c], wo_all.at[i, :, c], wod_sent.at[k], wod_landed.at[i], (there, e))
    for k in range(1, LINE):
        up_gather.forward(k)
    wo_gather.rest()
    for k in range(1, PLANE):
        there = lax.rem(i + k, PLANE)
        here = wo_all.at[there, :, c]
        remote(here, here, wod_sent.at[k], wod_landed.at[there], sibling).wait_recv()
        go(here, here, wod_passed.at[k], wod_far.at[there], sibling)
    for k in range(1, LINE):
        o_gather.forward(k)
    for k in range(1, PLANE):
        there = lax.rem(i + k, PLANE)
        far = wo_all.at[there, :, 1 - c]
        remote(far, far, wod_sent.at[k], wod_far.at[there], sibling).wait_recv()
    o_gather.rest()
    w_out = wo_all[...].reshape(D, D)
    for first in range(0, length, QUERY_BLOCK):
        span = slice(first, first + QUERY_BLOCK)
        slots = slice(first // rows, (first + QUERY_BLOCK) // rows)
        values = x_all[slots].reshape(QUERY_BLOCK, D).astype(f32) + dot(o_all[span], w_out, NT)
        r_all[slots] = values.reshape(-1, rows, D)
        h2_ref[span] = (values * rms_rows(values) * gain_two).astype(bf16)
    r_own[...] = r_all[e]
    up_gather.rest()
    for l in range(local):
        for k in (1, 2, 3):
            there = lax.rem(i + k, PLANE)
            remote(we_ref.at[l], we_all.at[l, there], we_sent.at[l, k], we_landed.at[l, there], sibling).wait_recv()
    for copy in live:
        copy.wait_send()
    for gather in (x_gather, up_gather, wo_gather, o_gather):
        gather.drain()


def call_start(x, up, wq, wo, we, pack, cosine, sine):
    f32, bf16 = jnp.float32, jnp.bfloat16
    rows, local = x.shape[0], we.shape[0]
    length = rows * SPAN
    part = wo.shape[0]
    shaped = jax.ShapeDtypeStruct
    vmem = pl.BlockSpec(memory_space=pltpu.VMEM)
    outs = [
        shaped((SPAN, rows, D), bf16),
        shaped((SPAN, rows, D), bf16),
        shaped((SPAN, rows, D), bf16),
        shaped((length, 256), bf16),
        shaped((length, 128), f32),
        shaped((PLANE, SPAN, part, 256), bf16),
        shaped((PLANE, LINE, 2, part, D), bf16),
        shaped((local, PLANE, we.shape[1], 3 * FF), bf16),
        shaped((length, 128), bf16),
        shaped((length, D), bf16),
        shaped((rows, D), f32),
        shaped((length, 128), f32),
        shaped((8, length), f32),
        shaped((8, D), f32),
    ]
    dma = pltpu.SemaphoreType.DMA
    line = [dma((LINE,)), dma((LINE - 1,)), dma((SPAN,))]
    scratch = [
        pltpu.VMEM((length, D), bf16),
        pltpu.VMEM((SPAN, rows, D), f32),
        pltpu.VMEM((SPAN, 8, rows), f32),
        pltpu.VMEM((PLANE, 2, 8, 128), f32),
        *line, *line, *line, *line,
        dma((SPAN,)), dma((SPAN,)), dma((SPAN,)), dma((SPAN,)),
        dma((PLANE,)), dma((PLANE,)), dma((PLANE,)), dma((PLANE,)),
        dma((PLANE,)), dma((PLANE,)), dma((PLANE,)), dma((PLANE,)),
        dma((local, PLANE)), dma((local, PLANE)),
    ]
    return pl.pallas_call(
        start_kernel,
        out_shape=outs,
        in_specs=[vmem] * 8,
        out_specs=[vmem] * len(outs),
        scratch_shapes=scratch,
        compiler_params=pltpu.CompilerParams(
            collective_id=0, has_side_effects=True, vmem_limit_bytes=60 * 2**20
        ),
        name="start",
    )(x, up, wq, wo, we, pack, cosine, sine)


def expert_kernel(h2_ref, up_ref, we_ref, cols_ref, y_ref, d_ref, act_ref, dgu_ref, y_sum, d_sum):
    f32, bf16 = jnp.float32, jnp.bfloat16
    local = we_ref.shape[0]
    size = 256
    for l in range(local):
        weights = we_ref[l].reshape(D, 3 * FF)

        def step(b, _, l=l, weights=weights):
            span = pl.ds(pl.multiple_of(b * size, size), size)
            gate = cols_ref[span, l : l + 1]
            routed = gate > 0
            gu = dot(h2_ref[span], weights[:, : 2 * FF], NN)
            g, u = gu[:, :FF], gu[:, FF:]
            sig = 1.0 / (1.0 + jnp.exp(-g))
            act = jnp.where(routed, g * sig * u, 0.0).astype(bf16)
            act_ref[l, span] = act
            y = gate * dot(act, weights[:, 2 * FF :], NT).astype(bf16).astype(f32)
            dy = (gate * up_ref[span].astype(f32)).astype(bf16)
            dact = dot(dy, weights[:, 2 * FF :], NN)
            dg = dact * u * sig * (1.0 + g * (1.0 - sig))
            du = dact * g * sig
            dgu = jnp.where(routed, jnp.concatenate([dg, du], axis=1), 0.0).astype(bf16)
            dgu_ref[l, span] = dgu
            d = dot(dgu, weights[:, : 2 * FF], NT).astype(bf16).astype(f32)
            if l == 0:
                y_sum[span] = y
                d_sum[span] = d
            elif l < local - 1:
                y_sum[span] += y
                d_sum[span] += d
            else:
                y_ref[span] = (y_sum[span] + y).astype(bf16)
                d_ref[span] = (d_sum[span] + d).astype(bf16)
            return 0

        lax.fori_loop(0, h2_ref.shape[0] // size, step, 0)


def call_experts(h2, up, we, cols):
    f32, bf16 = jnp.float32, jnp.bfloat16
    length, local = h2.shape[0], we.shape[0]
    shaped = jax.ShapeDtypeStruct
    vmem = pl.BlockSpec(memory_space=pltpu.VMEM)
    outs = [
        shaped((length, D), bf16),
        shaped((length, D), bf16),
        shaped((local, length, FF), bf16),
        shaped((local, length, 2 * FF), bf16),
    ]
    return pl.pallas_call(
        expert_kernel,
        out_shape=outs,
        in_specs=[vmem] * 4,
        out_specs=[vmem] * 4,
        scratch_shapes=[pltpu.VMEM((length, D), f32)] * 2,
        compiler_params=pltpu.CompilerParams(vmem_limit_bytes=60 * 2**20),
        name="experts",
    )(h2, up, we, cols)


class LineScatter:
    def __init__(self, part, where, pair, out, inbox, own, sems):
        self.part, self.where = part, where
        self.pair, self.out, self.inbox, self.own = pair, out, inbox, own
        self.pair_sent, self.pair_landed, self.sent, self.landed = sems
        self.live = []

    def _pair_copy(self, there):
        i, e, z, c = self.where
        return remote(
            self.part(there * 2 + 1 - c), self.pair.at[there],
            self.pair_sent.at[there], self.pair_landed.at[there], (i, z * 2 + 1 - c),
        )

    def start(self):
        _, _, z, _ = self.where
        for k in (2, 1, 3, 0):
            copy = self._pair_copy(lax.rem(z + k, LINE))
            copy.start()
            self.live.append(copy)

    def fold(self):
        i, e, z, c = self.where
        for k in (2, 1, 3, 0):
            there = lax.rem(z + k, LINE)
            self._pair_copy(there).wait_recv()
            mine = self.part(there * 2 + c)[...].astype(jnp.float32)
            both = mine + self.pair[there].astype(jnp.float32)
            if k == 0:
                self.own[...] = both
            else:
                self.out[there] = both.astype(jnp.bfloat16)
                copy = remote(
                    self.out.at[there], self.inbox.at[z], self.sent.at[there], self.landed.at[z],
                    (i, there * 2 + c),
                )
                copy.start()
                self.live.append(copy)

    def total(self):
        i, e, z, c = self.where
        summed = self.own[...]
        for k in range(1, LINE):
            there = lax.rem(z + k, LINE)
            slot = self.inbox.at[there]
            remote(slot, slot, self.sent.at[there], self.landed.at[there], (i, z * 2 + 1 - c)).wait_recv()
            summed = summed + self.inbox[there].astype(jnp.float32)
        return summed

    def drain(self):
        for copy in self.live:
            copy.wait_send()
        self.live = []


def norm_back(values, gain, upper):
    scale = rms_rows(values)
    scaled = upper * gain
    inner = jnp.mean(values * scaled, axis=-1, keepdims=True)
    return scale * scaled - values * (scale * scale * scale) * inner, upper * values * scale


def finish_kernel(
    x_all, up_all, h1_all, qkv_ref, lse_ref, w_mine, wo_all, o_own, h2_ref, r_own, cols_ref, docs_ref, gains_ref,
    y_ref, d_ref, act_ref, dgu_ref, cos_ref, sin_ref,
    block_ref, grad_ref, norm_ref, ge_ref, ga_ref, gn_ref,
    pair, out, inbox, y_pair, y_out, y_inbox, own, y_own, da_all, ge_out, ge_in, do_ref, dkv_ref, dqkv_ref,
    ga_out, ga_in, gs_ref, gn_in, dh_ref, mix_out, mix_in, sq_in, dr_ref, gwo_ref,
    d_sems, y_sems, h_sems, da_sent, da_passed, da_landed, ge_sent, ge_landed, ga_sent, ga_landed,
    gn_sent, gn_landed, gs_sent, gs_landed, mix_sent, mix_landed, sq_sent, sq_landed,
):
    f32, bf16 = jnp.float32, jnp.bfloat16
    where = i, e, z, c = whereabouts()
    sibling = (i, z * 2 + 1 - c)
    rows = x_all.shape[1]
    length = rows * SPAN
    local = act_ref.shape[0]
    deep = ge_ref.shape[1]
    live = []

    def go(*spec):
        copy = remote(*spec)
        copy.start()
        live.append(copy)

    def four(sems):
        return [sems.at[n] for n in range(4)]

    def block_of(ref):
        return lambda s: ref.at[pl.ds(pl.multiple_of(s * rows, rows), rows)]

    greet(i, e)
    d_scatter = LineScatter(block_of(d_ref), where, pair, out, inbox, own, four(d_sems))
    y_scatter = LineScatter(block_of(y_ref), where, y_pair, y_out, y_inbox, y_own, four(y_sems))
    d_scatter.start()

    def expert_chunk(l, there):
        span = pl.ds(pl.multiple_of(there * deep, deep), deep)
        gate = cols_ref[:, l : l + 1]
        inward = dot(h2_ref[:, span], dgu_ref[l], TN)
        dy = (gate * up_all[:, :, span].reshape(length, deep).astype(f32)).astype(bf16)
        return inward, dot(dy, act_ref[l], TN)

    def send_chunk(l, k):
        there = lax.rem(i + k, PLANE)
        inward, down = expert_chunk(l, there)
        ge_out[l, k - 1, :, : 2 * FF] = inward.astype(bf16)
        ge_out[l, k - 1, :, 2 * FF :] = down.astype(bf16)
        go(ge_out.at[l, k - 1], ge_in.at[l, k - 1], ge_sent.at[l, k - 1], ge_landed.at[l, k - 1], (there, e))

    send_chunk(0, 3)
    d_scatter.fold()
    y_scatter.start()
    for l, k in ((0, 2), (0, 1), (1, 3), (1, 2), (1, 1)):
        send_chunk(l, k)
    for l in range(local):
        inward, down = expert_chunk(l, i)
        ge_ref[l, :, : 2 * FF] = inward
        ge_ref[l, :, 2 * FF :] = down

    gain_one, gain_two = gains_ref[3:4], gains_ref[4:5]
    back, shares = norm_back(r_own[...], gain_two, d_scatter.total())
    dr = up_all[e].astype(f32) + back
    dr_ref[...] = dr
    gn_two = jnp.sum(shares, axis=0, keepdims=True)
    da_all[e] = dr.astype(bf16)
    da_gather = LineGather(lambda s: da_all.at[s], where, da_sent, da_passed, da_landed)
    da_gather.start()
    own_cols = pl.ds(pl.multiple_of(e * 128, 128), 128)
    wo_mine = wo_all[:, :, :, :, own_cols].reshape(D, 128)

    def through_output(s):
        do_ref[pl.ds(pl.multiple_of(s * rows, rows), rows)] = dot(da_all[s], wo_mine, NN).astype(bf16)

    through_output(e)
    for k in range(1, LINE):
        da_gather.forward(k)
        through_output(da_gather.near(k))
    da_gather.wait(da_gather.sibling())
    through_output(da_gather.sibling())
    for k in range(1, LINE):
        da_gather.wait(da_gather.far(k))
        through_output(da_gather.far(k))
    y_scatter.fold()

    docs_row = docs_ref[2:3]
    docs_col = cols_ref[:, 2:3]
    dkv_ref[...] = jnp.zeros_like(dkv_ref)
    for first in range(0, length, QUERY_BLOCK):
        low, high = block_view(first, length // 2)
        visible = visible_keys(first, low, high, docs_row, docs_col)
        span = slice(first, first + QUERY_BLOCK)
        keys, values = qkv_ref[low:high, 128:192], qkv_ref[low:high, 192:256]
        dqs, dk, dv = [], 0.0, 0.0
        for head in range(2):
            q = qkv_ref[span, head * HD : (head + 1) * HD]
            do = do_ref[span, head * HD : (head + 1) * HD]
            scores = dot(q, keys, NT) * HD**-0.5
            probs = jnp.exp(jnp.where(visible, scores - lse_ref[span, head : head + 1], -1e30))
            dp = dot(do, values, NT)
            delta = jnp.sum(probs * dp, axis=-1, keepdims=True)
            ds = (probs * (dp - delta)).astype(bf16)
            dqs.append(dot(ds, keys, NN))
            dk = dk + dot(ds, q, TN)
            dv = dv + dot(probs.astype(bf16), do, TN)
        dkv_ref[low:high] += jnp.concatenate([dk * HD**-0.5, dv], axis=1)
        dq = jnp.concatenate(dqs, axis=1) * HD**-0.5
        dqkv_ref[span, :128] = (dq * cos_ref[span, :128] - half_turn_tile(dq) * sin_ref[span, :128]).astype(bf16)
    for first in range(0, length, QUERY_BLOCK):
        span = slice(first, first + QUERY_BLOCK)
        dkv = dkv_ref[span]
        dqkv_ref[span, 128:] = (dkv * cos_ref[span, 128:] - half_turn_tile(dkv) * sin_ref[span, 128:]).astype(bf16)

    h1 = h1_all[...].reshape(length, D)
    da = da_all[...].reshape(length, D)
    o = o_own[...]
    dqkv = dqkv_ref[...]
    for k in (2, 1, 3, 0):
        there = lax.rem(i + k, PLANE)
        span = pl.ds(pl.multiple_of(there * deep, deep), deep)
        h1_part = h1_all[:, :, span].reshape(length, deep)
        da_part = da_all[:, :, span].reshape(length, deep)
        projections, output = dot(h1_part, dqkv, TN), dot(da_part, o, TN)
        if k == 0:
            gs_ref[:, :256] = projections
            gs_ref[:, 256:] = output
        else:
            ga_out[k - 1, :, :256] = projections.astype(bf16)
            ga_out[k - 1, :, 256:] = output.astype(bf16)
            go(ga_out.at[k - 1], ga_in.at[k - 1], ga_sent.at[k - 1], ga_landed.at[k - 1], (there, e))

    weights = w_mine[...].reshape(D, 256)
    gn_one = jnp.zeros((1, D), f32)
    for first in range(0, length, QUERY_BLOCK):
        span = slice(first, first + QUERY_BLOCK)
        slots = slice(first // rows, (first + QUERY_BLOCK) // rows)
        dh = dot(dqkv_ref[span], weights, NT)
        values = x_all[slots].reshape(QUERY_BLOCK, D).astype(f32)
        gn_one = gn_one + jnp.sum(dh * values * rms_rows(values), axis=0, keepdims=True)
        dh_ref[span] = dh.astype(bf16)
    h_scatter = LineScatter(block_of(dh_ref), where, pair, out, inbox, own, four(h_sems))
    d_scatter.drain()
    h_scatter.start()
    gn_in[i] = jnp.concatenate([gn_one, gn_two, jnp.zeros((6, D), f32)], axis=0)
    for k in range(1, PLANE):
        go(gn_in.at[i], gn_in.at[i], gn_sent.at[k], gn_landed.at[i], (lax.rem(i + k, PLANE), e))

    block_ref[...] = (r_own[...] + y_scatter.total()).astype(bf16)
    h_scatter.fold()
    for k in (2, 1, 3):
        there = lax.rem(i + k, PLANE)
        remote(ga_out.at[k - 1], ga_in.at[k - 1], ga_sent.at[k - 1], ga_landed.at[k - 1], sibling).wait_recv()
        gs_ref[...] += ga_in[k - 1].astype(f32)
        remote(gn_in.at[i], gn_in.at[there], gn_sent.at[k], gn_landed.at[there], sibling).wait_recv()
    part = gs_ref.shape[0] // SPAN
    for s in range(SPAN):
        mix = gs_ref[s * part : (s + 1) * part]
        gwo_ref[s] = mix
    for k in range(1, SPAN):
        there = lax.rem(e + k, SPAN)
        go(gwo_ref.at[there], ga_ref.at[e], gs_sent.at[there], gs_landed.at[e], (i, there))
    ga_ref[e] = gwo_ref[e]
    squares = jnp.sum(gs_ref[...] * gs_ref[...])
    for l in range(local):
        for k in (3, 2, 1):
            remote(
                ge_out.at[l, k - 1], ge_in.at[l, k - 1], ge_sent.at[l, k - 1], ge_landed.at[l, k - 1], sibling
            ).wait_recv()
        for first in range(0, deep, 64):
            span = slice(first, first + 64)
            summed = ge_ref[l, span]
            for k in (3, 2, 1):
                summed = summed + ge_in[l, k - 1, span].astype(f32)
            ge_ref[l, span] = summed
            squares = squares + jnp.sum(summed * summed)
    gains = gn_in[0] + gn_in[1] + gn_in[2] + gn_in[3]
    row = lax.broadcasted_iota(jnp.int32, gains.shape, 0)
    mix_in[e] = jnp.where(row == 2, squares, gains)
    for k in range(1, SPAN):
        there = lax.rem(e + k, SPAN)
        go(mix_in.at[e], mix_in.at[e], mix_sent.at[k], mix_landed.at[e], (i, there))
    for k in range(1, SPAN):
        there = lax.rem(e + k, SPAN)
        remote(mix_in.at[e], mix_in.at[there], mix_sent.at[k], mix_landed.at[there], sibling).wait_recv()
    mixed = mix_in[0]
    for s in range(1, SPAN):
        mixed = mixed + mix_in[s]
    gn_ref[...] = mixed
    sq_in[i] = jnp.broadcast_to(mixed[2:3, :128], (8, 128))
    for k in range(1, PLANE):
        go(sq_in.at[i], sq_in.at[i], sq_sent.at[k], sq_landed.at[i], (lax.rem(i + k, PLANE), e))
    gain_squares = jnp.sum(jnp.where(row < 2, mixed * mixed, 0.0))
    for k in range(1, PLANE):
        there = lax.rem(i + k, PLANE)
        remote(sq_in.at[i], sq_in.at[there], sq_sent.at[k], sq_landed.at[there], sibling).wait_recv()
    norm_ref[...] = jnp.sqrt(sq_in[0] + sq_in[1] + sq_in[2] + sq_in[3] + gain_squares)

    for k in range(1, SPAN):
        there = lax.rem(e + k, SPAN)
        remote(gwo_ref.at[there], ga_ref.at[there], gs_sent.at[there], gs_landed.at[there], sibling).wait_recv()
    back, _ = norm_back(x_all[e].astype(f32), gain_one, h_scatter.total())
    grad_ref[...] = dr_ref[...] + back
    for copy in live:
        copy.wait_send()
    for item in (da_gather, y_scatter, h_scatter):
        item.drain()


def call_finish(x, up, h1, qkv, lse, w_mine, w_out, o, h2, r, cols, docs, gains, y, d, act, dgu, cosine, sine):
    f32, bf16 = jnp.float32, jnp.bfloat16
    rows, length = x.shape[1], x.shape[0] * x.shape[1]
    local = act.shape[0]
    deep = D // PLANE
    part = deep // SPAN
    shaped = jax.ShapeDtypeStruct
    vmem = pl.BlockSpec(memory_space=pltpu.VMEM)
    outs = [
        shaped((rows, D), bf16),
        shaped((rows, D), f32),
        shaped((8, 128), f32),
        shaped((local, deep, 3 * FF), f32),
        shaped((SPAN, part, 384), f32),
        shaped((8, D), f32),
    ]
    dma, held = pltpu.SemaphoreType.DMA, pltpu.VMEM
    slots = held((LINE, rows, D), bf16)
    scratch = [
        slots, slots, slots, slots, slots, slots,
        held((rows, D), f32), held((rows, D), f32),
        held((SPAN, rows, D), bf16),
        held((local, PLANE - 1, deep, 3 * FF), bf16), held((local, PLANE - 1, deep, 3 * FF), bf16),
        held((length, 128), bf16), held((length, 128), f32), held((length, 256), bf16),
        held((PLANE - 1, deep, 384), bf16), held((PLANE - 1, deep, 384), bf16), held((deep, 384), f32),
        held((PLANE, 8, D), f32),
        held((length, D), bf16),
        held((8, D), f32), held((SPAN, 8, D), f32), held((PLANE, 8, 128), f32),
        held((rows, D), f32), held((SPAN, part, 384), f32),
        dma((4, LINE)), dma((4, LINE)), dma((4, LINE)),
        dma((LINE,)), dma((LINE - 1,)), dma((SPAN,)),
        dma((local, PLANE - 1)), dma((local, PLANE - 1)), dma((PLANE - 1,)), dma((PLANE - 1,)),
        dma((PLANE,)), dma((PLANE,)), dma((SPAN,)), dma((SPAN,)),
        dma((SPAN,)), dma((SPAN,)), dma((PLANE,)), dma((PLANE,)),
    ]
    args = (x, up, h1, qkv, lse, w_mine, w_out, o, h2, r, cols, docs, gains, y, d, act, dgu, cosine, sine)
    return pl.pallas_call(
        finish_kernel,
        out_shape=outs,
        in_specs=[vmem] * len(args),
        out_specs=[vmem] * len(outs),
        scratch_shapes=scratch,
        compiler_params=pltpu.CompilerParams(
            collective_id=1, has_side_effects=True, vmem_limit_bytes=62 * 2**20
        ),
        name="finish",
    )(*args)


def fast_body(
    activations,
    doc_ids,
    routes,
    gate_weights,
    cotangent,
    step_count,
    w_attn,
    norm_gains,
    w_expert,
    first_attn,
    second_attn,
    first_gains,
    second_gains,
    first_expert,
    second_expert,
):
    f32, bf16 = jnp.float32, jnp.bfloat16
    rows = activations.shape[1]
    span = lax.axis_size("expert")
    place = lax.axis_index("expert")
    length = rows * span
    local = w_expert.shape[0]
    total = local * span
    wa = w_attn.astype(bf16)
    grouped = group_columns(wa, span)[:, :, :256]
    hits = routes[0][:, :, None] == jnp.arange(total, dtype=jnp.int32)
    dense = jnp.sum(jnp.where(hits, gate_weights[0][:, :, None], 0.0), axis=1).T
    low = norm_gains.T
    lane = jnp.arange(rows)
    index = lax.axis_index("dp") * span + place
    spread = jnp.where(lane // low.shape[1] == index % (rows // low.shape[1]), jnp.tile(low, (1, rows // low.shape[1])), 0.0)
    shared = jnp.concatenate([doc_ids.astype(f32), spread], axis=0)
    pack = jnp.concatenate(
        [
            dense.reshape(span, local, rows),
            jnp.broadcast_to(shared[None], (span, 3, rows)),
            jnp.zeros((span, 8 - local - 3, rows), f32),
        ],
        axis=1,
    )
    cosine, sine = head_tables(length)
    x_all, up_all, h1, qkv, lse, w_mine, w_out, w_exp, o, h2, r_own, cols, docs, gains = call_start(
        activations[0], cotangent[0], grouped, wa[:, QKV:], w_expert.astype(bf16), pack, cosine, sine
    )
    y_part, d_part, act, dgu = call_experts(h2, up_all.reshape(length, D), w_exp, cols)
    block, input_total, norm, grad_expert, grad_grouped, gn = call_finish(
        x_all, up_all, h1, qkv, lse, w_mine, w_out, o, h2, r_own, cols, docs, gains,
        y_part, d_part, act, dgu, cosine, sine,
    )
    grad_norm = norm[0, 0]
    grad_attn = ungroup_columns(grad_grouped)
    grad_gains = lax.dynamic_slice_in_dim(gn[:2], index * low.shape[1], low.shape[1], 1).T
    clip = jnp.minimum(1.0, CLIP_NORM / (grad_norm + 1e-06))
    steps = step_count.astype(f32)
    attn = adam_update(
        w_attn, first_attn, second_attn, grad_attn * clip, steps, WEIGHT_DECAY, LEARN_RATE
    )
    gain = adam_update(
        norm_gains, first_gains, second_gains, grad_gains * clip, steps, 0.0, GAIN_RATE
    )
    expert = adam_update(
        w_expert, first_expert, second_expert, grad_expert * clip, steps, WEIGHT_DECAY, LEARN_RATE
    )
    return (block[None], input_total[None], grad_norm, *attn, *gain, *expert)


def solution(mesh):
    in_specs = (
        P("dp", "expert", None),
        P("dp", "expert"),
        P("dp", "expert", None),
        P("dp", "expert", None),
        P("dp", "expert", None),
        P(),
        P(("dp", "expert"), None),
        P(("dp", "expert"), None),
        P("expert", "dp", None),
        P(("dp", "expert"), None),
        P(("dp", "expert"), None),
        P(("dp", "expert"), None),
        P(("dp", "expert"), None),
        P("expert", "dp", None),
        P("expert", "dp", None),
    )
    out_specs = (
        P("dp", "expert", None),
        P("dp", "expert", None),
        P(),
        P(("dp", "expert"), None),
        P(("dp", "expert"), None),
        P(("dp", "expert"), None),
        P(("dp", "expert"), None),
        P(("dp", "expert"), None),
        P(("dp", "expert"), None),
        P("expert", "dp", None),
        P("expert", "dp", None),
        P("expert", "dp", None),
    )
    body = fast_body if fits(mesh) else general_body
    return jax.shard_map(body, mesh=mesh, in_specs=in_specs, out_specs=out_specs, check_vma=False)
```

```python
import jax
import jax.numpy as jnp
from jax import lax
from jax.sharding import PartitionSpec as P
import types

import numpy as np
from jax.experimental import pallas as pl
from jax.experimental.pallas import tpu as pltpu

D = 1024
H = 16
KVH = 8
HD = 64
FF = 512
TOP = 8
QD = 1024
KVD = 512
QKV = 2048


EPSILON = 1e-05
ROPE_BASE = 10000.0
CLIP_NORM = 1.0
BETA_ONE = 0.9
BETA_TWO = 0.95
ADAM_EPSILON = 1e-08
LEARN_RATE = 0.03
GAIN_RATE = 0.4
WEIGHT_DECAY = 0.1


def rms_scale(values, gain):
    return values * lax.rsqrt(jnp.mean(values * values, axis=-1, keepdims=True) + EPSILON) * gain


def rope_tables(positions, head_width):
    halves = jnp.arange(head_width // 2, dtype=jnp.float32)
    inverse = ROPE_BASE ** (-2.0 * halves / head_width)
    angles = positions.astype(jnp.float32)[:, None] * inverse[None, :]
    angles = jnp.concatenate([angles, angles], axis=-1)
    return (jnp.cos(angles)[:, None, :], jnp.sin(angles)[:, None, :])


def rotate(values, cosine, sine_table):
    middle = values.shape[-1] // 2
    turned = jnp.concatenate([-values[..., middle:], values[..., :middle]], axis=-1)
    return values * cosine + turned * sine_table


def unrotate(gradient, cosine, sine_table):
    middle = gradient.shape[-1] // 2
    product = gradient * sine_table
    turned = jnp.concatenate([product[..., middle:], -product[..., :middle]], axis=-1)
    return gradient * cosine + turned


def adam_update(weight, moment_one, second, gradient, steps_done, decay_rate, step_rate):
    first_new = BETA_ONE * moment_one + (1.0 - BETA_ONE) * gradient
    second_new = BETA_TWO * second + (1.0 - BETA_TWO) * gradient * gradient
    first_hat = first_new / (1.0 - BETA_ONE**steps_done)
    second_hat = second_new / (1.0 - BETA_TWO**steps_done)
    weight_new = weight - step_rate * (
        first_hat / (jnp.sqrt(second_hat) + ADAM_EPSILON) + decay_rate * weight
    )
    return (weight_new, first_new, second_new)


def attn_fetch(w_attn, norm_gains):
    return (
        lax.all_gather(w_attn.astype(jnp.bfloat16), ("dp", "expert"), axis=0, tiled=True),
        lax.all_gather(norm_gains.astype(jnp.bfloat16), ("dp", "expert"), axis=0, tiled=True),
    )


def expert_fetch(w_expert):
    return lax.all_gather(w_expert.astype(jnp.bfloat16), "dp", axis=1, tiled=True)


def to_owner(buffer):
    return lax.all_to_all(buffer, "expert", split_axis=0, concat_axis=1, tiled=True)


def to_sender(buffer):
    return lax.all_to_all(buffer, "expert", split_axis=1, concat_axis=0, tiled=True)


def expert_forward(received, expert_cols):
    gate_up = jnp.einsum(
        "esd,edf->esf", received, expert_cols[:, :, : 2 * FF], preferred_element_type=jnp.float32
    )
    activated = (jax.nn.silu(gate_up[..., :FF]) * gate_up[..., FF:]).astype(jnp.bfloat16)
    return (gate_up, activated)


def general_body(
    activations,
    doc_ids,
    routes,
    gate_weights,
    cotangent,
    step_count,
    w_attn,
    norm_gains,
    w_expert,
    first_attn,
    second_attn,
    first_gains,
    second_gains,
    first_expert,
    second_expert,
):
    row_count = activations.shape[1]
    span_size = lax.axis_size("expert")
    shard_pos = lax.axis_index("expert")
    seq_length = row_count * span_size
    expert_total = w_expert.shape[0] * span_size
    capacity = (row_count * TOP * 9 + expert_total * 8 - 1) // (expert_total * 8)
    group_size = H // KVH
    score_scale = HD ** (-0.5)
    hidden_in = activations[0].astype(jnp.float32)
    upstream = cotangent[0].astype(jnp.float32)
    attn_cols, gain_pair = attn_fetch(w_attn, norm_gains)
    expert_cols = expert_fetch(w_expert)
    gain_one = gain_pair[:, 0].astype(jnp.float32)
    gain_two = gain_pair[:, 1].astype(jnp.float32)
    w_project = attn_cols[:, :QKV]
    w_output = attn_cols[:, QKV:]
    normed = rms_scale(hidden_in, gain_one).astype(jnp.bfloat16)
    projected = jnp.dot(normed, w_project, preferred_element_type=jnp.float32)
    positions = shard_pos * row_count + jnp.arange(row_count, dtype=jnp.int32)
    cosine, sine_table = rope_tables(positions, HD)
    queries = rotate(projected[:, :QD].reshape(row_count, H, HD), cosine, sine_table).astype(
        jnp.bfloat16
    )
    key_heads = rotate(
        projected[:, QD : QD + KVD].reshape(row_count, KVH, HD), cosine, sine_table
    ).astype(jnp.bfloat16)
    value_heads = projected[:, QD + KVD :].astype(jnp.bfloat16)
    key_all, value_all, doc_all = (
        lax.all_gather(key_heads.reshape(row_count, KVD), "expert", axis=0, tiled=True),
        lax.all_gather(value_heads, "expert", axis=0, tiled=True),
        lax.all_gather(doc_ids[0].astype(jnp.bfloat16), "expert", axis=0, tiled=True),
    )
    key_docs = doc_all.astype(jnp.int32)
    query_docs = doc_ids[0]
    query_groups = queries.reshape(row_count, KVH, group_size, HD)
    key_block = min(512, seq_length)
    needed = (shard_pos * row_count + row_count + key_block - 1) // key_block

    def block_scores(block_id):
        first_key = block_id * key_block
        key_part = lax.dynamic_slice_in_dim(key_all, first_key, key_block, 0).reshape(
            key_block, KVH, HD
        )
        raw_scores = (
            jnp.einsum("tgrd,kgd->grtk", query_groups, key_part, preferred_element_type=jnp.float32)
            * score_scale
        )
        key_pos = first_key + jnp.arange(key_block, dtype=jnp.int32)
        key_doc = lax.dynamic_slice_in_dim(key_docs, first_key, key_block, 0)
        visible = (key_pos[None, :] <= positions[:, None]) & (
            key_doc[None, :] == query_docs[:, None]
        )
        return (raw_scores, visible, key_part)

    def value_part(block_id):
        return lax.dynamic_slice_in_dim(value_all, block_id * key_block, key_block, 0).reshape(
            key_block, KVH, HD
        )

    def total_step(block_id, running):
        row_peak, row_total = running
        raw_scores, visible, _ = block_scores(block_id)
        masked = jnp.where(visible, raw_scores, -1e30)
        new_peak = jnp.maximum(row_peak, jnp.max(masked, axis=-1))
        scaled = jnp.where(visible, jnp.exp(masked - new_peak[..., None]), 0.0)
        return (new_peak, row_total * jnp.exp(row_peak - new_peak) + jnp.sum(scaled, axis=-1))

    start_peak = jnp.full((KVH, group_size, row_count), -1e30, jnp.float32)
    start_total = jnp.zeros((KVH, group_size, row_count), jnp.float32)
    row_peak, row_total = lax.fori_loop(0, needed, total_step, (start_peak, start_total))
    log_total = row_peak + jnp.log(row_total)

    def exact_probs(raw_scores, visible):
        return jnp.exp(jnp.where(visible, raw_scores - log_total[..., None], -1e30))

    def output_step(block_id, summed):
        raw_scores, visible, _ = block_scores(block_id)
        weights_low = exact_probs(raw_scores, visible).astype(jnp.bfloat16)
        return summed + jnp.einsum(
            "grtk,kgd->tgrd", weights_low, value_part(block_id), preferred_element_type=jnp.float32
        )

    attended = lax.fori_loop(
        0, needed, output_step, jnp.zeros((row_count, KVH, group_size, HD), jnp.float32)
    )
    attended = attended.reshape(row_count, QD).astype(jnp.bfloat16)
    branch = jnp.einsum("tc,dc->td", attended, w_output, preferred_element_type=jnp.float32)
    residual = hidden_in + branch
    normed_two = rms_scale(residual, gain_two).astype(jnp.bfloat16)
    flat_routes = routes[0].reshape(-1)
    one_hot = (flat_routes[:, None] == jnp.arange(expert_total, dtype=jnp.int32)[None, :]).astype(
        jnp.int32
    )
    ranking = jnp.sum((jnp.cumsum(one_hot, axis=0) - 1) * one_hot, axis=1)
    places = flat_routes * capacity + ranking
    owners = jnp.arange(row_count * TOP, dtype=jnp.int32) // TOP
    source = jnp.zeros((expert_total * capacity,), jnp.int32).at[places].set(owners)
    filled = jnp.zeros((expert_total * capacity,), jnp.int32).at[places].set(1) > 0
    slot_gate = (
        jnp.zeros((expert_total * capacity,), jnp.float32)
        .at[places]
        .set(gate_weights[0].reshape(-1))
    )
    outgoing = jnp.where(filled[:, None], normed_two[source], jnp.zeros((), jnp.bfloat16)).reshape(
        expert_total, capacity, D
    )
    received = to_owner(outgoing)
    gate_up, activated = expert_forward(received, expert_cols)
    expert_out = jnp.einsum(
        "esf,edf->esd", activated, expert_cols[:, :, 2 * FF :], preferred_element_type=jnp.float32
    ).astype(jnp.bfloat16)
    returned = to_sender(expert_out).reshape(expert_total * capacity, D)
    picked = returned[places].reshape(row_count, TOP, D).astype(jnp.float32)
    combined = jnp.sum(gate_weights[0][..., None] * picked, axis=1)
    block_result = (residual + combined).astype(jnp.bfloat16)
    slot_grad = jnp.where(filled[:, None], slot_gate[:, None] * upstream[source], 0.0)
    slot_grad = slot_grad.astype(jnp.bfloat16).reshape(expert_total, capacity, D)
    owner_grad = to_owner(slot_grad)
    attn_cols, gain_pair = attn_fetch(w_attn, norm_gains)
    w_project = attn_cols[:, :QKV]
    w_output = attn_cols[:, QKV:]
    expert_cols = expert_fetch(w_expert)
    gate_up, activated = expert_forward(received, expert_cols)
    gate_part = gate_up[..., :FF]
    up_part = gate_up[..., FF:]
    sigmoid_gate = jax.nn.sigmoid(gate_part)
    act_grad = jnp.einsum(
        "esd,edf->esf", owner_grad, expert_cols[:, :, 2 * FF :], preferred_element_type=jnp.float32
    )
    gate_grad = act_grad * up_part * sigmoid_gate * (1.0 + gate_part * (1.0 - sigmoid_gate))
    lift_grad = act_grad * gate_part * sigmoid_gate
    mixed_grad = jnp.concatenate([gate_grad, lift_grad], axis=-1).astype(jnp.bfloat16)
    down_grad = jnp.einsum(
        "esf,esd->edf", activated, owner_grad, preferred_element_type=jnp.float32
    )
    inward_grad = jnp.einsum(
        "esd,esf->edf", received, mixed_grad, preferred_element_type=jnp.float32
    )
    row_grads = jnp.einsum(
        "esf,edf->esd", mixed_grad, expert_cols[:, :, : 2 * FF], preferred_element_type=jnp.float32
    ).astype(jnp.bfloat16)
    back_rows = to_sender(row_grads).reshape(expert_total * capacity, D)
    normed_two_grad = jnp.sum(
        back_rows[places].reshape(row_count, TOP, D).astype(jnp.float32), axis=1
    )
    _, second_pull = jax.vjp(rms_scale, residual, gain_two)
    resid_grad, gain_two_grad = second_pull(normed_two_grad)
    resid_grad = upstream + resid_grad
    branch_grad = resid_grad.astype(jnp.bfloat16)
    output_grad = jnp.einsum("td,tc->dc", branch_grad, attended, preferred_element_type=jnp.float32)
    attended_grad = jnp.dot(branch_grad, w_output, preferred_element_type=jnp.float32).astype(
        jnp.bfloat16
    )
    grad_groups = attended_grad.reshape(row_count, KVH, group_size, HD)

    def delta_step(block_id, summed):
        raw_scores, visible, _ = block_scores(block_id)
        probs_full = exact_probs(raw_scores, visible)
        prob_grad = jnp.einsum(
            "tgrd,kgd->grtk", grad_groups, value_part(block_id), preferred_element_type=jnp.float32
        )
        return summed + jnp.sum(probs_full * prob_grad, axis=-1)

    delta_rows = lax.fori_loop(
        0, needed, delta_step, jnp.zeros((KVH, group_size, row_count), jnp.float32)
    )

    def grad_step(block_id, running):
        query_grad, key_grad, value_grad = running
        raw_scores, visible, key_part = block_scores(block_id)
        probs_full = exact_probs(raw_scores, visible)
        prob_grad = jnp.einsum(
            "tgrd,kgd->grtk", grad_groups, value_part(block_id), preferred_element_type=jnp.float32
        )
        score_grad = (probs_full * (prob_grad - delta_rows[..., None])).astype(jnp.bfloat16)
        query_grad = (
            query_grad
            + jnp.einsum("grtk,kgd->tgrd", score_grad, key_part, preferred_element_type=jnp.float32)
            * score_scale
        )
        key_piece = (
            jnp.einsum(
                "grtk,tgrd->kgd", score_grad, query_groups, preferred_element_type=jnp.float32
            )
            * score_scale
        )
        value_piece = jnp.einsum(
            "grtk,tgrd->kgd",
            probs_full.astype(jnp.bfloat16),
            grad_groups,
            preferred_element_type=jnp.float32,
        )
        first_key = block_id * key_block
        key_grad = lax.dynamic_update_slice_in_dim(
            key_grad, key_piece.reshape(key_block, KVD), first_key, 0
        )
        value_grad = lax.dynamic_update_slice_in_dim(
            value_grad, value_piece.reshape(key_block, KVD), first_key, 0
        )
        return (query_grad, key_grad, value_grad)

    start_grads = (
        jnp.zeros((row_count, KVH, group_size, HD), jnp.float32),
        jnp.zeros((seq_length, KVD), jnp.float32),
        jnp.zeros((seq_length, KVD), jnp.float32),
    )
    query_grad, key_grad, value_grad = lax.fori_loop(0, needed, grad_step, start_grads)
    key_sum, value_sum = (
        lax.psum_scatter(key_grad, "expert", scatter_dimension=0, tiled=True),
        lax.psum_scatter(value_grad, "expert", scatter_dimension=0, tiled=True),
    )
    query_back = unrotate(query_grad.reshape(row_count, H, HD), cosine, sine_table).reshape(
        row_count, QD
    )
    key_back = unrotate(key_sum.reshape(row_count, KVH, HD), cosine, sine_table).reshape(
        row_count, KVD
    )
    project_grad = jnp.concatenate([query_back, key_back, value_sum], axis=1).astype(jnp.bfloat16)
    weight_grad_qkv = jnp.einsum(
        "td,tc->dc", normed, project_grad, preferred_element_type=jnp.float32
    )
    normed_grad = jnp.einsum(
        "tc,dc->td", project_grad, w_project, preferred_element_type=jnp.float32
    )
    _, first_pull = jax.vjp(rms_scale, hidden_in, gain_one)
    input_part, gain_one_grad = first_pull(normed_grad)
    input_total = resid_grad + input_part
    attn_partial = jnp.concatenate([weight_grad_qkv, output_grad], axis=1)
    gain_partial = jnp.stack([gain_one_grad, gain_two_grad], axis=1)
    grad_attn, grad_gains = (
        lax.psum_scatter(attn_partial, ("dp", "expert"), scatter_dimension=0, tiled=True),
        lax.psum_scatter(gain_partial, ("dp", "expert"), scatter_dimension=0, tiled=True),
    )
    grad_expert = lax.psum_scatter(
        jnp.concatenate([inward_grad, down_grad], axis=2).astype(jnp.bfloat16),
        "dp",
        scatter_dimension=1,
        tiled=True,
    ).astype(jnp.float32)
    local_squares = (
        jnp.sum(grad_attn * grad_attn)
        + jnp.sum(grad_gains * grad_gains)
        + jnp.sum(grad_expert * grad_expert)
    )
    grad_norm = jnp.sqrt(lax.psum(local_squares, ("dp", "expert")))
    clip_factor = jnp.minimum(1.0, CLIP_NORM / (grad_norm + 1e-06))
    steps_done = step_count.astype(jnp.float32)
    attn_new = adam_update(
        w_attn,
        first_attn,
        second_attn,
        grad_attn * clip_factor,
        steps_done,
        WEIGHT_DECAY,
        LEARN_RATE,
    )
    gains_new = adam_update(
        norm_gains, first_gains, second_gains, grad_gains * clip_factor, steps_done, 0.0, GAIN_RATE
    )
    expert_new = adam_update(
        w_expert,
        first_expert,
        second_expert,
        grad_expert * clip_factor,
        steps_done,
        WEIGHT_DECAY,
        LEARN_RATE,
    )
    return (
        block_result[None],
        input_total[None],
        grad_norm,
        attn_new[0],
        attn_new[1],
        attn_new[2],
        gains_new[0],
        gains_new[1],
        gains_new[2],
        expert_new[0],
        expert_new[1],
        expert_new[2],
    )


def fits(mesh):
    return dict(mesh.shape) == {"dp": 4, "expert": KVH}


def head_tables(length):
    halves = np.arange(HD // 2, dtype=np.float32)
    inverse = np.power(np.float32(ROPE_BASE), np.float32(-2.0) * halves / np.float32(HD))
    angles = np.arange(length, dtype=np.float32)[:, None] * inverse[None, :]
    cosine, sine = np.cos(angles), np.sin(angles)
    cosine = np.concatenate([cosine] * 4, axis=1)
    return jnp.asarray(cosine), jnp.asarray(np.concatenate([-sine, sine] * 2, axis=1))


LINE, SPAN, PLANE, PARTS = 4, 8, 4, 4
QUERY_BLOCK = 256
NN, NT, TN = ((1,), (0,)), ((1,), (1,)), ((0,), (0,))


def remote(source, target, sent, landed, device):
    return pltpu.make_async_remote_copy(
        src_ref=source,
        dst_ref=target,
        send_sem=sent,
        recv_sem=landed,
        device_id=device,
        device_id_type=pl.DeviceIdType.MESH,
    )


def whereabouts():
    i, e = lax.axis_index("dp"), lax.axis_index("expert")
    return i, e, e // 2, lax.rem(e, 2)


def partners(i, e):
    others = [(i, lax.rem(e + k, SPAN)) for k in range(1, SPAN)]
    return others + [(lax.rem(i + k, PLANE), e) for k in range(1, PLANE)]


def piece(j, size):
    return pl.ds(pl.multiple_of(j * size, size), size)


class LineGather:
    def __init__(self, slot, source, where, sems):
        self.slot, self.source, self.where = slot, source, where
        self.sent, self.passed, self.landed = sems

    def _own(self, j, k):
        i, e, z, c = self.where
        there = z * 2 + 1 - c if k == 0 else lax.rem(z + k, LINE) * 2 + c
        return remote(self.source(j), self.slot(e, j), self.sent.at[j, k], self.landed.at[j, e], (i, there))

    def _pass(self, j, k):
        i, e, z, c = self.where
        index = lax.rem(z + k, LINE) * 2 + c
        place = self.slot(index, j)
        return remote(place, place, self.passed.at[j, k], self.landed.at[j, index], (i, z * 2 + 1 - c))

    def _relay(self, j):
        i, e, z, c = self.where
        index = lax.rem(z + 2, LINE) * 2 + c
        place = self.slot(index, j)
        end = LINE - 1 - lax.rem(z + 2, LINE)
        return remote(place, place, self.passed.at[j, 0], self.landed.at[j, index], (i, end * 2 + c))

    def _each_own(self, j, act):
        z = self.where[2]
        act(self._own(j, 2))
        pl.when(z != LINE - 1)(lambda: act(self._own(j, 1)))
        pl.when(z != 0)(lambda: act(self._own(j, 3)))
        act(self._own(j, 0))

    def _when_inner(self, act):
        z = self.where[2]
        pl.when((z > 0) & (z < LINE - 1))(act)

    def start(self, j):
        self._each_own(j, lambda copy: copy.start())

    def wait(self, j, index):
        i, e, z, c = self.where
        place = self.slot(index, j)
        remote(place, place, self.sent.at[j, 0], self.landed.at[j, index], (i, z * 2 + 1 - c)).wait_recv()

    def sibling(self):
        _, e, z, c = self.where
        return z * 2 + 1 - c

    def near(self, k):
        _, e, z, c = self.where
        return lax.rem(z + k, LINE) * 2 + c

    def far(self, k):
        _, e, z, c = self.where
        return lax.rem(z + k, LINE) * 2 + 1 - c

    def forward(self, j, k):
        self.wait(j, self.near(k))
        if k == 2:
            self._when_inner(lambda: self._relay(j).start())
        self._pass(j, k).start()

    def forward_all(self, j):
        for k in (2, 1, 3):
            self.forward(j, k)

    def rest(self, j):
        self.wait(j, self.sibling())
        for k in range(1, LINE):
            self.wait(j, self.far(k))

    def drain(self, j):
        self._each_own(j, lambda copy: copy.wait_send())
        self._when_inner(lambda: self._relay(j).wait_send())
        for k in range(1, LINE):
            self._pass(j, k).wait_send()


class LineScatter:
    def __init__(self, data, where, pair, out, inbox, own, sems, size):
        self.data, self.where, self.size = data, where, size
        self.pair, self.out, self.inbox, self.own = pair, out, inbox, own
        self.pair_sent, self.pair_landed, self.sent, self.landed = sems

    def _pair(self, j, k):
        i, e, z, c = self.where
        there, rows = lax.rem(z + k, LINE), piece(j, self.size)
        return remote(
            self.data.at[there * 2 + 1 - c, rows], self.pair.at[there, rows],
            self.pair_sent.at[j, there], self.pair_landed.at[j, there], (i, z * 2 + 1 - c),
        )

    def _send(self, j, k):
        i, e, z, c = self.where
        there, rows = lax.rem(z + k, LINE), piece(j, self.size)
        crossing = {1: z // (LINE - 1), 2: 0, 3: (LINE - 1 - z) // (LINE - 1)}[k]
        chip = {1: z + 1 - 2 * crossing, 2: there, 3: z - 1 + 2 * crossing}[k]
        slot = z + crossing * (chip - z)
        return remote(
            self.out.at[there, rows], self.inbox.at[slot, rows],
            self.sent.at[j, there], self.landed.at[j, slot], (i, chip * 2 + c),
        )

    def _landed(self, j, slot):
        i, e, z, c = self.where
        place = self.inbox.at[slot, piece(j, self.size)]
        remote(place, place, self.sent.at[j, slot], self.landed.at[j, slot], (i, z * 2 + 1 - c)).wait_recv()

    def _both(self, j, there):
        c, rows = self.where[3], piece(j, self.size)
        return self.data[there * 2 + c, rows].astype(jnp.float32) + self.pair[there, rows].astype(jnp.float32)

    def _across(self, j):
        there, rows = lax.rem(self.where[2] + 2, LINE), piece(j, self.size)
        return there, rows, self._both(j, there)

    def start(self, j):
        for k in (1, 3, 2, 0):
            self._pair(j, k).start()

    def start_one(self, j, k):
        self._pair(j, k).start()

    def fold_one(self, j, k):
        z, rows = self.where[2], piece(j, self.size)
        self._pair(j, k).wait_recv()

        def send():
            there = lax.rem(z + k, LINE)
            self.out[there, rows] = self._both(j, there).astype(jnp.bfloat16)
            self._send(j, k).start()

        if k == 0:
            self.own[rows] = self._both(j, z)
        elif k == 2:
            pl.when((z == 0) | (z == LINE - 1))(send)
        else:
            send()

    def fold(self, j):
        for k in (1, 3, 2, 0):
            self.fold_one(j, k)

    def fold_late(self, j):
        z = self.where[2]

        @pl.when((z > 0) & (z < LINE - 1))
        def _():
            there, rows, both = self._across(j)
            self._landed(j, z)
            self.out[there, rows] = (both + self.inbox[z, rows].astype(jnp.float32)).astype(jnp.bfloat16)
            self._send(j, 2).start()

    def total(self, j):
        z, rows = self.where[2], piece(j, self.size)

        def add(k):
            there = lax.rem(z + k, LINE)
            self._landed(j, there)
            self.own[rows] += self.inbox[there, rows].astype(jnp.float32)

        pl.when(z != LINE - 1)(lambda: add(1))
        pl.when(z != 0)(lambda: add(3))
        add(2)
        return self.own[rows]

    def drain(self, j):
        for k in range(LINE):
            self._pair(j, k).wait_send()
        for k in range(1, LINE):
            self._send(j, k).wait_send()


class PlaneGather:
    def __init__(self, where, held, sems):
        i, self.e = where[0], where[1]
        self.i, self.held, self.sems = i, held, sems
        self.x = i // 2 * 2 + 1 - lax.rem(i, 2)
        self.y = (1 - i // 2) * 2 + lax.rem(i, 2)
        self.far = PLANE - 1 - i
        self.half = held.shape[2] // 2

    def _copy(self, l, n, source):
        rows = (slice(None), slice(None), slice(0, self.half), slice(self.half, None))[n]
        to = (self.x, self.y, self.y, self.x)[n]
        sent, landed = self.sems
        place = self.held.at[l, source, rows]
        return remote(place, place, sent.at[l, n], landed.at[l, n], (to, self.e))

    def start(self, l):
        self._copy(l, 0, self.i).start()
        self._copy(l, 1, self.i).start()

    def forward(self, l):
        self._copy(l, 0, self.x).wait_recv()
        self._copy(l, 2, self.x).start()
        self._copy(l, 1, self.y).wait_recv()
        self._copy(l, 3, self.y).start()

    def rest(self, l):
        self._copy(l, 2, self.far).wait_recv()
        self._copy(l, 3, self.far).wait_recv()

    def drain(self, l):
        for n, source in enumerate((self.i, self.i, self.x, self.y)):
            self._copy(l, n, source).wait_send()


class PlaneScatter:
    def __init__(self, plane, out, inbox, sems):
        self.plane, self.out, self.inbox = plane, out, inbox
        self.sent, self.landed = sems
        self.half = plane.half

    def _copy(self, l, chunk, part, n):
        first = slice(0, self.half) if part == 0 else slice(self.half, None)
        to_x = chunk == 1 or (chunk == 0 and part == 0)
        return remote(
            self.out.at[l, chunk, first], self.inbox.at[l, chunk, first], self.sent.at[l, n], self.landed.at[l, n],
            (self.plane.x if to_x else self.plane.y, self.plane.e),
        )

    def _at(self, l, chunk, part):
        return self._copy(l, chunk, part, chunk * 2 + part)

    def start(self, l, chunk):
        for part in ((0, 1), (0,), (1,))[chunk]:
            self._at(l, chunk, part).start()

    def combine(self, l):
        for chunk, part in ((1, 1), (2, 0)):
            rows = slice(part * self.half, (part + 1) * self.half)
            self._at(l, 0, part).wait_recv()
            mine = self.out[l, chunk, rows].astype(jnp.float32) + self.inbox[l, 0, rows].astype(jnp.float32)
            self.out[l, chunk, rows] = mine.astype(jnp.bfloat16)
            self._at(l, chunk, part).start()

    def rest(self, l):
        for chunk in (1, 2):
            for part in (0, 1):
                self._at(l, chunk, part).wait_recv()

    def drain(self, l):
        for chunk in range(3):
            for part in (0, 1):
                self._at(l, chunk, part).wait_send()


def half_turn_tile(part):
    lane = lax.broadcasted_iota(jnp.int32, part.shape, 1)
    ahead = pltpu.roll(part, 128 - HD // 2, 1)
    behind = pltpu.roll(part, HD // 2, 1)
    return jnp.where(lax.rem(lane, HD) < HD // 2, ahead, behind)


def rms_rows(values):
    return lax.rsqrt(jnp.mean(values * values, axis=-1, keepdims=True) + EPSILON)


def norm_back(values, gain, upper):
    scale = rms_rows(values)
    scaled = upper * gain
    inner = jnp.mean(values * scaled, axis=-1, keepdims=True)
    return scale * scaled - values * (scale * scale * scale) * inner, upper * values * scale


def dot(a, b, contract):
    return lax.dot_general(a, b, (contract, ((), ())), preferred_element_type=jnp.float32)


def visible_keys(first, low, high, docs_row, docs_col):
    shape = (QUERY_BLOCK, high - low)
    key = lax.broadcasted_iota(jnp.int32, shape, 1) + low
    query = lax.broadcasted_iota(jnp.int32, shape, 0) + first
    return (key <= query) & (docs_row[:, low:high] == docs_col)


def layer_kernel(x, up, wa, we, routes, gates, doc_ids, shard_gains, cos, sin, block, grad, norm, ge, ga, gn, **held):
    layer_body(
        types.SimpleNamespace(
            x=x, up=up, wa=wa, we=we, routes=routes, gates=gates, doc_ids=doc_ids, shard_gains=shard_gains,
            cos=cos, sin=sin,
            block=block, grad=grad, norm=norm, ge=ge, ga=ga, gn=gn, **held,
        )
    )


def layer_outputs(rows, local):
    f32 = jnp.float32
    shaped = jax.ShapeDtypeStruct
    deep = D // PLANE
    return [
        shaped((rows, D), jnp.bfloat16), shaped((rows, D), f32), shaped((8, 128), f32),
        shaped((local, deep, 3 * FF), f32), shaped((deep // SPAN, 3072), f32), shaped((8, rows), f32),
    ]


def layer_scratch(rows, local):
    f32, bf16 = jnp.float32, jnp.bfloat16
    held, sems = pltpu.VMEM, lambda *shape: pltpu.SemaphoreType.DMA(shape)
    deep = D // PLANE
    part = deep // SPAN
    blocks = held((SPAN, rows, D), bf16)
    quarter = held((LINE, rows, D), bf16)
    line = lambda parts: (sems(parts, LINE), sems(parts, LINE), sems(parts, SPAN))
    scatter = lambda parts: tuple(sems(parts, LINE) for _ in range(4))
    both = lambda *shape: (sems(*shape), sems(*shape))
    return dict(
        x_all=blocks, up_all=blocks, h1=blocks, o_all=blocks, h2=blocks, d=blocks, da_all=blocks,
        qkv=held((SPAN * rows, 256), bf16), lse=held((SPAN * rows, 128), f32),
        wq_out=held((SPAN, part, 256), bf16), w_mine=held((PLANE, SPAN, part, 256), bf16),
        wo_all=held((PLANE, LINE, 2, part, D), bf16), we_all=held((local, PLANE, deep, 3 * FF), bf16),
        o_own=held((SPAN, rows, 128), bf16),
        r_part=held((SPAN, rows // PARTS, D), f32), r_own=held((rows, D), f32),
        pack=held((SPAN, 8, rows), f32), pack_all=held((SPAN, 8, rows), f32), gain_sum=held((PLANE, 2, 8, 128), f32),
        cols=held((SPAN, rows, 128), f32), docs=held((8, SPAN * rows), f32), gains=held((8, D), f32),
        act=held((local, SPAN, rows, FF), bf16), dgu=held((local, SPAN, rows, 2 * FF), bf16),
        pair=quarter, out=quarter, inbox=quarter, own=held((rows, D), f32),
        y_pair=quarter, y_out=quarter, y_inbox=quarter, y_own=held((rows, D), f32),
        ge_in=held((local, PLANE - 1, deep, 3 * FF), bf16),
        do=held((SPAN, rows, 128), bf16), dkv=held((SPAN * rows, 128), f32), dqkv=held((SPAN * rows, 256), bf16),
        dr=held((rows, D), f32), gn_two=held((8, D), f32),
        ga_out=held((PLANE - 1, deep, 384), bf16), ga_in=held((PLANE - 1, deep, 384), bf16),
        gs=held((SPAN, part, 384), f32), ga_all=held((SPAN, part, 384), f32),
        gn_in=held((PLANE, 8, D), f32), mix_in=held((SPAN, 8, D), f32), sq_in=held((PLANE, 8, 128), f32),
        x_sems=line(1), up_sems=line(PARTS), wo_sems=line(1), o_sems=line(PARTS), da_sems=line(PARTS),
        d_sems=scatter(PARTS), y_sems=scatter(1), h_sems=scatter(1),
        load=sems(local), pack_sems=both(SPAN), wq_sems=both(SPAN), wqd_sems=both(PLANE), gd_sems=both(PLANE),
        wod_sems=both(PLANE), wop_sems=both(PLANE), we_sems=both(local, 4), ge_sems=both(local, 6),
        ga_sems=both(PLANE), gn_sems=both(PLANE), gs_sems=both(SPAN), mix_sems=both(SPAN), sq_sems=both(PLANE),
    )


def layer_body(v):
    f32, bf16 = jnp.float32, jnp.bfloat16
    where = i, e, z, c = whereabouts()
    sibling = (i, z * 2 + 1 - c)
    rows, local, deep = v.x.shape[0], v.we_all.shape[0], v.ge.shape[1]
    length, size = rows * SPAN, rows // PARTS
    own_cols = piece(e, 128)
    live = []

    def go(*spec):
        copy = remote(*spec)
        copy.start()
        live.append(copy)

    def along(k):
        return lax.rem(i + k, PLANE)

    def across(k):
        return lax.rem(e + k, SPAN)

    def line(sems, slot, source):
        return LineGather(slot, source, where, sems)

    x_line = line(v.x_sems, lambda s, j: v.x_all.at[s], lambda j: v.x)
    up_line = line(v.up_sems, lambda s, j: v.up_all.at[s, piece(j, size)], lambda j: v.up.at[piece(j, size)])
    wo_line = line(
        v.wo_sems, lambda s, j: v.wo_all.at[i, s // 2, lax.rem(s, 2)], lambda j: v.wo_all.at[i, z, c]
    )
    o_line = line(
        v.o_sems,
        lambda s, j: v.o_all.at[:, piece(j, size), piece(s, 128)],
        lambda j: v.o_own.at[:, piece(j, size)],
    )
    da_line = line(
        v.da_sems, lambda s, j: v.da_all.at[s, piece(j, size)], lambda j: v.da_all.at[e, piece(j, size)]
    )
    we_plane = PlaneGather(where, v.we_all, v.we_sems)
    ge_plane = PlaneScatter(we_plane, v.we_all, v.ge_in, v.ge_sems)
    d_scatter = LineScatter(v.d, where, v.pair, v.out, v.inbox, v.own, v.d_sems, size)
    y_scatter = LineScatter(v.o_all, where, v.y_pair, v.y_out, v.y_inbox, v.y_own, v.y_sems, rows)
    h_scatter = LineScatter(v.d, where, v.pair, v.out, v.inbox, v.own, v.h_sems, rows)

    loads = [pltpu.make_async_copy(v.we.at[l], v.ge.at[l], v.load.at[l]) for l in range(local)]
    for copy in loads:
        copy.start()
    barrier = pltpu.get_barrier_semaphore()
    for device in partners(i, e):
        pl.semaphore_signal(barrier, inc=1, device_id=device, device_id_type=pl.DeviceIdType.MESH)
    lane = lax.broadcasted_iota(jnp.int32, (2, rows), 1)
    index, few = i * SPAN + e, rows // v.shard_gains.shape[1]
    spread = jnp.concatenate([v.shard_gains[...]] * few, axis=1)
    spread = jnp.where(lane // (rows // few) == lax.rem(index, few), spread, 0.0)
    shared = [v.doc_ids[...].astype(f32), spread, jnp.zeros((3, rows), f32)]
    for g in range(SPAN):
        named = [
            jnp.sum(jnp.where(v.routes[...] == g * local + l, v.gates[...], 0.0), axis=0, keepdims=True)
            for l in range(local)
        ]
        v.pack[g] = jnp.concatenate(named + shared, axis=0)
    for g in range(SPAN):
        v.wq_out[g, :, :128] = v.wa[:, g * 128 : (g + 1) * 128].astype(bf16)
        key_value = [v.wa[:, first + g * HD : first + (g + 1) * HD] for first in (QD, QD + KVD)]
        v.wq_out[g, :, 128:] = jnp.concatenate(key_value, axis=1).astype(bf16)
    v.w_mine[i, e] = v.wq_out[e]
    v.wo_all[i, z, c] = v.wa[:, QKV:].astype(bf16)
    v.pack_all[e] = v.pack[e]
    v.x_all[e] = v.x[...]
    v.up_all[e] = v.up[...]
    pl.semaphore_wait(barrier, SPAN + PLANE - 2)
    for k in range(1, SPAN):
        go(v.pack.at[across(k)], v.pack_all.at[e], v.pack_sems[0].at[k], v.pack_sems[1].at[e], (i, across(k)))
    for k in range(1, SPAN):
        go(v.wq_out.at[across(k)], v.w_mine.at[i, e], v.wq_sems[0].at[k], v.wq_sems[1].at[e], (i, across(k)))
    wo_line.start(0)
    x_line.start(0)
    loads[0].wait()
    v.we_all[0, i] = v.ge[0].astype(bf16)

    for k in range(1, SPAN):
        slot = v.pack_all.at[across(k)]
        remote(slot, slot, v.pack_sems[0].at[k], v.pack_sems[1].at[across(k)], sibling).wait_recv()
    for half in range(2):
        summed = v.pack_all[4 * half]
        for s in range(1, 4):
            summed = summed + v.pack_all[4 * half + s]
        v.gain_sum[i, half] = summed
    for k in range(1, PLANE):
        go(v.gain_sum.at[i], v.gain_sum.at[i], v.gd_sems[0].at[k], v.gd_sems[1].at[i], (along(k), e))
    for k in range(1, SPAN):
        slot = v.w_mine.at[i, across(k)]
        remote(slot, slot, v.wq_sems[0].at[k], v.wq_sems[1].at[across(k)], sibling).wait_recv()
    for k in range(1, PLANE):
        go(v.w_mine.at[i], v.w_mine.at[i], v.wqd_sems[0].at[k], v.wqd_sems[1].at[i], (along(k), e))
    we_plane.start(0)
    loads[1].wait()
    v.we_all[1, i] = v.ge[1].astype(bf16)
    for s in range(SPAN):
        block = v.pack_all[s]
        tall = jnp.concatenate([block, jnp.zeros((rows - block.shape[0], rows), f32)], axis=0)
        v.cols[s] = tall.T
        v.docs[:, s * rows : (s + 1) * rows] = block
    for k in range(1, PLANE):
        slot = v.gain_sum.at[along(k)]
        remote(slot, slot, v.gd_sems[0].at[k], v.gd_sems[1].at[along(k)], sibling).wait_recv()
    for tile in range(2 * PLANE):
        v.gains[:, tile * 128 : (tile + 1) * 128] = v.gain_sum[tile // 2, tile % 2].astype(bf16).astype(f32)
    gain_one, gain_two = v.gains[3:4], v.gains[4:5]

    def first_norm(s):
        values = v.x_all[s].astype(f32)
        v.h1[s] = (values * rms_rows(values) * gain_one).astype(bf16)

    wo_line.forward_all(0)
    for k in range(1, PLANE):
        mine = v.wo_all.at[i, :, c]
        go(mine, mine, v.wod_sems[0].at[k], v.wod_sems[1].at[i], (along(k), e))
    first_norm(e)
    for k in (2, 1, 3):
        x_line.forward(0, k)
        first_norm(x_line.near(k))
    up_line.start(0)
    up_line.start(1)
    we_plane.forward(0)
    we_plane.start(1)
    x_line.wait(0, x_line.sibling())
    first_norm(x_line.sibling())
    for k in range(1, LINE):
        x_line.wait(0, x_line.far(k))
        first_norm(x_line.far(k))
    for k in range(1, PLANE):
        slot = v.w_mine.at[along(k)]
        remote(slot, slot, v.wqd_sems[0].at[k], v.wqd_sems[1].at[along(k)], sibling).wait_recv()

    weights = v.w_mine[...].reshape(D, 256)
    lane = lax.broadcasted_iota(jnp.int32, (QUERY_BLOCK, 128), 1)

    def tables(first):
        cosine, sine = v.cos[first : first + QUERY_BLOCK], v.sin[first : first + QUERY_BLOCK]
        return cosine, sine, jnp.where(lane < HD, cosine, 1.0), jnp.where(lane < HD, sine, 0.0)

    for first in range(0, length, QUERY_BLOCK):
        span = slice(first, first + QUERY_BLOCK)
        slots = slice(first // rows, (first + QUERY_BLOCK) // rows)
        raw = dot(v.h1[slots].reshape(QUERY_BLOCK, D), weights, NN)
        q_cos, q_sin, kv_cos, kv_sin = tables(first)
        q_raw, kv_raw = raw[:, :128], raw[:, 128:]
        v.qkv[span, :128] = (q_raw * q_cos + half_turn_tile(q_raw) * q_sin).astype(bf16)
        v.qkv[span, 128:] = (kv_raw * kv_cos + half_turn_tile(kv_raw) * kv_sin).astype(bf16)


    def block_masks(first):
        low, high = max(0, first - length // 2), first + QUERY_BLOCK
        slots = slice(first // rows, (first + QUERY_BLOCK) // rows)
        docs_col = v.cols[slots, :, 2:3].reshape(QUERY_BLOCK, 1)
        return low, high, slots, visible_keys(first, low, high, v.docs[2:3], docs_col)

    for first in range(0, length, QUERY_BLOCK):
        low, high, slots, visible = block_masks(first)
        span = slice(first, first + QUERY_BLOCK)
        outs, logs = [], []
        for head in range(2):
            q = v.qkv[span, head * HD : (head + 1) * HD]
            scores = dot(q, v.qkv[low:high, 128:192], NT) * HD**-0.5
            scores = jnp.where(visible, scores, -1e30)
            peak = jnp.max(scores, axis=-1, keepdims=True)
            raw = jnp.exp(scores - peak)
            total = jnp.sum(raw, axis=-1, keepdims=True)
            probs = raw * (1.0 / total)
            logs.append(peak + jnp.log(total))
            outs.append(dot(probs.astype(bf16), v.qkv[low:high, 192:256], NN))
        both = jnp.concatenate(outs, axis=1).astype(bf16).reshape(-1, rows, 128)
        v.o_own[slots] = both
        v.o_all[slots, :, own_cols] = both
        v.lse[span] = jnp.where(lane == 0, logs[0], logs[1])
    o_line.start(0)
    o_line.start(1)
    up_line.start(2)
    o_line.start(2)
    up_line.start(3)
    o_line.start(3)

    wo_line.rest(0)
    for k in range(1, PLANE):
        here = v.wo_all.at[along(k), :, c]
        remote(here, here, v.wod_sems[0].at[k], v.wod_sems[1].at[along(k)], sibling).wait_recv()
        go(here, here, v.wop_sems[0].at[k], v.wop_sems[1].at[along(k)], sibling)
    for k in range(1, PLANE):
        far = v.wo_all.at[along(k), :, 1 - c]
        remote(far, far, v.wod_sems[0].at[k], v.wop_sems[1].at[along(k)], sibling).wait_recv()

    def second_norm(j):
        part = piece(j, size)
        w_out = v.wo_all[...].reshape(D, D)
        branch = dot(v.o_all[:, part].reshape(-1, D), w_out, NT)
        values = v.x_all[:, part].reshape(-1, D).astype(f32) + branch
        v.r_part[...] = values.reshape(SPAN, size, D)
        v.r_own[part] = v.r_part[e]
        v.h2[:, part] = (values * rms_rows(values) * gain_two).astype(bf16).reshape(SPAN, size, D)

    def gate_of(l, part):
        return v.cols[:, part, l : l + 1].reshape(-1, 1)

    def expert(l, j):
        part = piece(j, size)
        weights = v.we_all[l].reshape(D, 3 * FF)
        gate = gate_of(l, part)
        routed = gate > 0
        gu = dot(v.h2[:, part].reshape(-1, D), weights[:, : 2 * FF], NN)
        g, u = gu[:, :FF], gu[:, FF:]
        sig = 1.0 / (1.0 + jnp.exp(-g))
        act = jnp.where(routed, g * sig * u, 0.0).astype(bf16)
        v.act[l, :, part] = act.reshape(SPAN, size, FF)
        dy = (gate * v.up_all[:, part].reshape(-1, D).astype(f32)).astype(bf16)
        dact = dot(dy, weights[:, 2 * FF :], NN)
        dg = dact * u * sig * (1.0 + g * (1.0 - sig))
        du = dact * g * sig
        dgu = jnp.where(routed, jnp.concatenate([dg, du], axis=1), 0.0).astype(bf16)
        v.dgu[l, :, part] = dgu.reshape(SPAN, size, 2 * FF)
        d = dot(dgu, weights[:, : 2 * FF], NT).astype(bf16)
        y = dot(act, weights[:, 2 * FF :], NT).astype(bf16)
        if l == 0:
            v.d[:, part] = d.reshape(SPAN, size, D)
            v.o_all[:, part] = y.reshape(SPAN, size, D)
        else:
            d = v.d[:, part].reshape(-1, D).astype(f32) + d.astype(f32)
            v.d[:, part] = d.astype(bf16).reshape(SPAN, size, D)
            y = gate_of(0, part) * v.o_all[:, part].reshape(-1, D).astype(f32) + gate * y.astype(f32)
            v.o_all[:, part] = y.astype(bf16).reshape(SPAN, size, D)

    we_plane.rest(0)

    def first_round(j, carry):
        @pl.when(j == PARTS - 1)
        def _():
            we_plane.forward(1)

        @pl.when(j < PARTS)
        def _():
            o_line.forward_all(j)
            up_line.forward_all(j)

        @pl.when(j > 0)
        def _():
            o_line.drain(j - 1)
            expert(0, j - 1)

        @pl.when(j < PARTS)
        def _():
            o_line.rest(j)
            up_line.rest(j)
            second_norm(j)

        return carry

    lax.fori_loop(0, PARTS + 1, first_round, 0)
    we_plane.rest(1)

    def second_round(j, carry):
        @pl.when(j < PARTS)
        def _():
            expert(1, j)
            d_scatter.start(j)

        @pl.when((j > 0) & (j <= PARTS))
        def _():
            d_scatter.fold(j - 1)

        @pl.when(j > 1)
        def _():
            d_scatter.fold_late(j - 2)

        return carry

    lax.fori_loop(0, PARTS + 2, second_round, 0)
    y_scatter.start(0)
    for l in range(local):
        we_plane.drain(l)

    def expert_chunk(l, there):
        span = piece(there, deep)
        inward = dot(v.h2[:, :, span].reshape(length, deep), v.dgu[l].reshape(length, 2 * FF), TN)
        gate = v.cols[:, :, l : l + 1].reshape(length, 1)
        dy = (gate * v.up_all[:, :, span].reshape(length, deep).astype(f32)).astype(bf16)
        return inward, dot(dy, v.act[l].reshape(length, FF), TN)

    def send_chunk(l, chunk):
        inward, down = expert_chunk(l, (we_plane.far, we_plane.x, we_plane.y)[chunk])
        v.we_all[l, chunk, :, : 2 * FF] = inward.astype(bf16)
        v.we_all[l, chunk, :, 2 * FF :] = down.astype(bf16)
        ge_plane.start(l, chunk)

    def keep_chunk(l):
        inward, down = expert_chunk(l, i)
        v.ge[l, :, : 2 * FF] = inward
        v.ge[l, :, 2 * FF :] = down

    v.gn_two[...] = jnp.zeros_like(v.gn_two)

    def second_back(j):
        part = piece(j, size)
        back, shares = norm_back(v.r_own[part], gain_two, d_scatter.total(j))
        dr = v.up_all[e, part].astype(f32) + back
        v.dr[part] = dr
        v.gn_two[:1] += jnp.sum(shares, axis=0, keepdims=True)
        v.da_all[e, part] = dr.astype(bf16)
        da_line.start(j)

    send_chunk(0, 0)
    send_chunk(1, 0)
    second_back(0)
    send_chunk(0, 1)
    send_chunk(0, 2)
    second_back(1)
    ge_plane.combine(0)
    send_chunk(1, 1)
    second_back(2)
    send_chunk(1, 2)
    ge_plane.combine(1)
    second_back(3)
    keep_chunk(0)
    keep_chunk(1)
    y_scatter.fold(0)
    wo_mine = v.wo_all[:, :, :, :, own_cols].reshape(D, 128)
    for j in range(PARTS):
        da_line.forward_all(j)
    y_scatter.fold_late(0)
    for j in range(PARTS):
        da_line.rest(j)
        part = piece(j, size)
        do = dot(v.da_all[:, part].reshape(-1, D), wo_mine, NN).astype(bf16)
        v.do[:, part] = do.reshape(SPAN, size, 128)

    v.dkv[...] = jnp.zeros_like(v.dkv)
    for first in range(0, length, QUERY_BLOCK):
        low, high, slots, visible = block_masks(first)
        span = slice(first, first + QUERY_BLOCK)
        keys, values = v.qkv[low:high, 128:192], v.qkv[low:high, 192:256]
        do_both = v.do[slots].reshape(QUERY_BLOCK, 128)
        dqs, dk, dv = [], 0.0, 0.0
        for head in range(2):
            q = v.qkv[span, head * HD : (head + 1) * HD]
            do = do_both[:, head * HD : (head + 1) * HD]
            scores = dot(q, keys, NT) * HD**-0.5
            probs = jnp.exp(jnp.where(visible, scores - v.lse[span, head : head + 1], -1e30))
            dp = dot(do, values, NT)
            delta = jnp.sum(probs * dp, axis=-1, keepdims=True)
            ds = (probs * (dp - delta)).astype(bf16)
            dqs.append(dot(ds, keys, NN))
            dk = dk + dot(ds, q, TN)
            dv = dv + dot(probs.astype(bf16), do, TN)
        v.dkv[low:high] += jnp.concatenate([dk * HD**-0.5, dv], axis=1)
        dq = jnp.concatenate(dqs, axis=1) * HD**-0.5
        cosine, sine = v.cos[span], v.sin[span]
        v.dqkv[span, :128] = (dq * cosine - half_turn_tile(dq) * sine).astype(bf16)
    for first in range(0, length, QUERY_BLOCK):
        span = slice(first, first + QUERY_BLOCK)
        dkv = v.dkv[span]
        _, _, cosine, sine = tables(first)
        v.dqkv[span, 128:] = (dkv * cosine - half_turn_tile(dkv) * sine).astype(bf16)

    o = v.o_own[...].reshape(length, 128)
    dqkv = v.dqkv[...]

    def rows_copy(k):
        return remote(v.ga_out.at[k - 1], v.ga_in.at[k - 1], v.ga_sems[0].at[k], v.ga_sems[1].at[k], (along(k), e))

    for k in (2, 1, 3, 0):
        span = piece(along(k), deep)
        projections = dot(v.h1[:, :, span].reshape(length, deep), dqkv, TN)
        output = dot(v.da_all[:, :, span].reshape(length, deep), o, TN)
        if k == 0:
            v.gs[:, :, :256] = projections.reshape(SPAN, -1, 256)
            v.gs[:, :, 256:] = output.reshape(SPAN, -1, 128)
        else:
            v.ga_out[k - 1, :, :256] = projections.astype(bf16)
            v.ga_out[k - 1, :, 256:] = output.astype(bf16)
            rows_copy(k).start()

    for j in range(PARTS):
        d_scatter.drain(j)
    gn_one = jnp.zeros((1, D), f32)
    order = (1, 3, 2, 0)
    for n, k in enumerate(order):
        chip = lax.rem(z + k, LINE)
        slots = piece(chip, 2)
        dh = dot(v.dqkv[piece(chip, 2 * rows)], weights, NT)
        values = v.x_all[slots].reshape(2 * rows, D).astype(f32)
        gn_one = gn_one + jnp.sum(dh * values * rms_rows(values), axis=0, keepdims=True)
        v.d[slots] = dh.astype(bf16).reshape(2, rows, D)
        h_scatter.start_one(0, k)
        if n > 0:
            h_scatter.fold_one(0, order[n - 1])
    h_scatter.fold_one(0, order[-1])
    v.gn_in[i] = jnp.concatenate([gn_one, v.gn_two[:1], jnp.zeros((6, D), f32)], axis=0)
    for k in range(1, PLANE):
        go(v.gn_in.at[i], v.gn_in.at[i], v.gn_sems[0].at[k], v.gn_sems[1].at[i], (along(k), e))
    v.block[...] = (v.r_own[...] + y_scatter.total(0)).astype(bf16)
    h_scatter.fold_late(0)

    for k in (2, 1, 3):
        rows_copy(k).wait_recv()
        v.gs[...] += v.ga_in[k - 1].reshape(v.gs.shape).astype(f32)
    squares = jnp.sum(v.gs[...] * v.gs[...])
    for k in range(1, SPAN):
        go(v.gs.at[across(k)], v.ga_all.at[e], v.gs_sems[0].at[k], v.gs_sems[1].at[e], (i, across(k)))
    v.ga_all[e] = v.gs[e]
    for l in range(local):
        ge_plane.rest(l)
        for first in range(0, deep, 64):
            span = slice(first, first + 64)
            summed = v.ge[l, span]
            for chunk in (1, 2):
                summed = summed + v.ge_in[l, chunk, span].astype(f32)
            v.ge[l, span] = summed
            squares = squares + jnp.sum(summed * summed)

    for k in range(1, PLANE):
        slot = v.gn_in.at[along(k)]
        remote(slot, slot, v.gn_sems[0].at[k], v.gn_sems[1].at[along(k)], sibling).wait_recv()
    gains = v.gn_in[0] + v.gn_in[1] + v.gn_in[2] + v.gn_in[3]
    row = lax.broadcasted_iota(jnp.int32, gains.shape, 0)
    v.mix_in[e] = jnp.where(row == 2, squares, gains)
    for k in range(1, SPAN):
        go(v.mix_in.at[e], v.mix_in.at[e], v.mix_sems[0].at[k], v.mix_sems[1].at[e], (i, across(k)))
    for k in range(1, SPAN):
        slot = v.mix_in.at[across(k)]
        remote(slot, slot, v.mix_sems[0].at[k], v.mix_sems[1].at[across(k)], sibling).wait_recv()
    mixed = v.mix_in[0]
    for s in range(1, SPAN):
        mixed = mixed + v.mix_in[s]
    v.gains[...] = mixed
    turned = pltpu.roll(v.gains[:, piece(index // few, rows)], rows - lax.rem(index, few) * (rows // few), 1)
    v.gn[...] = turned
    v.sq_in[i] = jnp.broadcast_to(mixed[2:3, :128], (8, 128))
    for k in range(1, PLANE):
        go(v.sq_in.at[i], v.sq_in.at[i], v.sq_sems[0].at[k], v.sq_sems[1].at[i], (along(k), e))
    gain_squares = jnp.sum(jnp.where(row < 2, mixed * mixed, 0.0))
    for k in range(1, SPAN):
        slot = v.ga_all.at[across(k)]
        remote(slot, slot, v.gs_sems[0].at[k], v.gs_sems[1].at[across(k)], sibling).wait_recv()
    for g in range(SPAN):
        v.ga[:, g * 128 : (g + 1) * 128] = v.ga_all[g, :, :128]
        v.ga[:, QKV + g * 128 : QKV + (g + 1) * 128] = v.ga_all[g, :, 256:]
    for g in range(0, SPAN, 2):
        for first, own in ((QD, 128), (QD + KVD, 192)):
            heads = [v.ga_all[g + n, :, own : own + HD] for n in range(2)]
            v.ga[:, first + g * HD : first + (g + 2) * HD] = jnp.concatenate(heads, axis=1)
    for k in range(1, PLANE):
        slot = v.sq_in.at[along(k)]
        remote(slot, slot, v.sq_sems[0].at[k], v.sq_sems[1].at[along(k)], sibling).wait_recv()
    v.norm[...] = jnp.sqrt(v.sq_in[0] + v.sq_in[1] + v.sq_in[2] + v.sq_in[3] + gain_squares)

    back, _ = norm_back(v.x_all[e].astype(f32), gain_one, h_scatter.total(0))
    v.grad[...] = v.dr[...] + back
    for copy in live:
        copy.wait_send()
    for k in (2, 1, 3):
        rows_copy(k).wait_send()
    for l in range(local):
        ge_plane.drain(l)
    for item in (x_line, wo_line, y_scatter, h_scatter):
        item.drain(0)
    for j in range(PARTS):
        up_line.drain(j)
        da_line.drain(j)


def call_layer(*args):
    vmem, anywhere = pl.BlockSpec(memory_space=pltpu.VMEM), pl.BlockSpec(memory_space=pl.ANY)
    rows, local = args[0].shape[0], args[3].shape[0]
    outs = layer_outputs(rows, local)
    return pl.pallas_call(
        layer_kernel,
        out_shape=outs,
        in_specs=[anywhere if n == 3 else vmem for n in range(len(args))],
        out_specs=[vmem] * len(outs),
        scratch_shapes=layer_scratch(rows, local),
        compiler_params=pltpu.CompilerParams(
            collective_id=0, has_side_effects=True, vmem_limit_bytes=64 * 2**20 - 2**18
        ),
        name="layer",
    )(*args)


def fast_body(
    activations,
    doc_ids,
    routes,
    gate_weights,
    cotangent,
    step_count,
    w_attn,
    norm_gains,
    w_expert,
    first_attn,
    second_attn,
    first_gains,
    second_gains,
    first_expert,
    second_expert,
):
    cosine, sine = head_tables(activations.shape[1] * lax.axis_size("expert"))
    block, input_total, norm, grad_expert, grad_attn, gn = call_layer(
        activations[0], cotangent[0], w_attn, w_expert, routes[0].T, gate_weights[0].T, doc_ids, norm_gains.T,
        cosine, sine,
    )
    grad_norm = norm[0, 0]
    clip = jnp.minimum(1.0, CLIP_NORM / (grad_norm + 1e-06))
    steps = step_count.astype(jnp.float32)
    attn = adam_update(
        w_attn, first_attn, second_attn, grad_attn * clip, steps, WEIGHT_DECAY, LEARN_RATE
    )
    gain = adam_update(
        norm_gains.T, first_gains.T, second_gains.T, gn[:2, : norm_gains.shape[0]] * clip, steps, 0.0, GAIN_RATE
    )
    expert = adam_update(
        w_expert, first_expert, second_expert, grad_expert * clip, steps, WEIGHT_DECAY, LEARN_RATE
    )
    return (block[None], input_total[None], grad_norm, *attn, *[a.T for a in gain], *expert)


def solution(mesh):
    in_specs = (
        P("dp", "expert", None),
        P("dp", "expert"),
        P("dp", "expert", None),
        P("dp", "expert", None),
        P("dp", "expert", None),
        P(),
        P(("dp", "expert"), None),
        P(("dp", "expert"), None),
        P("expert", "dp", None),
        P(("dp", "expert"), None),
        P(("dp", "expert"), None),
        P(("dp", "expert"), None),
        P(("dp", "expert"), None),
        P("expert", "dp", None),
        P("expert", "dp", None),
    )
    out_specs = (
        P("dp", "expert", None),
        P("dp", "expert", None),
        P(),
        P(("dp", "expert"), None),
        P(("dp", "expert"), None),
        P(("dp", "expert"), None),
        P(("dp", "expert"), None),
        P(("dp", "expert"), None),
        P(("dp", "expert"), None),
        P("expert", "dp", None),
        P("expert", "dp", None),
        P("expert", "dp", None),
    )
    body = fast_body if fits(mesh) else general_body
    return jax.shard_map(body, mesh=mesh, in_specs=in_specs, out_specs=out_specs, check_vma=False)
```

```python
import jax
import jax.numpy as jnp
from jax import lax
from jax.sharding import PartitionSpec as P
import types

import numpy as np
from jax.experimental import pallas as pl
from jax.experimental.pallas import tpu as pltpu

D = 1024
H = 16
KVH = 8
HD = 64
FF = 512
TOP = 8
QD = 1024
KVD = 512
QKV = 2048


EPSILON = 1e-05
ROPE_BASE = 10000.0
CLIP_NORM = 1.0
BETA_ONE = 0.9
BETA_TWO = 0.95
ADAM_EPSILON = 1e-08
LEARN_RATE = 0.03
GAIN_RATE = 0.4
WEIGHT_DECAY = 0.1


def rms_scale(values, gain):
    return values * lax.rsqrt(jnp.mean(values * values, axis=-1, keepdims=True) + EPSILON) * gain


def rope_tables(positions, head_width):
    halves = jnp.arange(head_width // 2, dtype=jnp.float32)
    inverse = ROPE_BASE ** (-2.0 * halves / head_width)
    angles = positions.astype(jnp.float32)[:, None] * inverse[None, :]
    angles = jnp.concatenate([angles, angles], axis=-1)
    return (jnp.cos(angles)[:, None, :], jnp.sin(angles)[:, None, :])


def rotate(values, cosine, sine_table):
    middle = values.shape[-1] // 2
    turned = jnp.concatenate([-values[..., middle:], values[..., :middle]], axis=-1)
    return values * cosine + turned * sine_table


def unrotate(gradient, cosine, sine_table):
    middle = gradient.shape[-1] // 2
    product = gradient * sine_table
    turned = jnp.concatenate([product[..., middle:], -product[..., :middle]], axis=-1)
    return gradient * cosine + turned


def adam_update(weight, moment_one, second, gradient, steps_done, decay_rate, step_rate):
    first_new = BETA_ONE * moment_one + (1.0 - BETA_ONE) * gradient
    second_new = BETA_TWO * second + (1.0 - BETA_TWO) * gradient * gradient
    first_hat = first_new / (1.0 - BETA_ONE**steps_done)
    second_hat = second_new / (1.0 - BETA_TWO**steps_done)
    weight_new = weight - step_rate * (
        first_hat / (jnp.sqrt(second_hat) + ADAM_EPSILON) + decay_rate * weight
    )
    return (weight_new, first_new, second_new)


def attn_fetch(w_attn, norm_gains):
    return (
        lax.all_gather(w_attn.astype(jnp.bfloat16), ("dp", "expert"), axis=0, tiled=True),
        lax.all_gather(norm_gains.astype(jnp.bfloat16), ("dp", "expert"), axis=0, tiled=True),
    )


def expert_fetch(w_expert):
    return lax.all_gather(w_expert.astype(jnp.bfloat16), "dp", axis=1, tiled=True)


def to_owner(buffer):
    return lax.all_to_all(buffer, "expert", split_axis=0, concat_axis=1, tiled=True)


def to_sender(buffer):
    return lax.all_to_all(buffer, "expert", split_axis=1, concat_axis=0, tiled=True)


def expert_forward(received, expert_cols):
    gate_up = jnp.einsum(
        "esd,edf->esf", received, expert_cols[:, :, : 2 * FF], preferred_element_type=jnp.float32
    )
    activated = (jax.nn.silu(gate_up[..., :FF]) * gate_up[..., FF:]).astype(jnp.bfloat16)
    return (gate_up, activated)


def general_body(
    activations,
    doc_ids,
    routes,
    gate_weights,
    cotangent,
    step_count,
    w_attn,
    norm_gains,
    w_expert,
    first_attn,
    second_attn,
    first_gains,
    second_gains,
    first_expert,
    second_expert,
):
    row_count = activations.shape[1]
    span_size = lax.axis_size("expert")
    shard_pos = lax.axis_index("expert")
    seq_length = row_count * span_size
    expert_total = w_expert.shape[0] * span_size
    capacity = (row_count * TOP * 9 + expert_total * 8 - 1) // (expert_total * 8)
    group_size = H // KVH
    score_scale = HD ** (-0.5)
    hidden_in = activations[0].astype(jnp.float32)
    upstream = cotangent[0].astype(jnp.float32)
    attn_cols, gain_pair = attn_fetch(w_attn, norm_gains)
    expert_cols = expert_fetch(w_expert)
    gain_one = gain_pair[:, 0].astype(jnp.float32)
    gain_two = gain_pair[:, 1].astype(jnp.float32)
    w_project = attn_cols[:, :QKV]
    w_output = attn_cols[:, QKV:]
    normed = rms_scale(hidden_in, gain_one).astype(jnp.bfloat16)
    projected = jnp.dot(normed, w_project, preferred_element_type=jnp.float32)
    positions = shard_pos * row_count + jnp.arange(row_count, dtype=jnp.int32)
    cosine, sine_table = rope_tables(positions, HD)
    queries = rotate(projected[:, :QD].reshape(row_count, H, HD), cosine, sine_table).astype(
        jnp.bfloat16
    )
    key_heads = rotate(
        projected[:, QD : QD + KVD].reshape(row_count, KVH, HD), cosine, sine_table
    ).astype(jnp.bfloat16)
    value_heads = projected[:, QD + KVD :].astype(jnp.bfloat16)
    key_all, value_all, doc_all = (
        lax.all_gather(key_heads.reshape(row_count, KVD), "expert", axis=0, tiled=True),
        lax.all_gather(value_heads, "expert", axis=0, tiled=True),
        lax.all_gather(doc_ids[0].astype(jnp.bfloat16), "expert", axis=0, tiled=True),
    )
    key_docs = doc_all.astype(jnp.int32)
    query_docs = doc_ids[0]
    query_groups = queries.reshape(row_count, KVH, group_size, HD)
    key_block = min(512, seq_length)
    needed = (shard_pos * row_count + row_count + key_block - 1) // key_block

    def block_scores(block_id):
        first_key = block_id * key_block
        key_part = lax.dynamic_slice_in_dim(key_all, first_key, key_block, 0).reshape(
            key_block, KVH, HD
        )
        raw_scores = (
            jnp.einsum("tgrd,kgd->grtk", query_groups, key_part, preferred_element_type=jnp.float32)
            * score_scale
        )
        key_pos = first_key + jnp.arange(key_block, dtype=jnp.int32)
        key_doc = lax.dynamic_slice_in_dim(key_docs, first_key, key_block, 0)
        visible = (key_pos[None, :] <= positions[:, None]) & (
            key_doc[None, :] == query_docs[:, None]
        )
        return (raw_scores, visible, key_part)

    def value_part(block_id):
        return lax.dynamic_slice_in_dim(value_all, block_id * key_block, key_block, 0).reshape(
            key_block, KVH, HD
        )

    def total_step(block_id, running):
        row_peak, row_total = running
        raw_scores, visible, _ = block_scores(block_id)
        masked = jnp.where(visible, raw_scores, -1e30)
        new_peak = jnp.maximum(row_peak, jnp.max(masked, axis=-1))
        scaled = jnp.where(visible, jnp.exp(masked - new_peak[..., None]), 0.0)
        return (new_peak, row_total * jnp.exp(row_peak - new_peak) + jnp.sum(scaled, axis=-1))

    start_peak = jnp.full((KVH, group_size, row_count), -1e30, jnp.float32)
    start_total = jnp.zeros((KVH, group_size, row_count), jnp.float32)
    row_peak, row_total = lax.fori_loop(0, needed, total_step, (start_peak, start_total))
    log_total = row_peak + jnp.log(row_total)

    def exact_probs(raw_scores, visible):
        return jnp.exp(jnp.where(visible, raw_scores - log_total[..., None], -1e30))

    def output_step(block_id, summed):
        raw_scores, visible, _ = block_scores(block_id)
        weights_low = exact_probs(raw_scores, visible).astype(jnp.bfloat16)
        return summed + jnp.einsum(
            "grtk,kgd->tgrd", weights_low, value_part(block_id), preferred_element_type=jnp.float32
        )

    attended = lax.fori_loop(
        0, needed, output_step, jnp.zeros((row_count, KVH, group_size, HD), jnp.float32)
    )
    attended = attended.reshape(row_count, QD).astype(jnp.bfloat16)
    branch = jnp.einsum("tc,dc->td", attended, w_output, preferred_element_type=jnp.float32)
    residual = hidden_in + branch
    normed_two = rms_scale(residual, gain_two).astype(jnp.bfloat16)
    flat_routes = routes[0].reshape(-1)
    one_hot = (flat_routes[:, None] == jnp.arange(expert_total, dtype=jnp.int32)[None, :]).astype(
        jnp.int32
    )
    ranking = jnp.sum((jnp.cumsum(one_hot, axis=0) - 1) * one_hot, axis=1)
    places = flat_routes * capacity + ranking
    owners = jnp.arange(row_count * TOP, dtype=jnp.int32) // TOP
    source = jnp.zeros((expert_total * capacity,), jnp.int32).at[places].set(owners)
    filled = jnp.zeros((expert_total * capacity,), jnp.int32).at[places].set(1) > 0
    slot_gate = (
        jnp.zeros((expert_total * capacity,), jnp.float32)
        .at[places]
        .set(gate_weights[0].reshape(-1))
    )
    outgoing = jnp.where(filled[:, None], normed_two[source], jnp.zeros((), jnp.bfloat16)).reshape(
        expert_total, capacity, D
    )
    received = to_owner(outgoing)
    gate_up, activated = expert_forward(received, expert_cols)
    expert_out = jnp.einsum(
        "esf,edf->esd", activated, expert_cols[:, :, 2 * FF :], preferred_element_type=jnp.float32
    ).astype(jnp.bfloat16)
    returned = to_sender(expert_out).reshape(expert_total * capacity, D)
    picked = returned[places].reshape(row_count, TOP, D).astype(jnp.float32)
    combined = jnp.sum(gate_weights[0][..., None] * picked, axis=1)
    block_result = (residual + combined).astype(jnp.bfloat16)
    slot_grad = jnp.where(filled[:, None], slot_gate[:, None] * upstream[source], 0.0)
    slot_grad = slot_grad.astype(jnp.bfloat16).reshape(expert_total, capacity, D)
    owner_grad = to_owner(slot_grad)
    attn_cols, gain_pair = attn_fetch(w_attn, norm_gains)
    w_project = attn_cols[:, :QKV]
    w_output = attn_cols[:, QKV:]
    expert_cols = expert_fetch(w_expert)
    gate_up, activated = expert_forward(received, expert_cols)
    gate_part = gate_up[..., :FF]
    up_part = gate_up[..., FF:]
    sigmoid_gate = jax.nn.sigmoid(gate_part)
    act_grad = jnp.einsum(
        "esd,edf->esf", owner_grad, expert_cols[:, :, 2 * FF :], preferred_element_type=jnp.float32
    )
    gate_grad = act_grad * up_part * sigmoid_gate * (1.0 + gate_part * (1.0 - sigmoid_gate))
    lift_grad = act_grad * gate_part * sigmoid_gate
    mixed_grad = jnp.concatenate([gate_grad, lift_grad], axis=-1).astype(jnp.bfloat16)
    down_grad = jnp.einsum(
        "esf,esd->edf", activated, owner_grad, preferred_element_type=jnp.float32
    )
    inward_grad = jnp.einsum(
        "esd,esf->edf", received, mixed_grad, preferred_element_type=jnp.float32
    )
    row_grads = jnp.einsum(
        "esf,edf->esd", mixed_grad, expert_cols[:, :, : 2 * FF], preferred_element_type=jnp.float32
    ).astype(jnp.bfloat16)
    back_rows = to_sender(row_grads).reshape(expert_total * capacity, D)
    normed_two_grad = jnp.sum(
        back_rows[places].reshape(row_count, TOP, D).astype(jnp.float32), axis=1
    )
    _, second_pull = jax.vjp(rms_scale, residual, gain_two)
    resid_grad, gain_two_grad = second_pull(normed_two_grad)
    resid_grad = upstream + resid_grad
    branch_grad = resid_grad.astype(jnp.bfloat16)
    output_grad = jnp.einsum("td,tc->dc", branch_grad, attended, preferred_element_type=jnp.float32)
    attended_grad = jnp.dot(branch_grad, w_output, preferred_element_type=jnp.float32).astype(
        jnp.bfloat16
    )
    grad_groups = attended_grad.reshape(row_count, KVH, group_size, HD)

    def delta_step(block_id, summed):
        raw_scores, visible, _ = block_scores(block_id)
        probs_full = exact_probs(raw_scores, visible)
        prob_grad = jnp.einsum(
            "tgrd,kgd->grtk", grad_groups, value_part(block_id), preferred_element_type=jnp.float32
        )
        return summed + jnp.sum(probs_full * prob_grad, axis=-1)

    delta_rows = lax.fori_loop(
        0, needed, delta_step, jnp.zeros((KVH, group_size, row_count), jnp.float32)
    )

    def grad_step(block_id, running):
        query_grad, key_grad, value_grad = running
        raw_scores, visible, key_part = block_scores(block_id)
        probs_full = exact_probs(raw_scores, visible)
        prob_grad = jnp.einsum(
            "tgrd,kgd->grtk", grad_groups, value_part(block_id), preferred_element_type=jnp.float32
        )
        score_grad = (probs_full * (prob_grad - delta_rows[..., None])).astype(jnp.bfloat16)
        query_grad = (
            query_grad
            + jnp.einsum("grtk,kgd->tgrd", score_grad, key_part, preferred_element_type=jnp.float32)
            * score_scale
        )
        key_piece = (
            jnp.einsum(
                "grtk,tgrd->kgd", score_grad, query_groups, preferred_element_type=jnp.float32
            )
            * score_scale
        )
        value_piece = jnp.einsum(
            "grtk,tgrd->kgd",
            probs_full.astype(jnp.bfloat16),
            grad_groups,
            preferred_element_type=jnp.float32,
        )
        first_key = block_id * key_block
        key_grad = lax.dynamic_update_slice_in_dim(
            key_grad, key_piece.reshape(key_block, KVD), first_key, 0
        )
        value_grad = lax.dynamic_update_slice_in_dim(
            value_grad, value_piece.reshape(key_block, KVD), first_key, 0
        )
        return (query_grad, key_grad, value_grad)

    start_grads = (
        jnp.zeros((row_count, KVH, group_size, HD), jnp.float32),
        jnp.zeros((seq_length, KVD), jnp.float32),
        jnp.zeros((seq_length, KVD), jnp.float32),
    )
    query_grad, key_grad, value_grad = lax.fori_loop(0, needed, grad_step, start_grads)
    key_sum, value_sum = (
        lax.psum_scatter(key_grad, "expert", scatter_dimension=0, tiled=True),
        lax.psum_scatter(value_grad, "expert", scatter_dimension=0, tiled=True),
    )
    query_back = unrotate(query_grad.reshape(row_count, H, HD), cosine, sine_table).reshape(
        row_count, QD
    )
    key_back = unrotate(key_sum.reshape(row_count, KVH, HD), cosine, sine_table).reshape(
        row_count, KVD
    )
    project_grad = jnp.concatenate([query_back, key_back, value_sum], axis=1).astype(jnp.bfloat16)
    weight_grad_qkv = jnp.einsum(
        "td,tc->dc", normed, project_grad, preferred_element_type=jnp.float32
    )
    normed_grad = jnp.einsum(
        "tc,dc->td", project_grad, w_project, preferred_element_type=jnp.float32
    )
    _, first_pull = jax.vjp(rms_scale, hidden_in, gain_one)
    input_part, gain_one_grad = first_pull(normed_grad)
    input_total = resid_grad + input_part
    attn_partial = jnp.concatenate([weight_grad_qkv, output_grad], axis=1)
    gain_partial = jnp.stack([gain_one_grad, gain_two_grad], axis=1)
    grad_attn, grad_gains = (
        lax.psum_scatter(attn_partial, ("dp", "expert"), scatter_dimension=0, tiled=True),
        lax.psum_scatter(gain_partial, ("dp", "expert"), scatter_dimension=0, tiled=True),
    )
    grad_expert = lax.psum_scatter(
        jnp.concatenate([inward_grad, down_grad], axis=2).astype(jnp.bfloat16),
        "dp",
        scatter_dimension=1,
        tiled=True,
    ).astype(jnp.float32)
    local_squares = (
        jnp.sum(grad_attn * grad_attn)
        + jnp.sum(grad_gains * grad_gains)
        + jnp.sum(grad_expert * grad_expert)
    )
    grad_norm = jnp.sqrt(lax.psum(local_squares, ("dp", "expert")))
    clip_factor = jnp.minimum(1.0, CLIP_NORM / (grad_norm + 1e-06))
    steps_done = step_count.astype(jnp.float32)
    attn_new = adam_update(
        w_attn,
        first_attn,
        second_attn,
        grad_attn * clip_factor,
        steps_done,
        WEIGHT_DECAY,
        LEARN_RATE,
    )
    gains_new = adam_update(
        norm_gains, first_gains, second_gains, grad_gains * clip_factor, steps_done, 0.0, GAIN_RATE
    )
    expert_new = adam_update(
        w_expert,
        first_expert,
        second_expert,
        grad_expert * clip_factor,
        steps_done,
        WEIGHT_DECAY,
        LEARN_RATE,
    )
    return (
        block_result[None],
        input_total[None],
        grad_norm,
        attn_new[0],
        attn_new[1],
        attn_new[2],
        gains_new[0],
        gains_new[1],
        gains_new[2],
        expert_new[0],
        expert_new[1],
        expert_new[2],
    )


def fits(mesh):
    return dict(mesh.shape) == {"dp": 4, "expert": KVH}


def head_tables(length):
    halves = np.arange(HD // 2, dtype=np.float32)
    inverse = np.power(np.float32(ROPE_BASE), np.float32(-2.0) * halves / np.float32(HD))
    angles = np.arange(length, dtype=np.float32)[:, None] * inverse[None, :]
    cosine, sine = np.cos(angles), np.sin(angles)
    cosine = np.concatenate([cosine] * 4, axis=1)
    return jnp.asarray(cosine), jnp.asarray(np.concatenate([-sine, sine] * 2, axis=1))


LINE, SPAN, PLANE, PARTS = 4, 8, 4, 4
QUERY_BLOCK = 256
NN, NT, TN = ((1,), (0,)), ((1,), (1,)), ((0,), (0,))


def remote(source, target, sent, landed, device):
    return pltpu.make_async_remote_copy(
        src_ref=source,
        dst_ref=target,
        send_sem=sent,
        recv_sem=landed,
        device_id=device,
        device_id_type=pl.DeviceIdType.MESH,
    )


def whereabouts():
    i, e = lax.axis_index("dp"), lax.axis_index("expert")
    return i, e, e // 2, lax.rem(e, 2)


def partners(i, e):
    others = [(i, lax.rem(e + k, SPAN)) for k in range(1, SPAN)]
    return others + [(lax.rem(i + k, PLANE), e) for k in range(1, PLANE)]


def piece(j, size):
    return pl.ds(pl.multiple_of(j * size, size), size)


class LineGather:
    def __init__(self, slot, source, where, sems):
        self.slot, self.source, self.where = slot, source, where
        self.sent, self.passed, self.landed = sems

    def _own(self, j, k):
        i, e, z, c = self.where
        there = z * 2 + 1 - c if k == 0 else lax.rem(z + k, LINE) * 2 + c
        return remote(self.source(j), self.slot(e, j), self.sent.at[j, k], self.landed.at[j, e], (i, there))

    def _pass(self, j, k):
        i, e, z, c = self.where
        index = lax.rem(z + k, LINE) * 2 + c
        place = self.slot(index, j)
        return remote(place, place, self.passed.at[j, k], self.landed.at[j, index], (i, z * 2 + 1 - c))

    def _relay(self, j):
        i, e, z, c = self.where
        index = lax.rem(z + 2, LINE) * 2 + c
        place = self.slot(index, j)
        end = LINE - 1 - lax.rem(z + 2, LINE)
        return remote(place, place, self.passed.at[j, 0], self.landed.at[j, index], (i, end * 2 + c))

    def _each_own(self, j, act):
        z = self.where[2]
        act(self._own(j, 2))
        pl.when(z != LINE - 1)(lambda: act(self._own(j, 1)))
        pl.when(z != 0)(lambda: act(self._own(j, 3)))
        act(self._own(j, 0))

    def _when_inner(self, act):
        z = self.where[2]
        pl.when((z > 0) & (z < LINE - 1))(act)

    def start(self, j):
        self._each_own(j, lambda copy: copy.start())

    def wait(self, j, index):
        i, e, z, c = self.where
        place = self.slot(index, j)
        remote(place, place, self.sent.at[j, 0], self.landed.at[j, index], (i, z * 2 + 1 - c)).wait_recv()

    def sibling(self):
        _, e, z, c = self.where
        return z * 2 + 1 - c

    def near(self, k):
        _, e, z, c = self.where
        return lax.rem(z + k, LINE) * 2 + c

    def far(self, k):
        _, e, z, c = self.where
        return lax.rem(z + k, LINE) * 2 + 1 - c

    def forward(self, j, k):
        self.wait(j, self.near(k))
        if k == 2:
            self._when_inner(lambda: self._relay(j).start())
        self._pass(j, k).start()

    def forward_all(self, j):
        for k in (2, 1, 3):
            self.forward(j, k)

    def rest(self, j):
        self.wait(j, self.sibling())
        for k in range(1, LINE):
            self.wait(j, self.far(k))

    def drain(self, j):
        self._each_own(j, lambda copy: copy.wait_send())
        self._when_inner(lambda: self._relay(j).wait_send())
        for k in range(1, LINE):
            self._pass(j, k).wait_send()


class LineScatter:
    def __init__(self, data, where, pair, out, inbox, own, sems, size):
        self.data, self.where, self.size = data, where, size
        self.pair, self.out, self.inbox, self.own = pair, out, inbox, own
        self.pair_sent, self.pair_landed, self.sent, self.landed = sems

    def _pair(self, j, k):
        i, e, z, c = self.where
        there, rows = lax.rem(z + k, LINE), piece(j, self.size)
        return remote(
            self.data.at[there * 2 + 1 - c, rows], self.pair.at[there, rows],
            self.pair_sent.at[j, there], self.pair_landed.at[j, there], (i, z * 2 + 1 - c),
        )

    def _send(self, j, k):
        i, e, z, c = self.where
        there, rows = lax.rem(z + k, LINE), piece(j, self.size)
        crossing = {1: z // (LINE - 1), 2: 0, 3: (LINE - 1 - z) // (LINE - 1)}[k]
        chip = {1: z + 1 - 2 * crossing, 2: there, 3: z - 1 + 2 * crossing}[k]
        slot = z + crossing * (chip - z)
        return remote(
            self.out.at[there, rows], self.inbox.at[slot, rows],
            self.sent.at[j, there], self.landed.at[j, slot], (i, chip * 2 + c),
        )

    def _landed(self, j, slot):
        i, e, z, c = self.where
        place = self.inbox.at[slot, piece(j, self.size)]
        remote(place, place, self.sent.at[j, slot], self.landed.at[j, slot], (i, z * 2 + 1 - c)).wait_recv()

    def _both(self, j, there):
        c, rows = self.where[3], piece(j, self.size)
        return self.data[there * 2 + c, rows].astype(jnp.float32) + self.pair[there, rows].astype(jnp.float32)

    def _across(self, j):
        there, rows = lax.rem(self.where[2] + 2, LINE), piece(j, self.size)
        return there, rows, self._both(j, there)

    def start(self, j):
        for k in (1, 3, 2, 0):
            self._pair(j, k).start()

    def start_one(self, j, k):
        self._pair(j, k).start()

    def fold_one(self, j, k):
        z, rows = self.where[2], piece(j, self.size)
        self._pair(j, k).wait_recv()

        def send():
            there = lax.rem(z + k, LINE)
            self.out[there, rows] = self._both(j, there).astype(jnp.bfloat16)
            self._send(j, k).start()

        if k == 0:
            self.own[rows] = self._both(j, z)
        elif k == 2:
            pl.when((z == 0) | (z == LINE - 1))(send)
        else:
            send()

    def fold(self, j):
        for k in (1, 3, 2, 0):
            self.fold_one(j, k)

    def fold_late(self, j):
        z = self.where[2]

        @pl.when((z > 0) & (z < LINE - 1))
        def _():
            there, rows, both = self._across(j)
            self._landed(j, z)
            self.out[there, rows] = (both + self.inbox[z, rows].astype(jnp.float32)).astype(jnp.bfloat16)
            self._send(j, 2).start()

    def total(self, j):
        z, rows = self.where[2], piece(j, self.size)

        def add(k):
            there = lax.rem(z + k, LINE)
            self._landed(j, there)
            self.own[rows] += self.inbox[there, rows].astype(jnp.float32)

        pl.when(z != LINE - 1)(lambda: add(1))
        pl.when(z != 0)(lambda: add(3))
        add(2)
        return self.own[rows]

    def drain(self, j):
        for k in range(LINE):
            self._pair(j, k).wait_send()
        for k in range(1, LINE):
            self._send(j, k).wait_send()


class PlaneGather:
    def __init__(self, where, held, sems):
        i, self.e = where[0], where[1]
        self.i, self.held, self.sems = i, held, sems
        self.x = i // 2 * 2 + 1 - lax.rem(i, 2)
        self.y = (1 - i // 2) * 2 + lax.rem(i, 2)
        self.far = PLANE - 1 - i
        self.half = held.shape[2] // 2

    def _copy(self, l, n, source):
        rows = (slice(None), slice(None), slice(0, self.half), slice(self.half, None))[n]
        to = (self.x, self.y, self.y, self.x)[n]
        sent, landed = self.sems
        place = self.held.at[l, source, rows]
        return remote(place, place, sent.at[l, n], landed.at[l, n], (to, self.e))

    def start(self, l):
        self._copy(l, 0, self.i).start()
        self._copy(l, 1, self.i).start()

    def forward(self, l):
        self._copy(l, 0, self.x).wait_recv()
        self._copy(l, 2, self.x).start()
        self._copy(l, 1, self.y).wait_recv()
        self._copy(l, 3, self.y).start()

    def rest(self, l):
        self._copy(l, 2, self.far).wait_recv()
        self._copy(l, 3, self.far).wait_recv()

    def drain(self, l):
        for n, source in enumerate((self.i, self.i, self.x, self.y)):
            self._copy(l, n, source).wait_send()


class PlaneScatter:
    def __init__(self, plane, out, inbox, sems):
        self.plane, self.out, self.inbox = plane, out, inbox
        self.sent, self.landed = sems
        self.half = plane.half

    def _copy(self, l, chunk, part, n):
        first = slice(0, self.half) if part == 0 else slice(self.half, None)
        to_x = chunk == 1 or (chunk == 0 and part == 0)
        return remote(
            self.out.at[l, chunk, first], self.inbox.at[l, chunk, first], self.sent.at[l, n], self.landed.at[l, n],
            (self.plane.x if to_x else self.plane.y, self.plane.e),
        )

    def _at(self, l, chunk, part):
        return self._copy(l, chunk, part, chunk * 2 + part)

    def start(self, l, chunk):
        for part in ((0, 1), (0,), (1,))[chunk]:
            self._at(l, chunk, part).start()

    def combine(self, l):
        for chunk, part in ((1, 1), (2, 0)):
            rows = slice(part * self.half, (part + 1) * self.half)
            self._at(l, 0, part).wait_recv()
            mine = self.out[l, chunk, rows].astype(jnp.float32) + self.inbox[l, 0, rows].astype(jnp.float32)
            self.out[l, chunk, rows] = mine.astype(jnp.bfloat16)
            self._at(l, chunk, part).start()

    def rest(self, l):
        for chunk in (1, 2):
            for part in (0, 1):
                self._at(l, chunk, part).wait_recv()

    def drain(self, l):
        for chunk in range(3):
            for part in (0, 1):
                self._at(l, chunk, part).wait_send()


def half_turn_tile(part):
    lane = lax.broadcasted_iota(jnp.int32, part.shape, 1)
    ahead = pltpu.roll(part, 128 - HD // 2, 1)
    behind = pltpu.roll(part, HD // 2, 1)
    return jnp.where(lax.rem(lane, HD) < HD // 2, ahead, behind)


def rms_rows(values):
    return lax.rsqrt(jnp.mean(values * values, axis=-1, keepdims=True) + EPSILON)


def norm_back(values, gain, upper):
    scale = rms_rows(values)
    scaled = upper * gain
    inner = jnp.mean(values * scaled, axis=-1, keepdims=True)
    return scale * scaled - values * (scale * scale * scale) * inner, upper * values * scale


def dot(a, b, contract):
    return lax.dot_general(a, b, (contract, ((), ())), preferred_element_type=jnp.float32)


def visible_keys(first, low, high, docs_row, docs_col):
    shape = (QUERY_BLOCK, high - low)
    key = lax.broadcasted_iota(jnp.int32, shape, 1) + low
    query = lax.broadcasted_iota(jnp.int32, shape, 0) + first
    return (key <= query) & (docs_row[:, low:high] == docs_col)


def layer_kernel(x, up, wa, we, routes, gates, doc_ids, shard_gains, cos, sin, block, grad, norm, ge_far, ga, gn, clip, **held):
    layer_body(
        types.SimpleNamespace(
            x=x, up=up, wa=wa, we=we, routes=routes, gates=gates, doc_ids=doc_ids, shard_gains=shard_gains,
            cos=cos, sin=sin,
            block=block, grad=grad, norm=norm, ge_far=ge_far, ga=ga, gn=gn, clip=clip, **held,
        )
    )


def layer_outputs(rows, local):
    f32 = jnp.float32
    shaped = jax.ShapeDtypeStruct
    deep = D // PLANE
    return [
        shaped((rows, D), jnp.bfloat16), shaped((rows, D), f32), shaped((1, 1), f32),
        shaped((local, deep, 3 * FF), f32), shaped((deep // SPAN, 3072), f32), shaped((8, rows), f32),
        shaped((1, 1), f32),
    ]


def layer_scratch(rows, local):
    f32, bf16 = jnp.float32, jnp.bfloat16
    held, sems = pltpu.VMEM, lambda *shape: pltpu.SemaphoreType.DMA(shape)
    deep = D // PLANE
    part = deep // SPAN
    blocks = held((SPAN, rows, D), bf16)
    quarter = held((LINE, rows, D), bf16)
    line = lambda parts: (sems(parts, LINE), sems(parts, LINE), sems(parts, SPAN))
    scatter = lambda parts: tuple(sems(parts, LINE) for _ in range(4))
    both = lambda *shape: (sems(*shape), sems(*shape))
    return dict(
        x_all=blocks, up_all=blocks, h1=blocks, o_all=blocks, h2=blocks, d=blocks, da_all=blocks,
        qkv=held((SPAN * rows, 256), bf16), lse=held((SPAN * rows, 128), f32),
        wq_out=held((SPAN, part, 256), bf16), w_mine=held((PLANE, SPAN, part, 256), bf16),
        wo_all=held((PLANE, LINE, 2, part, D), bf16), we_all=held((local, PLANE, deep, 3 * FF), bf16),
        o_own=held((SPAN, rows, 128), bf16),
        r_part=held((SPAN, rows // PARTS, D), f32), r_own=held((rows, D), f32),
        pack=held((SPAN, 8, rows), f32), pack_all=held((SPAN, 8, rows), f32), gain_sum=held((PLANE, 2, 8, 128), f32),
        cols=held((SPAN, rows, 128), f32), docs=held((8, SPAN * rows), f32), gains=held((8, D), f32),
        act=held((local, SPAN, rows, FF), bf16), dgu=held((local, SPAN, rows, 2 * FF), bf16),
        pair=quarter, out=quarter, inbox=quarter, own=held((rows, D), f32),
        y_pair=quarter, y_out=quarter, y_inbox=quarter, y_own=held((rows, D), f32),
        ge_in=held((local, PLANE - 1, deep, 3 * FF), bf16),
        do=held((SPAN, rows, 128), bf16), dkv=held((SPAN * rows, 128), f32), dqkv=held((SPAN * rows, 256), bf16),
        dr=held((rows, D), f32), gn_two=held((8, D), f32),
        ga_out=held((PLANE - 1, deep, 384), bf16), ga_in=held((PLANE - 1, deep, 384), bf16),
        gs=held((SPAN, part, 384), f32), gs_out=held((SPAN, part, 384), bf16), ga_all=held((SPAN, part, 384), bf16),
        gn_in=held((PLANE, 16, 128), f32), mix_in=held((SPAN, 24, 128), f32), sq_in=held((PLANE, 8, 128), f32),
        ge=held((local, deep, 3 * FF), f32), store=sems(local),
        x_sems=line(1), up_sems=line(PARTS), wo_sems=line(1), o_sems=line(PARTS), da_sems=line(PARTS),
        d_sems=scatter(PARTS), y_sems=scatter(1), h_sems=scatter(1),
        load=sems(local), pack_sems=both(SPAN), wq_sems=both(SPAN), wqd_sems=both(PLANE), gd_sems=both(PLANE),
        wod_sems=both(PLANE), wop_sems=both(PLANE), we_sems=both(local, 4), ge_sems=both(local, 6),
        ga_sems=both(PLANE), gn_sems=both(PLANE), gs_sems=both(SPAN), mix_sems=both(SPAN), sq_sems=both(PLANE),
    )


def layer_body(v):
    f32, bf16 = jnp.float32, jnp.bfloat16
    where = i, e, z, c = whereabouts()
    sibling = (i, z * 2 + 1 - c)
    rows, local, deep = v.x.shape[0], v.we_all.shape[0], v.ge.shape[1]
    length, size = rows * SPAN, rows // PARTS
    own_cols = piece(e, 128)
    live = []

    def go(*spec):
        copy = remote(*spec)
        copy.start()
        live.append(copy)

    def along(k):
        return lax.rem(i + k, PLANE)

    def across(k):
        return lax.rem(e + k, SPAN)

    def line(sems, slot, source):
        return LineGather(slot, source, where, sems)

    x_line = line(v.x_sems, lambda s, j: v.x_all.at[s], lambda j: v.x)
    up_line = line(v.up_sems, lambda s, j: v.up_all.at[s, piece(j, size)], lambda j: v.up.at[piece(j, size)])
    wo_line = line(
        v.wo_sems, lambda s, j: v.wo_all.at[i, s // 2, lax.rem(s, 2)], lambda j: v.wo_all.at[i, z, c]
    )
    o_line = line(
        v.o_sems,
        lambda s, j: v.o_all.at[:, piece(j, size), piece(s, 128)],
        lambda j: v.o_own.at[:, piece(j, size)],
    )
    da_line = line(
        v.da_sems, lambda s, j: v.da_all.at[s, piece(j, size)], lambda j: v.da_all.at[e, piece(j, size)]
    )
    we_plane = PlaneGather(where, v.we_all, v.we_sems)
    ge_plane = PlaneScatter(we_plane, v.we_all, v.ge_in, v.ge_sems)
    d_scatter = LineScatter(v.d, where, v.pair, v.out, v.inbox, v.own, v.d_sems, size)
    y_scatter = LineScatter(v.o_all, where, v.y_pair, v.y_out, v.y_inbox, v.y_own, v.y_sems, rows)
    h_scatter = LineScatter(v.d, where, v.pair, v.out, v.inbox, v.own, v.h_sems, rows)

    loads = [pltpu.make_async_copy(v.we.at[l], v.ge.at[l], v.load.at[l]) for l in range(local)]
    for copy in loads:
        copy.start()
    results = [pltpu.make_async_copy(v.ge.at[l], v.ge_far.at[l], v.store.at[l]) for l in range(local)]
    barrier = pltpu.get_barrier_semaphore()
    for device in partners(i, e):
        pl.semaphore_signal(barrier, inc=1, device_id=device, device_id_type=pl.DeviceIdType.MESH)
    lane = lax.broadcasted_iota(jnp.int32, (2, rows), 1)
    index, few = i * SPAN + e, rows // v.shard_gains.shape[1]
    spread = jnp.concatenate([v.shard_gains[...]] * few, axis=1)
    spread = jnp.where(lane // (rows // few) == lax.rem(index, few), spread, 0.0)
    shared = [v.doc_ids[...].astype(f32), spread, jnp.zeros((3, rows), f32)]
    for g in range(SPAN):
        named = [
            jnp.sum(jnp.where(v.routes[...] == g * local + l, v.gates[...], 0.0), axis=0, keepdims=True)
            for l in range(local)
        ]
        v.pack[g] = jnp.concatenate(named + shared, axis=0)
    for g in range(SPAN):
        v.wq_out[g, :, :128] = v.wa[:, g * 128 : (g + 1) * 128].astype(bf16)
        key_value = [v.wa[:, first + g * HD : first + (g + 1) * HD] for first in (QD, QD + KVD)]
        v.wq_out[g, :, 128:] = jnp.concatenate(key_value, axis=1).astype(bf16)
    v.w_mine[i, e] = v.wq_out[e]
    v.wo_all[i, z, c] = v.wa[:, QKV:].astype(bf16)
    v.pack_all[e] = v.pack[e]
    v.x_all[e] = v.x[...]
    v.up_all[e] = v.up[...]
    pl.semaphore_wait(barrier, SPAN + PLANE - 2)
    for k in range(1, SPAN):
        go(v.pack.at[across(k)], v.pack_all.at[e], v.pack_sems[0].at[k], v.pack_sems[1].at[e], (i, across(k)))
    for k in range(1, SPAN):
        go(v.wq_out.at[across(k)], v.w_mine.at[i, e], v.wq_sems[0].at[k], v.wq_sems[1].at[e], (i, across(k)))
    wo_line.start(0)
    x_line.start(0)
    loads[0].wait()
    v.we_all[0, i] = v.ge[0].astype(bf16)
    we_plane.start(0)

    for k in range(1, SPAN):
        slot = v.pack_all.at[across(k)]
        remote(slot, slot, v.pack_sems[0].at[k], v.pack_sems[1].at[across(k)], sibling).wait_recv()
    for half in range(2):
        summed = v.pack_all[4 * half]
        for s in range(1, 4):
            summed = summed + v.pack_all[4 * half + s]
        v.gain_sum[i, half] = summed
    for k in range(1, PLANE):
        go(v.gain_sum.at[i], v.gain_sum.at[i], v.gd_sems[0].at[k], v.gd_sems[1].at[i], (along(k), e))
    for k in range(1, SPAN):
        slot = v.w_mine.at[i, across(k)]
        remote(slot, slot, v.wq_sems[0].at[k], v.wq_sems[1].at[across(k)], sibling).wait_recv()
    for k in range(1, PLANE):
        go(v.w_mine.at[i], v.w_mine.at[i], v.wqd_sems[0].at[k], v.wqd_sems[1].at[i], (along(k), e))
    loads[1].wait()
    v.we_all[1, i] = v.ge[1].astype(bf16)
    for s in range(SPAN):
        block = v.pack_all[s]
        tall = jnp.concatenate([block, jnp.zeros((rows - block.shape[0], rows), f32)], axis=0)
        v.cols[s] = tall.T
        v.docs[:, s * rows : (s + 1) * rows] = block
    for k in range(1, PLANE):
        slot = v.gain_sum.at[along(k)]
        remote(slot, slot, v.gd_sems[0].at[k], v.gd_sems[1].at[along(k)], sibling).wait_recv()
    for tile in range(2 * PLANE):
        v.gains[:, tile * 128 : (tile + 1) * 128] = v.gain_sum[tile // 2, tile % 2].astype(bf16).astype(f32)
    gain_one, gain_two = v.gains[3:4], v.gains[4:5]

    def first_norm(s):
        values = v.x_all[s].astype(f32)
        v.h1[s] = (values * rms_rows(values) * gain_one).astype(bf16)

    wo_line.forward_all(0)
    for k in range(1, PLANE):
        mine = v.wo_all.at[i, :, c]
        go(mine, mine, v.wod_sems[0].at[k], v.wod_sems[1].at[i], (along(k), e))
    first_norm(e)
    for k in (2, 1, 3):
        x_line.forward(0, k)
        first_norm(x_line.near(k))
    up_line.start(0)
    up_line.start(1)
    we_plane.forward(0)
    we_plane.start(1)
    x_line.wait(0, x_line.sibling())
    first_norm(x_line.sibling())
    for k in range(1, LINE):
        x_line.wait(0, x_line.far(k))
        first_norm(x_line.far(k))
    for k in range(1, PLANE):
        slot = v.w_mine.at[along(k)]
        remote(slot, slot, v.wqd_sems[0].at[k], v.wqd_sems[1].at[along(k)], sibling).wait_recv()

    weights = v.w_mine[...].reshape(D, 256)
    lane = lax.broadcasted_iota(jnp.int32, (QUERY_BLOCK, 128), 1)

    def tables(first):
        cosine, sine = v.cos[first : first + QUERY_BLOCK], v.sin[first : first + QUERY_BLOCK]
        return cosine, sine, jnp.where(lane < HD, cosine, 1.0), jnp.where(lane < HD, sine, 0.0)

    for first in range(0, length, QUERY_BLOCK):
        span = slice(first, first + QUERY_BLOCK)
        slots = slice(first // rows, (first + QUERY_BLOCK) // rows)
        raw = dot(v.h1[slots].reshape(QUERY_BLOCK, D), weights, NN)
        q_cos, q_sin, kv_cos, kv_sin = tables(first)
        q_raw, kv_raw = raw[:, :128], raw[:, 128:]
        v.qkv[span, :128] = (q_raw * q_cos + half_turn_tile(q_raw) * q_sin).astype(bf16)
        v.qkv[span, 128:] = (kv_raw * kv_cos + half_turn_tile(kv_raw) * kv_sin).astype(bf16)


    def block_masks(first):
        low, high = max(0, first - length // 2), first + QUERY_BLOCK
        slots = slice(first // rows, (first + QUERY_BLOCK) // rows)
        docs_col = v.cols[slots, :, 2:3].reshape(QUERY_BLOCK, 1)
        return low, high, slots, visible_keys(first, low, high, v.docs[2:3], docs_col)

    for first in range(0, length, QUERY_BLOCK):
        low, high, slots, visible = block_masks(first)
        span = slice(first, first + QUERY_BLOCK)
        outs, logs = [], []
        for head in range(2):
            q = v.qkv[span, head * HD : (head + 1) * HD]
            scores = dot(q, v.qkv[low:high, 128:192], NT) * HD**-0.5
            scores = jnp.where(visible, scores, -1e30)
            peak = jnp.max(scores, axis=-1, keepdims=True)
            raw = jnp.exp(scores - peak)
            total = jnp.sum(raw, axis=-1, keepdims=True)
            probs = raw * (1.0 / total)
            logs.append(peak + jnp.log(total))
            outs.append(dot(probs.astype(bf16), v.qkv[low:high, 192:256], NN))
        both = jnp.concatenate(outs, axis=1).astype(bf16).reshape(-1, rows, 128)
        v.o_own[slots] = both
        v.o_all[slots, :, own_cols] = both
        v.lse[span] = jnp.where(lane == 0, logs[0], logs[1])
    o_line.start(0)
    o_line.start(1)
    up_line.start(2)
    o_line.start(2)
    up_line.start(3)
    o_line.start(3)

    wo_line.rest(0)
    for k in range(1, PLANE):
        here = v.wo_all.at[along(k), :, c]
        remote(here, here, v.wod_sems[0].at[k], v.wod_sems[1].at[along(k)], sibling).wait_recv()
        go(here, here, v.wop_sems[0].at[k], v.wop_sems[1].at[along(k)], sibling)
    for k in range(1, PLANE):
        far = v.wo_all.at[along(k), :, 1 - c]
        remote(far, far, v.wod_sems[0].at[k], v.wop_sems[1].at[along(k)], sibling).wait_recv()

    def second_norm(j):
        part = piece(j, size)
        w_out = v.wo_all[...].reshape(D, D)
        branch = dot(v.o_all[:, part].reshape(-1, D), w_out, NT)
        values = v.x_all[:, part].reshape(-1, D).astype(f32) + branch
        v.r_part[...] = values.reshape(SPAN, size, D)
        v.r_own[part] = v.r_part[e]
        v.h2[:, part] = (values * rms_rows(values) * gain_two).astype(bf16).reshape(SPAN, size, D)

    def gate_of(l, part):
        return v.cols[:, part, l : l + 1].reshape(-1, 1)

    def expert(l, j):
        part = piece(j, size)
        weights = v.we_all[l].reshape(D, 3 * FF)
        gate = gate_of(l, part)
        routed = gate > 0
        gu = dot(v.h2[:, part].reshape(-1, D), weights[:, : 2 * FF], NN)
        g, u = gu[:, :FF], gu[:, FF:]
        sig = 1.0 / (1.0 + jnp.exp(-g))
        act = jnp.where(routed, g * sig * u, 0.0).astype(bf16)
        v.act[l, :, part] = act.reshape(SPAN, size, FF)
        dy = (gate * v.up_all[:, part].reshape(-1, D).astype(f32)).astype(bf16)
        dact = dot(dy, weights[:, 2 * FF :], NN)
        dg = dact * u * sig * (1.0 + g * (1.0 - sig))
        du = dact * g * sig
        dgu = jnp.where(routed, jnp.concatenate([dg, du], axis=1), 0.0).astype(bf16)
        v.dgu[l, :, part] = dgu.reshape(SPAN, size, 2 * FF)
        d = dot(dgu, weights[:, : 2 * FF], NT).astype(bf16)
        y = dot(act, weights[:, 2 * FF :], NT).astype(bf16)
        if l == 0:
            v.d[:, part] = d.reshape(SPAN, size, D)
            v.o_all[:, part] = y.reshape(SPAN, size, D)
        else:
            d = v.d[:, part].reshape(-1, D).astype(f32) + d.astype(f32)
            v.d[:, part] = d.astype(bf16).reshape(SPAN, size, D)
            y = gate_of(0, part) * v.o_all[:, part].reshape(-1, D).astype(f32) + gate * y.astype(f32)
            v.o_all[:, part] = y.astype(bf16).reshape(SPAN, size, D)

    we_plane.rest(0)

    def first_round(j, carry):
        @pl.when(j == PARTS - 1)
        def _():
            we_plane.forward(1)

        @pl.when(j < PARTS)
        def _():
            o_line.forward_all(j)
            up_line.forward_all(j)

        @pl.when(j > 0)
        def _():
            o_line.drain(j - 1)
            expert(0, j - 1)

        @pl.when(j < PARTS)
        def _():
            o_line.rest(j)
            up_line.rest(j)
            second_norm(j)

        return carry

    lax.fori_loop(0, PARTS + 1, first_round, 0)
    we_plane.rest(1)

    def expert_chunk(l, there):
        span = piece(there, deep)
        inward = dot(v.h2[:, :, span].reshape(length, deep), v.dgu[l].reshape(length, 2 * FF), TN)
        gate = v.cols[:, :, l : l + 1].reshape(length, 1)
        dy = (gate * v.up_all[:, :, span].reshape(length, deep).astype(f32)).astype(bf16)
        return inward, dot(dy, v.act[l].reshape(length, FF), TN)

    def send_chunk(l, chunk):
        inward, down = expert_chunk(l, (we_plane.far, we_plane.x, we_plane.y)[chunk])
        v.we_all[l, chunk, :, : 2 * FF] = inward.astype(bf16)
        v.we_all[l, chunk, :, 2 * FF :] = down.astype(bf16)
        ge_plane.start(l, chunk)

    we_plane.drain(0)

    def second_round(j, carry):
        @pl.when(j < PARTS)
        def _():
            expert(1, j)
            d_scatter.start(j)

        for chunk in range(3):
            pl.when(j == chunk)(lambda chunk=chunk: send_chunk(0, chunk))

        @pl.when((j > 0) & (j <= PARTS))
        def _():
            d_scatter.fold(j - 1)

        @pl.when(j > 1)
        def _():
            d_scatter.fold_late(j - 2)

        return carry

    lax.fori_loop(0, PARTS + 2, second_round, 0)
    y_scatter.start(0)
    we_plane.drain(1)

    def keep_chunk(l):
        inward, down = expert_chunk(l, i)
        v.ge[l, :, : 2 * FF] = inward
        v.ge[l, :, 2 * FF :] = down

    v.gn_two[...] = jnp.zeros_like(v.gn_two)

    def second_back(j):
        part = piece(j, size)
        back, shares = norm_back(v.r_own[part], gain_two, d_scatter.total(j))
        dr = v.up_all[e, part].astype(f32) + back
        v.dr[part] = dr
        v.gn_two[:1] += jnp.sum(shares, axis=0, keepdims=True)
        v.da_all[e, part] = dr.astype(bf16)
        da_line.start(j)

    send_chunk(1, 0)
    second_back(0)
    ge_plane.combine(0)
    send_chunk(1, 1)
    second_back(1)
    send_chunk(1, 2)
    second_back(2)
    ge_plane.combine(1)
    second_back(3)
    keep_chunk(0)
    keep_chunk(1)
    y_scatter.fold(0)
    wo_mine = v.wo_all[:, :, :, :, own_cols].reshape(D, 128)
    for j in range(PARTS):
        da_line.forward_all(j)
    y_scatter.fold_late(0)
    for j in range(PARTS):
        da_line.rest(j)
        part = piece(j, size)
        do = dot(v.da_all[:, part].reshape(-1, D), wo_mine, NN).astype(bf16)
        v.do[:, part] = do.reshape(SPAN, size, 128)

    v.dkv[...] = jnp.zeros_like(v.dkv)
    for first in range(0, length, QUERY_BLOCK):
        low, high, slots, visible = block_masks(first)
        span = slice(first, first + QUERY_BLOCK)
        keys, values = v.qkv[low:high, 128:192], v.qkv[low:high, 192:256]
        do_both = v.do[slots].reshape(QUERY_BLOCK, 128)
        dqs, dk, dv = [], 0.0, 0.0
        for head in range(2):
            q = v.qkv[span, head * HD : (head + 1) * HD]
            do = do_both[:, head * HD : (head + 1) * HD]
            scores = dot(q, keys, NT) * HD**-0.5
            probs = jnp.exp(jnp.where(visible, scores - v.lse[span, head : head + 1], -1e30))
            dp = dot(do, values, NT)
            delta = jnp.sum(probs * dp, axis=-1, keepdims=True)
            ds = (probs * (dp - delta)).astype(bf16)
            dqs.append(dot(ds, keys, NN))
            dk = dk + dot(ds, q, TN)
            dv = dv + dot(probs.astype(bf16), do, TN)
        v.dkv[low:high] += jnp.concatenate([dk * HD**-0.5, dv], axis=1)
        dq = jnp.concatenate(dqs, axis=1) * HD**-0.5
        cosine, sine = v.cos[span], v.sin[span]
        v.dqkv[span, :128] = (dq * cosine - half_turn_tile(dq) * sine).astype(bf16)
    for first in range(0, length, QUERY_BLOCK):
        span = slice(first, first + QUERY_BLOCK)
        dkv = v.dkv[span]
        _, _, cosine, sine = tables(first)
        v.dqkv[span, 128:] = (dkv * cosine - half_turn_tile(dkv) * sine).astype(bf16)

    o = v.o_own[...].reshape(length, 128)
    dqkv = v.dqkv[...]

    def rows_copy(k):
        return remote(v.ga_out.at[k - 1], v.ga_in.at[k - 1], v.ga_sems[0].at[k], v.ga_sems[1].at[k], (along(k), e))

    for k in (2, 1, 3, 0):
        span = piece(along(k), deep)
        projections = dot(v.h1[:, :, span].reshape(length, deep), dqkv, TN)
        output = dot(v.da_all[:, :, span].reshape(length, deep), o, TN)
        if k == 0:
            v.gs[:, :, :256] = projections.reshape(SPAN, -1, 256)
            v.gs[:, :, 256:] = output.reshape(SPAN, -1, 128)
        else:
            v.ga_out[k - 1, :, :256] = projections.astype(bf16)
            v.ga_out[k - 1, :, 256:] = output.astype(bf16)
            rows_copy(k).start()

    for j in range(PARTS):
        d_scatter.drain(j)
    gn_one = jnp.zeros((1, D), f32)
    order = (1, 3, 2, 0)
    for n, k in enumerate(order):
        chip = lax.rem(z + k, LINE)
        slots = piece(chip, 2)
        dh = dot(v.dqkv[piece(chip, 2 * rows)], weights, NT)
        values = v.x_all[slots].reshape(2 * rows, D).astype(f32)
        gn_one = gn_one + jnp.sum(dh * values * rms_rows(values), axis=0, keepdims=True)
        v.d[slots] = dh.astype(bf16).reshape(2, rows, D)
        h_scatter.start_one(0, k)
        if n > 0:
            h_scatter.fold_one(0, order[n - 1])
    h_scatter.fold_one(0, order[-1])
    both_gains = jnp.concatenate([gn_one, v.gn_two[:1]], axis=0)
    v.gn_in[i] = jnp.concatenate([both_gains[:, t : t + 128] for t in range(0, D, 128)], axis=0)
    for k in range(1, PLANE):
        go(v.gn_in.at[i], v.gn_in.at[i], v.gn_sems[0].at[k], v.gn_sems[1].at[i], (along(k), e))
    v.block[...] = (v.r_own[...] + y_scatter.total(0)).astype(bf16)
    h_scatter.fold_late(0)

    for k in (2, 1, 3):
        rows_copy(k).wait_recv()
        v.gs[...] += v.ga_in[k - 1].reshape(v.gs.shape).astype(f32)
    squares = jnp.sum(v.gs[...] * v.gs[...])
    v.gs_out[...] = v.gs[...].astype(bf16)
    v.ga_all[e] = v.gs_out[e]
    for l in range(local):
        ge_plane.rest(l)
        for first in range(0, deep, 64):
            span = slice(first, first + 64)
            summed = v.ge[l, span]
            for chunk in (1, 2):
                summed = summed + v.ge_in[l, chunk, span].astype(f32)
            v.ge[l, span] = summed
            squares = squares + jnp.sum(summed * summed)
        results[l].start()

    for k in range(1, PLANE):
        slot = v.gn_in.at[along(k)]
        remote(slot, slot, v.gn_sems[0].at[k], v.gn_sems[1].at[along(k)], sibling).wait_recv()
    gains = v.gn_in[0] + v.gn_in[1] + v.gn_in[2] + v.gn_in[3]
    v.mix_in[e] = jnp.concatenate([gains, jnp.full((8, 128), squares)], axis=0)
    for k in range(1, SPAN):
        go(v.mix_in.at[e], v.mix_in.at[e], v.mix_sems[0].at[k], v.mix_sems[1].at[e], (i, across(k)))
    for k in range(1, SPAN):
        go(v.gs_out.at[across(k)], v.ga_all.at[e], v.gs_sems[0].at[k], v.gs_sems[1].at[e], (i, across(k)))
    for k in range(1, SPAN):
        slot = v.mix_in.at[across(k)]
        remote(slot, slot, v.mix_sems[0].at[k], v.mix_sems[1].at[across(k)], sibling).wait_recv()
    mixed = v.mix_in[0]
    for s in range(1, SPAN):
        mixed = mixed + v.mix_in[s]
    v.sq_in[i] = mixed[16:]
    for k in range(1, PLANE):
        go(v.sq_in.at[i], v.sq_in.at[i], v.sq_sems[0].at[k], v.sq_sems[1].at[i], (along(k), e))
    gain_squares = jnp.sum(mixed[:16] * mixed[:16])
    row = lax.broadcasted_iota(jnp.int32, (16, 128), 0)
    pick = lambda n: jnp.sum(jnp.where(row == index // few * 2 + n, mixed[:16], 0.0), axis=0, keepdims=True)
    own_gains = jnp.concatenate([pick(0), pick(1), jnp.zeros((6, 128), f32)], axis=0)
    v.gn[...] = pltpu.roll(own_gains, rows - lax.rem(index, few) * (rows // few), 1)
    for k in range(1, SPAN):
        slot = v.ga_all.at[across(k)]
        remote(slot, slot, v.gs_sems[0].at[k], v.gs_sems[1].at[across(k)], sibling).wait_recv()
    for g in range(SPAN):
        v.ga[:, g * 128 : (g + 1) * 128] = v.ga_all[g, :, :128].astype(f32)
        v.ga[:, QKV + g * 128 : QKV + (g + 1) * 128] = v.ga_all[g, :, 256:].astype(f32)
    for g in range(0, SPAN, 2):
        for first, own in ((QD, 128), (QD + KVD, 192)):
            heads = [v.ga_all[g + n, :, own : own + HD] for n in range(2)]
            v.ga[:, first + g * HD : first + (g + 2) * HD] = jnp.concatenate(heads, axis=1).astype(f32)
    for k in range(1, PLANE):
        slot = v.sq_in.at[along(k)]
        remote(slot, slot, v.sq_sems[0].at[k], v.sq_sems[1].at[along(k)], sibling).wait_recv()
    norm = jnp.sqrt(v.sq_in[0] + v.sq_in[1] + v.sq_in[2] + v.sq_in[3] + gain_squares)[:1, :1]
    v.norm[...] = norm
    v.clip[...] = jnp.minimum(1.0, CLIP_NORM / (norm + 1e-06))

    back, _ = norm_back(v.x_all[e].astype(f32), gain_one, h_scatter.total(0))
    v.grad[...] = v.dr[...] + back
    for copy in results:
        copy.wait()
    for copy in live:
        copy.wait_send()
    for k in (2, 1, 3):
        rows_copy(k).wait_send()
    for l in range(local):
        ge_plane.drain(l)
    for item in (x_line, wo_line, y_scatter, h_scatter):
        item.drain(0)
    for j in range(PARTS):
        up_line.drain(j)
        da_line.drain(j)


def call_layer(*args):
    vmem, anywhere = pl.BlockSpec(memory_space=pltpu.VMEM), pl.BlockSpec(memory_space=pl.ANY)
    rows, local = args[0].shape[0], args[3].shape[0]
    outs = layer_outputs(rows, local)
    return pl.pallas_call(
        layer_kernel,
        out_shape=outs,
        in_specs=[anywhere if n == 3 else vmem for n in range(len(args))],
        out_specs=[anywhere if n == 3 else vmem for n in range(len(outs))],
        scratch_shapes=layer_scratch(rows, local),
        compiler_params=pltpu.CompilerParams(
            collective_id=0, has_side_effects=True, vmem_limit_bytes=64 * 2**20 - 2**18
        ),
        name="layer",
    )(*args)


def fast_body(
    activations,
    doc_ids,
    routes,
    gate_weights,
    cotangent,
    step_count,
    w_attn,
    norm_gains,
    w_expert,
    first_attn,
    second_attn,
    first_gains,
    second_gains,
    first_expert,
    second_expert,
):
    cosine, sine = head_tables(activations.shape[1] * lax.axis_size("expert"))
    block, input_total, norm, grad_expert, grad_attn, gn, clip = call_layer(
        activations[0], cotangent[0], w_attn, w_expert, routes[0].T, gate_weights[0].T, doc_ids, norm_gains.T,
        cosine, sine,
    )
    grad_norm = norm.reshape(())
    steps = step_count.astype(jnp.float32)
    attn = adam_update(
        w_attn, first_attn, second_attn, grad_attn * clip, steps, WEIGHT_DECAY, LEARN_RATE
    )
    gain = adam_update(
        norm_gains.T, first_gains.T, second_gains.T, gn[:2, : norm_gains.shape[0]] * clip, steps, 0.0, GAIN_RATE
    )
    expert = adam_update(
        w_expert, first_expert, second_expert, grad_expert * clip[None], steps, WEIGHT_DECAY, LEARN_RATE
    )
    return (block[None], input_total[None], grad_norm, *attn, *[a.T for a in gain], *expert)


def solution(mesh):
    in_specs = (
        P("dp", "expert", None),
        P("dp", "expert"),
        P("dp", "expert", None),
        P("dp", "expert", None),
        P("dp", "expert", None),
        P(),
        P(("dp", "expert"), None),
        P(("dp", "expert"), None),
        P("expert", "dp", None),
        P(("dp", "expert"), None),
        P(("dp", "expert"), None),
        P(("dp", "expert"), None),
        P(("dp", "expert"), None),
        P("expert", "dp", None),
        P("expert", "dp", None),
    )
    out_specs = (
        P("dp", "expert", None),
        P("dp", "expert", None),
        P(),
        P(("dp", "expert"), None),
        P(("dp", "expert"), None),
        P(("dp", "expert"), None),
        P(("dp", "expert"), None),
        P(("dp", "expert"), None),
        P(("dp", "expert"), None),
        P("expert", "dp", None),
        P("expert", "dp", None),
        P("expert", "dp", None),
    )
    body = fast_body if fits(mesh) else general_body
    return jax.shard_map(body, mesh=mesh, in_specs=in_specs, out_specs=out_specs, check_vma=False)
```

```python
import jax
import jax.numpy as jnp
from jax import lax
from jax.sharding import PartitionSpec as P
import types

import numpy as np
from jax.experimental import pallas as pl
from jax.experimental.pallas import tpu as pltpu

D = 1024
H = 16
KVH = 8
HD = 64
FF = 512
TOP = 8
QD = 1024
KVD = 512
QKV = 2048


EPSILON = 1e-05
ROPE_BASE = 10000.0
CLIP_NORM = 1.0
BETA_ONE = 0.9
BETA_TWO = 0.95
ADAM_EPSILON = 1e-08
LEARN_RATE = 0.03
GAIN_RATE = 0.4
WEIGHT_DECAY = 0.1


def rms_scale(values, gain):
    return values * lax.rsqrt(jnp.mean(values * values, axis=-1, keepdims=True) + EPSILON) * gain


def rope_tables(positions, head_width):
    halves = jnp.arange(head_width // 2, dtype=jnp.float32)
    inverse = ROPE_BASE ** (-2.0 * halves / head_width)
    angles = positions.astype(jnp.float32)[:, None] * inverse[None, :]
    angles = jnp.concatenate([angles, angles], axis=-1)
    return (jnp.cos(angles)[:, None, :], jnp.sin(angles)[:, None, :])


def rotate(values, cosine, sine_table):
    middle = values.shape[-1] // 2
    turned = jnp.concatenate([-values[..., middle:], values[..., :middle]], axis=-1)
    return values * cosine + turned * sine_table


def unrotate(gradient, cosine, sine_table):
    middle = gradient.shape[-1] // 2
    product = gradient * sine_table
    turned = jnp.concatenate([product[..., middle:], -product[..., :middle]], axis=-1)
    return gradient * cosine + turned


def adam_update(weight, moment_one, second, gradient, steps_done, decay_rate, step_rate):
    first_new = BETA_ONE * moment_one + (1.0 - BETA_ONE) * gradient
    second_new = BETA_TWO * second + (1.0 - BETA_TWO) * gradient * gradient
    first_hat = first_new / (1.0 - BETA_ONE**steps_done)
    second_hat = second_new / (1.0 - BETA_TWO**steps_done)
    weight_new = weight - step_rate * (
        first_hat / (jnp.sqrt(second_hat) + ADAM_EPSILON) + decay_rate * weight
    )
    return (weight_new, first_new, second_new)


def attn_fetch(w_attn, norm_gains):
    return (
        lax.all_gather(w_attn.astype(jnp.bfloat16), ("dp", "expert"), axis=0, tiled=True),
        lax.all_gather(norm_gains.astype(jnp.bfloat16), ("dp", "expert"), axis=0, tiled=True),
    )


def expert_fetch(w_expert):
    return lax.all_gather(w_expert.astype(jnp.bfloat16), "dp", axis=1, tiled=True)


def to_owner(buffer):
    return lax.all_to_all(buffer, "expert", split_axis=0, concat_axis=1, tiled=True)


def to_sender(buffer):
    return lax.all_to_all(buffer, "expert", split_axis=1, concat_axis=0, tiled=True)


def expert_forward(received, expert_cols):
    gate_up = jnp.einsum(
        "esd,edf->esf", received, expert_cols[:, :, : 2 * FF], preferred_element_type=jnp.float32
    )
    activated = (jax.nn.silu(gate_up[..., :FF]) * gate_up[..., FF:]).astype(jnp.bfloat16)
    return (gate_up, activated)


def general_body(
    activations,
    doc_ids,
    routes,
    gate_weights,
    cotangent,
    step_count,
    w_attn,
    norm_gains,
    w_expert,
    first_attn,
    second_attn,
    first_gains,
    second_gains,
    first_expert,
    second_expert,
):
    row_count = activations.shape[1]
    span_size = lax.axis_size("expert")
    shard_pos = lax.axis_index("expert")
    seq_length = row_count * span_size
    expert_total = w_expert.shape[0] * span_size
    capacity = (row_count * TOP * 9 + expert_total * 8 - 1) // (expert_total * 8)
    group_size = H // KVH
    score_scale = HD ** (-0.5)
    hidden_in = activations[0].astype(jnp.float32)
    upstream = cotangent[0].astype(jnp.float32)
    attn_cols, gain_pair = attn_fetch(w_attn, norm_gains)
    expert_cols = expert_fetch(w_expert)
    gain_one = gain_pair[:, 0].astype(jnp.float32)
    gain_two = gain_pair[:, 1].astype(jnp.float32)
    w_project = attn_cols[:, :QKV]
    w_output = attn_cols[:, QKV:]
    normed = rms_scale(hidden_in, gain_one).astype(jnp.bfloat16)
    projected = jnp.dot(normed, w_project, preferred_element_type=jnp.float32)
    positions = shard_pos * row_count + jnp.arange(row_count, dtype=jnp.int32)
    cosine, sine_table = rope_tables(positions, HD)
    queries = rotate(projected[:, :QD].reshape(row_count, H, HD), cosine, sine_table).astype(
        jnp.bfloat16
    )
    key_heads = rotate(
        projected[:, QD : QD + KVD].reshape(row_count, KVH, HD), cosine, sine_table
    ).astype(jnp.bfloat16)
    value_heads = projected[:, QD + KVD :].astype(jnp.bfloat16)
    key_all, value_all, doc_all = (
        lax.all_gather(key_heads.reshape(row_count, KVD), "expert", axis=0, tiled=True),
        lax.all_gather(value_heads, "expert", axis=0, tiled=True),
        lax.all_gather(doc_ids[0].astype(jnp.bfloat16), "expert", axis=0, tiled=True),
    )
    key_docs = doc_all.astype(jnp.int32)
    query_docs = doc_ids[0]
    query_groups = queries.reshape(row_count, KVH, group_size, HD)
    key_block = min(512, seq_length)
    needed = (shard_pos * row_count + row_count + key_block - 1) // key_block

    def block_scores(block_id):
        first_key = block_id * key_block
        key_part = lax.dynamic_slice_in_dim(key_all, first_key, key_block, 0).reshape(
            key_block, KVH, HD
        )
        raw_scores = (
            jnp.einsum("tgrd,kgd->grtk", query_groups, key_part, preferred_element_type=jnp.float32)
            * score_scale
        )
        key_pos = first_key + jnp.arange(key_block, dtype=jnp.int32)
        key_doc = lax.dynamic_slice_in_dim(key_docs, first_key, key_block, 0)
        visible = (key_pos[None, :] <= positions[:, None]) & (
            key_doc[None, :] == query_docs[:, None]
        )
        return (raw_scores, visible, key_part)

    def value_part(block_id):
        return lax.dynamic_slice_in_dim(value_all, block_id * key_block, key_block, 0).reshape(
            key_block, KVH, HD
        )

    def total_step(block_id, running):
        row_peak, row_total = running
        raw_scores, visible, _ = block_scores(block_id)
        masked = jnp.where(visible, raw_scores, -1e30)
        new_peak = jnp.maximum(row_peak, jnp.max(masked, axis=-1))
        scaled = jnp.where(visible, jnp.exp(masked - new_peak[..., None]), 0.0)
        return (new_peak, row_total * jnp.exp(row_peak - new_peak) + jnp.sum(scaled, axis=-1))

    start_peak = jnp.full((KVH, group_size, row_count), -1e30, jnp.float32)
    start_total = jnp.zeros((KVH, group_size, row_count), jnp.float32)
    row_peak, row_total = lax.fori_loop(0, needed, total_step, (start_peak, start_total))
    log_total = row_peak + jnp.log(row_total)

    def exact_probs(raw_scores, visible):
        return jnp.exp(jnp.where(visible, raw_scores - log_total[..., None], -1e30))

    def output_step(block_id, summed):
        raw_scores, visible, _ = block_scores(block_id)
        weights_low = exact_probs(raw_scores, visible).astype(jnp.bfloat16)
        return summed + jnp.einsum(
            "grtk,kgd->tgrd", weights_low, value_part(block_id), preferred_element_type=jnp.float32
        )

    attended = lax.fori_loop(
        0, needed, output_step, jnp.zeros((row_count, KVH, group_size, HD), jnp.float32)
    )
    attended = attended.reshape(row_count, QD).astype(jnp.bfloat16)
    branch = jnp.einsum("tc,dc->td", attended, w_output, preferred_element_type=jnp.float32)
    residual = hidden_in + branch
    normed_two = rms_scale(residual, gain_two).astype(jnp.bfloat16)
    flat_routes = routes[0].reshape(-1)
    one_hot = (flat_routes[:, None] == jnp.arange(expert_total, dtype=jnp.int32)[None, :]).astype(
        jnp.int32
    )
    ranking = jnp.sum((jnp.cumsum(one_hot, axis=0) - 1) * one_hot, axis=1)
    places = flat_routes * capacity + ranking
    owners = jnp.arange(row_count * TOP, dtype=jnp.int32) // TOP
    source = jnp.zeros((expert_total * capacity,), jnp.int32).at[places].set(owners)
    filled = jnp.zeros((expert_total * capacity,), jnp.int32).at[places].set(1) > 0
    slot_gate = (
        jnp.zeros((expert_total * capacity,), jnp.float32)
        .at[places]
        .set(gate_weights[0].reshape(-1))
    )
    outgoing = jnp.where(filled[:, None], normed_two[source], jnp.zeros((), jnp.bfloat16)).reshape(
        expert_total, capacity, D
    )
    received = to_owner(outgoing)
    gate_up, activated = expert_forward(received, expert_cols)
    expert_out = jnp.einsum(
        "esf,edf->esd", activated, expert_cols[:, :, 2 * FF :], preferred_element_type=jnp.float32
    ).astype(jnp.bfloat16)
    returned = to_sender(expert_out).reshape(expert_total * capacity, D)
    picked = returned[places].reshape(row_count, TOP, D).astype(jnp.float32)
    combined = jnp.sum(gate_weights[0][..., None] * picked, axis=1)
    block_result = (residual + combined).astype(jnp.bfloat16)
    slot_grad = jnp.where(filled[:, None], slot_gate[:, None] * upstream[source], 0.0)
    slot_grad = slot_grad.astype(jnp.bfloat16).reshape(expert_total, capacity, D)
    owner_grad = to_owner(slot_grad)
    attn_cols, gain_pair = attn_fetch(w_attn, norm_gains)
    w_project = attn_cols[:, :QKV]
    w_output = attn_cols[:, QKV:]
    expert_cols = expert_fetch(w_expert)
    gate_up, activated = expert_forward(received, expert_cols)
    gate_part = gate_up[..., :FF]
    up_part = gate_up[..., FF:]
    sigmoid_gate = jax.nn.sigmoid(gate_part)
    act_grad = jnp.einsum(
        "esd,edf->esf", owner_grad, expert_cols[:, :, 2 * FF :], preferred_element_type=jnp.float32
    )
    gate_grad = act_grad * up_part * sigmoid_gate * (1.0 + gate_part * (1.0 - sigmoid_gate))
    lift_grad = act_grad * gate_part * sigmoid_gate
    mixed_grad = jnp.concatenate([gate_grad, lift_grad], axis=-1).astype(jnp.bfloat16)
    down_grad = jnp.einsum(
        "esf,esd->edf", activated, owner_grad, preferred_element_type=jnp.float32
    )
    inward_grad = jnp.einsum(
        "esd,esf->edf", received, mixed_grad, preferred_element_type=jnp.float32
    )
    row_grads = jnp.einsum(
        "esf,edf->esd", mixed_grad, expert_cols[:, :, : 2 * FF], preferred_element_type=jnp.float32
    ).astype(jnp.bfloat16)
    back_rows = to_sender(row_grads).reshape(expert_total * capacity, D)
    normed_two_grad = jnp.sum(
        back_rows[places].reshape(row_count, TOP, D).astype(jnp.float32), axis=1
    )
    _, second_pull = jax.vjp(rms_scale, residual, gain_two)
    resid_grad, gain_two_grad = second_pull(normed_two_grad)
    resid_grad = upstream + resid_grad
    branch_grad = resid_grad.astype(jnp.bfloat16)
    output_grad = jnp.einsum("td,tc->dc", branch_grad, attended, preferred_element_type=jnp.float32)
    attended_grad = jnp.dot(branch_grad, w_output, preferred_element_type=jnp.float32).astype(
        jnp.bfloat16
    )
    grad_groups = attended_grad.reshape(row_count, KVH, group_size, HD)

    def delta_step(block_id, summed):
        raw_scores, visible, _ = block_scores(block_id)
        probs_full = exact_probs(raw_scores, visible)
        prob_grad = jnp.einsum(
            "tgrd,kgd->grtk", grad_groups, value_part(block_id), preferred_element_type=jnp.float32
        )
        return summed + jnp.sum(probs_full * prob_grad, axis=-1)

    delta_rows = lax.fori_loop(
        0, needed, delta_step, jnp.zeros((KVH, group_size, row_count), jnp.float32)
    )

    def grad_step(block_id, running):
        query_grad, key_grad, value_grad = running
        raw_scores, visible, key_part = block_scores(block_id)
        probs_full = exact_probs(raw_scores, visible)
        prob_grad = jnp.einsum(
            "tgrd,kgd->grtk", grad_groups, value_part(block_id), preferred_element_type=jnp.float32
        )
        score_grad = (probs_full * (prob_grad - delta_rows[..., None])).astype(jnp.bfloat16)
        query_grad = (
            query_grad
            + jnp.einsum("grtk,kgd->tgrd", score_grad, key_part, preferred_element_type=jnp.float32)
            * score_scale
        )
        key_piece = (
            jnp.einsum(
                "grtk,tgrd->kgd", score_grad, query_groups, preferred_element_type=jnp.float32
            )
            * score_scale
        )
        value_piece = jnp.einsum(
            "grtk,tgrd->kgd",
            probs_full.astype(jnp.bfloat16),
            grad_groups,
            preferred_element_type=jnp.float32,
        )
        first_key = block_id * key_block
        key_grad = lax.dynamic_update_slice_in_dim(
            key_grad, key_piece.reshape(key_block, KVD), first_key, 0
        )
        value_grad = lax.dynamic_update_slice_in_dim(
            value_grad, value_piece.reshape(key_block, KVD), first_key, 0
        )
        return (query_grad, key_grad, value_grad)

    start_grads = (
        jnp.zeros((row_count, KVH, group_size, HD), jnp.float32),
        jnp.zeros((seq_length, KVD), jnp.float32),
        jnp.zeros((seq_length, KVD), jnp.float32),
    )
    query_grad, key_grad, value_grad = lax.fori_loop(0, needed, grad_step, start_grads)
    key_sum, value_sum = (
        lax.psum_scatter(key_grad, "expert", scatter_dimension=0, tiled=True),
        lax.psum_scatter(value_grad, "expert", scatter_dimension=0, tiled=True),
    )
    query_back = unrotate(query_grad.reshape(row_count, H, HD), cosine, sine_table).reshape(
        row_count, QD
    )
    key_back = unrotate(key_sum.reshape(row_count, KVH, HD), cosine, sine_table).reshape(
        row_count, KVD
    )
    project_grad = jnp.concatenate([query_back, key_back, value_sum], axis=1).astype(jnp.bfloat16)
    weight_grad_qkv = jnp.einsum(
        "td,tc->dc", normed, project_grad, preferred_element_type=jnp.float32
    )
    normed_grad = jnp.einsum(
        "tc,dc->td", project_grad, w_project, preferred_element_type=jnp.float32
    )
    _, first_pull = jax.vjp(rms_scale, hidden_in, gain_one)
    input_part, gain_one_grad = first_pull(normed_grad)
    input_total = resid_grad + input_part
    attn_partial = jnp.concatenate([weight_grad_qkv, output_grad], axis=1)
    gain_partial = jnp.stack([gain_one_grad, gain_two_grad], axis=1)
    grad_attn, grad_gains = (
        lax.psum_scatter(attn_partial, ("dp", "expert"), scatter_dimension=0, tiled=True),
        lax.psum_scatter(gain_partial, ("dp", "expert"), scatter_dimension=0, tiled=True),
    )
    grad_expert = lax.psum_scatter(
        jnp.concatenate([inward_grad, down_grad], axis=2).astype(jnp.bfloat16),
        "dp",
        scatter_dimension=1,
        tiled=True,
    ).astype(jnp.float32)
    local_squares = (
        jnp.sum(grad_attn * grad_attn)
        + jnp.sum(grad_gains * grad_gains)
        + jnp.sum(grad_expert * grad_expert)
    )
    grad_norm = jnp.sqrt(lax.psum(local_squares, ("dp", "expert")))
    clip_factor = jnp.minimum(1.0, CLIP_NORM / (grad_norm + 1e-06))
    steps_done = step_count.astype(jnp.float32)
    attn_new = adam_update(
        w_attn,
        first_attn,
        second_attn,
        grad_attn * clip_factor,
        steps_done,
        WEIGHT_DECAY,
        LEARN_RATE,
    )
    gains_new = adam_update(
        norm_gains, first_gains, second_gains, grad_gains * clip_factor, steps_done, 0.0, GAIN_RATE
    )
    expert_new = adam_update(
        w_expert,
        first_expert,
        second_expert,
        grad_expert * clip_factor,
        steps_done,
        WEIGHT_DECAY,
        LEARN_RATE,
    )
    return (
        block_result[None],
        input_total[None],
        grad_norm,
        attn_new[0],
        attn_new[1],
        attn_new[2],
        gains_new[0],
        gains_new[1],
        gains_new[2],
        expert_new[0],
        expert_new[1],
        expert_new[2],
    )


def fits(mesh):
    return dict(mesh.shape) == {"dp": 4, "expert": KVH}


def head_tables(length):
    halves = np.arange(HD // 2, dtype=np.float32)
    inverse = np.power(np.float32(ROPE_BASE), np.float32(-2.0) * halves / np.float32(HD))
    angles = np.arange(length, dtype=np.float32)[:, None] * inverse[None, :]
    cosine, sine = np.cos(angles), np.sin(angles)
    cosine = np.concatenate([cosine] * 4, axis=1)
    return jnp.asarray(cosine), jnp.asarray(np.concatenate([-sine, sine] * 2, axis=1))


LINE, SPAN, PLANE, PARTS = 4, 8, 4, 4
QUERY_BLOCK = 256
NN, NT, TN = ((1,), (0,)), ((1,), (1,)), ((0,), (0,))


def remote(source, target, sent, landed, device):
    return pltpu.make_async_remote_copy(
        src_ref=source,
        dst_ref=target,
        send_sem=sent,
        recv_sem=landed,
        device_id=device,
        device_id_type=pl.DeviceIdType.MESH,
    )


def whereabouts():
    i, e = lax.axis_index("dp"), lax.axis_index("expert")
    return i, e, e // 2, lax.rem(e, 2)


def partners(i, e):
    others = [(i, lax.rem(e + k, SPAN)) for k in range(1, SPAN)]
    return others + [(lax.rem(i + k, PLANE), e) for k in range(1, PLANE)]


def piece(j, size):
    return pl.ds(pl.multiple_of(j * size, size), size)


class LineGather:
    def __init__(self, slot, source, where, sems):
        self.slot, self.source, self.where = slot, source, where
        self.sent, self.passed, self.landed = sems

    def _own(self, j, k):
        i, e, z, c = self.where
        there = z * 2 + 1 - c if k == 0 else lax.rem(z + k, LINE) * 2 + c
        return remote(self.source(j), self.slot(e, j), self.sent.at[j, k], self.landed.at[j, e], (i, there))

    def _pass(self, j, k):
        i, e, z, c = self.where
        index = lax.rem(z + k, LINE) * 2 + c
        place = self.slot(index, j)
        return remote(place, place, self.passed.at[j, k], self.landed.at[j, index], (i, z * 2 + 1 - c))

    def _relay(self, j):
        i, e, z, c = self.where
        index = lax.rem(z + 2, LINE) * 2 + c
        place = self.slot(index, j)
        end = LINE - 1 - lax.rem(z + 2, LINE)
        return remote(place, place, self.passed.at[j, 0], self.landed.at[j, index], (i, end * 2 + c))

    def _each_own(self, j, act):
        z = self.where[2]
        act(self._own(j, 2))
        pl.when(z != LINE - 1)(lambda: act(self._own(j, 1)))
        pl.when(z != 0)(lambda: act(self._own(j, 3)))
        act(self._own(j, 0))

    def _when_inner(self, act):
        z = self.where[2]
        pl.when((z > 0) & (z < LINE - 1))(act)

    def start(self, j):
        self._each_own(j, lambda copy: copy.start())

    def wait(self, j, index):
        i, e, z, c = self.where
        place = self.slot(index, j)
        remote(place, place, self.sent.at[j, 0], self.landed.at[j, index], (i, z * 2 + 1 - c)).wait_recv()

    def sibling(self):
        _, e, z, c = self.where
        return z * 2 + 1 - c

    def near(self, k):
        _, e, z, c = self.where
        return lax.rem(z + k, LINE) * 2 + c

    def far(self, k):
        _, e, z, c = self.where
        return lax.rem(z + k, LINE) * 2 + 1 - c

    def forward(self, j, k):
        self.wait(j, self.near(k))
        if k == 2:
            self._when_inner(lambda: self._relay(j).start())
        self._pass(j, k).start()

    def forward_all(self, j):
        for k in (2, 1, 3):
            self.forward(j, k)

    def rest(self, j):
        self.wait(j, self.sibling())
        for k in range(1, LINE):
            self.wait(j, self.far(k))

    def drain(self, j):
        self._each_own(j, lambda copy: copy.wait_send())
        self._when_inner(lambda: self._relay(j).wait_send())
        for k in range(1, LINE):
            self._pass(j, k).wait_send()


class LineScatter:
    def __init__(self, data, where, pair, out, inbox, own, sems, size):
        self.data, self.where, self.size = data, where, size
        self.pair, self.out, self.inbox, self.own = pair, out, inbox, own
        self.pair_sent, self.pair_landed, self.sent, self.landed = sems

    def _pair(self, j, k):
        i, e, z, c = self.where
        there, rows = lax.rem(z + k, LINE), piece(j, self.size)
        return remote(
            self.data.at[there * 2 + 1 - c, rows], self.pair.at[there, rows],
            self.pair_sent.at[j, there], self.pair_landed.at[j, there], (i, z * 2 + 1 - c),
        )

    def _send(self, j, k):
        i, e, z, c = self.where
        there, rows = lax.rem(z + k, LINE), piece(j, self.size)
        crossing = {1: z // (LINE - 1), 2: 0, 3: (LINE - 1 - z) // (LINE - 1)}[k]
        chip = {1: z + 1 - 2 * crossing, 2: there, 3: z - 1 + 2 * crossing}[k]
        slot = z + crossing * (chip - z)
        return remote(
            self.out.at[there, rows], self.inbox.at[slot, rows],
            self.sent.at[j, there], self.landed.at[j, slot], (i, chip * 2 + c),
        )

    def _landed(self, j, slot):
        i, e, z, c = self.where
        place = self.inbox.at[slot, piece(j, self.size)]
        remote(place, place, self.sent.at[j, slot], self.landed.at[j, slot], (i, z * 2 + 1 - c)).wait_recv()

    def _both(self, j, there):
        c, rows = self.where[3], piece(j, self.size)
        return self.data[there * 2 + c, rows].astype(jnp.float32) + self.pair[there, rows].astype(jnp.float32)

    def _across(self, j):
        there, rows = lax.rem(self.where[2] + 2, LINE), piece(j, self.size)
        return there, rows, self._both(j, there)

    def start(self, j):
        for k in (1, 3, 2, 0):
            self._pair(j, k).start()

    def start_one(self, j, k):
        self._pair(j, k).start()

    def fold_one(self, j, k):
        z, rows = self.where[2], piece(j, self.size)
        self._pair(j, k).wait_recv()

        def send():
            there = lax.rem(z + k, LINE)
            self.out[there, rows] = self._both(j, there).astype(jnp.bfloat16)
            self._send(j, k).start()

        if k == 0:
            self.own[rows] = self._both(j, z)
        elif k == 2:
            pl.when((z == 0) | (z == LINE - 1))(send)
        else:
            send()

    def fold(self, j):
        for k in (1, 3, 2, 0):
            self.fold_one(j, k)

    def fold_late(self, j):
        z = self.where[2]

        @pl.when((z > 0) & (z < LINE - 1))
        def _():
            there, rows, both = self._across(j)
            self._landed(j, z)
            self.out[there, rows] = (both + self.inbox[z, rows].astype(jnp.float32)).astype(jnp.bfloat16)
            self._send(j, 2).start()

    def total(self, j):
        z, rows = self.where[2], piece(j, self.size)

        def add(k):
            there = lax.rem(z + k, LINE)
            self._landed(j, there)
            self.own[rows] += self.inbox[there, rows].astype(jnp.float32)

        pl.when(z != LINE - 1)(lambda: add(1))
        pl.when(z != 0)(lambda: add(3))
        add(2)
        return self.own[rows]

    def drain(self, j):
        for k in range(LINE):
            self._pair(j, k).wait_send()
        for k in range(1, LINE):
            self._send(j, k).wait_send()


class PlaneGather:
    def __init__(self, where, slot, size, sems):
        i, self.e = where[0], where[1]
        self.i, self.slot, self.sems = i, slot, sems
        self.x = i // 2 * 2 + 1 - lax.rem(i, 2)
        self.y = (1 - i // 2) * 2 + lax.rem(i, 2)
        self.far = PLANE - 1 - i
        self.half = size // 2

    def _copy(self, l, n, source):
        rows = (slice(None), slice(None), slice(0, self.half), slice(self.half, None))[n]
        to = (self.x, self.y, self.y, self.x)[n]
        sent, landed = self.sems
        place = self.slot(l, source, rows)
        return remote(place, place, sent.at[l, n], landed.at[l, n], (to, self.e))

    def start(self, l):
        self._copy(l, 0, self.i).start()
        self._copy(l, 1, self.i).start()

    def forward(self, l):
        self._copy(l, 0, self.x).wait_recv()
        self._copy(l, 2, self.x).start()
        self._copy(l, 1, self.y).wait_recv()
        self._copy(l, 3, self.y).start()

    def rest(self, l):
        self._copy(l, 2, self.far).wait_recv()
        self._copy(l, 3, self.far).wait_recv()

    def drain(self, l):
        for n, source in enumerate((self.i, self.i, self.x, self.y)):
            self._copy(l, n, source).wait_send()


class PlaneScatter:
    def __init__(self, plane, out, inbox, sems):
        self.plane, self.out, self.inbox = plane, out, inbox
        self.sent, self.landed = sems
        self.half = plane.half

    def _copy(self, l, chunk, part, n):
        first = slice(0, self.half) if part == 0 else slice(self.half, None)
        to_x = chunk == 1 or (chunk == 0 and part == 0)
        return remote(
            self.out.at[l, chunk, first], self.inbox.at[l, chunk, first], self.sent.at[l, n], self.landed.at[l, n],
            (self.plane.x if to_x else self.plane.y, self.plane.e),
        )

    def _at(self, l, chunk, part):
        return self._copy(l, chunk, part, chunk * 2 + part)

    def start(self, l, chunk):
        for part in ((0, 1), (0,), (1,))[chunk]:
            self._at(l, chunk, part).start()

    def combine(self, l):
        for chunk, part in ((1, 1), (2, 0)):
            rows = slice(part * self.half, (part + 1) * self.half)
            self._at(l, 0, part).wait_recv()
            mine = self.out[l, chunk, rows].astype(jnp.float32) + self.inbox[l, 0, rows].astype(jnp.float32)
            self.out[l, chunk, rows] = mine.astype(jnp.bfloat16)
            self._at(l, chunk, part).start()

    def rest(self, l):
        for chunk in (1, 2):
            for part in (0, 1):
                self._at(l, chunk, part).wait_recv()

    def drain(self, l):
        for chunk in range(3):
            for part in (0, 1):
                self._at(l, chunk, part).wait_send()


def half_turn_tile(part):
    lane = lax.broadcasted_iota(jnp.int32, part.shape, 1)
    ahead = pltpu.roll(part, 128 - HD // 2, 1)
    behind = pltpu.roll(part, HD // 2, 1)
    return jnp.where(lax.rem(lane, HD) < HD // 2, ahead, behind)


def rms_rows(values):
    return lax.rsqrt(jnp.mean(values * values, axis=-1, keepdims=True) + EPSILON)


def norm_back(values, gain, upper):
    scale = rms_rows(values)
    scaled = upper * gain
    inner = jnp.mean(values * scaled, axis=-1, keepdims=True)
    return scale * scaled - values * (scale * scale * scale) * inner, upper * values * scale


def dot(a, b, contract):
    return lax.dot_general(a, b, (contract, ((), ())), preferred_element_type=jnp.float32)


def visible_keys(first, low, high, docs_row, docs_col):
    shape = (QUERY_BLOCK, high - low)
    key = lax.broadcasted_iota(jnp.int32, shape, 1) + low
    query = lax.broadcasted_iota(jnp.int32, shape, 0) + first
    return (key <= query) & (docs_row[:, low:high] == docs_col)


def layer_kernel(x, up, wa, we, routes, gates, doc_ids, shard_gains, cos, sin, block, grad, norm, ge_far, ga, gn, clip, **held):
    layer_body(
        types.SimpleNamespace(
            x=x, up=up, wa=wa, we=we, routes=routes, gates=gates, doc_ids=doc_ids, shard_gains=shard_gains,
            cos=cos, sin=sin,
            block=block, grad=grad, norm=norm, ge_far=ge_far, ga=ga, gn=gn, clip=clip, **held,
        )
    )


def layer_outputs(rows, local):
    f32 = jnp.float32
    shaped = jax.ShapeDtypeStruct
    deep = D // PLANE
    return [
        shaped((rows, D), jnp.bfloat16), shaped((rows, D), f32), shaped((1, 1), f32),
        shaped((local, deep, 3 * FF), f32), shaped((deep // SPAN, 3072), f32), shaped((8, rows), f32),
        shaped((1, 1), f32),
    ]


def layer_scratch(rows, local):
    f32, bf16 = jnp.float32, jnp.bfloat16
    held, sems = pltpu.VMEM, lambda *shape: pltpu.SemaphoreType.DMA(shape)
    deep = D // PLANE
    part = deep // SPAN
    blocks = held((SPAN, rows, D), bf16)
    quarter = held((LINE, rows, D), bf16)
    line = lambda parts: (sems(parts, LINE), sems(parts, LINE), sems(parts, SPAN))
    scatter = lambda parts: tuple(sems(parts, LINE) for _ in range(4))
    both = lambda *shape: (sems(*shape), sems(*shape))
    return dict(
        x_all=blocks, up_all=blocks, h1=blocks, o_all=blocks, h2=blocks, d=blocks, da_all=blocks,
        qkv=held((SPAN * rows, 256), bf16), lse=held((SPAN * rows, 128), f32),
        wq_out=held((SPAN, part, 256), bf16), w_mine=held((PLANE, SPAN, part, 256), bf16),
        wo_all=held((PLANE, LINE, 2, part, D), bf16), we_all=held((local, PLANE, deep, 3 * FF), bf16),
        o_own=held((SPAN, rows, 128), bf16),
        r_own=held((rows, D), f32),
        pack=held((SPAN, 8, rows), f32), pack_all=held((SPAN, 8, rows), f32), gain_sum=held((PLANE, 2, 8, 128), f32),
        cols=held((SPAN, rows, 128), f32), docs=held((8, SPAN * rows), f32), gains=held((8, D), f32),
        act=held((local, SPAN, rows, FF), bf16), dgu=held((local, SPAN, rows, 2 * FF), bf16),
        pair=quarter, out=quarter, inbox=quarter, own=held((rows, D), f32),
        y_pair=quarter, y_out=quarter, y_inbox=quarter, y_own=held((rows, D), f32),
        ge_in=held((local, PLANE - 1, deep, 3 * FF), bf16),
        do=held((SPAN, rows, 128), bf16), dkv=held((SPAN * rows, 128), f32), dqkv=held((SPAN * rows, 256), bf16),
        dr=held((rows, D), f32), gn_two=held((8, D), f32),
        ga_out=held((PLANE - 1, deep, 384), bf16), ga_in=held((PLANE - 1, deep, 384), bf16),
        gs=held((SPAN, part, 384), f32), gs_out=held((SPAN, part, 384), bf16), ga_all=held((SPAN, part, 384), bf16),
        gn_in=held((PLANE, 16, 128), f32), mix_in=held((SPAN, 24, 128), f32), sq_in=held((PLANE, 8, 128), f32),
        ge=held((local, deep, 3 * FF), f32), store=sems(local),
        x_sems=line(1), up_sems=line(PARTS), wo_sems=line(1), o_sems=line(PARTS), da_sems=line(PARTS),
        d_sems=scatter(PARTS), y_sems=scatter(1), h_sems=scatter(1),
        load=sems(local), pack_sems=both(SPAN), wq_sems=both(SPAN), wqd_sems=both(PLANE), gd_sems=both(PLANE),
        wod_sems=both(1, 4), wop_sems=both(PLANE), we_sems=both(local, 4), ge_sems=both(local, 6),
        ga_sems=both(PLANE), gn_sems=both(PLANE), gs_sems=both(SPAN), mix_sems=both(SPAN), sq_sems=both(PLANE),
    )


def layer_body(v):
    f32, bf16 = jnp.float32, jnp.bfloat16
    where = i, e, z, c = whereabouts()
    sibling = (i, z * 2 + 1 - c)
    rows, local, deep = v.x.shape[0], v.we_all.shape[0], v.ge.shape[1]
    length, size = rows * SPAN, rows // PARTS
    own_cols = piece(e, 128)
    live = []

    def go(*spec):
        copy = remote(*spec)
        copy.start()
        live.append(copy)

    def along(k):
        return lax.rem(i + k, PLANE)

    def across(k):
        return lax.rem(e + k, SPAN)

    def line(sems, slot, source):
        return LineGather(slot, source, where, sems)

    x_line = line(v.x_sems, lambda s, j: v.x_all.at[s], lambda j: v.x)
    up_line = line(v.up_sems, lambda s, j: v.up_all.at[s, piece(j, size)], lambda j: v.up.at[piece(j, size)])
    wo_line = line(
        v.wo_sems, lambda s, j: v.wo_all.at[i, s // 2, lax.rem(s, 2)], lambda j: v.wo_all.at[i, z, c]
    )
    o_line = line(
        v.o_sems,
        lambda s, j: v.o_all.at[:, piece(j, size), piece(s, 128)],
        lambda j: v.o_own.at[:, piece(j, size)],
    )
    da_line = line(
        v.da_sems, lambda s, j: v.da_all.at[s, piece(j, size)], lambda j: v.da_all.at[e, piece(j, size)]
    )
    we_plane = PlaneGather(where, lambda l, s, part: v.we_all.at[l, s, part], deep, v.we_sems)
    wo_plane = PlaneGather(where, lambda l, s, part: v.wo_all.at[s, part, c], LINE, v.wod_sems)
    ge_plane = PlaneScatter(we_plane, v.we_all, v.ge_in, v.ge_sems)
    d_scatter = LineScatter(v.d, where, v.pair, v.out, v.inbox, v.own, v.d_sems, size)
    y_scatter = LineScatter(v.o_all, where, v.y_pair, v.y_out, v.y_inbox, v.y_own, v.y_sems, rows)
    h_scatter = LineScatter(v.d, where, v.pair, v.out, v.inbox, v.own, v.h_sems, rows)

    loads = [pltpu.make_async_copy(v.we.at[l], v.ge.at[l], v.load.at[l]) for l in range(local)]
    for copy in loads:
        copy.start()
    results = [pltpu.make_async_copy(v.ge.at[l], v.ge_far.at[l], v.store.at[l]) for l in range(local)]
    barrier = pltpu.get_barrier_semaphore()
    for device in partners(i, e):
        pl.semaphore_signal(barrier, inc=1, device_id=device, device_id_type=pl.DeviceIdType.MESH)
    lane = lax.broadcasted_iota(jnp.int32, (2, rows), 1)
    index, few = i * SPAN + e, rows // v.shard_gains.shape[1]
    spread = jnp.concatenate([v.shard_gains[...]] * few, axis=1)
    spread = jnp.where(lane // (rows // few) == lax.rem(index, few), spread, 0.0)
    shared = [v.doc_ids[...].astype(f32), spread, jnp.zeros((3, rows), f32)]
    for g in range(SPAN):
        named = [
            jnp.sum(jnp.where(v.routes[...] == g * local + l, v.gates[...], 0.0), axis=0, keepdims=True)
            for l in range(local)
        ]
        v.pack[g] = jnp.concatenate(named + shared, axis=0)
    for g in range(SPAN):
        v.wq_out[g, :, :128] = v.wa[:, g * 128 : (g + 1) * 128].astype(bf16)
        key_value = [v.wa[:, first + g * HD : first + (g + 1) * HD] for first in (QD, QD + KVD)]
        v.wq_out[g, :, 128:] = jnp.concatenate(key_value, axis=1).astype(bf16)
    v.w_mine[i, e] = v.wq_out[e]
    v.wo_all[i, z, c] = v.wa[:, QKV:].astype(bf16)
    v.pack_all[e] = v.pack[e]
    v.x_all[e] = v.x[...]
    v.up_all[e] = v.up[...]
    pl.semaphore_wait(barrier, SPAN + PLANE - 2)
    for k in range(1, SPAN):
        go(v.pack.at[across(k)], v.pack_all.at[e], v.pack_sems[0].at[k], v.pack_sems[1].at[e], (i, across(k)))
    for k in range(1, SPAN):
        go(v.wq_out.at[across(k)], v.w_mine.at[i, e], v.wq_sems[0].at[k], v.wq_sems[1].at[e], (i, across(k)))
    wo_line.start(0)
    x_line.start(0)
    loads[0].wait()
    v.we_all[0, i] = v.ge[0].astype(bf16)
    we_plane.start(0)

    for k in range(1, SPAN):
        slot = v.pack_all.at[across(k)]
        remote(slot, slot, v.pack_sems[0].at[k], v.pack_sems[1].at[across(k)], sibling).wait_recv()
    for half in range(2):
        summed = v.pack_all[4 * half]
        for s in range(1, 4):
            summed = summed + v.pack_all[4 * half + s]
        v.gain_sum[i, half] = summed
    for k in range(1, PLANE):
        go(v.gain_sum.at[i], v.gain_sum.at[i], v.gd_sems[0].at[k], v.gd_sems[1].at[i], (along(k), e))
    for k in range(1, SPAN):
        slot = v.w_mine.at[i, across(k)]
        remote(slot, slot, v.wq_sems[0].at[k], v.wq_sems[1].at[across(k)], sibling).wait_recv()
    for k in range(1, PLANE):
        go(v.w_mine.at[i], v.w_mine.at[i], v.wqd_sems[0].at[k], v.wqd_sems[1].at[i], (along(k), e))
    loads[1].wait()
    v.we_all[1, i] = v.ge[1].astype(bf16)
    for s in range(SPAN):
        block = v.pack_all[s]
        tall = jnp.concatenate([block, jnp.zeros((rows - block.shape[0], rows), f32)], axis=0)
        v.cols[s] = tall.T
        v.docs[:, s * rows : (s + 1) * rows] = block
    for k in range(1, PLANE):
        slot = v.gain_sum.at[along(k)]
        remote(slot, slot, v.gd_sems[0].at[k], v.gd_sems[1].at[along(k)], sibling).wait_recv()
    for tile in range(2 * PLANE):
        v.gains[:, tile * 128 : (tile + 1) * 128] = v.gain_sum[tile // 2, tile % 2].astype(bf16).astype(f32)
    gain_one, gain_two = v.gains[3:4], v.gains[4:5]

    def first_norm(s):
        values = v.x_all[s].astype(f32)
        v.h1[s] = (values * rms_rows(values) * gain_one).astype(bf16)

    wo_line.forward_all(0)
    wo_plane.start(0)
    first_norm(e)
    for k in (2, 1, 3):
        x_line.forward(0, k)
        first_norm(x_line.near(k))
    up_line.start(0)
    up_line.start(1)
    we_plane.forward(0)
    x_line.wait(0, x_line.sibling())
    first_norm(x_line.sibling())
    for k in range(1, LINE):
        x_line.wait(0, x_line.far(k))
        first_norm(x_line.far(k))
    for k in range(1, PLANE):
        slot = v.w_mine.at[along(k)]
        remote(slot, slot, v.wqd_sems[0].at[k], v.wqd_sems[1].at[along(k)], sibling).wait_recv()

    weights = v.w_mine[...].reshape(D, 256)
    lane = lax.broadcasted_iota(jnp.int32, (QUERY_BLOCK, 128), 1)

    def tables(first):
        cosine, sine = v.cos[first : first + QUERY_BLOCK], v.sin[first : first + QUERY_BLOCK]
        return cosine, sine, jnp.where(lane < HD, cosine, 1.0), jnp.where(lane < HD, sine, 0.0)

    for first in range(0, length, QUERY_BLOCK):
        span = slice(first, first + QUERY_BLOCK)
        slots = slice(first // rows, (first + QUERY_BLOCK) // rows)
        raw = dot(v.h1[slots].reshape(QUERY_BLOCK, D), weights, NN)
        q_cos, q_sin, kv_cos, kv_sin = tables(first)
        q_raw, kv_raw = raw[:, :128], raw[:, 128:]
        v.qkv[span, :128] = (q_raw * q_cos + half_turn_tile(q_raw) * q_sin).astype(bf16)
        v.qkv[span, 128:] = (kv_raw * kv_cos + half_turn_tile(kv_raw) * kv_sin).astype(bf16)


    def block_masks(first):
        low, high = max(0, first - length // 2), first + QUERY_BLOCK
        slots = slice(first // rows, (first + QUERY_BLOCK) // rows)
        docs_col = v.cols[slots, :, 2:3].reshape(QUERY_BLOCK, 1)
        return low, high, slots, visible_keys(first, low, high, v.docs[2:3], docs_col)

    for first in range(0, length, QUERY_BLOCK):
        low, high, slots, visible = block_masks(first)
        span = slice(first, first + QUERY_BLOCK)
        outs, logs = [], []
        for head in range(2):
            q = v.qkv[span, head * HD : (head + 1) * HD]
            scores = dot(q, v.qkv[low:high, 128:192], NT) * HD**-0.5
            scores = jnp.where(visible, scores, -1e30)
            peak = jnp.max(scores, axis=-1, keepdims=True)
            raw = jnp.exp(scores - peak)
            total = jnp.sum(raw, axis=-1, keepdims=True)
            probs = raw * (1.0 / total)
            logs.append(peak + jnp.log(total))
            outs.append(dot(probs.astype(bf16), v.qkv[low:high, 192:256], NN))
        both = jnp.concatenate(outs, axis=1).astype(bf16).reshape(-1, rows, 128)
        v.o_own[slots] = both
        v.o_all[slots, :, own_cols] = both
        v.lse[span] = jnp.where(lane == 0, logs[0], logs[1])
    o_line.start(0)
    o_line.start(1)
    up_line.start(2)
    o_line.start(2)
    up_line.start(3)
    o_line.start(3)
    wo_plane.forward(0)
    we_plane.start(1)

    wo_line.rest(0)
    wo_plane.rest(0)
    for k in range(1, PLANE):
        here = v.wo_all.at[along(k), :, c]
        go(here, here, v.wop_sems[0].at[k], v.wop_sems[1].at[along(k)], sibling)
    for k in range(1, PLANE):
        far = v.wo_all.at[along(k), :, 1 - c]
        remote(far, far, v.wop_sems[0].at[k], v.wop_sems[1].at[along(k)], sibling).wait_recv()

    def second_norm(j):
        part = piece(j, size)
        w_out = v.wo_all[...].reshape(D, D)
        branch = dot(v.o_all[:, part].reshape(-1, D), w_out, NT)
        values = v.x_all[:, part].reshape(-1, D).astype(f32) + branch
        split = values.reshape(SPAN, size, D)
        v.r_own[part] = sum(jnp.where(e == s, split[s], 0.0) for s in range(SPAN))
        v.h2[:, part] = (values * rms_rows(values) * gain_two).astype(bf16).reshape(SPAN, size, D)

    def gate_of(l, part):
        return v.cols[:, part, l : l + 1].reshape(-1, 1)

    def expert(l, j):
        part = piece(j, size)
        weights = v.we_all[l].reshape(D, 3 * FF)
        gate = gate_of(l, part)
        routed = gate > 0
        gu = dot(v.h2[:, part].reshape(-1, D), weights[:, : 2 * FF], NN)
        g, u = gu[:, :FF], gu[:, FF:]
        sig = 1.0 / (1.0 + jnp.exp(-g))
        act = jnp.where(routed, g * sig * u, 0.0).astype(bf16)
        v.act[l, :, part] = act.reshape(SPAN, size, FF)
        dy = (gate * v.up_all[:, part].reshape(-1, D).astype(f32)).astype(bf16)
        dact = dot(dy, weights[:, 2 * FF :], NN)
        dg = dact * u * sig * (1.0 + g * (1.0 - sig))
        du = dact * g * sig
        dgu = jnp.where(routed, jnp.concatenate([dg, du], axis=1), 0.0).astype(bf16)
        v.dgu[l, :, part] = dgu.reshape(SPAN, size, 2 * FF)
        d = dot(dgu, weights[:, : 2 * FF], NT).astype(bf16)
        y = dot(act, weights[:, 2 * FF :], NT).astype(bf16)
        if l == 0:
            v.d[:, part] = d.reshape(SPAN, size, D)
            v.o_all[:, part] = y.reshape(SPAN, size, D)
        else:
            d = v.d[:, part].reshape(-1, D).astype(f32) + d.astype(f32)
            v.d[:, part] = d.astype(bf16).reshape(SPAN, size, D)
            y = gate_of(0, part) * v.o_all[:, part].reshape(-1, D).astype(f32) + gate * y.astype(f32)
            v.o_all[:, part] = y.astype(bf16).reshape(SPAN, size, D)

    we_plane.rest(0)

    def first_round(j, carry):
        @pl.when(j == PARTS - 1)
        def _():
            we_plane.forward(1)

        @pl.when(j < PARTS)
        def _():
            o_line.forward_all(j)
            up_line.forward_all(j)

        @pl.when(j > 0)
        def _():
            o_line.drain(j - 1)
            expert(0, j - 1)

        @pl.when(j < PARTS)
        def _():
            o_line.rest(j)
            up_line.rest(j)
            second_norm(j)

        return carry

    lax.fori_loop(0, PARTS + 1, first_round, 0)
    we_plane.rest(1)

    def expert_chunk(l, there):
        span = piece(there, deep)
        inward = dot(v.h2[:, :, span].reshape(length, deep), v.dgu[l].reshape(length, 2 * FF), TN)
        gate = v.cols[:, :, l : l + 1].reshape(length, 1)
        dy = (gate * v.up_all[:, :, span].reshape(length, deep).astype(f32)).astype(bf16)
        return inward, dot(dy, v.act[l].reshape(length, FF), TN)

    def send_chunk(l, chunk):
        inward, down = expert_chunk(l, (we_plane.far, we_plane.x, we_plane.y)[chunk])
        v.we_all[l, chunk, :, : 2 * FF] = inward.astype(bf16)
        v.we_all[l, chunk, :, 2 * FF :] = down.astype(bf16)
        ge_plane.start(l, chunk)

    def second_round(j, carry):
        @pl.when(j < PARTS)
        def _():
            expert(1, j)
            d_scatter.start(j)

        @pl.when(j == 0)
        def _():
            we_plane.drain(0)

        for chunk in range(3):
            pl.when(j == chunk)(lambda chunk=chunk: send_chunk(0, chunk))

        @pl.when((j > 0) & (j <= PARTS))
        def _():
            d_scatter.fold(j - 1)

        @pl.when(j > 1)
        def _():
            d_scatter.fold_late(j - 2)

        return carry

    lax.fori_loop(0, PARTS + 2, second_round, 0)
    y_scatter.start(0)
    we_plane.drain(1)

    def keep_chunk(l):
        inward, down = expert_chunk(l, i)
        v.ge[l, :, : 2 * FF] = inward
        v.ge[l, :, 2 * FF :] = down

    v.gn_two[...] = jnp.zeros_like(v.gn_two)

    def second_back(j):
        part = piece(j, size)
        back, shares = norm_back(v.r_own[part], gain_two, d_scatter.total(j))
        dr = v.up_all[e, part].astype(f32) + back
        v.dr[part] = dr
        v.gn_two[:1] += jnp.sum(shares, axis=0, keepdims=True)
        v.da_all[e, part] = dr.astype(bf16)
        da_line.start(j)

    send_chunk(1, 0)
    second_back(0)
    ge_plane.combine(0)
    send_chunk(1, 1)
    second_back(1)
    send_chunk(1, 2)
    second_back(2)
    ge_plane.combine(1)
    second_back(3)
    da_line.forward_all(0)
    da_line.forward_all(1)
    keep_chunk(0)
    da_line.forward_all(2)
    keep_chunk(1)
    da_line.forward_all(3)
    y_scatter.fold(0)
    wo_mine = v.wo_all[:, :, :, :, own_cols].reshape(D, 128)
    for j in range(PARTS):
        da_line.rest(j)
        part = piece(j, size)
        do = dot(v.da_all[:, part].reshape(-1, D), wo_mine, NN).astype(bf16)
        v.do[:, part] = do.reshape(SPAN, size, 128)

    v.dkv[...] = jnp.zeros_like(v.dkv)
    for first in range(0, length, QUERY_BLOCK):
        low, high, slots, visible = block_masks(first)
        span = slice(first, first + QUERY_BLOCK)
        keys, values = v.qkv[low:high, 128:192], v.qkv[low:high, 192:256]
        do_both = v.do[slots].reshape(QUERY_BLOCK, 128)
        dqs, dk, dv = [], 0.0, 0.0
        for head in range(2):
            q = v.qkv[span, head * HD : (head + 1) * HD]
            do = do_both[:, head * HD : (head + 1) * HD]
            scores = dot(q, keys, NT) * HD**-0.5
            probs = jnp.exp(jnp.where(visible, scores - v.lse[span, head : head + 1], -1e30))
            dp = dot(do, values, NT)
            delta = jnp.sum(probs * dp, axis=-1, keepdims=True)
            ds = (probs * (dp - delta)).astype(bf16)
            dqs.append(dot(ds, keys, NN))
            dk = dk + dot(ds, q, TN)
            dv = dv + dot(probs.astype(bf16), do, TN)
        v.dkv[low:high] += jnp.concatenate([dk * HD**-0.5, dv], axis=1)
        dq = jnp.concatenate(dqs, axis=1) * HD**-0.5
        cosine, sine = v.cos[span], v.sin[span]
        v.dqkv[span, :128] = (dq * cosine - half_turn_tile(dq) * sine).astype(bf16)
    for first in range(0, length, QUERY_BLOCK):
        span = slice(first, first + QUERY_BLOCK)
        dkv = v.dkv[span]
        _, _, cosine, sine = tables(first)
        v.dqkv[span, 128:] = (dkv * cosine - half_turn_tile(dkv) * sine).astype(bf16)

    y_scatter.fold_late(0)

    o = v.o_own[...].reshape(length, 128)
    dqkv = v.dqkv[...]

    def rows_copy(k):
        return remote(v.ga_out.at[k - 1], v.ga_in.at[k - 1], v.ga_sems[0].at[k], v.ga_sems[1].at[k], (along(k), e))

    for k in (2, 1, 3, 0):
        span = piece(along(k), deep)
        projections = dot(v.h1[:, :, span].reshape(length, deep), dqkv, TN)
        output = dot(v.da_all[:, :, span].reshape(length, deep), o, TN)
        if k == 0:
            v.gs[:, :, :256] = projections.reshape(SPAN, -1, 256)
            v.gs[:, :, 256:] = output.reshape(SPAN, -1, 128)
        else:
            v.ga_out[k - 1, :, :256] = projections.astype(bf16)
            v.ga_out[k - 1, :, 256:] = output.astype(bf16)
            rows_copy(k).start()

    for j in range(PARTS):
        d_scatter.drain(j)
    gn_one = jnp.zeros((1, D), f32)
    order = (1, 3, 2, 0)
    for n, k in enumerate(order):
        chip = lax.rem(z + k, LINE)
        slots = piece(chip, 2)
        dh = dot(v.dqkv[piece(chip, 2 * rows)], weights, NT)
        values = v.x_all[slots].reshape(2 * rows, D).astype(f32)
        gn_one = gn_one + jnp.sum(dh * values * rms_rows(values), axis=0, keepdims=True)
        v.d[slots] = dh.astype(bf16).reshape(2, rows, D)
        h_scatter.start_one(0, k)
        if n > 0:
            h_scatter.fold_one(0, order[n - 1])
    h_scatter.fold_one(0, order[-1])
    both_gains = jnp.concatenate([gn_one, v.gn_two[:1]], axis=0)
    v.gn_in[i] = jnp.concatenate([both_gains[:, t : t + 128] for t in range(0, D, 128)], axis=0)
    for k in range(1, PLANE):
        go(v.gn_in.at[i], v.gn_in.at[i], v.gn_sems[0].at[k], v.gn_sems[1].at[i], (along(k), e))
    v.block[...] = (v.r_own[...] + y_scatter.total(0)).astype(bf16)
    h_scatter.fold_late(0)

    for k in (2, 1, 3):
        rows_copy(k).wait_recv()
        v.gs[...] += v.ga_in[k - 1].reshape(v.gs.shape).astype(f32)
    squares = jnp.sum(v.gs[...] * v.gs[...])
    v.gs_out[...] = v.gs[...].astype(bf16)
    v.ga_all[e] = v.gs_out[e]
    for l in range(local):
        ge_plane.rest(l)
        for first in range(0, deep, 64):
            span = slice(first, first + 64)
            summed = v.ge[l, span]
            for chunk in (1, 2):
                summed = summed + v.ge_in[l, chunk, span].astype(f32)
            v.ge[l, span] = summed
            squares = squares + jnp.sum(summed * summed)
        results[l].start()

    for k in range(1, PLANE):
        slot = v.gn_in.at[along(k)]
        remote(slot, slot, v.gn_sems[0].at[k], v.gn_sems[1].at[along(k)], sibling).wait_recv()
    gains = v.gn_in[0] + v.gn_in[1] + v.gn_in[2] + v.gn_in[3]
    v.mix_in[e] = jnp.concatenate([gains, jnp.full((8, 128), squares)], axis=0)
    for k in range(1, SPAN):
        go(v.mix_in.at[e], v.mix_in.at[e], v.mix_sems[0].at[k], v.mix_sems[1].at[e], (i, across(k)))
    for k in range(1, SPAN):
        go(v.gs_out.at[across(k)], v.ga_all.at[e], v.gs_sems[0].at[k], v.gs_sems[1].at[e], (i, across(k)))
    for k in range(1, SPAN):
        slot = v.mix_in.at[across(k)]
        remote(slot, slot, v.mix_sems[0].at[k], v.mix_sems[1].at[across(k)], sibling).wait_recv()
    mixed = v.mix_in[0]
    for s in range(1, SPAN):
        mixed = mixed + v.mix_in[s]
    v.sq_in[i] = mixed[16:]
    for k in range(1, PLANE):
        go(v.sq_in.at[i], v.sq_in.at[i], v.sq_sems[0].at[k], v.sq_sems[1].at[i], (along(k), e))
    gain_squares = jnp.sum(mixed[:16] * mixed[:16])
    row = lax.broadcasted_iota(jnp.int32, (16, 128), 0)
    pick = lambda n: jnp.sum(jnp.where(row == index // few * 2 + n, mixed[:16], 0.0), axis=0, keepdims=True)
    own_gains = jnp.concatenate([pick(0), pick(1), jnp.zeros((6, 128), f32)], axis=0)
    v.gn[...] = pltpu.roll(own_gains, rows - lax.rem(index, few) * (rows // few), 1)
    for k in range(1, SPAN):
        slot = v.ga_all.at[across(k)]
        remote(slot, slot, v.gs_sems[0].at[k], v.gs_sems[1].at[across(k)], sibling).wait_recv()
    for g in range(SPAN):
        v.ga[:, g * 128 : (g + 1) * 128] = v.ga_all[g, :, :128].astype(f32)
        v.ga[:, QKV + g * 128 : QKV + (g + 1) * 128] = v.ga_all[g, :, 256:].astype(f32)
    for g in range(0, SPAN, 2):
        for first, own in ((QD, 128), (QD + KVD, 192)):
            heads = [v.ga_all[g + n, :, own : own + HD] for n in range(2)]
            v.ga[:, first + g * HD : first + (g + 2) * HD] = jnp.concatenate(heads, axis=1).astype(f32)
    for k in range(1, PLANE):
        slot = v.sq_in.at[along(k)]
        remote(slot, slot, v.sq_sems[0].at[k], v.sq_sems[1].at[along(k)], sibling).wait_recv()
    norm = jnp.sqrt(v.sq_in[0] + v.sq_in[1] + v.sq_in[2] + v.sq_in[3] + gain_squares)[:1, :1]
    v.norm[...] = norm
    v.clip[...] = jnp.minimum(1.0, CLIP_NORM / (norm + 1e-06))

    back, _ = norm_back(v.x_all[e].astype(f32), gain_one, h_scatter.total(0))
    v.grad[...] = v.dr[...] + back
    for copy in results:
        copy.wait()
    for copy in live:
        copy.wait_send()
    for k in (2, 1, 3):
        rows_copy(k).wait_send()
    for l in range(local):
        ge_plane.drain(l)
    for item in (x_line, wo_line, wo_plane, y_scatter, h_scatter):
        item.drain(0)
    for j in range(PARTS):
        up_line.drain(j)
        da_line.drain(j)


def call_layer(*args):
    vmem, anywhere = pl.BlockSpec(memory_space=pltpu.VMEM), pl.BlockSpec(memory_space=pl.ANY)
    rows, local = args[0].shape[0], args[3].shape[0]
    outs = layer_outputs(rows, local)
    return pl.pallas_call(
        layer_kernel,
        out_shape=outs,
        in_specs=[anywhere if n == 3 else vmem for n in range(len(args))],
        out_specs=[anywhere if n == 3 else vmem for n in range(len(outs))],
        scratch_shapes=layer_scratch(rows, local),
        compiler_params=pltpu.CompilerParams(
            collective_id=0, has_side_effects=True, vmem_limit_bytes=63 * 2**20 + 2**19
        ),
        name="layer",
    )(*args)


def small_kernel(clip, rates, gn, block_in, grad_in, wa, ma, va, ga, wg, mg, vg, block, grad, *outs):
    c, one, two = clip[...], rates[:1, :1], rates[:1, 1:2]

    def update(refs, gradient, decay, rate, results):
        w, g = refs[0][...], gradient * c
        first = BETA_ONE * refs[1][...] + (1.0 - BETA_ONE) * g
        second = BETA_TWO * refs[2][...] + (1.0 - BETA_TWO) * g * g
        step = (first * one) / (jnp.sqrt(second * two) + ADAM_EPSILON)
        results[0][...] = w - rate * (step + decay * w)
        results[1][...] = first
        results[2][...] = second

    update((wa, ma, va), ga[...], WEIGHT_DECAY, LEARN_RATE, outs[:3])
    update((wg, mg, vg), gn[: wg.shape[0], : wg.shape[1]], 0.0, GAIN_RATE, outs[3:])
    block[...] = block_in[...]
    grad[...] = grad_in[...]


def call_small(clip, rates, gn, block, grad, attn, ga, gains):
    vmem = pl.BlockSpec(memory_space=pltpu.VMEM)
    outs = [jax.ShapeDtypeStruct(a.shape, a.dtype) for a in (block, grad, *attn, *gains)]
    args = (clip, rates, gn, block, grad, *attn, ga, *gains)
    return pl.pallas_call(
        small_kernel,
        out_shape=outs,
        in_specs=[vmem] * len(args),
        out_specs=[vmem] * len(outs),
        compiler_params=pltpu.CompilerParams(vmem_limit_bytes=63 * 2**20 + 2**19),
        name="small",
    )(*args)


def fast_body(
    activations,
    doc_ids,
    routes,
    gate_weights,
    cotangent,
    step_count,
    w_attn,
    norm_gains,
    w_expert,
    first_attn,
    second_attn,
    first_gains,
    second_gains,
    first_expert,
    second_expert,
):
    cosine, sine = head_tables(activations.shape[1] * lax.axis_size("expert"))
    block, input_total, norm, grad_expert, grad_attn, gn, clip = call_layer(
        activations[0], cotangent[0], w_attn, w_expert, routes[0].T, gate_weights[0].T, doc_ids, norm_gains.T,
        cosine, sine,
    )
    grad_norm = norm.reshape(())
    steps = step_count.astype(jnp.float32)
    rates = 1.0 / (1.0 - jnp.stack([BETA_ONE**steps, BETA_TWO**steps]))[None]
    block, input_total, *small = call_small(
        clip, rates, gn, block, input_total,
        (w_attn, first_attn, second_attn), grad_attn, (norm_gains.T, first_gains.T, second_gains.T),
    )
    attn, gain = small[:3], small[3:]
    expert = adam_update(
        w_expert, first_expert, second_expert, grad_expert * clip[None], steps, WEIGHT_DECAY, LEARN_RATE
    )
    return (block[None], input_total[None], grad_norm, *attn, *[a.T for a in gain], *expert)


def solution(mesh):
    in_specs = (
        P("dp", "expert", None),
        P("dp", "expert"),
        P("dp", "expert", None),
        P("dp", "expert", None),
        P("dp", "expert", None),
        P(),
        P(("dp", "expert"), None),
        P(("dp", "expert"), None),
        P("expert", "dp", None),
        P(("dp", "expert"), None),
        P(("dp", "expert"), None),
        P(("dp", "expert"), None),
        P(("dp", "expert"), None),
        P("expert", "dp", None),
        P("expert", "dp", None),
    )
    out_specs = (
        P("dp", "expert", None),
        P("dp", "expert", None),
        P(),
        P(("dp", "expert"), None),
        P(("dp", "expert"), None),
        P(("dp", "expert"), None),
        P(("dp", "expert"), None),
        P(("dp", "expert"), None),
        P(("dp", "expert"), None),
        P("expert", "dp", None),
        P("expert", "dp", None),
        P("expert", "dp", None),
    )
    body = fast_body if fits(mesh) else general_body
    return jax.shard_map(body, mesh=mesh, in_specs=in_specs, out_specs=out_specs, check_vma=False)
```

```python
import jax
import jax.numpy as jnp
from jax import lax
from jax.sharding import PartitionSpec as P
import types

import numpy as np
from jax.experimental import pallas as pl
from jax.experimental.pallas import tpu as pltpu

D = 1024
H = 16
KVH = 8
HD = 64
FF = 512
TOP = 8
QD = 1024
KVD = 512
QKV = 2048


EPSILON = 1e-05
ROPE_BASE = 10000.0
CLIP_NORM = 1.0
BETA_ONE = 0.9
BETA_TWO = 0.95
ADAM_EPSILON = 1e-08
LEARN_RATE = 0.03
GAIN_RATE = 0.4
WEIGHT_DECAY = 0.1


def rms_scale(values, gain):
    return values * lax.rsqrt(jnp.mean(values * values, axis=-1, keepdims=True) + EPSILON) * gain


def rope_tables(positions, head_width):
    halves = jnp.arange(head_width // 2, dtype=jnp.float32)
    inverse = ROPE_BASE ** (-2.0 * halves / head_width)
    angles = positions.astype(jnp.float32)[:, None] * inverse[None, :]
    angles = jnp.concatenate([angles, angles], axis=-1)
    return (jnp.cos(angles)[:, None, :], jnp.sin(angles)[:, None, :])


def rotate(values, cosine, sine_table):
    middle = values.shape[-1] // 2
    turned = jnp.concatenate([-values[..., middle:], values[..., :middle]], axis=-1)
    return values * cosine + turned * sine_table


def unrotate(gradient, cosine, sine_table):
    middle = gradient.shape[-1] // 2
    product = gradient * sine_table
    turned = jnp.concatenate([product[..., middle:], -product[..., :middle]], axis=-1)
    return gradient * cosine + turned


def adam_update(weight, moment_one, second, gradient, steps_done, decay_rate, step_rate):
    first_new = BETA_ONE * moment_one + (1.0 - BETA_ONE) * gradient
    second_new = BETA_TWO * second + (1.0 - BETA_TWO) * gradient * gradient
    first_hat = first_new / (1.0 - BETA_ONE**steps_done)
    second_hat = second_new / (1.0 - BETA_TWO**steps_done)
    weight_new = weight - step_rate * (
        first_hat / (jnp.sqrt(second_hat) + ADAM_EPSILON) + decay_rate * weight
    )
    return (weight_new, first_new, second_new)


def attn_fetch(w_attn, norm_gains):
    return (
        lax.all_gather(w_attn.astype(jnp.bfloat16), ("dp", "expert"), axis=0, tiled=True),
        lax.all_gather(norm_gains.astype(jnp.bfloat16), ("dp", "expert"), axis=0, tiled=True),
    )


def expert_fetch(w_expert):
    return lax.all_gather(w_expert.astype(jnp.bfloat16), "dp", axis=1, tiled=True)


def to_owner(buffer):
    return lax.all_to_all(buffer, "expert", split_axis=0, concat_axis=1, tiled=True)


def to_sender(buffer):
    return lax.all_to_all(buffer, "expert", split_axis=1, concat_axis=0, tiled=True)


def expert_forward(received, expert_cols):
    gate_up = jnp.einsum(
        "esd,edf->esf", received, expert_cols[:, :, : 2 * FF], preferred_element_type=jnp.float32
    )
    activated = (jax.nn.silu(gate_up[..., :FF]) * gate_up[..., FF:]).astype(jnp.bfloat16)
    return (gate_up, activated)


def general_body(
    activations,
    doc_ids,
    routes,
    gate_weights,
    cotangent,
    step_count,
    w_attn,
    norm_gains,
    w_expert,
    first_attn,
    second_attn,
    first_gains,
    second_gains,
    first_expert,
    second_expert,
):
    row_count = activations.shape[1]
    span_size = lax.axis_size("expert")
    shard_pos = lax.axis_index("expert")
    seq_length = row_count * span_size
    expert_total = w_expert.shape[0] * span_size
    capacity = (row_count * TOP * 9 + expert_total * 8 - 1) // (expert_total * 8)
    group_size = H // KVH
    score_scale = HD ** (-0.5)
    hidden_in = activations[0].astype(jnp.float32)
    upstream = cotangent[0].astype(jnp.float32)
    attn_cols, gain_pair = attn_fetch(w_attn, norm_gains)
    expert_cols = expert_fetch(w_expert)
    gain_one = gain_pair[:, 0].astype(jnp.float32)
    gain_two = gain_pair[:, 1].astype(jnp.float32)
    w_project = attn_cols[:, :QKV]
    w_output = attn_cols[:, QKV:]
    normed = rms_scale(hidden_in, gain_one).astype(jnp.bfloat16)
    projected = jnp.dot(normed, w_project, preferred_element_type=jnp.float32)
    positions = shard_pos * row_count + jnp.arange(row_count, dtype=jnp.int32)
    cosine, sine_table = rope_tables(positions, HD)
    queries = rotate(projected[:, :QD].reshape(row_count, H, HD), cosine, sine_table).astype(
        jnp.bfloat16
    )
    key_heads = rotate(
        projected[:, QD : QD + KVD].reshape(row_count, KVH, HD), cosine, sine_table
    ).astype(jnp.bfloat16)
    value_heads = projected[:, QD + KVD :].astype(jnp.bfloat16)
    key_all, value_all, doc_all = (
        lax.all_gather(key_heads.reshape(row_count, KVD), "expert", axis=0, tiled=True),
        lax.all_gather(value_heads, "expert", axis=0, tiled=True),
        lax.all_gather(doc_ids[0].astype(jnp.bfloat16), "expert", axis=0, tiled=True),
    )
    key_docs = doc_all.astype(jnp.int32)
    query_docs = doc_ids[0]
    query_groups = queries.reshape(row_count, KVH, group_size, HD)
    key_block = min(512, seq_length)
    needed = (shard_pos * row_count + row_count + key_block - 1) // key_block

    def block_scores(block_id):
        first_key = block_id * key_block
        key_part = lax.dynamic_slice_in_dim(key_all, first_key, key_block, 0).reshape(
            key_block, KVH, HD
        )
        raw_scores = (
            jnp.einsum("tgrd,kgd->grtk", query_groups, key_part, preferred_element_type=jnp.float32)
            * score_scale
        )
        key_pos = first_key + jnp.arange(key_block, dtype=jnp.int32)
        key_doc = lax.dynamic_slice_in_dim(key_docs, first_key, key_block, 0)
        visible = (key_pos[None, :] <= positions[:, None]) & (
            key_doc[None, :] == query_docs[:, None]
        )
        return (raw_scores, visible, key_part)

    def value_part(block_id):
        return lax.dynamic_slice_in_dim(value_all, block_id * key_block, key_block, 0).reshape(
            key_block, KVH, HD
        )

    def total_step(block_id, running):
        row_peak, row_total = running
        raw_scores, visible, _ = block_scores(block_id)
        masked = jnp.where(visible, raw_scores, -1e30)
        new_peak = jnp.maximum(row_peak, jnp.max(masked, axis=-1))
        scaled = jnp.where(visible, jnp.exp(masked - new_peak[..., None]), 0.0)
        return (new_peak, row_total * jnp.exp(row_peak - new_peak) + jnp.sum(scaled, axis=-1))

    start_peak = jnp.full((KVH, group_size, row_count), -1e30, jnp.float32)
    start_total = jnp.zeros((KVH, group_size, row_count), jnp.float32)
    row_peak, row_total = lax.fori_loop(0, needed, total_step, (start_peak, start_total))
    log_total = row_peak + jnp.log(row_total)

    def exact_probs(raw_scores, visible):
        return jnp.exp(jnp.where(visible, raw_scores - log_total[..., None], -1e30))

    def output_step(block_id, summed):
        raw_scores, visible, _ = block_scores(block_id)
        weights_low = exact_probs(raw_scores, visible).astype(jnp.bfloat16)
        return summed + jnp.einsum(
            "grtk,kgd->tgrd", weights_low, value_part(block_id), preferred_element_type=jnp.float32
        )

    attended = lax.fori_loop(
        0, needed, output_step, jnp.zeros((row_count, KVH, group_size, HD), jnp.float32)
    )
    attended = attended.reshape(row_count, QD).astype(jnp.bfloat16)
    branch = jnp.einsum("tc,dc->td", attended, w_output, preferred_element_type=jnp.float32)
    residual = hidden_in + branch
    normed_two = rms_scale(residual, gain_two).astype(jnp.bfloat16)
    flat_routes = routes[0].reshape(-1)
    one_hot = (flat_routes[:, None] == jnp.arange(expert_total, dtype=jnp.int32)[None, :]).astype(
        jnp.int32
    )
    ranking = jnp.sum((jnp.cumsum(one_hot, axis=0) - 1) * one_hot, axis=1)
    places = flat_routes * capacity + ranking
    owners = jnp.arange(row_count * TOP, dtype=jnp.int32) // TOP
    source = jnp.zeros((expert_total * capacity,), jnp.int32).at[places].set(owners)
    filled = jnp.zeros((expert_total * capacity,), jnp.int32).at[places].set(1) > 0
    slot_gate = (
        jnp.zeros((expert_total * capacity,), jnp.float32)
        .at[places]
        .set(gate_weights[0].reshape(-1))
    )
    outgoing = jnp.where(filled[:, None], normed_two[source], jnp.zeros((), jnp.bfloat16)).reshape(
        expert_total, capacity, D
    )
    received = to_owner(outgoing)
    gate_up, activated = expert_forward(received, expert_cols)
    expert_out = jnp.einsum(
        "esf,edf->esd", activated, expert_cols[:, :, 2 * FF :], preferred_element_type=jnp.float32
    ).astype(jnp.bfloat16)
    returned = to_sender(expert_out).reshape(expert_total * capacity, D)
    picked = returned[places].reshape(row_count, TOP, D).astype(jnp.float32)
    combined = jnp.sum(gate_weights[0][..., None] * picked, axis=1)
    block_result = (residual + combined).astype(jnp.bfloat16)
    slot_grad = jnp.where(filled[:, None], slot_gate[:, None] * upstream[source], 0.0)
    slot_grad = slot_grad.astype(jnp.bfloat16).reshape(expert_total, capacity, D)
    owner_grad = to_owner(slot_grad)
    attn_cols, gain_pair = attn_fetch(w_attn, norm_gains)
    w_project = attn_cols[:, :QKV]
    w_output = attn_cols[:, QKV:]
    expert_cols = expert_fetch(w_expert)
    gate_up, activated = expert_forward(received, expert_cols)
    gate_part = gate_up[..., :FF]
    up_part = gate_up[..., FF:]
    sigmoid_gate = jax.nn.sigmoid(gate_part)
    act_grad = jnp.einsum(
        "esd,edf->esf", owner_grad, expert_cols[:, :, 2 * FF :], preferred_element_type=jnp.float32
    )
    gate_grad = act_grad * up_part * sigmoid_gate * (1.0 + gate_part * (1.0 - sigmoid_gate))
    lift_grad = act_grad * gate_part * sigmoid_gate
    mixed_grad = jnp.concatenate([gate_grad, lift_grad], axis=-1).astype(jnp.bfloat16)
    down_grad = jnp.einsum(
        "esf,esd->edf", activated, owner_grad, preferred_element_type=jnp.float32
    )
    inward_grad = jnp.einsum(
        "esd,esf->edf", received, mixed_grad, preferred_element_type=jnp.float32
    )
    row_grads = jnp.einsum(
        "esf,edf->esd", mixed_grad, expert_cols[:, :, : 2 * FF], preferred_element_type=jnp.float32
    ).astype(jnp.bfloat16)
    back_rows = to_sender(row_grads).reshape(expert_total * capacity, D)
    normed_two_grad = jnp.sum(
        back_rows[places].reshape(row_count, TOP, D).astype(jnp.float32), axis=1
    )
    _, second_pull = jax.vjp(rms_scale, residual, gain_two)
    resid_grad, gain_two_grad = second_pull(normed_two_grad)
    resid_grad = upstream + resid_grad
    branch_grad = resid_grad.astype(jnp.bfloat16)
    output_grad = jnp.einsum("td,tc->dc", branch_grad, attended, preferred_element_type=jnp.float32)
    attended_grad = jnp.dot(branch_grad, w_output, preferred_element_type=jnp.float32).astype(
        jnp.bfloat16
    )
    grad_groups = attended_grad.reshape(row_count, KVH, group_size, HD)

    def delta_step(block_id, summed):
        raw_scores, visible, _ = block_scores(block_id)
        probs_full = exact_probs(raw_scores, visible)
        prob_grad = jnp.einsum(
            "tgrd,kgd->grtk", grad_groups, value_part(block_id), preferred_element_type=jnp.float32
        )
        return summed + jnp.sum(probs_full * prob_grad, axis=-1)

    delta_rows = lax.fori_loop(
        0, needed, delta_step, jnp.zeros((KVH, group_size, row_count), jnp.float32)
    )

    def grad_step(block_id, running):
        query_grad, key_grad, value_grad = running
        raw_scores, visible, key_part = block_scores(block_id)
        probs_full = exact_probs(raw_scores, visible)
        prob_grad = jnp.einsum(
            "tgrd,kgd->grtk", grad_groups, value_part(block_id), preferred_element_type=jnp.float32
        )
        score_grad = (probs_full * (prob_grad - delta_rows[..., None])).astype(jnp.bfloat16)
        query_grad = (
            query_grad
            + jnp.einsum("grtk,kgd->tgrd", score_grad, key_part, preferred_element_type=jnp.float32)
            * score_scale
        )
        key_piece = (
            jnp.einsum(
                "grtk,tgrd->kgd", score_grad, query_groups, preferred_element_type=jnp.float32
            )
            * score_scale
        )
        value_piece = jnp.einsum(
            "grtk,tgrd->kgd",
            probs_full.astype(jnp.bfloat16),
            grad_groups,
            preferred_element_type=jnp.float32,
        )
        first_key = block_id * key_block
        key_grad = lax.dynamic_update_slice_in_dim(
            key_grad, key_piece.reshape(key_block, KVD), first_key, 0
        )
        value_grad = lax.dynamic_update_slice_in_dim(
            value_grad, value_piece.reshape(key_block, KVD), first_key, 0
        )
        return (query_grad, key_grad, value_grad)

    start_grads = (
        jnp.zeros((row_count, KVH, group_size, HD), jnp.float32),
        jnp.zeros((seq_length, KVD), jnp.float32),
        jnp.zeros((seq_length, KVD), jnp.float32),
    )
    query_grad, key_grad, value_grad = lax.fori_loop(0, needed, grad_step, start_grads)
    key_sum, value_sum = (
        lax.psum_scatter(key_grad, "expert", scatter_dimension=0, tiled=True),
        lax.psum_scatter(value_grad, "expert", scatter_dimension=0, tiled=True),
    )
    query_back = unrotate(query_grad.reshape(row_count, H, HD), cosine, sine_table).reshape(
        row_count, QD
    )
    key_back = unrotate(key_sum.reshape(row_count, KVH, HD), cosine, sine_table).reshape(
        row_count, KVD
    )
    project_grad = jnp.concatenate([query_back, key_back, value_sum], axis=1).astype(jnp.bfloat16)
    weight_grad_qkv = jnp.einsum(
        "td,tc->dc", normed, project_grad, preferred_element_type=jnp.float32
    )
    normed_grad = jnp.einsum(
        "tc,dc->td", project_grad, w_project, preferred_element_type=jnp.float32
    )
    _, first_pull = jax.vjp(rms_scale, hidden_in, gain_one)
    input_part, gain_one_grad = first_pull(normed_grad)
    input_total = resid_grad + input_part
    attn_partial = jnp.concatenate([weight_grad_qkv, output_grad], axis=1)
    gain_partial = jnp.stack([gain_one_grad, gain_two_grad], axis=1)
    grad_attn, grad_gains = (
        lax.psum_scatter(attn_partial, ("dp", "expert"), scatter_dimension=0, tiled=True),
        lax.psum_scatter(gain_partial, ("dp", "expert"), scatter_dimension=0, tiled=True),
    )
    grad_expert = lax.psum_scatter(
        jnp.concatenate([inward_grad, down_grad], axis=2).astype(jnp.bfloat16),
        "dp",
        scatter_dimension=1,
        tiled=True,
    ).astype(jnp.float32)
    local_squares = (
        jnp.sum(grad_attn * grad_attn)
        + jnp.sum(grad_gains * grad_gains)
        + jnp.sum(grad_expert * grad_expert)
    )
    grad_norm = jnp.sqrt(lax.psum(local_squares, ("dp", "expert")))
    clip_factor = jnp.minimum(1.0, CLIP_NORM / (grad_norm + 1e-06))
    steps_done = step_count.astype(jnp.float32)
    attn_new = adam_update(
        w_attn,
        first_attn,
        second_attn,
        grad_attn * clip_factor,
        steps_done,
        WEIGHT_DECAY,
        LEARN_RATE,
    )
    gains_new = adam_update(
        norm_gains, first_gains, second_gains, grad_gains * clip_factor, steps_done, 0.0, GAIN_RATE
    )
    expert_new = adam_update(
        w_expert,
        first_expert,
        second_expert,
        grad_expert * clip_factor,
        steps_done,
        WEIGHT_DECAY,
        LEARN_RATE,
    )
    return (
        block_result[None],
        input_total[None],
        grad_norm,
        attn_new[0],
        attn_new[1],
        attn_new[2],
        gains_new[0],
        gains_new[1],
        gains_new[2],
        expert_new[0],
        expert_new[1],
        expert_new[2],
    )


def fits(mesh):
    return dict(mesh.shape) == {"dp": 4, "expert": KVH}


def head_tables(length):
    halves = np.arange(HD // 2, dtype=np.float32)
    inverse = np.power(np.float32(ROPE_BASE), np.float32(-2.0) * halves / np.float32(HD))
    angles = np.arange(length, dtype=np.float32)[:, None] * inverse[None, :]
    cosine, sine = np.cos(angles), np.sin(angles)
    cosine = np.concatenate([cosine] * 4, axis=1)
    return jnp.asarray(cosine), jnp.asarray(np.concatenate([-sine, sine] * 2, axis=1))


LINE, SPAN, PLANE, PARTS = 4, 8, 4, 4
QUERY_BLOCK = 256
NN, NT, TN = ((1,), (0,)), ((1,), (1,)), ((0,), (0,))


def remote(source, target, sent, landed, device):
    return pltpu.make_async_remote_copy(
        src_ref=source,
        dst_ref=target,
        send_sem=sent,
        recv_sem=landed,
        device_id=device,
        device_id_type=pl.DeviceIdType.MESH,
    )


def whereabouts():
    i, e = lax.axis_index("dp"), lax.axis_index("expert")
    return i, e, e // 2, lax.rem(e, 2)


def partners(i, e):
    others = [(i, lax.rem(e + k, SPAN)) for k in range(1, SPAN)]
    return others + [(lax.rem(i + k, PLANE), e) for k in range(1, PLANE)]


def piece(j, size):
    return pl.ds(pl.multiple_of(j * size, size), size)


class LineGather:
    def __init__(self, slot, source, where, sems):
        self.slot, self.source, self.where = slot, source, where
        self.sent, self.passed, self.landed = sems

    def _own(self, j, k):
        i, e, z, c = self.where
        there = z * 2 + 1 - c if k == 0 else lax.rem(z + k, LINE) * 2 + c
        return remote(self.source(j), self.slot(e, j), self.sent.at[j, k], self.landed.at[j, e], (i, there))

    def _pass(self, j, k):
        i, e, z, c = self.where
        index = lax.rem(z + k, LINE) * 2 + c
        place = self.slot(index, j)
        return remote(place, place, self.passed.at[j, k], self.landed.at[j, index], (i, z * 2 + 1 - c))

    def _relay(self, j):
        i, e, z, c = self.where
        index = lax.rem(z + 2, LINE) * 2 + c
        place = self.slot(index, j)
        end = LINE - 1 - lax.rem(z + 2, LINE)
        return remote(place, place, self.passed.at[j, 0], self.landed.at[j, index], (i, end * 2 + c))

    def _each_own(self, j, act):
        z = self.where[2]
        act(self._own(j, 2))
        pl.when(z != LINE - 1)(lambda: act(self._own(j, 1)))
        pl.when(z != 0)(lambda: act(self._own(j, 3)))
        act(self._own(j, 0))

    def _when_inner(self, act):
        z = self.where[2]
        pl.when((z > 0) & (z < LINE - 1))(act)

    def start(self, j):
        self._each_own(j, lambda copy: copy.start())

    def wait(self, j, index):
        i, e, z, c = self.where
        place = self.slot(index, j)
        remote(place, place, self.sent.at[j, 0], self.landed.at[j, index], (i, z * 2 + 1 - c)).wait_recv()

    def sibling(self):
        _, e, z, c = self.where
        return z * 2 + 1 - c

    def near(self, k):
        _, e, z, c = self.where
        return lax.rem(z + k, LINE) * 2 + c

    def far(self, k):
        _, e, z, c = self.where
        return lax.rem(z + k, LINE) * 2 + 1 - c

    def forward(self, j, k):
        self.wait(j, self.near(k))
        if k == 2:
            self._when_inner(lambda: self._relay(j).start())
        self._pass(j, k).start()

    def forward_all(self, j):
        for k in (2, 1, 3):
            self.forward(j, k)

    def rest(self, j):
        self.wait(j, self.sibling())
        for k in range(1, LINE):
            self.wait(j, self.far(k))

    def drain(self, j):
        self._each_own(j, lambda copy: copy.wait_send())
        self._when_inner(lambda: self._relay(j).wait_send())
        for k in range(1, LINE):
            self._pass(j, k).wait_send()


class LineScatter:
    def __init__(self, data, where, pair, out, inbox, own, sems, size):
        self.data, self.where, self.size = data, where, size
        self.pair, self.out, self.inbox, self.own = pair, out, inbox, own
        self.pair_sent, self.pair_landed, self.sent, self.landed = sems

    def _pair(self, j, k):
        i, e, z, c = self.where
        there, rows = lax.rem(z + k, LINE), piece(j, self.size)
        return remote(
            self.data.at[there * 2 + 1 - c, rows], self.pair.at[there, rows],
            self.pair_sent.at[j, there], self.pair_landed.at[j, there], (i, z * 2 + 1 - c),
        )

    def _send(self, j, k):
        i, e, z, c = self.where
        there, rows = lax.rem(z + k, LINE), piece(j, self.size)
        crossing = {1: z // (LINE - 1), 2: 0, 3: (LINE - 1 - z) // (LINE - 1)}[k]
        chip = {1: z + 1 - 2 * crossing, 2: there, 3: z - 1 + 2 * crossing}[k]
        slot = z + crossing * (chip - z)
        return remote(
            self.out.at[there, rows], self.inbox.at[slot, rows],
            self.sent.at[j, there], self.landed.at[j, slot], (i, chip * 2 + c),
        )

    def _landed(self, j, slot):
        i, e, z, c = self.where
        place = self.inbox.at[slot, piece(j, self.size)]
        remote(place, place, self.sent.at[j, slot], self.landed.at[j, slot], (i, z * 2 + 1 - c)).wait_recv()

    def _both(self, j, there):
        c, rows = self.where[3], piece(j, self.size)
        return self.data[there * 2 + c, rows].astype(jnp.float32) + self.pair[there, rows].astype(jnp.float32)

    def _across(self, j):
        there, rows = lax.rem(self.where[2] + 2, LINE), piece(j, self.size)
        return there, rows, self._both(j, there)

    def start(self, j):
        for k in (1, 3, 2, 0):
            self._pair(j, k).start()

    def start_one(self, j, k):
        self._pair(j, k).start()

    def fold_one(self, j, k):
        z, rows = self.where[2], piece(j, self.size)
        self._pair(j, k).wait_recv()

        def send():
            there = lax.rem(z + k, LINE)
            self.out[there, rows] = self._both(j, there).astype(jnp.bfloat16)
            self._send(j, k).start()

        if k == 0:
            self.own[rows] = self._both(j, z)
        elif k == 2:
            pl.when((z == 0) | (z == LINE - 1))(send)
        else:
            send()

    def fold(self, j):
        for k in (1, 3, 2, 0):
            self.fold_one(j, k)

    def fold_late(self, j):
        z = self.where[2]

        @pl.when((z > 0) & (z < LINE - 1))
        def _():
            there, rows, both = self._across(j)
            self._landed(j, z)
            self.out[there, rows] = (both + self.inbox[z, rows].astype(jnp.float32)).astype(jnp.bfloat16)
            self._send(j, 2).start()

    def total(self, j):
        z, rows = self.where[2], piece(j, self.size)

        def add(k):
            there = lax.rem(z + k, LINE)
            self._landed(j, there)
            self.own[rows] += self.inbox[there, rows].astype(jnp.float32)

        pl.when(z != LINE - 1)(lambda: add(1))
        pl.when(z != 0)(lambda: add(3))
        add(2)
        return self.own[rows]

    def drain(self, j):
        for k in range(LINE):
            self._pair(j, k).wait_send()
        for k in range(1, LINE):
            self._send(j, k).wait_send()


class PlaneGather:
    def __init__(self, where, slot, size, sems):
        i, self.e = where[0], where[1]
        self.i, self.slot, self.sems = i, slot, sems
        self.x = i // 2 * 2 + 1 - lax.rem(i, 2)
        self.y = (1 - i // 2) * 2 + lax.rem(i, 2)
        self.far = PLANE - 1 - i
        self.half = size // 2

    def _copy(self, l, n, source):
        rows = (slice(None), slice(None), slice(0, self.half), slice(self.half, None))[n]
        to = (self.x, self.y, self.y, self.x)[n]
        sent, landed = self.sems
        place = self.slot(l, source, rows)
        return remote(place, place, sent.at[l, n], landed.at[l, n], (to, self.e))

    def start(self, l):
        self._copy(l, 0, self.i).start()
        self._copy(l, 1, self.i).start()

    def forward(self, l):
        self._copy(l, 0, self.x).wait_recv()
        self._copy(l, 2, self.x).start()
        self._copy(l, 1, self.y).wait_recv()
        self._copy(l, 3, self.y).start()

    def rest(self, l):
        self._copy(l, 2, self.far).wait_recv()
        self._copy(l, 3, self.far).wait_recv()

    def drain(self, l):
        for n, source in enumerate((self.i, self.i, self.x, self.y)):
            self._copy(l, n, source).wait_send()


class PlaneScatter:
    def __init__(self, plane, out, inbox, sems):
        self.plane, self.out, self.inbox = plane, out, inbox
        self.sent, self.landed = sems
        self.half = plane.half

    def _copy(self, l, chunk, part, n):
        first = slice(0, self.half) if part == 0 else slice(self.half, None)
        to_x = chunk == 1 or (chunk == 0 and part == 0)
        return remote(
            self.out.at[l, chunk, first], self.inbox.at[l, chunk, first], self.sent.at[l, n], self.landed.at[l, n],
            (self.plane.x if to_x else self.plane.y, self.plane.e),
        )

    def _at(self, l, chunk, part):
        return self._copy(l, chunk, part, chunk * 2 + part)

    def start(self, l, chunk):
        for part in ((0, 1), (0,), (1,))[chunk]:
            self._at(l, chunk, part).start()

    def combine(self, l):
        for chunk, part in ((1, 1), (2, 0)):
            rows = slice(part * self.half, (part + 1) * self.half)
            self._at(l, 0, part).wait_recv()
            mine = self.out[l, chunk, rows].astype(jnp.float32) + self.inbox[l, 0, rows].astype(jnp.float32)
            self.out[l, chunk, rows] = mine.astype(jnp.bfloat16)
            self._at(l, chunk, part).start()

    def rest(self, l):
        for chunk in (1, 2):
            for part in (0, 1):
                self._at(l, chunk, part).wait_recv()

    def drain(self, l):
        for chunk in range(3):
            for part in (0, 1):
                self._at(l, chunk, part).wait_send()


def half_turn_tile(part):
    lane = lax.broadcasted_iota(jnp.int32, part.shape, 1)
    ahead = pltpu.roll(part, 128 - HD // 2, 1)
    behind = pltpu.roll(part, HD // 2, 1)
    return jnp.where(lax.rem(lane, HD) < HD // 2, ahead, behind)


def rms_rows(values):
    return lax.rsqrt(jnp.mean(values * values, axis=-1, keepdims=True) + EPSILON)


def norm_back(values, gain, upper):
    scale = rms_rows(values)
    scaled = upper * gain
    inner = jnp.mean(values * scaled, axis=-1, keepdims=True)
    return scale * scaled - values * (scale * scale * scale) * inner, upper * values * scale


def dot(a, b, contract):
    return lax.dot_general(a, b, (contract, ((), ())), preferred_element_type=jnp.float32)


def visible_keys(first, low, high, docs_row, docs_col):
    shape = (QUERY_BLOCK, high - low)
    key = lax.broadcasted_iota(jnp.int32, shape, 1) + low
    query = lax.broadcasted_iota(jnp.int32, shape, 0) + first
    return (key <= query) & (docs_row[:, low:high] == docs_col)


def layer_kernel(x, up, wa, we, routes, gates, doc_ids, shard_gains, cos, sin, block, grad, norm, ge_far, ga, gn, clip, **held):
    layer_body(
        types.SimpleNamespace(
            x=x, up=up, wa=wa, we=we, routes=routes, gates=gates, doc_ids=doc_ids, shard_gains=shard_gains,
            cos=cos, sin=sin,
            block=block, grad=grad, norm=norm, ge_far=ge_far, ga=ga, gn=gn, clip=clip, **held,
        )
    )


def layer_outputs(rows, local):
    f32 = jnp.float32
    shaped = jax.ShapeDtypeStruct
    deep = D // PLANE
    return [
        shaped((rows, D), jnp.bfloat16), shaped((rows, D), f32), shaped((1, 1), f32),
        shaped((local, deep, 3 * FF), f32), shaped((deep // SPAN, 3072), f32), shaped((8, rows), f32),
        shaped((1, 1), f32),
    ]


def layer_scratch(rows, local):
    f32, bf16 = jnp.float32, jnp.bfloat16
    held, sems = pltpu.VMEM, lambda *shape: pltpu.SemaphoreType.DMA(shape)
    deep = D // PLANE
    part = deep // SPAN
    blocks = held((SPAN, rows, D), bf16)
    quarter = held((LINE, rows, D), bf16)
    line = lambda parts: (sems(parts, LINE), sems(parts, LINE), sems(parts, SPAN))
    scatter = lambda parts: tuple(sems(parts, LINE) for _ in range(4))
    both = lambda *shape: (sems(*shape), sems(*shape))
    return dict(
        x_all=blocks, up_all=blocks, h1=blocks, o_all=blocks, h2=blocks, d=blocks, da_all=blocks,
        qkv=held((SPAN * rows, 256), bf16), lse=held((SPAN * rows, 128), f32),
        wq_out=held((SPAN, part, 256), bf16), w_mine=held((PLANE, SPAN, part, 256), bf16),
        wo_all=held((PLANE, LINE, 2, part, D), bf16), we_all=held((local, PLANE, deep, 3 * FF), bf16),
        o_own=held((SPAN, rows, 128), bf16),
        r_own=held((rows, D), f32),
        pack=held((SPAN, 8, rows), f32), pack_all=held((SPAN, 8, rows), f32), gain_sum=held((PLANE, 2, 8, 128), f32),
        cols=held((SPAN, rows, 128), f32), docs=held((8, SPAN * rows), f32), gains=held((8, D), f32),
        act=held((local, SPAN, rows, FF), bf16), dgu=held((local, SPAN, rows, 2 * FF), bf16),
        pair=quarter, out=quarter, inbox=quarter, own=held((rows, D), f32),
        y_pair=quarter, y_out=quarter, y_inbox=quarter, y_own=held((rows, D), f32),
        ge_in=held((local, PLANE - 1, deep, 3 * FF), bf16),
        do=held((SPAN, rows, 128), bf16), dkv=held((SPAN * rows, 128), f32), dqkv=held((SPAN * rows, 256), bf16),
        dr=held((rows, D), f32), gn_two=held((8, D), f32),
        ga_out=held((PLANE - 1, deep, 384), bf16), ga_in=held((PLANE - 1, deep, 384), bf16),
        gs=held((SPAN, part, 384), f32), gs_out=held((SPAN, part, 384), bf16), ga_all=held((SPAN, part, 384), bf16),
        gn_in=held((PLANE, 16, 128), f32), mix_in=held((SPAN, 24, 128), f32), sq_in=held((PLANE, 8, 128), f32),
        ge=held((local, deep, 3 * FF), f32), store=sems(local),
        x_sems=line(1), up_sems=line(PARTS), wo_sems=line(1), o_sems=line(PARTS), da_sems=line(PARTS),
        d_sems=scatter(PARTS), y_sems=scatter(1), h_sems=scatter(1),
        load=sems(local), pack_sems=both(SPAN), wq_sems=both(SPAN), wqd_sems=both(PLANE), gd_sems=both(PLANE),
        wod_sems=both(1, 4), wop_sems=both(PLANE), we_sems=both(local, 4), ge_sems=both(local, 6),
        ga_sems=both(PLANE), gn_sems=both(PLANE), gs_sems=both(SPAN), mix_sems=both(SPAN), sq_sems=both(PLANE),
    )


def layer_body(v):
    f32, bf16 = jnp.float32, jnp.bfloat16
    where = i, e, z, c = whereabouts()
    sibling = (i, z * 2 + 1 - c)
    rows, local, deep = v.x.shape[0], v.we_all.shape[0], v.ge.shape[1]
    length, size = rows * SPAN, rows // PARTS
    own_cols = piece(e, 128)
    live = []

    def go(*spec):
        copy = remote(*spec)
        copy.start()
        live.append(copy)

    def along(k):
        return lax.rem(i + k, PLANE)

    def across(k):
        return lax.rem(e + k, SPAN)

    def line(sems, slot, source):
        return LineGather(slot, source, where, sems)

    x_line = line(v.x_sems, lambda s, j: v.x_all.at[s], lambda j: v.x)
    up_line = line(v.up_sems, lambda s, j: v.up_all.at[s, piece(j, size)], lambda j: v.up.at[piece(j, size)])
    wo_line = line(
        v.wo_sems, lambda s, j: v.wo_all.at[i, s // 2, lax.rem(s, 2)], lambda j: v.wo_all.at[i, z, c]
    )
    o_line = line(
        v.o_sems,
        lambda s, j: v.o_all.at[:, piece(j, size), piece(s, 128)],
        lambda j: v.o_own.at[:, piece(j, size)],
    )
    da_line = line(
        v.da_sems, lambda s, j: v.da_all.at[s, piece(j, size)], lambda j: v.da_all.at[e, piece(j, size)]
    )
    we_plane = PlaneGather(where, lambda l, s, part: v.we_all.at[l, s, part], deep, v.we_sems)
    wo_plane = PlaneGather(where, lambda l, s, part: v.wo_all.at[s, part, c], LINE, v.wod_sems)
    ge_plane = PlaneScatter(we_plane, v.we_all, v.ge_in, v.ge_sems)
    d_scatter = LineScatter(v.d, where, v.pair, v.out, v.inbox, v.own, v.d_sems, size)
    y_scatter = LineScatter(v.o_all, where, v.y_pair, v.y_out, v.y_inbox, v.y_own, v.y_sems, rows)
    h_scatter = LineScatter(v.d, where, v.pair, v.out, v.inbox, v.own, v.h_sems, rows)

    loads = [pltpu.make_async_copy(v.we.at[l], v.ge.at[l], v.load.at[l]) for l in range(local)]
    for copy in loads:
        copy.start()
    results = [pltpu.make_async_copy(v.ge.at[l], v.ge_far.at[l], v.store.at[l]) for l in range(local)]
    barrier = pltpu.get_barrier_semaphore()
    for device in partners(i, e):
        pl.semaphore_signal(barrier, inc=1, device_id=device, device_id_type=pl.DeviceIdType.MESH)
    lane = lax.broadcasted_iota(jnp.int32, (2, rows), 1)
    index, few = i * SPAN + e, rows // v.shard_gains.shape[1]
    spread = jnp.concatenate([v.shard_gains[...]] * few, axis=1)
    spread = jnp.where(lane // (rows // few) == lax.rem(index, few), spread, 0.0)
    shared = [v.doc_ids[...].astype(f32), spread, jnp.zeros((3, rows), f32)]
    for g in range(SPAN):
        named = [
            jnp.sum(jnp.where(v.routes[...] == g * local + l, v.gates[...], 0.0), axis=0, keepdims=True)
            for l in range(local)
        ]
        v.pack[g] = jnp.concatenate(named + shared, axis=0)
    for g in range(SPAN):
        v.wq_out[g, :, :128] = v.wa[:, g * 128 : (g + 1) * 128].astype(bf16)
        key_value = [v.wa[:, first + g * HD : first + (g + 1) * HD] for first in (QD, QD + KVD)]
        v.wq_out[g, :, 128:] = jnp.concatenate(key_value, axis=1).astype(bf16)
    v.w_mine[i, e] = v.wq_out[e]
    v.wo_all[i, z, c] = v.wa[:, QKV:].astype(bf16)
    v.pack_all[e] = v.pack[e]
    v.x_all[e] = v.x[...]
    v.up_all[e] = v.up[...]
    pl.semaphore_wait(barrier, SPAN + PLANE - 2)
    for k in range(1, SPAN):
        go(v.pack.at[across(k)], v.pack_all.at[e], v.pack_sems[0].at[k], v.pack_sems[1].at[e], (i, across(k)))
    for k in range(1, SPAN):
        go(v.wq_out.at[across(k)], v.w_mine.at[i, e], v.wq_sems[0].at[k], v.wq_sems[1].at[e], (i, across(k)))
    wo_line.start(0)
    x_line.start(0)
    loads[0].wait()
    v.we_all[0, i] = v.ge[0].astype(bf16)
    we_plane.start(0)

    for k in range(1, SPAN):
        slot = v.pack_all.at[across(k)]
        remote(slot, slot, v.pack_sems[0].at[k], v.pack_sems[1].at[across(k)], sibling).wait_recv()
    for half in range(2):
        summed = v.pack_all[4 * half]
        for s in range(1, 4):
            summed = summed + v.pack_all[4 * half + s]
        v.gain_sum[i, half] = summed
    for k in range(1, PLANE):
        go(v.gain_sum.at[i], v.gain_sum.at[i], v.gd_sems[0].at[k], v.gd_sems[1].at[i], (along(k), e))
    for k in range(1, SPAN):
        slot = v.w_mine.at[i, across(k)]
        remote(slot, slot, v.wq_sems[0].at[k], v.wq_sems[1].at[across(k)], sibling).wait_recv()
    for k in range(1, PLANE):
        go(v.w_mine.at[i], v.w_mine.at[i], v.wqd_sems[0].at[k], v.wqd_sems[1].at[i], (along(k), e))
    loads[1].wait()
    v.we_all[1, i] = v.ge[1].astype(bf16)
    for s in range(SPAN):
        block = v.pack_all[s]
        tall = jnp.concatenate([block, jnp.zeros((rows - block.shape[0], rows), f32)], axis=0)
        v.cols[s] = tall.T
        v.docs[:, s * rows : (s + 1) * rows] = block
    for k in range(1, PLANE):
        slot = v.gain_sum.at[along(k)]
        remote(slot, slot, v.gd_sems[0].at[k], v.gd_sems[1].at[along(k)], sibling).wait_recv()
    for tile in range(2 * PLANE):
        v.gains[:, tile * 128 : (tile + 1) * 128] = v.gain_sum[tile // 2, tile % 2].astype(bf16).astype(f32)
    gain_one, gain_two = v.gains[3:4], v.gains[4:5]

    def first_norm(s):
        values = v.x_all[s].astype(f32)
        v.h1[s] = (values * rms_rows(values) * gain_one).astype(bf16)

    wo_line.forward_all(0)
    wo_plane.start(0)
    first_norm(e)
    for k in (2, 1, 3):
        x_line.forward(0, k)
        first_norm(x_line.near(k))
    up_line.start(0)
    up_line.start(1)
    we_plane.forward(0)
    x_line.wait(0, x_line.sibling())
    first_norm(x_line.sibling())
    for k in range(1, LINE):
        x_line.wait(0, x_line.far(k))
        first_norm(x_line.far(k))
    for k in range(1, PLANE):
        slot = v.w_mine.at[along(k)]
        remote(slot, slot, v.wqd_sems[0].at[k], v.wqd_sems[1].at[along(k)], sibling).wait_recv()

    weights = v.w_mine[...].reshape(D, 256)
    lane = lax.broadcasted_iota(jnp.int32, (QUERY_BLOCK, 128), 1)

    def tables(first):
        cosine, sine = v.cos[first : first + QUERY_BLOCK], v.sin[first : first + QUERY_BLOCK]
        return cosine, sine, jnp.where(lane < HD, cosine, 1.0), jnp.where(lane < HD, sine, 0.0)

    for first in range(0, length, QUERY_BLOCK):
        span = slice(first, first + QUERY_BLOCK)
        slots = slice(first // rows, (first + QUERY_BLOCK) // rows)
        raw = dot(v.h1[slots].reshape(QUERY_BLOCK, D), weights, NN)
        q_cos, q_sin, kv_cos, kv_sin = tables(first)
        q_raw, kv_raw = raw[:, :128], raw[:, 128:]
        v.qkv[span, :128] = (q_raw * q_cos + half_turn_tile(q_raw) * q_sin).astype(bf16)
        v.qkv[span, 128:] = (kv_raw * kv_cos + half_turn_tile(kv_raw) * kv_sin).astype(bf16)


    def block_masks(first):
        low, high = max(0, first - length // 2), first + QUERY_BLOCK
        slots = slice(first // rows, (first + QUERY_BLOCK) // rows)
        docs_col = v.cols[slots, :, 2:3].reshape(QUERY_BLOCK, 1)
        return low, high, slots, visible_keys(first, low, high, v.docs[2:3], docs_col)

    for first in range(0, length, QUERY_BLOCK):
        low, high, slots, visible = block_masks(first)
        span = slice(first, first + QUERY_BLOCK)
        outs, logs = [], []
        for head in range(2):
            q = v.qkv[span, head * HD : (head + 1) * HD]
            scores = dot(q, v.qkv[low:high, 128:192], NT) * HD**-0.5
            scores = jnp.where(visible, scores, -1e30)
            peak = jnp.max(scores, axis=-1, keepdims=True)
            raw = jnp.exp(scores - peak)
            total = jnp.sum(raw, axis=-1, keepdims=True)
            probs = raw * (1.0 / total)
            logs.append(peak + jnp.log(total))
            outs.append(dot(probs.astype(bf16), v.qkv[low:high, 192:256], NN))
        both = jnp.concatenate(outs, axis=1).astype(bf16).reshape(-1, rows, 128)
        v.o_own[slots] = both
        v.o_all[slots, :, own_cols] = both
        v.lse[span] = jnp.where(lane == 0, logs[0], logs[1])
    o_line.start(0)
    o_line.start(1)
    up_line.start(2)
    o_line.start(2)
    up_line.start(3)
    o_line.start(3)
    wo_plane.forward(0)
    we_plane.start(1)

    wo_line.rest(0)
    wo_plane.rest(0)
    for k in range(1, PLANE):
        here = v.wo_all.at[along(k), :, c]
        go(here, here, v.wop_sems[0].at[k], v.wop_sems[1].at[along(k)], sibling)
    for k in range(1, PLANE):
        far = v.wo_all.at[along(k), :, 1 - c]
        remote(far, far, v.wop_sems[0].at[k], v.wop_sems[1].at[along(k)], sibling).wait_recv()

    def second_norm(j):
        part = piece(j, size)
        w_out = v.wo_all[...].reshape(D, D)
        branch = dot(v.o_all[:, part].reshape(-1, D), w_out, NT)
        values = v.x_all[:, part].reshape(-1, D).astype(f32) + branch
        split = values.reshape(SPAN, size, D)
        v.r_own[part] = sum(jnp.where(e == s, split[s], 0.0) for s in range(SPAN))
        v.h2[:, part] = (values * rms_rows(values) * gain_two).astype(bf16).reshape(SPAN, size, D)

    def gate_of(l, part):
        return v.cols[:, part, l : l + 1].reshape(-1, 1)

    def expert(l, j):
        part = piece(j, size)
        weights = v.we_all[l].reshape(D, 3 * FF)
        gate = gate_of(l, part)
        routed = gate > 0
        gu = dot(v.h2[:, part].reshape(-1, D), weights[:, : 2 * FF], NN)
        g, u = gu[:, :FF], gu[:, FF:]
        sig = 1.0 / (1.0 + jnp.exp(-g))
        act = jnp.where(routed, g * sig * u, 0.0).astype(bf16)
        v.act[l, :, part] = act.reshape(SPAN, size, FF)
        dy = (gate * v.up_all[:, part].reshape(-1, D).astype(f32)).astype(bf16)
        dact = dot(dy, weights[:, 2 * FF :], NN)
        dg = dact * u * sig * (1.0 + g * (1.0 - sig))
        du = dact * g * sig
        dgu = jnp.where(routed, jnp.concatenate([dg, du], axis=1), 0.0).astype(bf16)
        v.dgu[l, :, part] = dgu.reshape(SPAN, size, 2 * FF)
        d = dot(dgu, weights[:, : 2 * FF], NT).astype(bf16)
        y = dot(act, weights[:, 2 * FF :], NT).astype(bf16)
        if l == 0:
            v.d[:, part] = d.reshape(SPAN, size, D)
            v.o_all[:, part] = y.reshape(SPAN, size, D)
        else:
            d = v.d[:, part].reshape(-1, D).astype(f32) + d.astype(f32)
            v.d[:, part] = d.astype(bf16).reshape(SPAN, size, D)
            y = gate_of(0, part) * v.o_all[:, part].reshape(-1, D).astype(f32) + gate * y.astype(f32)
            v.o_all[:, part] = y.astype(bf16).reshape(SPAN, size, D)

    we_plane.rest(0)

    def first_round(j, carry):
        @pl.when(j == PARTS - 1)
        def _():
            we_plane.forward(1)

        @pl.when(j < PARTS)
        def _():
            o_line.forward_all(j)
            up_line.forward_all(j)

        @pl.when(j > 0)
        def _():
            o_line.drain(j - 1)
            expert(0, j - 1)

        @pl.when(j < PARTS)
        def _():
            o_line.rest(j)
            up_line.rest(j)
            second_norm(j)

        return carry

    lax.fori_loop(0, PARTS + 1, first_round, 0)
    we_plane.rest(1)

    def expert_chunk(l, there):
        span = piece(there, deep)
        inward = dot(v.h2[:, :, span].reshape(length, deep), v.dgu[l].reshape(length, 2 * FF), TN)
        gate = v.cols[:, :, l : l + 1].reshape(length, 1)
        dy = (gate * v.up_all[:, :, span].reshape(length, deep).astype(f32)).astype(bf16)
        return inward, dot(dy, v.act[l].reshape(length, FF), TN)

    def send_chunk(l, chunk):
        inward, down = expert_chunk(l, (we_plane.far, we_plane.x, we_plane.y)[chunk])
        v.we_all[l, chunk, :, : 2 * FF] = inward.astype(bf16)
        v.we_all[l, chunk, :, 2 * FF :] = down.astype(bf16)
        ge_plane.start(l, chunk)

    def second_round(j, carry):
        @pl.when((j > 0) & (j <= PARTS))
        def _():
            d_scatter.fold(j - 1)

        @pl.when(j > 1)
        def _():
            d_scatter.fold_late(j - 2)

        @pl.when(j < PARTS)
        def _():
            expert(1, j)
            d_scatter.start(j)

        @pl.when(j == 0)
        def _():
            we_plane.drain(0)

        for chunk in range(3):
            pl.when(j == chunk)(lambda chunk=chunk: send_chunk(0, chunk))

        return carry

    lax.fori_loop(0, PARTS + 2, second_round, 0)
    y_scatter.start(0)
    we_plane.drain(1)

    def keep_chunk(l):
        inward, down = expert_chunk(l, i)
        v.ge[l, :, : 2 * FF] = inward
        v.ge[l, :, 2 * FF :] = down

    v.gn_two[...] = jnp.zeros_like(v.gn_two)

    def second_back(j):
        part = piece(j, size)
        back, shares = norm_back(v.r_own[part], gain_two, d_scatter.total(j))
        dr = v.up_all[e, part].astype(f32) + back
        v.dr[part] = dr
        v.gn_two[:1] += jnp.sum(shares, axis=0, keepdims=True)
        v.da_all[e, part] = dr.astype(bf16)
        da_line.start(j)

    send_chunk(1, 0)
    second_back(0)
    ge_plane.combine(0)
    send_chunk(1, 1)
    second_back(1)
    send_chunk(1, 2)
    second_back(2)
    ge_plane.combine(1)
    second_back(3)
    da_line.forward_all(0)
    da_line.forward_all(1)
    keep_chunk(0)
    da_line.forward_all(2)
    keep_chunk(1)
    da_line.forward_all(3)
    y_scatter.fold(0)
    wo_mine = v.wo_all[:, :, :, :, own_cols].reshape(D, 128)
    for j in range(PARTS):
        da_line.rest(j)
        part = piece(j, size)
        do = dot(v.da_all[:, part].reshape(-1, D), wo_mine, NN).astype(bf16)
        v.do[:, part] = do.reshape(SPAN, size, 128)

    v.dkv[...] = jnp.zeros_like(v.dkv)
    for first in range(0, length, QUERY_BLOCK):
        low, high, slots, visible = block_masks(first)
        span = slice(first, first + QUERY_BLOCK)
        keys, values = v.qkv[low:high, 128:192], v.qkv[low:high, 192:256]
        do_both = v.do[slots].reshape(QUERY_BLOCK, 128)
        dqs, dk, dv = [], 0.0, 0.0
        for head in range(2):
            q = v.qkv[span, head * HD : (head + 1) * HD]
            do = do_both[:, head * HD : (head + 1) * HD]
            scores = dot(q, keys, NT) * HD**-0.5
            probs = jnp.exp(jnp.where(visible, scores - v.lse[span, head : head + 1], -1e30))
            dp = dot(do, values, NT)
            delta = jnp.sum(probs * dp, axis=-1, keepdims=True)
            ds = (probs * (dp - delta)).astype(bf16)
            dqs.append(dot(ds, keys, NN))
            dk = dk + dot(ds, q, TN)
            dv = dv + dot(probs.astype(bf16), do, TN)
        v.dkv[low:high] += jnp.concatenate([dk * HD**-0.5, dv], axis=1)
        dq = jnp.concatenate(dqs, axis=1) * HD**-0.5
        cosine, sine = v.cos[span], v.sin[span]
        v.dqkv[span, :128] = (dq * cosine - half_turn_tile(dq) * sine).astype(bf16)
    for first in range(0, length, QUERY_BLOCK):
        span = slice(first, first + QUERY_BLOCK)
        dkv = v.dkv[span]
        _, _, cosine, sine = tables(first)
        v.dqkv[span, 128:] = (dkv * cosine - half_turn_tile(dkv) * sine).astype(bf16)

    y_scatter.fold_late(0)

    o = v.o_own[...].reshape(length, 128)
    dqkv = v.dqkv[...]

    def rows_copy(k):
        return remote(v.ga_out.at[k - 1], v.ga_in.at[k - 1], v.ga_sems[0].at[k], v.ga_sems[1].at[k], (along(k), e))

    for k in (2, 1, 3, 0):
        span = piece(along(k), deep)
        projections = dot(v.h1[:, :, span].reshape(length, deep), dqkv, TN)
        output = dot(v.da_all[:, :, span].reshape(length, deep), o, TN)
        if k == 0:
            v.gs[:, :, :256] = projections.reshape(SPAN, -1, 256)
            v.gs[:, :, 256:] = output.reshape(SPAN, -1, 128)
        else:
            v.ga_out[k - 1, :, :256] = projections.astype(bf16)
            v.ga_out[k - 1, :, 256:] = output.astype(bf16)
            rows_copy(k).start()

    for j in range(PARTS):
        d_scatter.drain(j)
    gn_one = jnp.zeros((1, D), f32)
    order = (1, 3, 2, 0)
    for n, k in enumerate(order):
        chip = lax.rem(z + k, LINE)
        slots = piece(chip, 2)
        dh = dot(v.dqkv[piece(chip, 2 * rows)], weights, NT)
        values = v.x_all[slots].reshape(2 * rows, D).astype(f32)
        gn_one = gn_one + jnp.sum(dh * values * rms_rows(values), axis=0, keepdims=True)
        v.d[slots] = dh.astype(bf16).reshape(2, rows, D)
        h_scatter.start_one(0, k)
        if n > 0:
            h_scatter.fold_one(0, order[n - 1])
    h_scatter.fold_one(0, order[-1])
    both_gains = jnp.concatenate([gn_one, v.gn_two[:1]], axis=0)
    v.gn_in[i] = jnp.concatenate([both_gains[:, t : t + 128] for t in range(0, D, 128)], axis=0)
    for k in range(1, PLANE):
        go(v.gn_in.at[i], v.gn_in.at[i], v.gn_sems[0].at[k], v.gn_sems[1].at[i], (along(k), e))
    v.block[...] = (v.r_own[...] + y_scatter.total(0)).astype(bf16)
    h_scatter.fold_late(0)

    for k in (2, 1, 3):
        rows_copy(k).wait_recv()
        v.gs[...] += v.ga_in[k - 1].reshape(v.gs.shape).astype(f32)
    squares = jnp.sum(v.gs[...] * v.gs[...])
    v.gs_out[...] = v.gs[...].astype(bf16)
    v.ga_all[e] = v.gs_out[e]
    for l in range(local):
        ge_plane.rest(l)
        for first in range(0, deep, 64):
            span = slice(first, first + 64)
            summed = v.ge[l, span]
            for chunk in (1, 2):
                summed = summed + v.ge_in[l, chunk, span].astype(f32)
            v.ge[l, span] = summed
            squares = squares + jnp.sum(summed * summed)
        results[l].start()

    for k in range(1, PLANE):
        slot = v.gn_in.at[along(k)]
        remote(slot, slot, v.gn_sems[0].at[k], v.gn_sems[1].at[along(k)], sibling).wait_recv()
    gains = v.gn_in[0] + v.gn_in[1] + v.gn_in[2] + v.gn_in[3]
    v.mix_in[e] = jnp.concatenate([gains, jnp.full((8, 128), squares)], axis=0)
    for k in range(1, SPAN):
        go(v.mix_in.at[e], v.mix_in.at[e], v.mix_sems[0].at[k], v.mix_sems[1].at[e], (i, across(k)))
    for k in range(1, SPAN):
        go(v.gs_out.at[across(k)], v.ga_all.at[e], v.gs_sems[0].at[k], v.gs_sems[1].at[e], (i, across(k)))
    for k in range(1, SPAN):
        slot = v.mix_in.at[across(k)]
        remote(slot, slot, v.mix_sems[0].at[k], v.mix_sems[1].at[across(k)], sibling).wait_recv()
    mixed = v.mix_in[0]
    for s in range(1, SPAN):
        mixed = mixed + v.mix_in[s]
    v.sq_in[i] = mixed[16:]
    for k in range(1, PLANE):
        go(v.sq_in.at[i], v.sq_in.at[i], v.sq_sems[0].at[k], v.sq_sems[1].at[i], (along(k), e))
    gain_squares = jnp.sum(mixed[:16] * mixed[:16])
    row = lax.broadcasted_iota(jnp.int32, (16, 128), 0)
    pick = lambda n: jnp.sum(jnp.where(row == index // few * 2 + n, mixed[:16], 0.0), axis=0, keepdims=True)
    own_gains = jnp.concatenate([pick(0), pick(1), jnp.zeros((6, 128), f32)], axis=0)
    v.gn[...] = pltpu.roll(own_gains, rows - lax.rem(index, few) * (rows // few), 1)
    for k in range(1, SPAN):
        slot = v.ga_all.at[across(k)]
        remote(slot, slot, v.gs_sems[0].at[k], v.gs_sems[1].at[across(k)], sibling).wait_recv()
    for g in range(SPAN):
        v.ga[:, g * 128 : (g + 1) * 128] = v.ga_all[g, :, :128].astype(f32)
        v.ga[:, QKV + g * 128 : QKV + (g + 1) * 128] = v.ga_all[g, :, 256:].astype(f32)
    for g in range(0, SPAN, 2):
        for first, own in ((QD, 128), (QD + KVD, 192)):
            heads = [v.ga_all[g + n, :, own : own + HD] for n in range(2)]
            v.ga[:, first + g * HD : first + (g + 2) * HD] = jnp.concatenate(heads, axis=1).astype(f32)
    for k in range(1, PLANE):
        slot = v.sq_in.at[along(k)]
        remote(slot, slot, v.sq_sems[0].at[k], v.sq_sems[1].at[along(k)], sibling).wait_recv()
    norm = jnp.sqrt(v.sq_in[0] + v.sq_in[1] + v.sq_in[2] + v.sq_in[3] + gain_squares)[:1, :1]
    v.norm[...] = norm
    v.clip[...] = jnp.minimum(1.0, CLIP_NORM / (norm + 1e-06))

    back, _ = norm_back(v.x_all[e].astype(f32), gain_one, h_scatter.total(0))
    v.grad[...] = v.dr[...] + back
    for copy in results:
        copy.wait()
    for copy in live:
        copy.wait_send()
    for k in (2, 1, 3):
        rows_copy(k).wait_send()
    for l in range(local):
        ge_plane.drain(l)
    for item in (x_line, wo_line, wo_plane, y_scatter, h_scatter):
        item.drain(0)
    for j in range(PARTS):
        up_line.drain(j)
        da_line.drain(j)


def call_layer(*args):
    vmem, anywhere = pl.BlockSpec(memory_space=pltpu.VMEM), pl.BlockSpec(memory_space=pl.ANY)
    rows, local = args[0].shape[0], args[3].shape[0]
    outs = layer_outputs(rows, local)
    return pl.pallas_call(
        layer_kernel,
        out_shape=outs,
        in_specs=[anywhere if n == 3 else vmem for n in range(len(args))],
        out_specs=[anywhere if n == 3 else vmem for n in range(len(outs))],
        scratch_shapes=layer_scratch(rows, local),
        compiler_params=pltpu.CompilerParams(
            collective_id=0, has_side_effects=True, vmem_limit_bytes=63 * 2**20 + 2**19
        ),
        name="layer",
    )(*args)


def small_kernel(clip, rates, gn, block_in, grad_in, wa, ma, va, ga, wg, mg, vg, block, grad, *outs):
    c, one, two = clip[...], rates[:1, :1], rates[:1, 1:2]

    def update(refs, gradient, decay, rate, results):
        w, g = refs[0][...], gradient * c
        first = BETA_ONE * refs[1][...] + (1.0 - BETA_ONE) * g
        second = BETA_TWO * refs[2][...] + (1.0 - BETA_TWO) * g * g
        step = (first * one) / (jnp.sqrt(second * two) + ADAM_EPSILON)
        results[0][...] = w - rate * (step + decay * w)
        results[1][...] = first
        results[2][...] = second

    update((wa, ma, va), ga[...], WEIGHT_DECAY, LEARN_RATE, outs[:3])
    update((wg, mg, vg), gn[: wg.shape[0], : wg.shape[1]], 0.0, GAIN_RATE, outs[3:])
    block[...] = block_in[...]
    grad[...] = grad_in[...]


def call_small(clip, rates, gn, block, grad, attn, ga, gains):
    vmem = pl.BlockSpec(memory_space=pltpu.VMEM)
    outs = [jax.ShapeDtypeStruct(a.shape, a.dtype) for a in (block, grad, *attn, *gains)]
    args = (clip, rates, gn, block, grad, *attn, ga, *gains)
    return pl.pallas_call(
        small_kernel,
        out_shape=outs,
        in_specs=[vmem] * len(args),
        out_specs=[vmem] * len(outs),
        compiler_params=pltpu.CompilerParams(vmem_limit_bytes=63 * 2**20 + 2**19),
        name="small",
    )(*args)


def fast_body(
    activations,
    doc_ids,
    routes,
    gate_weights,
    cotangent,
    step_count,
    w_attn,
    norm_gains,
    w_expert,
    first_attn,
    second_attn,
    first_gains,
    second_gains,
    first_expert,
    second_expert,
):
    cosine, sine = head_tables(activations.shape[1] * lax.axis_size("expert"))
    block, input_total, norm, grad_expert, grad_attn, gn, clip = call_layer(
        activations[0], cotangent[0], w_attn, w_expert, routes[0].T, gate_weights[0].T, doc_ids, norm_gains.T,
        cosine, sine,
    )
    grad_norm = norm.reshape(())
    steps = step_count.astype(jnp.float32)
    rates = 1.0 / (1.0 - jnp.stack([BETA_ONE**steps, BETA_TWO**steps]))[None]
    block, input_total, *small = call_small(
        clip, rates, gn, block, input_total,
        (w_attn, first_attn, second_attn), grad_attn, (norm_gains.T, first_gains.T, second_gains.T),
    )
    attn, gain = small[:3], small[3:]
    expert = adam_update(
        w_expert, first_expert, second_expert, grad_expert * clip[None], steps, WEIGHT_DECAY, LEARN_RATE
    )
    return (block[None], input_total[None], grad_norm, *attn, *[a.T for a in gain], *expert)


def solution(mesh):
    in_specs = (
        P("dp", "expert", None),
        P("dp", "expert"),
        P("dp", "expert", None),
        P("dp", "expert", None),
        P("dp", "expert", None),
        P(),
        P(("dp", "expert"), None),
        P(("dp", "expert"), None),
        P("expert", "dp", None),
        P(("dp", "expert"), None),
        P(("dp", "expert"), None),
        P(("dp", "expert"), None),
        P(("dp", "expert"), None),
        P("expert", "dp", None),
        P("expert", "dp", None),
    )
    out_specs = (
        P("dp", "expert", None),
        P("dp", "expert", None),
        P(),
        P(("dp", "expert"), None),
        P(("dp", "expert"), None),
        P(("dp", "expert"), None),
        P(("dp", "expert"), None),
        P(("dp", "expert"), None),
        P(("dp", "expert"), None),
        P("expert", "dp", None),
        P("expert", "dp", None),
        P("expert", "dp", None),
    )
    body = fast_body if fits(mesh) else general_body
    return jax.shard_map(body, mesh=mesh, in_specs=in_specs, out_specs=out_specs, check_vma=False)
```

```python
import jax
import jax.numpy as jnp
from jax import lax
from jax.sharding import PartitionSpec as P
import types

import numpy as np
from jax.experimental import pallas as pl
from jax.experimental.pallas import tpu as pltpu

D = 1024
H = 16
KVH = 8
HD = 64
FF = 512
TOP = 8
QD = 1024
KVD = 512
QKV = 2048


EPSILON = 1e-05
ROPE_BASE = 10000.0
CLIP_NORM = 1.0
BETA_ONE = 0.9
BETA_TWO = 0.95
ADAM_EPSILON = 1e-08
LEARN_RATE = 0.03
GAIN_RATE = 0.4
WEIGHT_DECAY = 0.1


def rms_scale(values, gain):
    return values * lax.rsqrt(jnp.mean(values * values, axis=-1, keepdims=True) + EPSILON) * gain


def rope_tables(positions, head_width):
    halves = jnp.arange(head_width // 2, dtype=jnp.float32)
    inverse = ROPE_BASE ** (-2.0 * halves / head_width)
    angles = positions.astype(jnp.float32)[:, None] * inverse[None, :]
    angles = jnp.concatenate([angles, angles], axis=-1)
    return (jnp.cos(angles)[:, None, :], jnp.sin(angles)[:, None, :])


def rotate(values, cosine, sine_table):
    middle = values.shape[-1] // 2
    turned = jnp.concatenate([-values[..., middle:], values[..., :middle]], axis=-1)
    return values * cosine + turned * sine_table


def unrotate(gradient, cosine, sine_table):
    middle = gradient.shape[-1] // 2
    product = gradient * sine_table
    turned = jnp.concatenate([product[..., middle:], -product[..., :middle]], axis=-1)
    return gradient * cosine + turned


def adam_update(weight, moment_one, second, gradient, steps_done, decay_rate, step_rate):
    first_new = BETA_ONE * moment_one + (1.0 - BETA_ONE) * gradient
    second_new = BETA_TWO * second + (1.0 - BETA_TWO) * gradient * gradient
    first_hat = first_new / (1.0 - BETA_ONE**steps_done)
    second_hat = second_new / (1.0 - BETA_TWO**steps_done)
    weight_new = weight - step_rate * (
        first_hat / (jnp.sqrt(second_hat) + ADAM_EPSILON) + decay_rate * weight
    )
    return (weight_new, first_new, second_new)


def attn_fetch(w_attn, norm_gains):
    return (
        lax.all_gather(w_attn.astype(jnp.bfloat16), ("dp", "expert"), axis=0, tiled=True),
        lax.all_gather(norm_gains.astype(jnp.bfloat16), ("dp", "expert"), axis=0, tiled=True),
    )


def expert_fetch(w_expert):
    return lax.all_gather(w_expert.astype(jnp.bfloat16), "dp", axis=1, tiled=True)


def to_owner(buffer):
    return lax.all_to_all(buffer, "expert", split_axis=0, concat_axis=1, tiled=True)


def to_sender(buffer):
    return lax.all_to_all(buffer, "expert", split_axis=1, concat_axis=0, tiled=True)


def expert_forward(received, expert_cols):
    gate_up = jnp.einsum(
        "esd,edf->esf", received, expert_cols[:, :, : 2 * FF], preferred_element_type=jnp.float32
    )
    activated = (jax.nn.silu(gate_up[..., :FF]) * gate_up[..., FF:]).astype(jnp.bfloat16)
    return (gate_up, activated)


def general_body(
    activations,
    doc_ids,
    routes,
    gate_weights,
    cotangent,
    step_count,
    w_attn,
    norm_gains,
    w_expert,
    first_attn,
    second_attn,
    first_gains,
    second_gains,
    first_expert,
    second_expert,
):
    row_count = activations.shape[1]
    span_size = lax.axis_size("expert")
    shard_pos = lax.axis_index("expert")
    seq_length = row_count * span_size
    expert_total = w_expert.shape[0] * span_size
    capacity = (row_count * TOP * 9 + expert_total * 8 - 1) // (expert_total * 8)
    group_size = H // KVH
    score_scale = HD ** (-0.5)
    hidden_in = activations[0].astype(jnp.float32)
    upstream = cotangent[0].astype(jnp.float32)
    attn_cols, gain_pair = attn_fetch(w_attn, norm_gains)
    expert_cols = expert_fetch(w_expert)
    gain_one = gain_pair[:, 0].astype(jnp.float32)
    gain_two = gain_pair[:, 1].astype(jnp.float32)
    w_project = attn_cols[:, :QKV]
    w_output = attn_cols[:, QKV:]
    normed = rms_scale(hidden_in, gain_one).astype(jnp.bfloat16)
    projected = jnp.dot(normed, w_project, preferred_element_type=jnp.float32)
    positions = shard_pos * row_count + jnp.arange(row_count, dtype=jnp.int32)
    cosine, sine_table = rope_tables(positions, HD)
    queries = rotate(projected[:, :QD].reshape(row_count, H, HD), cosine, sine_table).astype(
        jnp.bfloat16
    )
    key_heads = rotate(
        projected[:, QD : QD + KVD].reshape(row_count, KVH, HD), cosine, sine_table
    ).astype(jnp.bfloat16)
    value_heads = projected[:, QD + KVD :].astype(jnp.bfloat16)
    key_all, value_all, doc_all = (
        lax.all_gather(key_heads.reshape(row_count, KVD), "expert", axis=0, tiled=True),
        lax.all_gather(value_heads, "expert", axis=0, tiled=True),
        lax.all_gather(doc_ids[0].astype(jnp.bfloat16), "expert", axis=0, tiled=True),
    )
    key_docs = doc_all.astype(jnp.int32)
    query_docs = doc_ids[0]
    query_groups = queries.reshape(row_count, KVH, group_size, HD)
    key_block = min(512, seq_length)
    needed = (shard_pos * row_count + row_count + key_block - 1) // key_block

    def block_scores(block_id):
        first_key = block_id * key_block
        key_part = lax.dynamic_slice_in_dim(key_all, first_key, key_block, 0).reshape(
            key_block, KVH, HD
        )
        raw_scores = (
            jnp.einsum("tgrd,kgd->grtk", query_groups, key_part, preferred_element_type=jnp.float32)
            * score_scale
        )
        key_pos = first_key + jnp.arange(key_block, dtype=jnp.int32)
        key_doc = lax.dynamic_slice_in_dim(key_docs, first_key, key_block, 0)
        visible = (key_pos[None, :] <= positions[:, None]) & (
            key_doc[None, :] == query_docs[:, None]
        )
        return (raw_scores, visible, key_part)

    def value_part(block_id):
        return lax.dynamic_slice_in_dim(value_all, block_id * key_block, key_block, 0).reshape(
            key_block, KVH, HD
        )

    def total_step(block_id, running):
        row_peak, row_total = running
        raw_scores, visible, _ = block_scores(block_id)
        masked = jnp.where(visible, raw_scores, -1e30)
        new_peak = jnp.maximum(row_peak, jnp.max(masked, axis=-1))
        scaled = jnp.where(visible, jnp.exp(masked - new_peak[..., None]), 0.0)
        return (new_peak, row_total * jnp.exp(row_peak - new_peak) + jnp.sum(scaled, axis=-1))

    start_peak = jnp.full((KVH, group_size, row_count), -1e30, jnp.float32)
    start_total = jnp.zeros((KVH, group_size, row_count), jnp.float32)
    row_peak, row_total = lax.fori_loop(0, needed, total_step, (start_peak, start_total))
    log_total = row_peak + jnp.log(row_total)

    def exact_probs(raw_scores, visible):
        return jnp.exp(jnp.where(visible, raw_scores - log_total[..., None], -1e30))

    def output_step(block_id, summed):
        raw_scores, visible, _ = block_scores(block_id)
        weights_low = exact_probs(raw_scores, visible).astype(jnp.bfloat16)
        return summed + jnp.einsum(
            "grtk,kgd->tgrd", weights_low, value_part(block_id), preferred_element_type=jnp.float32
        )

    attended = lax.fori_loop(
        0, needed, output_step, jnp.zeros((row_count, KVH, group_size, HD), jnp.float32)
    )
    attended = attended.reshape(row_count, QD).astype(jnp.bfloat16)
    branch = jnp.einsum("tc,dc->td", attended, w_output, preferred_element_type=jnp.float32)
    residual = hidden_in + branch
    normed_two = rms_scale(residual, gain_two).astype(jnp.bfloat16)
    flat_routes = routes[0].reshape(-1)
    one_hot = (flat_routes[:, None] == jnp.arange(expert_total, dtype=jnp.int32)[None, :]).astype(
        jnp.int32
    )
    ranking = jnp.sum((jnp.cumsum(one_hot, axis=0) - 1) * one_hot, axis=1)
    places = flat_routes * capacity + ranking
    owners = jnp.arange(row_count * TOP, dtype=jnp.int32) // TOP
    source = jnp.zeros((expert_total * capacity,), jnp.int32).at[places].set(owners)
    filled = jnp.zeros((expert_total * capacity,), jnp.int32).at[places].set(1) > 0
    slot_gate = (
        jnp.zeros((expert_total * capacity,), jnp.float32)
        .at[places]
        .set(gate_weights[0].reshape(-1))
    )
    outgoing = jnp.where(filled[:, None], normed_two[source], jnp.zeros((), jnp.bfloat16)).reshape(
        expert_total, capacity, D
    )
    received = to_owner(outgoing)
    gate_up, activated = expert_forward(received, expert_cols)
    expert_out = jnp.einsum(
        "esf,edf->esd", activated, expert_cols[:, :, 2 * FF :], preferred_element_type=jnp.float32
    ).astype(jnp.bfloat16)
    returned = to_sender(expert_out).reshape(expert_total * capacity, D)
    picked = returned[places].reshape(row_count, TOP, D).astype(jnp.float32)
    combined = jnp.sum(gate_weights[0][..., None] * picked, axis=1)
    block_result = (residual + combined).astype(jnp.bfloat16)
    slot_grad = jnp.where(filled[:, None], slot_gate[:, None] * upstream[source], 0.0)
    slot_grad = slot_grad.astype(jnp.bfloat16).reshape(expert_total, capacity, D)
    owner_grad = to_owner(slot_grad)
    attn_cols, gain_pair = attn_fetch(w_attn, norm_gains)
    w_project = attn_cols[:, :QKV]
    w_output = attn_cols[:, QKV:]
    expert_cols = expert_fetch(w_expert)
    gate_up, activated = expert_forward(received, expert_cols)
    gate_part = gate_up[..., :FF]
    up_part = gate_up[..., FF:]
    sigmoid_gate = jax.nn.sigmoid(gate_part)
    act_grad = jnp.einsum(
        "esd,edf->esf", owner_grad, expert_cols[:, :, 2 * FF :], preferred_element_type=jnp.float32
    )
    gate_grad = act_grad * up_part * sigmoid_gate * (1.0 + gate_part * (1.0 - sigmoid_gate))
    lift_grad = act_grad * gate_part * sigmoid_gate
    mixed_grad = jnp.concatenate([gate_grad, lift_grad], axis=-1).astype(jnp.bfloat16)
    down_grad = jnp.einsum(
        "esf,esd->edf", activated, owner_grad, preferred_element_type=jnp.float32
    )
    inward_grad = jnp.einsum(
        "esd,esf->edf", received, mixed_grad, preferred_element_type=jnp.float32
    )
    row_grads = jnp.einsum(
        "esf,edf->esd", mixed_grad, expert_cols[:, :, : 2 * FF], preferred_element_type=jnp.float32
    ).astype(jnp.bfloat16)
    back_rows = to_sender(row_grads).reshape(expert_total * capacity, D)
    normed_two_grad = jnp.sum(
        back_rows[places].reshape(row_count, TOP, D).astype(jnp.float32), axis=1
    )
    _, second_pull = jax.vjp(rms_scale, residual, gain_two)
    resid_grad, gain_two_grad = second_pull(normed_two_grad)
    resid_grad = upstream + resid_grad
    branch_grad = resid_grad.astype(jnp.bfloat16)
    output_grad = jnp.einsum("td,tc->dc", branch_grad, attended, preferred_element_type=jnp.float32)
    attended_grad = jnp.dot(branch_grad, w_output, preferred_element_type=jnp.float32).astype(
        jnp.bfloat16
    )
    grad_groups = attended_grad.reshape(row_count, KVH, group_size, HD)

    def delta_step(block_id, summed):
        raw_scores, visible, _ = block_scores(block_id)
        probs_full = exact_probs(raw_scores, visible)
        prob_grad = jnp.einsum(
            "tgrd,kgd->grtk", grad_groups, value_part(block_id), preferred_element_type=jnp.float32
        )
        return summed + jnp.sum(probs_full * prob_grad, axis=-1)

    delta_rows = lax.fori_loop(
        0, needed, delta_step, jnp.zeros((KVH, group_size, row_count), jnp.float32)
    )

    def grad_step(block_id, running):
        query_grad, key_grad, value_grad = running
        raw_scores, visible, key_part = block_scores(block_id)
        probs_full = exact_probs(raw_scores, visible)
        prob_grad = jnp.einsum(
            "tgrd,kgd->grtk", grad_groups, value_part(block_id), preferred_element_type=jnp.float32
        )
        score_grad = (probs_full * (prob_grad - delta_rows[..., None])).astype(jnp.bfloat16)
        query_grad = (
            query_grad
            + jnp.einsum("grtk,kgd->tgrd", score_grad, key_part, preferred_element_type=jnp.float32)
            * score_scale
        )
        key_piece = (
            jnp.einsum(
                "grtk,tgrd->kgd", score_grad, query_groups, preferred_element_type=jnp.float32
            )
            * score_scale
        )
        value_piece = jnp.einsum(
            "grtk,tgrd->kgd",
            probs_full.astype(jnp.bfloat16),
            grad_groups,
            preferred_element_type=jnp.float32,
        )
        first_key = block_id * key_block
        key_grad = lax.dynamic_update_slice_in_dim(
            key_grad, key_piece.reshape(key_block, KVD), first_key, 0
        )
        value_grad = lax.dynamic_update_slice_in_dim(
            value_grad, value_piece.reshape(key_block, KVD), first_key, 0
        )
        return (query_grad, key_grad, value_grad)

    start_grads = (
        jnp.zeros((row_count, KVH, group_size, HD), jnp.float32),
        jnp.zeros((seq_length, KVD), jnp.float32),
        jnp.zeros((seq_length, KVD), jnp.float32),
    )
    query_grad, key_grad, value_grad = lax.fori_loop(0, needed, grad_step, start_grads)
    key_sum, value_sum = (
        lax.psum_scatter(key_grad, "expert", scatter_dimension=0, tiled=True),
        lax.psum_scatter(value_grad, "expert", scatter_dimension=0, tiled=True),
    )
    query_back = unrotate(query_grad.reshape(row_count, H, HD), cosine, sine_table).reshape(
        row_count, QD
    )
    key_back = unrotate(key_sum.reshape(row_count, KVH, HD), cosine, sine_table).reshape(
        row_count, KVD
    )
    project_grad = jnp.concatenate([query_back, key_back, value_sum], axis=1).astype(jnp.bfloat16)
    weight_grad_qkv = jnp.einsum(
        "td,tc->dc", normed, project_grad, preferred_element_type=jnp.float32
    )
    normed_grad = jnp.einsum(
        "tc,dc->td", project_grad, w_project, preferred_element_type=jnp.float32
    )
    _, first_pull = jax.vjp(rms_scale, hidden_in, gain_one)
    input_part, gain_one_grad = first_pull(normed_grad)
    input_total = resid_grad + input_part
    attn_partial = jnp.concatenate([weight_grad_qkv, output_grad], axis=1)
    gain_partial = jnp.stack([gain_one_grad, gain_two_grad], axis=1)
    grad_attn, grad_gains = (
        lax.psum_scatter(attn_partial, ("dp", "expert"), scatter_dimension=0, tiled=True),
        lax.psum_scatter(gain_partial, ("dp", "expert"), scatter_dimension=0, tiled=True),
    )
    grad_expert = lax.psum_scatter(
        jnp.concatenate([inward_grad, down_grad], axis=2).astype(jnp.bfloat16),
        "dp",
        scatter_dimension=1,
        tiled=True,
    ).astype(jnp.float32)
    local_squares = (
        jnp.sum(grad_attn * grad_attn)
        + jnp.sum(grad_gains * grad_gains)
        + jnp.sum(grad_expert * grad_expert)
    )
    grad_norm = jnp.sqrt(lax.psum(local_squares, ("dp", "expert")))
    clip_factor = jnp.minimum(1.0, CLIP_NORM / (grad_norm + 1e-06))
    steps_done = step_count.astype(jnp.float32)
    attn_new = adam_update(
        w_attn,
        first_attn,
        second_attn,
        grad_attn * clip_factor,
        steps_done,
        WEIGHT_DECAY,
        LEARN_RATE,
    )
    gains_new = adam_update(
        norm_gains, first_gains, second_gains, grad_gains * clip_factor, steps_done, 0.0, GAIN_RATE
    )
    expert_new = adam_update(
        w_expert,
        first_expert,
        second_expert,
        grad_expert * clip_factor,
        steps_done,
        WEIGHT_DECAY,
        LEARN_RATE,
    )
    return (
        block_result[None],
        input_total[None],
        grad_norm,
        attn_new[0],
        attn_new[1],
        attn_new[2],
        gains_new[0],
        gains_new[1],
        gains_new[2],
        expert_new[0],
        expert_new[1],
        expert_new[2],
    )


def fits(mesh):
    return dict(mesh.shape) == {"dp": 4, "expert": KVH}


def head_tables(length):
    halves = np.arange(HD // 2, dtype=np.float32)
    inverse = np.power(np.float32(ROPE_BASE), np.float32(-2.0) * halves / np.float32(HD))
    angles = np.arange(length, dtype=np.float32)[:, None] * inverse[None, :]
    cosine, sine = np.cos(angles), np.sin(angles)
    cosine = np.concatenate([cosine] * 4, axis=1)
    return jnp.asarray(cosine), jnp.asarray(np.concatenate([-sine, sine] * 2, axis=1))


LINE, SPAN, PLANE, PARTS = 4, 8, 4, 4
QUERY_BLOCK = 256
NN, NT, TN = ((1,), (0,)), ((1,), (1,)), ((0,), (0,))


def remote(source, target, sent, landed, device):
    return pltpu.make_async_remote_copy(
        src_ref=source,
        dst_ref=target,
        send_sem=sent,
        recv_sem=landed,
        device_id=device,
        device_id_type=pl.DeviceIdType.MESH,
    )


def whereabouts():
    i, e = lax.axis_index("dp"), lax.axis_index("expert")
    return i, e, e // 2, lax.rem(e, 2)


def partners(i, e):
    others = [(i, lax.rem(e + k, SPAN)) for k in range(1, SPAN)]
    return others + [(lax.rem(i + k, PLANE), e) for k in range(1, PLANE)]


def piece(j, size):
    return pl.ds(pl.multiple_of(j * size, size), size)


class LineGather:
    def __init__(self, slot, source, where, sems):
        self.slot, self.source, self.where = slot, source, where
        self.sent, self.passed, self.landed = sems

    def _own(self, j, k):
        i, e, z, c = self.where
        there = z * 2 + 1 - c if k == 0 else lax.rem(z + k, LINE) * 2 + c
        return remote(self.source(j), self.slot(e, j), self.sent.at[j, k], self.landed.at[j, e], (i, there))

    def _pass(self, j, k):
        i, e, z, c = self.where
        index = lax.rem(z + k, LINE) * 2 + c
        place = self.slot(index, j)
        return remote(place, place, self.passed.at[j, k], self.landed.at[j, index], (i, z * 2 + 1 - c))

    def _relay(self, j):
        i, e, z, c = self.where
        index = lax.rem(z + 2, LINE) * 2 + c
        place = self.slot(index, j)
        end = LINE - 1 - lax.rem(z + 2, LINE)
        return remote(place, place, self.passed.at[j, 0], self.landed.at[j, index], (i, end * 2 + c))

    def _each_own(self, j, act):
        z = self.where[2]
        act(self._own(j, 2))
        pl.when(z != LINE - 1)(lambda: act(self._own(j, 1)))
        pl.when(z != 0)(lambda: act(self._own(j, 3)))
        act(self._own(j, 0))

    def _when_inner(self, act):
        z = self.where[2]
        pl.when((z > 0) & (z < LINE - 1))(act)

    def start(self, j):
        self._each_own(j, lambda copy: copy.start())

    def wait(self, j, index):
        i, e, z, c = self.where
        place = self.slot(index, j)
        remote(place, place, self.sent.at[j, 0], self.landed.at[j, index], (i, z * 2 + 1 - c)).wait_recv()

    def sibling(self):
        _, e, z, c = self.where
        return z * 2 + 1 - c

    def near(self, k):
        _, e, z, c = self.where
        return lax.rem(z + k, LINE) * 2 + c

    def far(self, k):
        _, e, z, c = self.where
        return lax.rem(z + k, LINE) * 2 + 1 - c

    def forward(self, j, k):
        self.wait(j, self.near(k))
        if k == 2:
            self._when_inner(lambda: self._relay(j).start())
        self._pass(j, k).start()

    def forward_all(self, j):
        for k in (2, 1, 3):
            self.forward(j, k)

    def rest(self, j):
        self.wait(j, self.sibling())
        for k in range(1, LINE):
            self.wait(j, self.far(k))

    def drain(self, j):
        self._each_own(j, lambda copy: copy.wait_send())
        self._when_inner(lambda: self._relay(j).wait_send())
        for k in range(1, LINE):
            self._pass(j, k).wait_send()


class LineScatter:
    def __init__(self, data, where, pair, out, inbox, own, sems, size):
        self.data, self.where, self.size = data, where, size
        self.pair, self.out, self.inbox, self.own = pair, out, inbox, own
        self.pair_sent, self.pair_landed, self.sent, self.landed = sems

    def _pair(self, j, k):
        i, e, z, c = self.where
        there, rows = lax.rem(z + k, LINE), piece(j, self.size)
        return remote(
            self.data.at[there * 2 + 1 - c, rows], self.pair.at[there, rows],
            self.pair_sent.at[j, there], self.pair_landed.at[j, there], (i, z * 2 + 1 - c),
        )

    def _send(self, j, k):
        i, e, z, c = self.where
        there, rows = lax.rem(z + k, LINE), piece(j, self.size)
        crossing = {1: z // (LINE - 1), 2: 0, 3: (LINE - 1 - z) // (LINE - 1)}[k]
        chip = {1: z + 1 - 2 * crossing, 2: there, 3: z - 1 + 2 * crossing}[k]
        slot = z + crossing * (chip - z)
        return remote(
            self.out.at[there, rows], self.inbox.at[slot, rows],
            self.sent.at[j, there], self.landed.at[j, slot], (i, chip * 2 + c),
        )

    def _landed(self, j, slot):
        i, e, z, c = self.where
        place = self.inbox.at[slot, piece(j, self.size)]
        remote(place, place, self.sent.at[j, slot], self.landed.at[j, slot], (i, z * 2 + 1 - c)).wait_recv()

    def _both(self, j, there):
        c, rows = self.where[3], piece(j, self.size)
        return self.data[there * 2 + c, rows].astype(jnp.float32) + self.pair[there, rows].astype(jnp.float32)

    def _across(self, j):
        there, rows = lax.rem(self.where[2] + 2, LINE), piece(j, self.size)
        return there, rows, self._both(j, there)

    def start(self, j):
        for k in (1, 3, 2, 0):
            self._pair(j, k).start()

    def start_one(self, j, k):
        self._pair(j, k).start()

    def fold_one(self, j, k):
        z, rows = self.where[2], piece(j, self.size)
        self._pair(j, k).wait_recv()

        def send():
            there = lax.rem(z + k, LINE)
            self.out[there, rows] = self._both(j, there).astype(jnp.bfloat16)
            self._send(j, k).start()

        if k == 0:
            self.own[rows] = self._both(j, z)
        elif k == 2:
            pl.when((z == 0) | (z == LINE - 1))(send)
        else:
            send()

    def fold(self, j):
        for k in (1, 3, 2, 0):
            self.fold_one(j, k)

    def fold_late(self, j):
        z = self.where[2]

        @pl.when((z > 0) & (z < LINE - 1))
        def _():
            there, rows, both = self._across(j)
            self._landed(j, z)
            self.out[there, rows] = (both + self.inbox[z, rows].astype(jnp.float32)).astype(jnp.bfloat16)
            self._send(j, 2).start()

    def total(self, j):
        z, rows = self.where[2], piece(j, self.size)

        def add(k):
            there = lax.rem(z + k, LINE)
            self._landed(j, there)
            self.own[rows] += self.inbox[there, rows].astype(jnp.float32)

        pl.when(z != LINE - 1)(lambda: add(1))
        pl.when(z != 0)(lambda: add(3))
        add(2)
        return self.own[rows]

    def drain(self, j):
        for k in range(LINE):
            self._pair(j, k).wait_send()
        for k in range(1, LINE):
            self._send(j, k).wait_send()


class PlaneGather:
    def __init__(self, where, slot, size, sems):
        i, self.e = where[0], where[1]
        self.i, self.slot, self.sems = i, slot, sems
        self.x = i // 2 * 2 + 1 - lax.rem(i, 2)
        self.y = (1 - i // 2) * 2 + lax.rem(i, 2)
        self.far = PLANE - 1 - i
        self.half = size // 2

    def _copy(self, l, n, source):
        rows = (slice(None), slice(None), slice(0, self.half), slice(self.half, None))[n]
        to = (self.x, self.y, self.y, self.x)[n]
        sent, landed = self.sems
        place = self.slot(l, source, rows)
        return remote(place, place, sent.at[l, n], landed.at[l, n], (to, self.e))

    def start(self, l):
        self._copy(l, 0, self.i).start()
        self._copy(l, 1, self.i).start()

    def forward(self, l):
        self._copy(l, 0, self.x).wait_recv()
        self._copy(l, 2, self.x).start()
        self._copy(l, 1, self.y).wait_recv()
        self._copy(l, 3, self.y).start()

    def rest(self, l):
        self._copy(l, 2, self.far).wait_recv()
        self._copy(l, 3, self.far).wait_recv()

    def drain(self, l):
        for n, source in enumerate((self.i, self.i, self.x, self.y)):
            self._copy(l, n, source).wait_send()


class PlaneScatter:
    def __init__(self, plane, out, inbox, sems):
        self.plane, self.out, self.inbox = plane, out, inbox
        self.sent, self.landed = sems
        self.half = plane.half

    def _copy(self, l, chunk, part, n):
        first = slice(0, self.half) if part == 0 else slice(self.half, None)
        to_x = chunk == 1 or (chunk == 0 and part == 0)
        return remote(
            self.out.at[l, chunk, first], self.inbox.at[l, chunk, first], self.sent.at[l, n], self.landed.at[l, n],
            (self.plane.x if to_x else self.plane.y, self.plane.e),
        )

    def _at(self, l, chunk, part):
        return self._copy(l, chunk, part, chunk * 2 + part)

    def start(self, l, chunk):
        for part in ((0, 1), (0,), (1,))[chunk]:
            self._at(l, chunk, part).start()

    def combine(self, l):
        for chunk, part in ((1, 1), (2, 0)):
            rows = slice(part * self.half, (part + 1) * self.half)
            self._at(l, 0, part).wait_recv()
            mine = self.out[l, chunk, rows].astype(jnp.float32) + self.inbox[l, 0, rows].astype(jnp.float32)
            self.out[l, chunk, rows] = mine.astype(jnp.bfloat16)
            self._at(l, chunk, part).start()

    def rest(self, l):
        for chunk in (1, 2):
            for part in (0, 1):
                self._at(l, chunk, part).wait_recv()

    def drain(self, l):
        for chunk in range(3):
            for part in (0, 1):
                self._at(l, chunk, part).wait_send()


def half_turn_tile(part):
    lane = lax.broadcasted_iota(jnp.int32, part.shape, 1)
    ahead = pltpu.roll(part, 128 - HD // 2, 1)
    behind = pltpu.roll(part, HD // 2, 1)
    return jnp.where(lax.rem(lane, HD) < HD // 2, ahead, behind)


def rms_rows(values):
    return lax.rsqrt(jnp.mean(values * values, axis=-1, keepdims=True) + EPSILON)


def norm_back(values, gain, upper):
    scale = rms_rows(values)
    scaled = upper * gain
    inner = jnp.mean(values * scaled, axis=-1, keepdims=True)
    return scale * scaled - values * (scale * scale * scale) * inner, upper * values * scale


def dot(a, b, contract):
    return lax.dot_general(a, b, (contract, ((), ())), preferred_element_type=jnp.float32)


def visible_keys(first, low, high, docs_row, docs_col):
    shape = (QUERY_BLOCK, high - low)
    key = lax.broadcasted_iota(jnp.int32, shape, 1) + low
    query = lax.broadcasted_iota(jnp.int32, shape, 0) + first
    return (key <= query) & (docs_row[:, low:high] == docs_col)


def layer_kernel(x, up, wa, we, routes, gates, doc_ids, shard_gains, cos, sin, block, grad, norm, ge_far, ga, gn, clip, **held):
    layer_body(
        types.SimpleNamespace(
            x=x, up=up, wa=wa, we=we, routes=routes, gates=gates, doc_ids=doc_ids, shard_gains=shard_gains,
            cos=cos, sin=sin,
            block=block, grad=grad, norm=norm, ge_far=ge_far, ga=ga, gn=gn, clip=clip, **held,
        )
    )


def layer_outputs(rows, local):
    f32 = jnp.float32
    shaped = jax.ShapeDtypeStruct
    deep = D // PLANE
    return [
        shaped((rows, D), jnp.bfloat16), shaped((rows, D), f32), shaped((1, 1), f32),
        shaped((local, deep, 3 * FF), f32), shaped((deep // SPAN, 3072), f32), shaped((8, rows), f32),
        shaped((1, 1), f32),
    ]


def layer_scratch(rows, local):
    f32, bf16 = jnp.float32, jnp.bfloat16
    held, sems = pltpu.VMEM, lambda *shape: pltpu.SemaphoreType.DMA(shape)
    deep = D // PLANE
    part = deep // SPAN
    blocks = held((SPAN, rows, D), bf16)
    quarter = held((LINE, rows, D), bf16)
    line = lambda parts: (sems(parts, LINE), sems(parts, LINE), sems(parts, SPAN))
    scatter = lambda parts: tuple(sems(parts, LINE) for _ in range(4))
    both = lambda *shape: (sems(*shape), sems(*shape))
    return dict(
        x_all=blocks, up_all=blocks, h1=blocks, o_all=blocks, h2=blocks, d=blocks, da_all=blocks,
        qkv=held((SPAN * rows, 256), bf16), lse=held((SPAN * rows, 128), f32),
        wq_out=held((SPAN, part, 256), bf16), w_mine=held((PLANE, SPAN, part, 256), bf16),
        wo_all=held((PLANE, LINE, 2, part, D), bf16), we_all=held((local, PLANE, deep, 3 * FF), bf16),
        o_own=held((SPAN, rows, 128), bf16),
        r_own=held((rows, D), f32),
        pack=held((SPAN, 8, rows), f32), pack_all=held((SPAN, 8, rows), f32), gain_sum=held((PLANE, 2, 8, 128), f32),
        cols=held((SPAN, rows, 128), f32), docs=held((8, SPAN * rows), f32), gains=held((8, D), f32),
        act=held((local, SPAN, rows, FF), bf16), dgu=held((local, SPAN, rows, 2 * FF), bf16),
        pair=quarter, out=quarter, inbox=quarter, own=held((rows, D), f32),
        y_pair=quarter, y_out=quarter, y_inbox=quarter, y_own=held((rows, D), f32),
        ge_in=held((local, PLANE - 1, deep, 3 * FF), bf16),
        do=held((SPAN, rows, 128), bf16), dkv=held((SPAN * rows, 128), f32), dqkv=held((SPAN * rows, 256), bf16),
        dr=held((rows, D), f32), gn_two=held((8, D), f32),
        ga_out=held((PLANE - 1, deep, 384), bf16), ga_in=held((PLANE - 1, deep, 384), bf16),
        gs=held((SPAN, part, 384), f32), gs_out=held((SPAN, part, 384), bf16), ga_all=held((SPAN, part, 384), bf16),
        gn_in=held((PLANE, 16, 128), f32), mix_in=held((SPAN, 24, 128), f32), sq_in=held((PLANE, 8, 128), f32),
        ge=held((local, deep, 3 * FF), f32), store=sems(local),
        x_sems=line(1), up_sems=line(PARTS), wo_sems=line(1), o_sems=line(PARTS), da_sems=line(PARTS),
        d_sems=scatter(PARTS), y_sems=scatter(1), h_sems=scatter(1),
        load=sems(local), pack_sems=both(SPAN), wq_sems=both(SPAN), wqd_sems=both(PLANE), gd_sems=both(PLANE),
        wod_sems=both(1, 4), wop_sems=both(PLANE), we_sems=both(local, 4), ge_sems=both(local, 6),
        ga_sems=both(PLANE), gn_sems=both(PLANE), gs_sems=both(SPAN), mix_sems=both(SPAN), sq_sems=both(PLANE),
    )


def layer_body(v):
    f32, bf16 = jnp.float32, jnp.bfloat16
    where = i, e, z, c = whereabouts()
    sibling = (i, z * 2 + 1 - c)
    rows, local, deep = v.x.shape[0], v.we_all.shape[0], v.ge.shape[1]
    length, size = rows * SPAN, rows // PARTS
    own_cols = piece(e, 128)
    live = []

    def go(*spec):
        copy = remote(*spec)
        copy.start()
        live.append(copy)

    def along(k):
        return lax.rem(i + k, PLANE)

    def across(k):
        return lax.rem(e + k, SPAN)

    def line(sems, slot, source):
        return LineGather(slot, source, where, sems)

    x_line = line(v.x_sems, lambda s, j: v.x_all.at[s], lambda j: v.x)
    up_line = line(v.up_sems, lambda s, j: v.up_all.at[s, piece(j, size)], lambda j: v.up.at[piece(j, size)])
    wo_line = line(
        v.wo_sems, lambda s, j: v.wo_all.at[i, s // 2, lax.rem(s, 2)], lambda j: v.wo_all.at[i, z, c]
    )
    o_line = line(
        v.o_sems,
        lambda s, j: v.o_all.at[:, piece(j, size), piece(s, 128)],
        lambda j: v.o_own.at[:, piece(j, size)],
    )
    da_line = line(
        v.da_sems, lambda s, j: v.da_all.at[s, piece(j, size)], lambda j: v.da_all.at[e, piece(j, size)]
    )
    we_plane = PlaneGather(where, lambda l, s, part: v.we_all.at[l, s, part], deep, v.we_sems)
    wo_plane = PlaneGather(where, lambda l, s, part: v.wo_all.at[s, part, c], LINE, v.wod_sems)
    ge_plane = PlaneScatter(we_plane, v.we_all, v.ge_in, v.ge_sems)
    d_scatter = LineScatter(v.d, where, v.pair, v.out, v.inbox, v.own, v.d_sems, size)
    y_scatter = LineScatter(v.o_all, where, v.y_pair, v.y_out, v.y_inbox, v.y_own, v.y_sems, rows)
    h_scatter = LineScatter(v.d, where, v.pair, v.out, v.inbox, v.own, v.h_sems, rows)

    loads = [pltpu.make_async_copy(v.we.at[l], v.ge.at[l], v.load.at[l]) for l in range(local)]
    for copy in loads:
        copy.start()
    results = [pltpu.make_async_copy(v.ge.at[l], v.ge_far.at[l], v.store.at[l]) for l in range(local)]
    barrier = pltpu.get_barrier_semaphore()
    for device in partners(i, e):
        pl.semaphore_signal(barrier, inc=1, device_id=device, device_id_type=pl.DeviceIdType.MESH)
    lane = lax.broadcasted_iota(jnp.int32, (2, rows), 1)
    index, few = i * SPAN + e, rows // v.shard_gains.shape[1]
    spread = jnp.concatenate([v.shard_gains[...]] * few, axis=1)
    spread = jnp.where(lane // (rows // few) == lax.rem(index, few), spread, 0.0)
    shared = [v.doc_ids[...].astype(f32), spread, jnp.zeros((3, rows), f32)]
    for g in range(SPAN):
        named = [
            jnp.sum(jnp.where(v.routes[...] == g * local + l, v.gates[...], 0.0), axis=0, keepdims=True)
            for l in range(local)
        ]
        v.pack[g] = jnp.concatenate(named + shared, axis=0)
    for g in range(SPAN):
        v.wq_out[g, :, :128] = v.wa[:, g * 128 : (g + 1) * 128].astype(bf16)
        key_value = [v.wa[:, first + g * HD : first + (g + 1) * HD] for first in (QD, QD + KVD)]
        v.wq_out[g, :, 128:] = jnp.concatenate(key_value, axis=1).astype(bf16)
    v.w_mine[i, e] = v.wq_out[e]
    v.wo_all[i, z, c] = v.wa[:, QKV:].astype(bf16)
    v.pack_all[e] = v.pack[e]
    v.x_all[e] = v.x[...]
    v.up_all[e] = v.up[...]
    pl.semaphore_wait(barrier, SPAN + PLANE - 2)
    for k in range(1, SPAN):
        go(v.pack.at[across(k)], v.pack_all.at[e], v.pack_sems[0].at[k], v.pack_sems[1].at[e], (i, across(k)))
    for k in range(1, SPAN):
        go(v.wq_out.at[across(k)], v.w_mine.at[i, e], v.wq_sems[0].at[k], v.wq_sems[1].at[e], (i, across(k)))
    wo_line.start(0)
    x_line.start(0)
    loads[0].wait()
    v.we_all[0, i] = v.ge[0].astype(bf16)
    we_plane.start(0)

    for k in range(1, SPAN):
        slot = v.pack_all.at[across(k)]
        remote(slot, slot, v.pack_sems[0].at[k], v.pack_sems[1].at[across(k)], sibling).wait_recv()
    for half in range(2):
        summed = v.pack_all[4 * half]
        for s in range(1, 4):
            summed = summed + v.pack_all[4 * half + s]
        v.gain_sum[i, half] = summed
    for k in range(1, PLANE):
        go(v.gain_sum.at[i], v.gain_sum.at[i], v.gd_sems[0].at[k], v.gd_sems[1].at[i], (along(k), e))
    for k in range(1, SPAN):
        slot = v.w_mine.at[i, across(k)]
        remote(slot, slot, v.wq_sems[0].at[k], v.wq_sems[1].at[across(k)], sibling).wait_recv()
    for k in range(1, PLANE):
        go(v.w_mine.at[i], v.w_mine.at[i], v.wqd_sems[0].at[k], v.wqd_sems[1].at[i], (along(k), e))
    loads[1].wait()
    v.we_all[1, i] = v.ge[1].astype(bf16)
    for s in range(SPAN):
        block = v.pack_all[s]
        tall = jnp.concatenate([block, jnp.zeros((rows - block.shape[0], rows), f32)], axis=0)
        v.cols[s] = tall.T
        v.docs[:, s * rows : (s + 1) * rows] = block
    for k in range(1, PLANE):
        slot = v.gain_sum.at[along(k)]
        remote(slot, slot, v.gd_sems[0].at[k], v.gd_sems[1].at[along(k)], sibling).wait_recv()
    for tile in range(2 * PLANE):
        v.gains[:, tile * 128 : (tile + 1) * 128] = v.gain_sum[tile // 2, tile % 2].astype(bf16).astype(f32)
    gain_one, gain_two = v.gains[3:4], v.gains[4:5]

    def first_norm(s):
        values = v.x_all[s].astype(f32)
        v.h1[s] = (values * rms_rows(values) * gain_one).astype(bf16)

    wo_line.forward_all(0)
    wo_plane.start(0)
    first_norm(e)
    for k in (2, 1, 3):
        x_line.forward(0, k)
        first_norm(x_line.near(k))
    up_line.start(0)
    up_line.start(1)
    we_plane.forward(0)
    x_line.wait(0, x_line.sibling())
    first_norm(x_line.sibling())
    for k in range(1, LINE):
        x_line.wait(0, x_line.far(k))
        first_norm(x_line.far(k))
    for k in range(1, PLANE):
        slot = v.w_mine.at[along(k)]
        remote(slot, slot, v.wqd_sems[0].at[k], v.wqd_sems[1].at[along(k)], sibling).wait_recv()

    weights = v.w_mine[...].reshape(D, 256)
    lane = lax.broadcasted_iota(jnp.int32, (QUERY_BLOCK, 128), 1)

    def tables(first):
        cosine, sine = v.cos[first : first + QUERY_BLOCK], v.sin[first : first + QUERY_BLOCK]
        return cosine, sine, jnp.where(lane < HD, cosine, 1.0), jnp.where(lane < HD, sine, 0.0)

    for first in range(0, length, QUERY_BLOCK):
        span = slice(first, first + QUERY_BLOCK)
        slots = slice(first // rows, (first + QUERY_BLOCK) // rows)
        raw = dot(v.h1[slots].reshape(QUERY_BLOCK, D), weights, NN)
        q_cos, q_sin, kv_cos, kv_sin = tables(first)
        q_raw, kv_raw = raw[:, :128], raw[:, 128:]
        v.qkv[span, :128] = (q_raw * q_cos + half_turn_tile(q_raw) * q_sin).astype(bf16)
        v.qkv[span, 128:] = (kv_raw * kv_cos + half_turn_tile(kv_raw) * kv_sin).astype(bf16)


    def block_masks(first):
        low, high = max(0, first - length // 2), first + QUERY_BLOCK
        slots = slice(first // rows, (first + QUERY_BLOCK) // rows)
        docs_col = v.cols[slots, :, 2:3].reshape(QUERY_BLOCK, 1)
        return low, high, slots, visible_keys(first, low, high, v.docs[2:3], docs_col)

    for first in range(0, length, QUERY_BLOCK):
        low, high, slots, visible = block_masks(first)
        span = slice(first, first + QUERY_BLOCK)
        outs, logs = [], []
        for head in range(2):
            q = v.qkv[span, head * HD : (head + 1) * HD]
            scores = dot(q, v.qkv[low:high, 128:192], NT) * HD**-0.5
            scores = jnp.where(visible, scores, -1e30)
            peak = jnp.max(scores, axis=-1, keepdims=True)
            raw = jnp.exp(scores - peak)
            total = jnp.sum(raw, axis=-1, keepdims=True)
            probs = raw * (1.0 / total)
            logs.append(peak + jnp.log(total))
            outs.append(dot(probs.astype(bf16), v.qkv[low:high, 192:256], NN))
        both = jnp.concatenate(outs, axis=1).astype(bf16).reshape(-1, rows, 128)
        v.o_own[slots] = both
        v.o_all[slots, :, own_cols] = both
        v.lse[span] = jnp.where(lane == 0, logs[0], logs[1])
    o_line.start(0)
    o_line.start(1)
    up_line.start(2)
    o_line.start(2)
    up_line.start(3)
    o_line.start(3)
    wo_plane.forward(0)
    we_plane.start(1)

    wo_line.rest(0)
    wo_plane.rest(0)
    for k in range(1, PLANE):
        here = v.wo_all.at[along(k), :, c]
        go(here, here, v.wop_sems[0].at[k], v.wop_sems[1].at[along(k)], sibling)
    for k in range(1, PLANE):
        far = v.wo_all.at[along(k), :, 1 - c]
        remote(far, far, v.wop_sems[0].at[k], v.wop_sems[1].at[along(k)], sibling).wait_recv()

    def second_norm(j):
        part = piece(j, size)
        w_out = v.wo_all[...].reshape(D, D)
        branch = dot(v.o_all[:, part].reshape(-1, D), w_out, NT)
        values = v.x_all[:, part].reshape(-1, D).astype(f32) + branch
        split = values.reshape(SPAN, size, D)
        v.r_own[part] = sum(jnp.where(e == s, split[s], 0.0) for s in range(SPAN))
        v.h2[:, part] = (values * rms_rows(values) * gain_two).astype(bf16).reshape(SPAN, size, D)

    def gate_of(l, part):
        return v.cols[:, part, l : l + 1].reshape(-1, 1)

    def expert(l, j):
        part = piece(j, size)
        weights = v.we_all[l].reshape(D, 3 * FF)
        gate = gate_of(l, part)
        routed = gate > 0
        gu = dot(v.h2[:, part].reshape(-1, D), weights[:, : 2 * FF], NN)
        g, u = gu[:, :FF], gu[:, FF:]
        sig = 1.0 / (1.0 + jnp.exp(-g))
        act = jnp.where(routed, g * sig * u, 0.0).astype(bf16)
        v.act[l, :, part] = act.reshape(SPAN, size, FF)
        dy = (gate * v.up_all[:, part].reshape(-1, D).astype(f32)).astype(bf16)
        dact = dot(dy, weights[:, 2 * FF :], NN)
        dg = dact * u * sig * (1.0 + g * (1.0 - sig))
        du = dact * g * sig
        dgu = jnp.where(routed, jnp.concatenate([dg, du], axis=1), 0.0).astype(bf16)
        v.dgu[l, :, part] = dgu.reshape(SPAN, size, 2 * FF)
        d = dot(dgu, weights[:, : 2 * FF], NT).astype(bf16)
        if l > 0:
            summed = v.d[:, part].reshape(-1, D).astype(f32) + d.astype(f32)
            v.d[:, part] = summed.astype(bf16).reshape(SPAN, size, D)
            d_scatter.start(j)
        y = dot(act, weights[:, 2 * FF :], NT).astype(bf16)
        if l == 0:
            v.d[:, part] = d.reshape(SPAN, size, D)
            v.o_all[:, part] = y.reshape(SPAN, size, D)
        else:
            y = gate_of(0, part) * v.o_all[:, part].reshape(-1, D).astype(f32) + gate * y.astype(f32)
            v.o_all[:, part] = y.astype(bf16).reshape(SPAN, size, D)

    we_plane.rest(0)

    def first_round(j, carry):
        @pl.when(j == PARTS - 1)
        def _():
            we_plane.forward(1)

        @pl.when(j < PARTS)
        def _():
            o_line.forward_all(j)
            up_line.forward_all(j)

        @pl.when(j > 0)
        def _():
            o_line.drain(j - 1)
            expert(0, j - 1)

        @pl.when(j < PARTS)
        def _():
            o_line.rest(j)
            up_line.rest(j)
            second_norm(j)

        return carry

    lax.fori_loop(0, PARTS + 1, first_round, 0)
    we_plane.rest(1)

    def expert_chunk(l, there):
        span = piece(there, deep)
        inward = dot(v.h2[:, :, span].reshape(length, deep), v.dgu[l].reshape(length, 2 * FF), TN)
        gate = v.cols[:, :, l : l + 1].reshape(length, 1)
        dy = (gate * v.up_all[:, :, span].reshape(length, deep).astype(f32)).astype(bf16)
        return inward, dot(dy, v.act[l].reshape(length, FF), TN)

    def send_chunk(l, chunk):
        inward, down = expert_chunk(l, (we_plane.far, we_plane.x, we_plane.y)[chunk])
        v.we_all[l, chunk, :, : 2 * FF] = inward.astype(bf16)
        v.we_all[l, chunk, :, 2 * FF :] = down.astype(bf16)
        ge_plane.start(l, chunk)

    def second_round(j, carry):
        @pl.when((j > 0) & (j <= PARTS))
        def _():
            d_scatter.fold(j - 1)

        @pl.when(j > 1)
        def _():
            d_scatter.fold_late(j - 2)

        @pl.when(j < PARTS)
        def _():
            expert(1, j)

        @pl.when(j == 0)
        def _():
            we_plane.drain(0)

        for chunk in range(3):
            pl.when(j == chunk)(lambda chunk=chunk: send_chunk(0, chunk))

        return carry

    lax.fori_loop(0, PARTS + 2, second_round, 0)
    y_scatter.start(0)
    we_plane.drain(1)

    def keep_chunk(l):
        inward, down = expert_chunk(l, i)
        v.ge[l, :, : 2 * FF] = inward
        v.ge[l, :, 2 * FF :] = down

    v.gn_two[...] = jnp.zeros_like(v.gn_two)

    def second_back(j):
        part = piece(j, size)
        back, shares = norm_back(v.r_own[part], gain_two, d_scatter.total(j))
        dr = v.up_all[e, part].astype(f32) + back
        v.dr[part] = dr
        v.gn_two[:1] += jnp.sum(shares, axis=0, keepdims=True)
        v.da_all[e, part] = dr.astype(bf16)
        da_line.start(j)

    second_back(0)
    send_chunk(1, 0)
    ge_plane.combine(0)
    send_chunk(1, 1)
    second_back(1)
    send_chunk(1, 2)
    second_back(2)
    ge_plane.combine(1)
    second_back(3)
    da_line.forward_all(0)
    da_line.forward_all(1)
    keep_chunk(0)
    da_line.forward_all(2)
    keep_chunk(1)
    da_line.forward_all(3)
    y_scatter.fold(0)
    wo_mine = v.wo_all[:, :, :, :, own_cols].reshape(D, 128)
    for j in range(PARTS):
        da_line.rest(j)
        part = piece(j, size)
        do = dot(v.da_all[:, part].reshape(-1, D), wo_mine, NN).astype(bf16)
        v.do[:, part] = do.reshape(SPAN, size, 128)

    v.dkv[...] = jnp.zeros_like(v.dkv)
    for first in range(0, length, QUERY_BLOCK):
        low, high, slots, visible = block_masks(first)
        span = slice(first, first + QUERY_BLOCK)
        keys, values = v.qkv[low:high, 128:192], v.qkv[low:high, 192:256]
        do_both = v.do[slots].reshape(QUERY_BLOCK, 128)
        dqs, dk, dv = [], 0.0, 0.0
        for head in range(2):
            q = v.qkv[span, head * HD : (head + 1) * HD]
            do = do_both[:, head * HD : (head + 1) * HD]
            scores = dot(q, keys, NT) * HD**-0.5
            probs = jnp.exp(jnp.where(visible, scores - v.lse[span, head : head + 1], -1e30))
            dp = dot(do, values, NT)
            delta = jnp.sum(probs * dp, axis=-1, keepdims=True)
            ds = (probs * (dp - delta)).astype(bf16)
            dqs.append(dot(ds, keys, NN))
            dk = dk + dot(ds, q, TN)
            dv = dv + dot(probs.astype(bf16), do, TN)
        v.dkv[low:high] += jnp.concatenate([dk * HD**-0.5, dv], axis=1)
        dq = jnp.concatenate(dqs, axis=1) * HD**-0.5
        cosine, sine = v.cos[span], v.sin[span]
        v.dqkv[span, :128] = (dq * cosine - half_turn_tile(dq) * sine).astype(bf16)
    for first in range(0, length, QUERY_BLOCK):
        span = slice(first, first + QUERY_BLOCK)
        dkv = v.dkv[span]
        _, _, cosine, sine = tables(first)
        v.dqkv[span, 128:] = (dkv * cosine - half_turn_tile(dkv) * sine).astype(bf16)

    y_scatter.fold_late(0)

    o = v.o_own[...].reshape(length, 128)
    dqkv = v.dqkv[...]

    def rows_copy(k):
        return remote(v.ga_out.at[k - 1], v.ga_in.at[k - 1], v.ga_sems[0].at[k], v.ga_sems[1].at[k], (along(k), e))

    for k in (2, 1, 3, 0):
        span = piece(along(k), deep)
        projections = dot(v.h1[:, :, span].reshape(length, deep), dqkv, TN)
        output = dot(v.da_all[:, :, span].reshape(length, deep), o, TN)
        if k == 0:
            v.gs[:, :, :256] = projections.reshape(SPAN, -1, 256)
            v.gs[:, :, 256:] = output.reshape(SPAN, -1, 128)
        else:
            v.ga_out[k - 1, :, :256] = projections.astype(bf16)
            v.ga_out[k - 1, :, 256:] = output.astype(bf16)
            rows_copy(k).start()

    for j in range(PARTS):
        d_scatter.drain(j)
    gn_one = jnp.zeros((1, D), f32)
    order = (1, 3, 2, 0)
    for n, k in enumerate(order):
        chip = lax.rem(z + k, LINE)
        slots = piece(chip, 2)
        dh = dot(v.dqkv[piece(chip, 2 * rows)], weights, NT)
        values = v.x_all[slots].reshape(2 * rows, D).astype(f32)
        gn_one = gn_one + jnp.sum(dh * values * rms_rows(values), axis=0, keepdims=True)
        v.d[slots] = dh.astype(bf16).reshape(2, rows, D)
        h_scatter.start_one(0, k)
        if n > 0:
            h_scatter.fold_one(0, order[n - 1])
    h_scatter.fold_one(0, order[-1])
    both_gains = jnp.concatenate([gn_one, v.gn_two[:1]], axis=0)
    v.gn_in[i] = jnp.concatenate([both_gains[:, t : t + 128] for t in range(0, D, 128)], axis=0)
    for k in range(1, PLANE):
        go(v.gn_in.at[i], v.gn_in.at[i], v.gn_sems[0].at[k], v.gn_sems[1].at[i], (along(k), e))
    v.block[...] = (v.r_own[...] + y_scatter.total(0)).astype(bf16)
    h_scatter.fold_late(0)

    for k in (2, 1, 3):
        rows_copy(k).wait_recv()
        v.gs[...] += v.ga_in[k - 1].reshape(v.gs.shape).astype(f32)
    squares = jnp.sum(v.gs[...] * v.gs[...])
    v.gs_out[...] = v.gs[...].astype(bf16)
    v.ga_all[e] = v.gs_out[e]
    for l in range(local):
        ge_plane.rest(l)
        for first in range(0, deep, 64):
            span = slice(first, first + 64)
            summed = v.ge[l, span]
            for chunk in (1, 2):
                summed = summed + v.ge_in[l, chunk, span].astype(f32)
            v.ge[l, span] = summed
            squares = squares + jnp.sum(summed * summed)
        results[l].start()

    for k in range(1, PLANE):
        slot = v.gn_in.at[along(k)]
        remote(slot, slot, v.gn_sems[0].at[k], v.gn_sems[1].at[along(k)], sibling).wait_recv()
    gains = v.gn_in[0] + v.gn_in[1] + v.gn_in[2] + v.gn_in[3]
    v.mix_in[e] = jnp.concatenate([gains, jnp.full((8, 128), squares)], axis=0)
    for k in range(1, SPAN):
        go(v.mix_in.at[e], v.mix_in.at[e], v.mix_sems[0].at[k], v.mix_sems[1].at[e], (i, across(k)))
    for k in range(1, SPAN):
        go(v.gs_out.at[across(k)], v.ga_all.at[e], v.gs_sems[0].at[k], v.gs_sems[1].at[e], (i, across(k)))
    for k in range(1, SPAN):
        slot = v.mix_in.at[across(k)]
        remote(slot, slot, v.mix_sems[0].at[k], v.mix_sems[1].at[across(k)], sibling).wait_recv()
    mixed = v.mix_in[0]
    for s in range(1, SPAN):
        mixed = mixed + v.mix_in[s]
    v.sq_in[i] = mixed[16:]
    for k in range(1, PLANE):
        go(v.sq_in.at[i], v.sq_in.at[i], v.sq_sems[0].at[k], v.sq_sems[1].at[i], (along(k), e))
    gain_squares = jnp.sum(mixed[:16] * mixed[:16])
    row = lax.broadcasted_iota(jnp.int32, (16, 128), 0)
    pick = lambda n: jnp.sum(jnp.where(row == index // few * 2 + n, mixed[:16], 0.0), axis=0, keepdims=True)
    own_gains = jnp.concatenate([pick(0), pick(1), jnp.zeros((6, 128), f32)], axis=0)
    v.gn[...] = pltpu.roll(own_gains, rows - lax.rem(index, few) * (rows // few), 1)
    for k in range(1, SPAN):
        slot = v.ga_all.at[across(k)]
        remote(slot, slot, v.gs_sems[0].at[k], v.gs_sems[1].at[across(k)], sibling).wait_recv()
    for g in range(SPAN):
        v.ga[:, g * 128 : (g + 1) * 128] = v.ga_all[g, :, :128].astype(f32)
        v.ga[:, QKV + g * 128 : QKV + (g + 1) * 128] = v.ga_all[g, :, 256:].astype(f32)
    for g in range(0, SPAN, 2):
        for first, own in ((QD, 128), (QD + KVD, 192)):
            heads = [v.ga_all[g + n, :, own : own + HD] for n in range(2)]
            v.ga[:, first + g * HD : first + (g + 2) * HD] = jnp.concatenate(heads, axis=1).astype(f32)
    for k in range(1, PLANE):
        slot = v.sq_in.at[along(k)]
        remote(slot, slot, v.sq_sems[0].at[k], v.sq_sems[1].at[along(k)], sibling).wait_recv()
    norm = jnp.sqrt(v.sq_in[0] + v.sq_in[1] + v.sq_in[2] + v.sq_in[3] + gain_squares)[:1, :1]
    v.norm[...] = norm
    v.clip[...] = jnp.minimum(1.0, CLIP_NORM / (norm + 1e-06))

    back, _ = norm_back(v.x_all[e].astype(f32), gain_one, h_scatter.total(0))
    v.grad[...] = v.dr[...] + back
    for copy in results:
        copy.wait()
    for copy in live:
        copy.wait_send()
    for k in (2, 1, 3):
        rows_copy(k).wait_send()
    for l in range(local):
        ge_plane.drain(l)
    for item in (x_line, wo_line, wo_plane, y_scatter, h_scatter):
        item.drain(0)
    for j in range(PARTS):
        up_line.drain(j)
        da_line.drain(j)


def call_layer(*args):
    vmem, anywhere = pl.BlockSpec(memory_space=pltpu.VMEM), pl.BlockSpec(memory_space=pl.ANY)
    rows, local = args[0].shape[0], args[3].shape[0]
    outs = layer_outputs(rows, local)
    return pl.pallas_call(
        layer_kernel,
        out_shape=outs,
        in_specs=[anywhere if n == 3 else vmem for n in range(len(args))],
        out_specs=[anywhere if n == 3 else vmem for n in range(len(outs))],
        scratch_shapes=layer_scratch(rows, local),
        compiler_params=pltpu.CompilerParams(
            collective_id=0, has_side_effects=True, vmem_limit_bytes=63 * 2**20 + 2**19
        ),
        name="layer",
    )(*args)


def small_kernel(clip, rates, gn, block_in, grad_in, wa, ma, va, ga, wg, mg, vg, block, grad, *outs):
    c, one, two = clip[...], rates[:1, :1], rates[:1, 1:2]

    def update(refs, gradient, decay, rate, results):
        w, g = refs[0][...], gradient * c
        first = BETA_ONE * refs[1][...] + (1.0 - BETA_ONE) * g
        second = BETA_TWO * refs[2][...] + (1.0 - BETA_TWO) * g * g
        step = (first * one) / (jnp.sqrt(second * two) + ADAM_EPSILON)
        results[0][...] = w - rate * (step + decay * w)
        results[1][...] = first
        results[2][...] = second

    update((wa, ma, va), ga[...], WEIGHT_DECAY, LEARN_RATE, outs[:3])
    update((wg, mg, vg), gn[: wg.shape[0], : wg.shape[1]], 0.0, GAIN_RATE, outs[3:])
    block[...] = block_in[...]
    grad[...] = grad_in[...]


def call_small(clip, rates, gn, block, grad, attn, ga, gains):
    vmem = pl.BlockSpec(memory_space=pltpu.VMEM)
    outs = [jax.ShapeDtypeStruct(a.shape, a.dtype) for a in (block, grad, *attn, *gains)]
    args = (clip, rates, gn, block, grad, *attn, ga, *gains)
    return pl.pallas_call(
        small_kernel,
        out_shape=outs,
        in_specs=[vmem] * len(args),
        out_specs=[vmem] * len(outs),
        compiler_params=pltpu.CompilerParams(vmem_limit_bytes=63 * 2**20 + 2**19),
        name="small",
    )(*args)


def fast_body(
    activations,
    doc_ids,
    routes,
    gate_weights,
    cotangent,
    step_count,
    w_attn,
    norm_gains,
    w_expert,
    first_attn,
    second_attn,
    first_gains,
    second_gains,
    first_expert,
    second_expert,
):
    cosine, sine = head_tables(activations.shape[1] * lax.axis_size("expert"))
    block, input_total, norm, grad_expert, grad_attn, gn, clip = call_layer(
        activations[0], cotangent[0], w_attn, w_expert, routes[0].T, gate_weights[0].T, doc_ids, norm_gains.T,
        cosine, sine,
    )
    grad_norm = norm.reshape(())
    steps = step_count.astype(jnp.float32)
    rates = 1.0 / (1.0 - jnp.stack([BETA_ONE**steps, BETA_TWO**steps]))[None]
    block, input_total, *small = call_small(
        clip, rates, gn, block, input_total,
        (w_attn, first_attn, second_attn), grad_attn, (norm_gains.T, first_gains.T, second_gains.T),
    )
    attn, gain = small[:3], small[3:]
    expert = adam_update(
        w_expert, first_expert, second_expert, grad_expert * clip[None], steps, WEIGHT_DECAY, LEARN_RATE
    )
    return (block[None], input_total[None], grad_norm, *attn, *[a.T for a in gain], *expert)


def solution(mesh):
    in_specs = (
        P("dp", "expert", None),
        P("dp", "expert"),
        P("dp", "expert", None),
        P("dp", "expert", None),
        P("dp", "expert", None),
        P(),
        P(("dp", "expert"), None),
        P(("dp", "expert"), None),
        P("expert", "dp", None),
        P(("dp", "expert"), None),
        P(("dp", "expert"), None),
        P(("dp", "expert"), None),
        P(("dp", "expert"), None),
        P("expert", "dp", None),
        P("expert", "dp", None),
    )
    out_specs = (
        P("dp", "expert", None),
        P("dp", "expert", None),
        P(),
        P(("dp", "expert"), None),
        P(("dp", "expert"), None),
        P(("dp", "expert"), None),
        P(("dp", "expert"), None),
        P(("dp", "expert"), None),
        P(("dp", "expert"), None),
        P("expert", "dp", None),
        P("expert", "dp", None),
        P("expert", "dp", None),
    )
    body = fast_body if fits(mesh) else general_body
    return jax.shard_map(body, mesh=mesh, in_specs=in_specs, out_specs=out_specs, check_vma=False)
```
